32 devices in a mesh: dp: 8 (over z, x), mp: 4 (over y, core).
Axes of the slice: x: 2, y: 2, z: 4, core: 2. Of those that a mesh axis runs over, the one named last changes fastest.
Arguments:
- block_input: bfloat16 [24576, 1024], P(('dp', 'mp')), may hold values from -6 to 6
- sequence_lengths: int32 [8, 6], P('dp'), may hold values from 0 to 1024, as said below
- first_gain: float32 [1024], replicated, may hold values from 0.5 to 1.5
- first_shift: float32 [1024], replicated, may hold values from -3 to 3
- second_gain: float32 [1024], replicated, may hold values from 0.5 to 1.5
- second_shift: float32 [1024], replicated, may hold values from -3 to 3
- triple_weight: bfloat16 [1024, 3072], P(None, 'mp'), may hold values from -0.1875 to 0.1875
- triple_left: bfloat16 [1024, 128], replicated, may hold values from -0.1875 to 0.1875
- triple_right: bfloat16 [128, 3072], replicated, may hold values from -0.25 to 0.25
- output_weight: bfloat16 [1024, 1024], P('mp'), may hold values from -0.5 to 0.5
- output_left: bfloat16 [1024, 128], replicated, may hold values from -0.5 to 0.5
- output_right: bfloat16 [128, 1024], replicated, may hold values from -0.25 to 0.25
- expand_weight: bfloat16 [1024, 4096], P(None, 'mp'), may hold values from -0.1875 to 0.1875
- expand_left: bfloat16 [1024, 128], replicated, may hold values from -0.1875 to 0.1875
- expand_right: bfloat16 [128, 4096], replicated, may hold values from -0.25 to 0.25
- shrink_weight: bfloat16 [4096, 1024], P('mp'), may hold values from -0.09375 to 0.09375
- shrink_left: bfloat16 [4096, 128], replicated, may hold values from -0.09375 to 0.09375
- shrink_right: bfloat16 [128, 1024], replicated, may hold values from -0.25 to 0.25
- cotangent: bfloat16 [24576, 1024], P(('dp', 'mp')), may hold values from -6 to 6
Outputs:
- block_output: bfloat16 [24576, 1024], P(('dp', 'mp'))
- input_gradient: float32 [24576, 1024], P(('dp', 'mp'))
- first_gain_gradient: float32 [1024], replicated
- first_shift_gradient: float32 [1024], replicated
- second_gain_gradient: float32 [1024], replicated
- second_shift_gradient: float32 [1024], replicated
- triple_left_gradient: float32 [1024, 128], replicated
- triple_right_gradient: float32 [128, 3072], replicated
- output_left_gradient: float32 [1024, 128], replicated
- output_right_gradient: float32 [128, 1024], replicated
- expand_left_gradient: float32 [1024, 128], replicated
- expand_right_gradient: float32 [128, 4096], replicated
- shrink_left_gradient: float32 [4096, 128], replicated
- shrink_right_gradient: float32 [128, 1024], replicated
The draws below stay inside these ranges and needn't reach their ends.
Inputs may be any that keep to these rules, and one draw needn't show every extreme that they name: `sequence_lengths`: row g lists the lengths of the sequences of group g in order, each 512 or 1024, then zeros; every row sums to 3072 and holds at least one sequence of 1024.
All inputs are finite; a program needn't handle non-finite values.
Results may differ from the reference program's by a relative error of at most 0.012.
The reference program's roundings to bfloat16 on the way count: a program that leaves them out, or rounds other values in their place, can miss the bound.
Values may be sent and summed in bfloat16 or wider, within the bound.
A program may use at most 256 MiB of HBM per device.

```python
import math
import jax
import jax.numpy as jnp
from jax import lax

D = 1024
HEADS = 16
HEAD_DIM = 64
ROT = 16
FF = 4096
RANK = 128
SHORT = 512
TOK_GRP = 3072
SLOTS = 6
TOKENS = 24576


def draw_sequence_lengths(key, part):
    key = jax.random.fold_in(key, 11)
    groups = TOKENS // TOK_GRP
    pair_count = TOK_GRP // (2 * SHORT)
    bit_key, pick_key = jax.random.split(key)
    long_bits = jax.random.randint(bit_key, (groups, pair_count), 0, 2)
    forced = jax.random.randint(pick_key, (groups, 1), 0, pair_count)
    long_bits = jnp.where(jnp.arange(pair_count)[None, :] == forced, 1, long_bits)
    leading = jnp.where(long_bits == 1, 2 * SHORT, SHORT)
    trailing = jnp.where(long_bits == 1, 0, SHORT)
    raw_lengths = jnp.stack([leading, trailing], axis=-1).reshape(groups, 2 * pair_count)
    order_index = jnp.argsort((raw_lengths == 0).astype(jnp.int32), axis=-1, stable=True)
    return jnp.take_along_axis(raw_lengths, order_index, axis=-1).astype(jnp.int32)


def block_scale(own_key, dims, pieces, low, top_value):
    level = 1.0
    for position, blocks in pieces:
        heights = jax.random.uniform(jax.random.fold_in(jax.random.fold_in(own_key, 6), position), (blocks,), jnp.float32, low / len(pieces), top_value / len(pieces))
        level = level * jnp.repeat(jnp.exp(heights), dims[position] // blocks).reshape((-1,) + (1,) * (len(dims) - 1 - position))
    return level


def normal_values(stream_key, dims, width, limit, cuts=(), held_as=jnp.bfloat16):
    entries = jax.random.normal(stream_key, dims, jnp.float32) * width
    if len(cuts) > 0:
        entries = block_scale(stream_key, dims, cuts, -0.22, 0.18) * entries
    return jnp.clip(entries, min=-limit, max=limit).astype(held_as)


def setup_inputs(seed: int = 0) -> dict:
    splits = jax.random.split(jax.random.key(seed), 20)
    return {
        "block_input": normal_values(splits[0], (TOKENS, D), 1.0, 6.0, ((0, 32),)),
        "sequence_lengths": draw_sequence_lengths(jax.random.fold_in(splits[19], 71), 0),
        "first_gain": jnp.clip(1.0 + 0.1 * jax.random.normal(splits[2], (D,), jnp.float32), 0.5, 1.5),
        "first_shift": normal_values(splits[3], (D,), 0.5, 3.0, (), jnp.float32),
        "second_gain": jnp.clip(1.0 + 0.1 * jax.random.normal(splits[4], (D,), jnp.float32), 0.5, 1.5),
        "second_shift": normal_values(splits[5], (D,), 0.5, 3.0, (), jnp.float32),
        "triple_weight": normal_values(splits[6], (D, 3 * D), D ** -0.5, 0.1875, ((1, 4),)),
        "triple_left": normal_values(splits[7], (D, RANK), D ** -0.5, 0.1875),
        "triple_right": normal_values(splits[8], (RANK, 3 * D), (4 * RANK) ** -0.5, 0.25),
        "output_weight": normal_values(splits[9], (D, D), (D // 8) ** -0.5, 0.5, ((0, 4),)),
        "output_left": normal_values(splits[10], (D, RANK), (D // 8) ** -0.5, 0.5),
        "output_right": normal_values(splits[11], (RANK, D), (4 * RANK) ** -0.5, 0.25),
        "expand_weight": normal_values(splits[12], (D, FF), D ** -0.5, 0.1875, ((1, 4),)),
        "expand_left": normal_values(splits[13], (D, RANK), D ** -0.5, 0.1875),
        "expand_right": normal_values(splits[14], (RANK, FF), (4 * RANK) ** -0.5, 0.25),
        "shrink_weight": normal_values(splits[15], (FF, D), FF ** -0.5, 0.09375, ((0, 4),)),
        "shrink_left": normal_values(splits[16], (FF, RANK), FF ** -0.5, 0.09375),
        "shrink_right": normal_values(splits[17], (RANK, D), (4 * RANK) ** -0.5, 0.25),
        "cotangent": normal_values(splits[18], (TOKENS, D), 1.0, 6.0, ((0, 32),)),
    }


EPS = 1e-05
HIGHEST = lax.Precision.HIGHEST

@jax.custom_vjp
def low(v):
    return lax.optimization_barrier(v.astype(jnp.bfloat16)).astype(jnp.float32)

@jax.custom_vjp
def low_back(v):
    return v

def low_keep(v):
    return (low(v), None)

def low_pass(kept, grad):
    return (grad,)

def back_keep(v):
    return (v, None)

def back_low(kept, grad):
    return (low(grad),)
low.defvjp(low_keep, low_pass)
low_back.defvjp(back_keep, back_low)

def matmul(former, latter):
    return jnp.dot(former, latter, precision=HIGHEST, preferred_element_type=jnp.float32)

def layer_norm(values, norm_gain, norm_shift):
    center = values - lax.optimization_barrier(jnp.mean(values, axis=-1, keepdims=True))
    spread = lax.optimization_barrier(jnp.mean(center * center, axis=-1, keepdims=True))
    return center * lax.rsqrt(spread + EPS) * norm_gain + norm_shift

def find_flags(group_lengths):
    seq_ends = jnp.cumsum(group_lengths, dtype=jnp.int32)
    starts = seq_ends - group_lengths
    block_starts = jnp.arange(SLOTS, dtype=jnp.int32) * SHORT
    begins = jnp.any((starts[None, :] == block_starts[:, None]) & (group_lengths[None, :] > 0), axis=1)
    return jnp.where(begins, 0, 1).astype(jnp.int32)

def rotary_tables(continues):
    row_index = jnp.arange(TOK_GRP, dtype=jnp.int32)
    positions = row_index % SHORT + SHORT * jnp.repeat(continues, SHORT)
    half_rot = ROT // 2
    frequency = jnp.exp(jnp.arange(half_rot, dtype=jnp.float32) * (-2.0 * math.log(10000.0) / ROT))
    angles = positions.astype(jnp.float32)[:, None] * frequency[None, :]
    return (jnp.cos(angles), jnp.sin(angles))

def rotate(head_rows, cosine, sine_table):
    half_rot = ROT // 2
    first_half = head_rows[:, :, :half_rot]
    second_half = head_rows[:, :, half_rot:ROT]
    cosine = cosine[:, None, :]
    sine_table = sine_table[:, None, :]
    return jnp.concatenate([first_half * cosine - second_half * sine_table, second_half * cosine + first_half * sine_table, head_rows[:, :, ROT:]], axis=2)

def causal_mask(continued):
    query_index = jnp.arange(SHORT, dtype=jnp.int32)[:, None]
    key_index = jnp.arange(2 * SHORT, dtype=jnp.int32)[None, :]
    return jnp.where(key_index < SHORT, continued > 0, key_index - SHORT <= query_index)

def key_windows(key_rows):
    padded = jnp.concatenate([jnp.zeros((SHORT,) + key_rows.shape[1:], key_rows.dtype), key_rows], axis=0)
    blocks = padded.reshape((SLOTS + 1, SHORT) + key_rows.shape[1:])
    return jnp.concatenate([blocks[:-1], blocks[1:]], axis=1)

def attend(queries, key_rows, value_rows, continues):
    score_scale = HEAD_DIM ** (-0.5)

    def one_block(block_items):
        query_blk, key_win, value_win, continued = block_items
        scores = jnp.einsum('qhd,khd->hqk', query_blk, key_win, precision=HIGHEST) * score_scale
        scores = low_back(scores)
        scores = jnp.where(causal_mask(continued)[None], scores, -1e+30)
        row_peak = lax.optimization_barrier(jnp.max(scores, axis=-1, keepdims=True))
        exp_scores = jnp.exp(scores - row_peak)
        weights_low = low(exp_scores / lax.optimization_barrier(jnp.sum(exp_scores, axis=-1, keepdims=True)))
        return jnp.einsum('hqk,khd->qhd', weights_low, value_win, precision=HIGHEST)
    query_blocks = queries.reshape((SLOTS, SHORT) + queries.shape[1:])
    attended = lax.map(jax.checkpoint(one_block), (query_blocks, key_windows(key_rows), key_windows(value_rows), continues))
    return attended.reshape(queries.shape)

def group_forward(group_input, group_lengths, frozen, trainable):
    triple_weight, output_weight, expand_weight, shrink_weight = frozen
    first_gain, first_shift, second_gain, second_shift, triple_left, triple_right, output_left, output_right, expand_left, expand_right, shrink_left, shrink_right = trainable
    continues = find_flags(group_lengths)
    cosine, sine_table = rotary_tables(continues)
    normed_first = low(layer_norm(group_input, first_gain, first_shift))
    normed_second = low(layer_norm(group_input, second_gain, second_shift))
    mixed = matmul(normed_first, triple_weight) + matmul(low(matmul(normed_first, triple_left)), triple_right)
    mixed = low_back(mixed).reshape(TOK_GRP, HEADS, 3, HEAD_DIM)
    queries = low(rotate(mixed[:, :, 0], cosine, sine_table))
    key_rows = low(rotate(mixed[:, :, 1], cosine, sine_table))
    value_rows = low(mixed[:, :, 2])
    attended = attend(queries, key_rows, value_rows, continues).reshape(TOK_GRP, D)
    attended = low(low_back(attended))
    attention_out = matmul(attended, output_weight) + matmul(low_back(low(matmul(attended, output_left))), output_right)
    hidden_pre = low_back(matmul(normed_second, expand_weight) + matmul(low(matmul(normed_second, expand_left)), expand_right))
    activated = low(jax.nn.gelu(hidden_pre, approximate=False))
    feed_out = matmul(activated, shrink_weight) + matmul(low_back(low(matmul(activated, shrink_left))), shrink_right)
    return group_input + attention_out + feed_out

def reference(block_input, sequence_lengths, first_gain, first_shift, second_gain, second_shift, triple_weight, triple_left, triple_right, output_weight, output_left, output_right, expand_weight, expand_left, expand_right, shrink_weight, shrink_left, shrink_right, cotangent):
    frozen = (triple_weight.astype(jnp.float32), output_weight.astype(jnp.float32), expand_weight.astype(jnp.float32), shrink_weight.astype(jnp.float32))
    trainable = (first_gain.astype(jnp.float32), first_shift.astype(jnp.float32), second_gain.astype(jnp.float32), second_shift.astype(jnp.float32), triple_left.astype(jnp.float32), triple_right.astype(jnp.float32), output_left.astype(jnp.float32), output_right.astype(jnp.float32), expand_left.astype(jnp.float32), expand_right.astype(jnp.float32), shrink_left.astype(jnp.float32), shrink_right.astype(jnp.float32))

    def forward(inputs, trainable_now):
        grouped = inputs.reshape(TOKENS // TOK_GRP, TOK_GRP, D)

        def per_group(group_items):
            return group_forward(group_items[0], group_items[1], frozen, trainable_now)
        return lax.map(jax.checkpoint(per_group), (grouped, sequence_lengths)).reshape(TOKENS, D)
    output, pullback = jax.vjp(forward, block_input.astype(jnp.float32), trainable)
    input_grad, train_grads = pullback(cotangent.astype(jnp.float32))
    return (output.astype(jnp.bfloat16), input_grad, train_grads[0], train_grads[1], train_grads[2], train_grads[3], train_grads[4], train_grads[5], train_grads[6], train_grads[7], train_grads[8], train_grads[9], train_grads[10], train_grads[11])
```

```python
import functools
import math

import jax
import jax.numpy as jnp
import numpy as np
from jax import lax
from jax.experimental import pallas as pl
from jax.experimental.pallas import tpu as pltpu
from jax.sharding import PartitionSpec as P

HEAD_DIM = 64
ROT = 16
SHORT = 512
TOK_GRP = 3072
SLOTS = 6
EPS = 1e-05
LANES = 128
MESH = pl.DeviceIdType.MESH
BF16 = jnp.bfloat16
F32 = jnp.float32
VMEM_LIMIT = 56 * 1024 * 1024


def dot_nn(former, latter):
    return lax.dot_general(
        former, latter, (((1,), (0,)), ((), ())), preferred_element_type=F32
    )


def dot_nt(former, latter):
    return lax.dot_general(
        former, latter, (((1,), (1,)), ((), ())), preferred_element_type=F32
    )


def dot_tn(former, latter):
    return lax.dot_general(
        former, latter, (((0,), (0,)), ((), ())), preferred_element_type=F32
    )


def find_flags(group_lengths):
    seq_ends = jnp.cumsum(group_lengths, dtype=jnp.int32)
    starts = seq_ends - group_lengths
    block_starts = jnp.arange(SLOTS, dtype=jnp.int32) * SHORT
    begins = jnp.any(
        (starts[None, :] == block_starts[:, None]) & (group_lengths[None, :] > 0), axis=1
    )
    return jnp.where(begins, 0, 1).astype(jnp.int32)


def rotary_tables():
    half = ROT // 2
    frequency = np.exp(
        np.arange(half, dtype=np.float32) * np.float32(-2.0 * math.log(10000.0) / ROT)
    ).astype(np.float32)
    angles = np.arange(2 * SHORT, dtype=np.float32)[:, None] * frequency[None, :]
    cosine = np.ones((2 * SHORT, LANES), np.float32)
    minus = np.zeros((2 * SHORT, LANES), np.float32)
    plus = np.zeros((2 * SHORT, LANES), np.float32)
    for base in range(0, LANES, HEAD_DIM):
        cosine[:, base : base + half] = np.cos(angles)
        cosine[:, base + half : base + ROT] = np.cos(angles)
        minus[:, base : base + half] = -np.sin(angles)
        plus[:, base + half : base + ROT] = np.sin(angles)
    return jnp.asarray(cosine), jnp.asarray(minus), jnp.asarray(plus)


def gather_columns(width):
    old = np.arange(width).reshape(width // (3 * HEAD_DIM), 3, HEAD_DIM)
    order = old.transpose(1, 0, 2).reshape(-1)
    matrix = np.zeros((width, width), np.float32)
    matrix[order, np.arange(width)] = 1.0
    return jnp.asarray(matrix, BF16)


def rotate(pair, cosine, minus, plus):
    half = ROT // 2
    return (
        pair * cosine
        + pltpu.roll(pair, LANES - half, 1) * minus
        + pltpu.roll(pair, half, 1) * plus
    )


def unrotate(pair, cosine, minus, plus):
    half = ROT // 2
    return (
        pair * cosine
        - pltpu.roll(pair, LANES - half, 1) * minus
        - pltpu.roll(pair, half, 1) * plus
    )


def normalize(values, gain, shift):
    center = values - jnp.mean(values, axis=-1, keepdims=True)
    spread = jnp.mean(center * center, axis=-1, keepdims=True)
    return center * lax.rsqrt(spread + EPS) * gain + shift


def whole(shape):
    return pl.BlockSpec(
        shape, lambda *idx: (0,) * len(shape), pipeline_mode=pl.Buffered(1)
    )


def held(shape):
    return pl.BlockSpec(shape, lambda *idx: (0,) * len(shape))


def rows_of(tile, width):
    return pl.BlockSpec((tile, width), lambda i, *refs: (i, 0))


def shaped(shape, dtype):
    return jax.ShapeDtypeStruct(shape, dtype)


def params(semantics=1):
    return pltpu.CompilerParams(
        dimension_semantics=("arbitrary",) * semantics, vmem_limit_bytes=VMEM_LIMIT
    )


def unit_gather_kernel(unit, x_ref, d_ref, xg_ref, dg_ref, local_sem, send_sem, recv_sem):
    dp = lax.axis_index("dp")
    mp = lax.axis_index("mp")
    place = lax.rem(mp, unit)
    base = mp - place
    peers = [(dp, base + lax.rem(place + j, unit)) for j in range(1, unit)]
    barrier = pltpu.get_barrier_semaphore()
    for peer in peers:
        pl.semaphore_signal(barrier, inc=1, device_id=peer, device_id_type=MESH)
    pl.semaphore_wait(barrier, unit - 1)
    rows = x_ref.shape[0]
    span = pl.ds(pl.multiple_of(place * rows, rows), rows)
    copies = []
    for which, (src, dst) in enumerate(((x_ref, xg_ref), (d_ref, dg_ref))):
        for j, peer in enumerate(peers):
            copies.append(
                pltpu.make_async_remote_copy(
                    src_ref=src,
                    dst_ref=dst.at[span],
                    send_sem=send_sem.at[which, j],
                    recv_sem=recv_sem.at[which, j],
                    device_id=peer,
                    device_id_type=MESH,
                )
            )
        copies.append(pltpu.make_async_copy(src, dst.at[span], local_sem.at[which]))
    for copy in copies:
        copy.start()
    for copy in copies:
        copy.wait()


def unit_gather(unit, x, d):
    rows, width = x.shape
    anywhere = pl.BlockSpec(memory_space=pl.ANY)
    return pl.pallas_call(
        functools.partial(unit_gather_kernel, unit),
        out_shape=[shaped((rows * unit, width), x.dtype)] * 2,
        in_specs=[anywhere] * 2,
        out_specs=[anywhere] * 2,
        scratch_shapes=[
            pltpu.SemaphoreType.DMA((2,)),
            pltpu.SemaphoreType.DMA((2, unit - 1)),
            pltpu.SemaphoreType.DMA((2, unit - 1)),
        ],
        compiler_params=pltpu.CompilerParams(collective_id=1, has_side_effects=True),
        name="unit_gather",
    )(x, d)


def gelu_parts(hidden):
    cdf = 0.5 + 0.5 * lax.erf(hidden * math.sqrt(0.5))
    density = jnp.exp(-0.5 * hidden * hidden) * (1.0 / math.sqrt(2.0 * math.pi))
    return hidden * cdf, cdf + hidden * density


def feed_core(
    normed, low, dy, grad_low, up_ref, up_right_ref, down_ref, down_left_ref, act_ref, grad_ref, hidden_step
):
    hidden_width = up_ref.shape[1]
    for start in range(0, hidden_width, hidden_step):
        cols = pl.ds(start, hidden_step)
        hidden = dot_nn(normed, up_ref[:, cols]) + dot_nn(low, up_right_ref[:, cols])
        grad_act = dot_nt(dy, down_ref[cols, :]) + dot_nt(grad_low, down_left_ref[cols, :])
        activated, slope = gelu_parts(hidden)
        act_ref[:, cols] = activated.astype(BF16)
        grad_ref[:, cols] = (grad_act * slope).astype(BF16)


def feed_first_kernel(
    x_ref, dy_ref, gain_ref, shift_ref, up_ref, up_left_ref, up_right_ref, down_ref, down_left_ref, rights_ref,
    normed_ref, low_ref, grad_lows_ref, out_ref, grad_ref, low_act_ref, grad_low_ref, up_right_grad_ref,
    down_left_grad_ref, act_ref, gh_ref,
):
    normed = normalize(x_ref[...].astype(F32), gain_ref[...], shift_ref[...]).astype(BF16)
    normed_ref[...] = normed
    dy = dy_ref[...]
    low = dot_nn(normed, up_left_ref[...]).astype(BF16)
    low_ref[...] = low
    grad_lows = dot_nt(dy, rights_ref[...]).astype(BF16)
    grad_lows_ref[...] = grad_lows
    grad_low = grad_lows[:, LANES:]
    feed_core(normed, low, dy, grad_low, up_ref, up_right_ref, down_ref, down_left_ref, act_ref, gh_ref, 256)
    act = act_ref[...]
    gh = gh_ref[...]
    out_ref[...] = dot_nn(act, down_ref[...])
    grad_ref[...] = dot_nt(gh, up_ref[...])
    low_act_ref[...] = dot_nn(act, down_left_ref[...])
    grad_low_ref[...] = dot_nt(gh, up_right_ref[...])

    @pl.when(pl.program_id(0) == 0)
    def _():
        up_right_grad_ref[...] = jnp.zeros_like(up_right_grad_ref)
        down_left_grad_ref[...] = jnp.zeros_like(down_left_grad_ref)

    up_right_grad_ref[...] += dot_tn(low, gh)
    down_left_grad_ref[...] += dot_tn(grad_low, act)


def feed_first(x, dy, gain, shift, up, up_left, up_right, down, down_left, rights, tile):
    rows, width = x.shape
    hidden = up.shape[1]
    return pl.pallas_call(
        feed_first_kernel,
        grid=(rows // tile,),
        in_specs=[
            rows_of(tile, width),
            rows_of(tile, width),
            whole((1, width)),
            whole((1, width)),
            whole(up.shape),
            whole(up_left.shape),
            whole(up_right.shape),
            whole(down.shape),
            whole(down_left.shape),
            whole(rights.shape),
        ],
        out_specs=[
            rows_of(tile, width),
            rows_of(tile, LANES),
            rows_of(tile, 2 * LANES),
            rows_of(tile, width),
            rows_of(tile, width),
            rows_of(tile, LANES),
            rows_of(tile, LANES),
            held((LANES, hidden)),
            held((LANES, hidden)),
        ],
        out_shape=[
            shaped((rows, width), BF16),
            shaped((rows, LANES), BF16),
            shaped((rows, 2 * LANES), BF16),
            shaped((rows, width), F32),
            shaped((rows, width), F32),
            shaped((rows, LANES), F32),
            shaped((rows, LANES), F32),
            shaped((LANES, hidden), F32),
            shaped((LANES, hidden), F32),
        ],
        scratch_shapes=[pltpu.VMEM((tile, hidden), BF16), pltpu.VMEM((tile, hidden), BF16)],
        compiler_params=params(),
        cost_estimate=pl.CostEstimate(
            flops=10 * rows * width * hidden, bytes_accessed=30 * rows * width, transcendentals=2 * rows * hidden
        ),
        name="feed_first",
    )(x, dy, gain, shift, up, up_left, up_right, down, down_left, rights)


def feed_second_kernel(
    send_tiles, order_ref, normed_ref, low_ref, dy_ref, grad_lows_ref, out_in_ref, grad_in_ref, low_act_in_ref,
    grad_low_in_ref, up_ref, up_left_ref, up_right_ref, down_ref, down_left_ref, out_send_ref, out_keep_ref,
    grad_send_ref, grad_keep_ref, low_act_send_ref, low_act_keep_ref, up_right_grad_ref, down_left_grad_ref,
    up_left_grad_ref, act_ref, gh_ref,
):
    step = pl.program_id(0)
    normed = normed_ref[...]
    low = low_ref[...]
    dy = dy_ref[...]
    grad_low = grad_lows_ref[:, LANES:]
    feed_core(normed, low, dy, grad_low, up_ref, up_right_ref, down_ref, down_left_ref, act_ref, gh_ref, 256)
    act = act_ref[...]
    gh = gh_ref[...]
    grad_low_up = (grad_low_in_ref[...] + dot_nt(gh, up_right_ref[...])).astype(BF16)
    out = (out_in_ref[...] + dot_nn(act, down_ref[...])).astype(BF16)
    low_act = (low_act_in_ref[...] + dot_nn(act, down_left_ref[...])).astype(BF16)
    grad = (
        grad_in_ref[...] + dot_nt(gh, up_ref[...]) + dot_nt(grad_low_up, up_left_ref[...])
    ).astype(BF16)

    @pl.when(step < send_tiles)
    def _():
        out_send_ref[...] = out
        grad_send_ref[...] = grad
        low_act_send_ref[...] = low_act

    @pl.when(step >= send_tiles)
    def _():
        out_keep_ref[...] = out
        grad_keep_ref[...] = grad
        low_act_keep_ref[...] = low_act

    @pl.when(step == 0)
    def _():
        up_right_grad_ref[...] = jnp.zeros_like(up_right_grad_ref)
        down_left_grad_ref[...] = jnp.zeros_like(down_left_grad_ref)
        up_left_grad_ref[...] = jnp.zeros_like(up_left_grad_ref)

    up_right_grad_ref[...] += dot_tn(low, gh)
    down_left_grad_ref[...] += dot_tn(grad_low, act)
    up_left_grad_ref[...] += dot_tn(grad_low_up, normed)


def ordered(tile, width):
    return pl.BlockSpec((tile, width), lambda i, order: (order[i], 0))


def sent(tile, width, tiles):
    return pl.BlockSpec((tile, width), lambda i, order: (jnp.minimum(i, tiles - 1), 0))


def kept(tile, width, tiles):
    return pl.BlockSpec((tile, width), lambda i, order: (jnp.maximum(i - tiles, 0), 0))


def feed_second(order, normed, low, dy, grad_lows, out, grad, low_act, grad_low, up, up_left, up_right, down,
                down_left, own_rows, tile):
    rows, width = normed.shape
    hidden = up.shape[1]
    send_rows = rows - own_rows
    tiles = send_rows // tile
    return pl.pallas_call(
        functools.partial(feed_second_kernel, tiles),
        grid_spec=pltpu.PrefetchScalarGridSpec(
            num_scalar_prefetch=1,
            grid=(rows // tile,),
            in_specs=[
                ordered(tile, width),
                ordered(tile, LANES),
                ordered(tile, width),
                ordered(tile, 2 * LANES),
                ordered(tile, width),
                ordered(tile, width),
                ordered(tile, LANES),
                ordered(tile, LANES),
                whole(up.shape),
                whole(up_left.shape),
                whole(up_right.shape),
                whole(down.shape),
                whole(down_left.shape),
            ],
            out_specs=[
                sent(tile, width, tiles),
                kept(tile, width, tiles),
                sent(tile, width, tiles),
                kept(tile, width, tiles),
                sent(tile, LANES, tiles),
                kept(tile, LANES, tiles),
                held((LANES, hidden)),
                held((LANES, hidden)),
                held((LANES, width)),
            ],
            scratch_shapes=[pltpu.VMEM((tile, hidden), BF16), pltpu.VMEM((tile, hidden), BF16)],
        ),
        out_shape=[
            shaped((send_rows, width), BF16),
            shaped((own_rows, width), BF16),
            shaped((send_rows, width), BF16),
            shaped((own_rows, width), BF16),
            shaped((send_rows, LANES), BF16),
            shaped((own_rows, LANES), BF16),
            shaped((LANES, hidden), F32),
            shaped((LANES, hidden), F32),
            shaped((LANES, width), F32),
        ],
        compiler_params=params(),
        cost_estimate=pl.CostEstimate(
            flops=10 * rows * width * hidden, bytes_accessed=30 * rows * width, transcendentals=2 * rows * hidden
        ),
        name="feed_second",
    )(order, normed, low, dy, grad_lows, out, grad, low_act, grad_low, up, up_left, up_right, down, down_left)


def project_body(
    normed, low, dy_ref, grad_lows_ref, triple_ref, right_ref, output_ref, output_left_ref, cos_ref, minus_ref,
    plus_ref, q_ref, k_ref, v_ref, g_ref,
):
    tables = (cos_ref[...], minus_ref[...], plus_ref[...])
    head_width = output_ref.shape[0]
    mixed = dot_nn(normed, triple_ref[...]) + dot_nn(low, right_ref[...])
    for start in range(0, head_width, LANES):
        cols = slice(start, start + LANES)
        query = rotate(mixed[:, cols], *tables).astype(BF16)
        q_ref[:, cols] = query * HEAD_DIM**-0.5
        k_ref[:, cols] = rotate(
            mixed[:, head_width + start : head_width + start + LANES], *tables
        ).astype(BF16)
    v_ref[...] = mixed[:, 2 * head_width :].astype(BF16)
    g_ref[...] = (
        dot_nt(dy_ref[...], output_ref[...]) + dot_nt(grad_lows_ref[:, :LANES], output_left_ref[...])
    ).astype(BF16)


def project_first_kernel(
    cont_ref, x_ref, dy_ref, grad_lows_ref, gain_ref, shift_ref, triple_ref, left_ref, right_ref, output_ref,
    output_left_ref, cos_ref, minus_ref, plus_ref, normed_ref, low_ref, q_ref, k_ref, v_ref, g_ref,
):
    normed = normalize(x_ref[...].astype(F32), gain_ref[...], shift_ref[...]).astype(BF16)
    normed_ref[...] = normed
    low = dot_nn(normed, left_ref[...]).astype(BF16)
    low_ref[...] = low
    project_body(
        normed, low, dy_ref, grad_lows_ref, triple_ref, right_ref, output_ref, output_left_ref, cos_ref, minus_ref,
        plus_ref, q_ref, k_ref, v_ref, g_ref,
    )


def project_second_kernel(
    cont_ref, normed_ref, low_ref, dy_ref, grad_lows_ref, triple_ref, right_ref, output_ref, output_left_ref, cos_ref,
    minus_ref, plus_ref, q_ref, k_ref, v_ref, g_ref,
):
    project_body(
        normed_ref[...], low_ref[...], dy_ref, grad_lows_ref, triple_ref, right_ref, output_ref, output_left_ref,
        cos_ref, minus_ref, plus_ref, q_ref, k_ref, v_ref, g_ref,
    )


def project(first, conts, inputs, dy, grad_lows, norm, triple, left, right, output, output_left, tables, tile):
    rows, width = dy.shape
    head_width = output.shape[0]
    per_block = SHORT // tile

    def table_index(i, cont):
        return (cont[i // per_block] * per_block + lax.rem(i, per_block), 0)

    table = pl.BlockSpec((tile, LANES), table_index)
    row_specs = [rows_of(tile, value.shape[1]) for value in inputs]
    row_specs += [rows_of(tile, width), rows_of(tile, 2 * LANES)]
    fixed = list(norm) + [triple] + ([left] if first else []) + [right, output, output_left]
    new_specs = [rows_of(tile, width), rows_of(tile, LANES)] if first else []
    new_shapes = [shaped((rows, width), BF16), shaped((rows, LANES), BF16)] if first else []
    return pl.pallas_call(
        project_first_kernel if first else project_second_kernel,
        grid_spec=pltpu.PrefetchScalarGridSpec(
            num_scalar_prefetch=1,
            grid=(rows // tile,),
            in_specs=row_specs + [whole(value.shape) for value in fixed] + [table] * 3,
            out_specs=new_specs + [rows_of(tile, head_width)] * 4,
        ),
        out_shape=new_shapes + [shaped((rows, head_width), BF16)] * 4,
        compiler_params=params(),
        cost_estimate=pl.CostEstimate(
            flops=8 * rows * width * head_width, bytes_accessed=8 * rows * width, transcendentals=0
        ),
        name="project_first" if first else "project_second",
    )(conts, *inputs, dy, grad_lows, *fixed, *tables)


def attend_rows(with_prev, start, count, q_ref, k_ref, v_ref, g_ref, kp_ref, vp_ref, tables, att_ref, gq_ref,
                dk_ref, dv_ref, dkp_ref, dvp_ref):
    first_head = lax.broadcasted_iota(jnp.int32, (1, LANES), 1) < HEAD_DIM
    span = pl.ds(start, count)
    known = start + count
    zero = jnp.zeros((), BF16)

    def stack(pair):
        return jnp.concatenate([jnp.where(first_head, pair, zero), jnp.where(first_head, zero, pair)], axis=0)

    def unstack(both):
        return jnp.where(first_head, both[:count], both[count:])

    queries = stack(q_ref[span, :])
    grads = stack(g_ref[span, :])
    keys = k_ref[pl.ds(0, known), :]
    values = v_ref[pl.ds(0, known), :]
    scores = dot_nt(queries, keys)
    row = lax.broadcasted_iota(jnp.int32, (2 * count, known), 0)
    column = lax.broadcasted_iota(jnp.int32, (2 * count, known), 1)
    row = jnp.where(row >= count, row - count, row) + start
    scores = jnp.where(column <= row, scores, -1e30)
    peak = jnp.max(scores, axis=1, keepdims=True)
    if with_prev:
        prev_scores = dot_nt(queries, kp_ref[...])
        peak = jnp.maximum(peak, jnp.max(prev_scores, axis=1, keepdims=True))
        prev_exp = jnp.exp(prev_scores - peak)
    exp = jnp.exp(scores - peak)
    total = jnp.sum(exp, axis=1, keepdims=True)
    if with_prev:
        total = total + jnp.sum(prev_exp, axis=1, keepdims=True)
    scale = 1.0 / total
    weights = exp * scale
    weights_low = weights.astype(BF16)
    attended = dot_nn(weights_low, values)
    grad_weights = dot_nt(grads, values)
    inner = jnp.sum(weights * grad_weights, axis=1, keepdims=True)
    if with_prev:
        prev_weights = prev_exp * scale
        prev_low = prev_weights.astype(BF16)
        attended = attended + dot_nn(prev_low, vp_ref[...])
        prev_grad = dot_nt(grads, vp_ref[...])
        inner = inner + jnp.sum(prev_weights * prev_grad, axis=1, keepdims=True)
        prev_ds = (prev_weights * (prev_grad - inner)).astype(BF16)
    ds = (weights * (grad_weights - inner)).astype(BF16)
    grad_query = dot_nn(ds, keys)
    if with_prev:
        grad_query = grad_query + dot_nn(prev_ds, kp_ref[...])
        dkp_ref[...] += dot_tn(prev_ds, queries)
        dvp_ref[...] += dot_tn(prev_low, grads)
    dk_ref[pl.ds(0, known), :] += dot_tn(ds, queries)
    dv_ref[pl.ds(0, known), :] += dot_tn(weights_low, grads)
    att_ref[span, :] = unstack(attended).astype(BF16)
    grad_query = unstack(grad_query) * HEAD_DIM**-0.5
    gq_ref[span, :] = unrotate(grad_query, *[table[start : start + count] for table in tables]).astype(BF16)


def attend_kernel(
    blocks, count, cont_ref, q_ref, k_ref, v_ref, g_ref, k_before_ref, v_before_ref, k_halo_ref, v_halo_ref, cos_ref,
    minus_ref, plus_ref, att_ref, gq_ref, gk_ref, gv_ref, dk_halo_ref, dv_halo_ref, kp_ref, vp_ref, dk_ref, dv_ref,
    dkp_ref, dvp_ref,
):
    step = pl.program_id(1)
    block = blocks - 1 - step
    continued = cont_ref[block]
    offset = pl.multiple_of(continued * SHORT, SHORT)
    tables = tuple(ref[pl.ds(offset, SHORT), :] for ref in (cos_ref, minus_ref, plus_ref))

    @pl.when(step == 0)
    def _():
        dk_ref[...] = jnp.zeros_like(dk_ref)
        dv_ref[...] = jnp.zeros_like(dv_ref)

    @pl.when(step > 0)
    def _():
        dk_ref[...] = dkp_ref[...]
        dv_ref[...] = dvp_ref[...]

    dkp_ref[...] = jnp.zeros_like(dkp_ref)
    dvp_ref[...] = jnp.zeros_like(dvp_ref)
    args = (q_ref, k_ref, v_ref, g_ref, kp_ref, vp_ref, tables, att_ref, gq_ref, dk_ref, dv_ref, dkp_ref, dvp_ref)

    @pl.when(continued == 0)
    def _():
        for start in range(0, SHORT, count):
            attend_rows(False, start, count, *args)

    @pl.when(continued != 0)
    def _():
        @pl.when(block == 0)
        def _():
            kp_ref[...] = k_halo_ref[...]
            vp_ref[...] = v_halo_ref[...]

        @pl.when(block != 0)
        def _():
            kp_ref[...] = k_before_ref[...]
            vp_ref[...] = v_before_ref[...]

        for start in range(0, SHORT, count):
            attend_rows(True, start, count, *args)

    gk_ref[...] = unrotate(dk_ref[...], *tables).astype(BF16)
    gv_ref[...] = dv_ref[...].astype(BF16)

    @pl.when(block == 0)
    def _():
        base = tuple(ref[pl.ds(0, SHORT), :] for ref in (cos_ref, minus_ref, plus_ref))
        dk_halo_ref[...] = unrotate(dkp_ref[...], *base).astype(BF16)
        dv_halo_ref[...] = dvp_ref[...].astype(BF16)


def attend(conts, q, k, v, g, k_halo, v_halo, tables, count):
    rows, head_width = q.shape
    blocks = rows // SHORT
    here = pl.BlockSpec((SHORT, LANES), lambda p, i, cont: (blocks - 1 - i, p))
    before = pl.BlockSpec((SHORT, LANES), lambda p, i, cont: (jnp.maximum(blocks - 2 - i, 0), p))
    halo = pl.BlockSpec((SHORT, LANES), lambda p, i, cont: (0, p))
    return pl.pallas_call(
        functools.partial(attend_kernel, blocks, count),
        grid_spec=pltpu.PrefetchScalarGridSpec(
            num_scalar_prefetch=1,
            grid=(head_width // LANES, blocks),
            in_specs=[here] * 4 + [before] * 2 + [halo] * 2 + [whole(table.shape) for table in tables],
            out_specs=[here] * 4 + [halo] * 2,
            scratch_shapes=[pltpu.VMEM((SHORT, LANES), BF16)] * 2 + [pltpu.VMEM((SHORT, LANES), F32)] * 4,
        ),
        out_shape=[shaped((rows, head_width), BF16)] * 4 + [shaped((SHORT, head_width), BF16)] * 2,
        compiler_params=params(2),
        cost_estimate=pl.CostEstimate(
            flops=12 * rows * 3 * SHORT * head_width, bytes_accessed=16 * rows * head_width,
            transcendentals=rows * SHORT * head_width // HEAD_DIM,
        ),
        name="attend",
    )(conts, q, k, v, g, k, v, k_halo, v_halo, *tables)


def settle_kernel(
    send_tiles, halo_start, order_ref, normed_ref, low_ref, grad_lows_ref, out_in_ref,
    att0_ref, att1_ref, gq0_ref, gq1_ref, gk0_ref, gk1_ref, gv0_ref, gv1_ref, hk0_ref, hk1_ref, hv0_ref, hv1_ref,
    triple0_ref, triple1_ref, right0_ref, right1_ref, left_ref, output0_ref, output1_ref, output_left0_ref,
    output_left1_ref, out_ref, grad_send_ref, grad_keep_ref, low_att_send_ref, low_att_keep_ref, right_grad0_ref,
    right_grad1_ref, left_grad_ref, output_left_grad0_ref, output_left_grad1_ref,
):
    step = pl.program_id(0)
    here = (order_ref[step] >= halo_start).astype(F32)
    normed = normed_ref[...]
    low = low_ref[...]
    grad_low_out = grad_lows_ref[:, :LANES]
    att0, att1 = att0_ref[...], att1_ref[...]

    def mixed(gq, gk, gv, hk, hv):
        key = (gk[...].astype(F32) + here * hk[...].astype(F32)).astype(BF16)
        value = (gv[...].astype(F32) + here * hv[...].astype(F32)).astype(BF16)
        return jnp.concatenate([gq[...], key, value], axis=1)

    grad0 = mixed(gq0_ref, gk0_ref, gv0_ref, hk0_ref, hv0_ref)
    grad1 = mixed(gq1_ref, gk1_ref, gv1_ref, hk1_ref, hv1_ref)
    grad_low = (dot_nt(grad0, right0_ref[...]) + dot_nt(grad1, right1_ref[...])).astype(BF16)
    grad = (
        dot_nt(grad0, triple0_ref[...]) + dot_nt(grad1, triple1_ref[...]) + dot_nt(grad_low, left_ref[...])
    ).astype(BF16)
    out_ref[...] = out_in_ref[...] + dot_nn(att0, output0_ref[...]) + dot_nn(att1, output1_ref[...])
    low_att = (dot_nn(att0, output_left0_ref[...]) + dot_nn(att1, output_left1_ref[...])).astype(BF16)

    @pl.when(step < send_tiles)
    def _():
        grad_send_ref[...] = grad
        low_att_send_ref[...] = low_att

    @pl.when(step >= send_tiles)
    def _():
        grad_keep_ref[...] = grad
        low_att_keep_ref[...] = low_att

    sums = (right_grad0_ref, right_grad1_ref, left_grad_ref, output_left_grad0_ref, output_left_grad1_ref)

    @pl.when(step == 0)
    def _():
        for ref in sums:
            ref[...] = jnp.zeros_like(ref)

    right_grad0_ref[...] += dot_tn(low, grad0)
    right_grad1_ref[...] += dot_tn(low, grad1)
    left_grad_ref[...] += dot_tn(grad_low, normed)
    output_left_grad0_ref[...] += dot_tn(grad_low_out, att0)
    output_left_grad1_ref[...] += dot_tn(grad_low_out, att1)


def settle(order, normed, low, grad_lows, out, pairs, halos, weights, own_rows, tile):
    rows, width = normed.shape
    head_width = pairs[0].shape[1]
    send_rows = rows - own_rows
    tiles = send_rows // tile
    halo_start = (rows - SHORT) // tile
    halo = pl.BlockSpec((tile, head_width), lambda i, order: (jnp.maximum(order[i] - halo_start, 0), 0))
    return pl.pallas_call(
        functools.partial(settle_kernel, tiles, halo_start),
        grid_spec=pltpu.PrefetchScalarGridSpec(
            num_scalar_prefetch=1,
            grid=(rows // tile,),
            in_specs=[ordered(tile, width), ordered(tile, LANES), ordered(tile, 2 * LANES), ordered(tile, width)]
            + [ordered(tile, head_width)] * 8
            + [halo] * 4
            + [whole(value.shape) for value in weights],
            out_specs=[
                ordered(tile, width),
                sent(tile, width, tiles),
                kept(tile, width, tiles),
                sent(tile, LANES, tiles),
                kept(tile, LANES, tiles),
                held((LANES, 3 * head_width)),
                held((LANES, 3 * head_width)),
                held((LANES, width)),
                held((LANES, head_width)),
                held((LANES, head_width)),
            ],
        ),
        out_shape=[
            shaped((rows, width), F32),
            shaped((send_rows, width), BF16),
            shaped((own_rows, width), BF16),
            shaped((send_rows, LANES), BF16),
            shaped((own_rows, LANES), BF16),
            shaped((LANES, 3 * head_width), F32),
            shaped((LANES, 3 * head_width), F32),
            shaped((LANES, width), F32),
            shaped((LANES, head_width), F32),
            shaped((LANES, head_width), F32),
        ],
        compiler_params=params(),
        cost_estimate=pl.CostEstimate(
            flops=20 * rows * width * head_width, bytes_accessed=16 * rows * width, transcendentals=0
        ),
        name="settle",
    )(order, normed, low, grad_lows, out, *pairs, *halos, *weights)


def finish_kernel(
    peers, x_ref, dy_ref, gain1_ref, gain2_ref, output_right_ref, shrink_right_ref, out_ref, first_ref, second_ref,
    low_att_ref, low_act_ref, *refs,
):
    others = refs[: 5 * peers]
    y_ref, dx_ref, norms_ref, output_right_grad_ref, shrink_right_grad_ref = refs[5 * peers :]

    def total(own, which):
        value = own[...].astype(F32)
        for j in range(peers):
            value = value + others[5 * j + which][...].astype(F32)
        return value

    out = total(out_ref, 0)
    first = total(first_ref, 1)
    second = total(second_ref, 2)
    low_att = total(low_att_ref, 3).astype(BF16)
    low_act = total(low_act_ref, 4).astype(BF16)
    x = x_ref[...].astype(F32)
    dy = dy_ref[...]
    y_ref[...] = (
        x + out + dot_nn(low_att, output_right_ref[...]) + dot_nn(low_act, shrink_right_ref[...])
    ).astype(BF16)
    center = x - jnp.mean(x, axis=-1, keepdims=True)
    spread = jnp.mean(center * center, axis=-1, keepdims=True)
    inverse = lax.rsqrt(spread + EPS)
    unit = center * inverse
    scaled = first * gain1_ref[...] + second * gain2_ref[...]
    mean = jnp.mean(scaled, axis=-1, keepdims=True)
    inner = jnp.mean(scaled * unit, axis=-1, keepdims=True)
    dx_ref[...] = dy.astype(F32) + (scaled - mean - unit * inner) * inverse

    @pl.when(pl.program_id(0) == 0)
    def _():
        norms_ref[...] = jnp.zeros_like(norms_ref)
        output_right_grad_ref[...] = jnp.zeros_like(output_right_grad_ref)
        shrink_right_grad_ref[...] = jnp.zeros_like(shrink_right_grad_ref)

    norms_ref[0:1, :] += jnp.sum(first * unit, axis=0, keepdims=True)
    norms_ref[1:2, :] += jnp.sum(first, axis=0, keepdims=True)
    norms_ref[2:3, :] += jnp.sum(second * unit, axis=0, keepdims=True)
    norms_ref[3:4, :] += jnp.sum(second, axis=0, keepdims=True)
    output_right_grad_ref[...] += dot_tn(low_att, dy)
    shrink_right_grad_ref[...] += dot_tn(low_act, dy)


def finish(x, dy, gain1, gain2, output_right, shrink_right, own, others, tile):
    rows, width = x.shape
    peers = len(others)
    widths = (width, width, width, LANES, LANES)
    return pl.pallas_call(
        functools.partial(finish_kernel, peers),
        grid=(rows // tile,),
        in_specs=[rows_of(tile, width)] * 2
        + [whole((1, width))] * 2
        + [whole(output_right.shape)] * 2
        + [rows_of(tile, size) for size in widths] * (1 + peers),
        out_specs=[rows_of(tile, width)] * 2 + [held((8, width)), held((LANES, width)), held((LANES, width))],
        out_shape=[
            shaped((rows, width), BF16),
            shaped((rows, width), F32),
            shaped((8, width), F32),
            shaped((LANES, width), F32),
            shaped((LANES, width), F32),
        ],
        compiler_params=params(),
        cost_estimate=pl.CostEstimate(
            flops=60 * rows * width, bytes_accessed=20 * rows * width, transcendentals=0
        ),
        name="finish",
    )(x, dy, gain1, gain2, output_right, shrink_right, *own, *[value for other in others for value in other])


def shards(
    ranks,
    block_input,
    sequence_lengths,
    first_gain,
    first_shift,
    second_gain,
    second_shift,
    triple_weight,
    triple_left,
    triple_right,
    output_weight,
    output_left,
    output_right,
    expand_weight,
    expand_left,
    expand_right,
    shrink_weight,
    shrink_left,
    shrink_right,
    cotangent,
):
    unit = ranks // 2
    own_rows, width = block_input.shape
    rows = own_rows * unit
    blocks = rows // SHORT
    tile = math.gcd(own_rows, 256)
    triple_width = triple_weight.shape[1]
    head_width = output_weight.shape[0]
    hidden = expand_weight.shape[1]
    mp = lax.axis_index("mp")
    half = mp // unit
    place = lax.rem(mp, unit)
    far = lax.rem(mp + unit, ranks)
    swap = [(m, (m + unit) % ranks) for m in range(ranks)]
    onward = [(m, m + unit) for m in range(unit)]
    back = [(m + unit, m) for m in range(unit)]

    tables = rotary_tables()
    perm = gather_columns(triple_width)
    continues = find_flags(sequence_lengths[0])
    conts = lax.dynamic_slice_in_dim(continues, half * blocks, blocks, 0)
    per_device = own_rows // tile
    order = jnp.concatenate(
        [
            lax.rem(place + j, unit) * per_device + jnp.arange(per_device, dtype=jnp.int32)
            for j in list(range(1, unit)) + [0]
        ]
    ).astype(jnp.int32)

    def cols(matrix, size, shard):
        return lax.dynamic_slice_in_dim(matrix, shard * size, size, 1)

    def tall(matrix, size, shard):
        return lax.dynamic_slice_in_dim(matrix, shard * size, size, 0)

    def arranged(matrix):
        return jnp.dot(matrix, perm, preferred_element_type=F32).astype(BF16)

    triple_own = arranged(triple_weight)
    triple_far = lax.ppermute(triple_own, "mp", swap)
    output_far = lax.ppermute(output_weight, "mp", swap)
    expand_late, shrink_late, triple_far, output_far = lax.optimization_barrier(
        (expand_weight, shrink_weight, triple_far, output_far)
    )
    expand_far = lax.ppermute(expand_late, "mp", swap)
    shrink_far = lax.ppermute(shrink_late, "mp", swap)

    gain1, shift1 = first_gain[None, :], first_shift[None, :]
    gain2, shift2 = second_gain[None, :], second_shift[None, :]
    rights = jnp.concatenate([output_right, shrink_right], axis=0)

    x, dy = unit_gather(unit, block_input, cotangent)

    (normed2, low2, grad_lows, out, grad2, low_act, grad_low2, expand_right_own, shrink_left_own) = feed_first(
        x, dy, gain2, shift2, expand_weight, expand_left, cols(expand_right, hidden, mp), shrink_weight,
        tall(shrink_left, hidden, mp), rights, tile,
    )

    right_own = arranged(cols(triple_right, triple_width, mp))
    right_far = arranged(cols(triple_right, triple_width, far))
    output_left_own = tall(output_left, head_width, mp)
    output_left_far = tall(output_left, head_width, far)
    normed1, low1, q_own, k_own, v_own, g_own = project(
        True, conts, (x,), dy, grad_lows, (gain1, shift1), triple_own, triple_left, right_own, output_weight,
        output_left_own, tables, tile,
    )
    last = slice(rows - SHORT, rows)
    halo_far = lax.ppermute(jnp.concatenate([k_own[last], v_own[last]], axis=0), "mp", onward)
    q_far, k_far, v_far, g_far = project(
        False, conts, (normed1, low1), dy, grad_lows, (), triple_far, None, right_far, output_far, output_left_far,
        tables, tile,
    )
    halo_own = lax.ppermute(jnp.concatenate([k_far[last], v_far[last]], axis=0), "mp", onward)
    count = 256
    att_far, gq_far, gk_far, gv_far, hk, hv = attend(
        conts, q_far, k_far, v_far, g_far, halo_far[:SHORT], halo_far[SHORT:], tables, count
    )
    back_own = lax.ppermute(jnp.concatenate([hk, hv], axis=0), "mp", back)
    att_own, gq_own, gk_own, gv_own, hk, hv = attend(
        conts, q_own, k_own, v_own, g_own, halo_own[:SHORT], halo_own[SHORT:], tables, count
    )
    back_far = lax.ppermute(jnp.concatenate([hk, hv], axis=0), "mp", back)
    (out, grad1_send, grad1_keep, low_att_send, low_att_keep, triple_right_own, triple_right_far, triple_left_sum,
     output_left_sum_own, output_left_sum_far) = settle(
        order, normed1, low1, grad_lows, out,
        (att_own, att_far, gq_own, gq_far, gk_own, gk_far, gv_own, gv_far),
        (back_own[:SHORT], back_far[:SHORT], back_own[SHORT:], back_far[SHORT:]),
        (triple_own, triple_far, right_own, right_far, triple_left, output_weight, output_far, output_left_own,
         output_left_far),
        own_rows, tile,
    )

    (out_send, out_keep, grad2_send, grad2_keep, low_act_send, low_act_keep, expand_right_far, shrink_left_far,
     expand_left_sum) = feed_second(
        order, normed2, low2, dy, grad_lows, out, grad2, low_act, grad_low2, expand_far, expand_left,
        cols(expand_right, hidden, far), shrink_far, tall(shrink_left, hidden, far), own_rows, tile,
    )

    def pass_on(sent_rows):
        got = []
        for j in range(1, unit):
            ring = [(m, m - m % unit + (m % unit + j) % unit) for m in range(ranks)]
            got.append(lax.ppermute(sent_rows[(j - 1) * own_rows : j * own_rows], "mp", ring))
        return got

    sends = (out_send, grad1_send, grad2_send, low_att_send, low_act_send)
    arrived = list(zip(*[pass_on(value) for value in sends]))
    block_output, input_gradient, norms, output_right_sum, shrink_right_sum = finish(
        block_input, cotangent, gain1, gain2, output_right, shrink_right,
        (out_keep, grad1_keep, grad2_keep, low_att_keep, low_act_keep), arrived, tile,
    )

    def place(total, own, other, size):
        wide = jnp.zeros((LANES, total), BF16)
        wide = lax.dynamic_update_slice_in_dim(wide, own.astype(BF16), mp * size, 1)
        return lax.dynamic_update_slice_in_dim(wide, other.astype(BF16), far * size, 1)

    sums = lax.psum(
        (
            norms,
            triple_left_sum.astype(BF16),
            place(triple_right.shape[1], triple_right_own, triple_right_far, triple_width),
            place(output_left.shape[0], output_left_sum_own, output_left_sum_far, head_width),
            output_right_sum.astype(BF16),
            expand_left_sum.astype(BF16),
            place(expand_right.shape[1], expand_right_own, expand_right_far, hidden),
            place(shrink_left.shape[0], shrink_left_own, shrink_left_far, hidden),
            shrink_right_sum.astype(BF16),
        ),
        ("dp", "mp"),
    )
    norms = sums[0]
    sums = [value.astype(F32) for value in sums[1:]]
    triple_right_sum = (
        sums[1].reshape(LANES, ranks, 3, head_width // HEAD_DIM, HEAD_DIM).transpose(0, 1, 3, 2, 4)
    ).reshape(triple_right.shape)
    return (
        block_output,
        input_gradient,
        norms[0],
        norms[1],
        norms[2],
        norms[3],
        sums[0].T,
        triple_right_sum,
        sums[2].T,
        sums[3],
        sums[4].T,
        sums[5],
        sums[6].T,
        sums[7],
    )


def solution(mesh):
    placed = (
        P(("dp", "mp"), None),
        P("dp", None),
        P(),
        P(),
        P(),
        P(),
        P(None, "mp"),
        P(),
        P(),
        P("mp", None),
        P(),
        P(),
        P(None, "mp"),
        P(),
        P(),
        P("mp", None),
        P(),
        P(),
        P(("dp", "mp"), None),
    )
    return jax.shard_map(
        functools.partial(shards, mesh.shape["mp"]),
        mesh=mesh,
        in_specs=placed,
        out_specs=(P(("dp", "mp"), None), P(("dp", "mp"), None)) + (P(),) * 12,
        check_vma=False,
    )
```

```python
import functools
import math

import jax
import jax.numpy as jnp
import numpy as np
from jax import lax
from jax.experimental import pallas as pl
from jax.experimental.pallas import tpu as pltpu
from jax.sharding import PartitionSpec as P

HEAD_DIM = 64
ROT = 16
SHORT = 512
TOK_GRP = 3072
SLOTS = 6
EPS = 1e-05
LANES = 128
MESH = pl.DeviceIdType.MESH
BF16 = jnp.bfloat16
F32 = jnp.float32
VMEM_LIMIT = 56 * 1024 * 1024
BRIEF = pl.CostEstimate(flops=1, bytes_accessed=1, transcendentals=0)


def dot_nn(former, latter):
    return lax.dot_general(
        former, latter, (((1,), (0,)), ((), ())), preferred_element_type=F32
    )


def dot_nt(former, latter):
    return lax.dot_general(
        former, latter, (((1,), (1,)), ((), ())), preferred_element_type=F32
    )


def dot_tn(former, latter):
    return lax.dot_general(
        former, latter, (((0,), (0,)), ((), ())), preferred_element_type=F32
    )


def find_flags(group_lengths):
    seq_ends = jnp.cumsum(group_lengths, dtype=jnp.int32)
    starts = seq_ends - group_lengths
    block_starts = jnp.arange(SLOTS, dtype=jnp.int32) * SHORT
    begins = jnp.any(
        (starts[None, :] == block_starts[:, None]) & (group_lengths[None, :] > 0), axis=1
    )
    return jnp.where(begins, 0, 1).astype(jnp.int32)


def rotary_tables():
    half = ROT // 2
    frequency = np.exp(
        np.arange(half, dtype=np.float32) * np.float32(-2.0 * math.log(10000.0) / ROT)
    ).astype(np.float32)
    angles = np.arange(2 * SHORT, dtype=np.float32)[:, None] * frequency[None, :]
    cosine = np.ones((2 * SHORT, LANES), np.float32)
    minus = np.zeros((2 * SHORT, LANES), np.float32)
    plus = np.zeros((2 * SHORT, LANES), np.float32)
    for base in range(0, LANES, HEAD_DIM):
        cosine[:, base : base + half] = np.cos(angles)
        cosine[:, base + half : base + ROT] = np.cos(angles)
        minus[:, base : base + half] = -np.sin(angles)
        plus[:, base + half : base + ROT] = np.sin(angles)
    return jnp.asarray(cosine), jnp.asarray(minus), jnp.asarray(plus)


def gather_columns(width):
    old = np.arange(width).reshape(width // (3 * HEAD_DIM), 3, HEAD_DIM)
    order = old.transpose(1, 0, 2).reshape(-1)
    matrix = np.zeros((width, width), np.float32)
    matrix[order, np.arange(width)] = 1.0
    return jnp.asarray(matrix, BF16)


def rotate(pair, cosine, minus, plus):
    half = ROT // 2
    return (
        pair * cosine
        + pltpu.roll(pair, LANES - half, 1) * minus
        + pltpu.roll(pair, half, 1) * plus
    )


def unrotate(pair, cosine, minus, plus):
    half = ROT // 2
    return (
        pair * cosine
        - pltpu.roll(pair, LANES - half, 1) * minus
        - pltpu.roll(pair, half, 1) * plus
    )


def normalize(values, gain, shift):
    center = values - jnp.mean(values, axis=-1, keepdims=True)
    spread = jnp.mean(center * center, axis=-1, keepdims=True)
    return center * lax.rsqrt(spread + EPS) * gain + shift


def whole(shape):
    return pl.BlockSpec(
        shape, lambda *idx: (0,) * len(shape), pipeline_mode=pl.Buffered(1)
    )


def held(shape):
    return pl.BlockSpec(shape, lambda *idx: (0,) * len(shape))


def rows_of(tile, width):
    return pl.BlockSpec((tile, width), lambda i, *refs: (i, 0))


def shaped(shape, dtype):
    return jax.ShapeDtypeStruct(shape, dtype)


def params(semantics=1):
    return pltpu.CompilerParams(
        dimension_semantics=("arbitrary",) * semantics, vmem_limit_bytes=VMEM_LIMIT
    )


def unit_gather_kernel(unit, x_ref, d_ref, xg_ref, dg_ref, local_sem, send_sem, recv_sem):
    dp = lax.axis_index("dp")
    mp = lax.axis_index("mp")
    place = lax.rem(mp, unit)
    base = mp - place
    peers = [(dp, base + lax.rem(place + j, unit)) for j in range(1, unit)]
    barrier = pltpu.get_barrier_semaphore()
    for peer in peers:
        pl.semaphore_signal(barrier, inc=1, device_id=peer, device_id_type=MESH)
    pl.semaphore_wait(barrier, unit - 1)
    rows = x_ref.shape[0]
    span = pl.ds(pl.multiple_of(place * rows, rows), rows)
    copies = []
    for which, (src, dst) in enumerate(((x_ref, xg_ref), (d_ref, dg_ref))):
        for j, peer in enumerate(peers):
            copies.append(
                pltpu.make_async_remote_copy(
                    src_ref=src,
                    dst_ref=dst.at[span],
                    send_sem=send_sem.at[which, j],
                    recv_sem=recv_sem.at[which, j],
                    device_id=peer,
                    device_id_type=MESH,
                )
            )
        copies.append(pltpu.make_async_copy(src, dst.at[span], local_sem.at[which]))
    for copy in copies:
        copy.start()
    for copy in copies:
        copy.wait()


def unit_gather(unit, x, d):
    rows, width = x.shape
    anywhere = pl.BlockSpec(memory_space=pl.ANY)
    return pl.pallas_call(
        functools.partial(unit_gather_kernel, unit),
        out_shape=[shaped((rows * unit, width), x.dtype)] * 2,
        in_specs=[pl.BlockSpec(memory_space=pltpu.VMEM)] * 2,
        out_specs=[anywhere] * 2,
        scratch_shapes=[
            pltpu.SemaphoreType.DMA((2,)),
            pltpu.SemaphoreType.DMA((2, unit - 1)),
            pltpu.SemaphoreType.DMA((2, unit - 1)),
        ],
        compiler_params=pltpu.CompilerParams(
            collective_id=1, has_side_effects=True, vmem_limit_bytes=VMEM_LIMIT
        ),
        cost_estimate=BRIEF,
        name="unit_gather",
    )(x, d)


def gelu_parts(hidden):
    cdf = 0.5 + 0.5 * lax.erf(hidden * math.sqrt(0.5))
    density = jnp.exp(-0.5 * hidden * hidden) * (1.0 / math.sqrt(2.0 * math.pi))
    return hidden * cdf, cdf + hidden * density


def feed_core(
    normed, low, dy, grad_low, up_ref, up_right_ref, down_ref, down_left_ref, act_ref, grad_ref, hidden_step
):
    hidden_width = up_ref.shape[1]
    for start in range(0, hidden_width, hidden_step):
        cols = pl.ds(start, hidden_step)
        hidden = dot_nn(normed, up_ref[:, cols]) + dot_nn(low, up_right_ref[:, cols])
        grad_act = dot_nt(dy, down_ref[cols, :]) + dot_nt(grad_low, down_left_ref[cols, :])
        activated, slope = gelu_parts(hidden)
        act_ref[:, cols] = activated.astype(BF16)
        grad_ref[:, cols] = (grad_act * slope).astype(BF16)


def feed_first_kernel(
    x_ref, dy_ref, gain_ref, shift_ref, up_ref, up_left_ref, up_right_ref, down_ref, down_left_ref, rights_ref,
    normed_ref, low_ref, grad_lows_ref, out_ref, grad_ref, low_act_ref, grad_low_ref, up_right_grad_ref,
    down_left_grad_ref, act_ref, gh_ref,
):
    normed = normalize(x_ref[...].astype(F32), gain_ref[...], shift_ref[...]).astype(BF16)
    normed_ref[...] = normed
    dy = dy_ref[...]
    low = dot_nn(normed, up_left_ref[...]).astype(BF16)
    low_ref[...] = low
    grad_lows = dot_nt(dy, rights_ref[...]).astype(BF16)
    grad_lows_ref[...] = grad_lows
    grad_low = grad_lows[:, LANES:]
    feed_core(normed, low, dy, grad_low, up_ref, up_right_ref, down_ref, down_left_ref, act_ref, gh_ref, 256)
    act = act_ref[...]
    gh = gh_ref[...]
    out_ref[...] = dot_nn(act, down_ref[...])
    grad_ref[...] = dot_nt(gh, up_ref[...])
    low_act_ref[...] = dot_nn(act, down_left_ref[...])
    grad_low_ref[...] = dot_nt(gh, up_right_ref[...])

    @pl.when(pl.program_id(0) == 0)
    def _():
        up_right_grad_ref[...] = jnp.zeros_like(up_right_grad_ref)
        down_left_grad_ref[...] = jnp.zeros_like(down_left_grad_ref)

    up_right_grad_ref[...] += dot_tn(low, gh)
    down_left_grad_ref[...] += dot_tn(grad_low, act)


def feed_first(x, dy, gain, shift, up, up_left, up_right, down, down_left, rights, tile):
    rows, width = x.shape
    hidden = up.shape[1]
    return pl.pallas_call(
        feed_first_kernel,
        grid=(rows // tile,),
        in_specs=[
            rows_of(tile, width),
            rows_of(tile, width),
            whole((1, width)),
            whole((1, width)),
            whole(up.shape),
            whole(up_left.shape),
            whole(up_right.shape),
            whole(down.shape),
            whole(down_left.shape),
            whole(rights.shape),
        ],
        out_specs=[
            rows_of(tile, width),
            rows_of(tile, LANES),
            rows_of(tile, 2 * LANES),
            rows_of(tile, width),
            rows_of(tile, width),
            rows_of(tile, LANES),
            rows_of(tile, LANES),
            held((LANES, hidden)),
            held((LANES, hidden)),
        ],
        out_shape=[
            shaped((rows, width), BF16),
            shaped((rows, LANES), BF16),
            shaped((rows, 2 * LANES), BF16),
            shaped((rows, width), F32),
            shaped((rows, width), F32),
            shaped((rows, LANES), F32),
            shaped((rows, LANES), F32),
            shaped((LANES, hidden), F32),
            shaped((LANES, hidden), F32),
        ],
        scratch_shapes=[pltpu.VMEM((tile, hidden), BF16), pltpu.VMEM((tile, hidden), BF16)],
        compiler_params=params(),
        cost_estimate=BRIEF,
        name="feed_first",
    )(x, dy, gain, shift, up, up_left, up_right, down, down_left, rights)


def feed_second_kernel(
    send_tiles, order_ref, normed_ref, low_ref, dy_ref, grad_lows_ref, out_in_ref, grad_in_ref, low_act_in_ref,
    grad_low_in_ref, up_ref, up_left_ref, up_right_ref, down_ref, down_left_ref, out_send_ref, out_keep_ref,
    grad_send_ref, grad_keep_ref, low_act_send_ref, low_act_keep_ref, up_right_grad_ref, down_left_grad_ref,
    up_left_grad_ref, act_ref, gh_ref,
):
    step = pl.program_id(0)
    normed = normed_ref[...]
    low = low_ref[...]
    dy = dy_ref[...]
    grad_low = grad_lows_ref[:, LANES:]
    feed_core(normed, low, dy, grad_low, up_ref, up_right_ref, down_ref, down_left_ref, act_ref, gh_ref, 256)
    act = act_ref[...]
    gh = gh_ref[...]
    grad_low_up = (grad_low_in_ref[...] + dot_nt(gh, up_right_ref[...])).astype(BF16)
    out = (out_in_ref[...] + dot_nn(act, down_ref[...])).astype(BF16)
    low_act = (low_act_in_ref[...] + dot_nn(act, down_left_ref[...])).astype(BF16)
    grad = (
        grad_in_ref[...] + dot_nt(gh, up_ref[...]) + dot_nt(grad_low_up, up_left_ref[...])
    ).astype(BF16)

    @pl.when(step < send_tiles)
    def _():
        out_send_ref[...] = out
        grad_send_ref[...] = grad
        low_act_send_ref[...] = low_act

    @pl.when(step >= send_tiles)
    def _():
        out_keep_ref[...] = out
        grad_keep_ref[...] = grad
        low_act_keep_ref[...] = low_act

    @pl.when(step == 0)
    def _():
        up_right_grad_ref[...] = jnp.zeros_like(up_right_grad_ref)
        down_left_grad_ref[...] = jnp.zeros_like(down_left_grad_ref)
        up_left_grad_ref[...] = jnp.zeros_like(up_left_grad_ref)

    up_right_grad_ref[...] += dot_tn(low, gh)
    down_left_grad_ref[...] += dot_tn(grad_low, act)
    up_left_grad_ref[...] += dot_tn(grad_low_up, normed)


def ordered(tile, width):
    return pl.BlockSpec((tile, width), lambda i, order: (order[i], 0))


def sent(tile, width, tiles):
    return pl.BlockSpec((tile, width), lambda i, order: (jnp.minimum(i, tiles - 1), 0))


def kept(tile, width, tiles):
    return pl.BlockSpec((tile, width), lambda i, order: (jnp.maximum(i - tiles, 0), 0))


def feed_second(order, normed, low, dy, grad_lows, out, grad, low_act, grad_low, up, up_left, up_right, down,
                down_left, own_rows, tile):
    rows, width = normed.shape
    hidden = up.shape[1]
    send_rows = rows - own_rows
    tiles = send_rows // tile
    return pl.pallas_call(
        functools.partial(feed_second_kernel, tiles),
        grid_spec=pltpu.PrefetchScalarGridSpec(
            num_scalar_prefetch=1,
            grid=(rows // tile,),
            in_specs=[
                ordered(tile, width),
                ordered(tile, LANES),
                ordered(tile, width),
                ordered(tile, 2 * LANES),
                ordered(tile, width),
                ordered(tile, width),
                ordered(tile, LANES),
                ordered(tile, LANES),
                whole(up.shape),
                whole(up_left.shape),
                whole(up_right.shape),
                whole(down.shape),
                whole(down_left.shape),
            ],
            out_specs=[
                sent(tile, width, tiles),
                kept(tile, width, tiles),
                sent(tile, width, tiles),
                kept(tile, width, tiles),
                sent(tile, LANES, tiles),
                kept(tile, LANES, tiles),
                held((LANES, hidden)),
                held((LANES, hidden)),
                held((LANES, width)),
            ],
            scratch_shapes=[pltpu.VMEM((tile, hidden), BF16), pltpu.VMEM((tile, hidden), BF16)],
        ),
        out_shape=[
            shaped((send_rows, width), BF16),
            shaped((own_rows, width), BF16),
            shaped((send_rows, width), BF16),
            shaped((own_rows, width), BF16),
            shaped((send_rows, LANES), BF16),
            shaped((own_rows, LANES), BF16),
            shaped((LANES, hidden), F32),
            shaped((LANES, hidden), F32),
            shaped((LANES, width), F32),
        ],
        compiler_params=params(),
        cost_estimate=BRIEF,
        name="feed_second",
    )(order, normed, low, dy, grad_lows, out, grad, low_act, grad_low, up, up_left, up_right, down, down_left)


def project_body(
    normed, low, dy_ref, grad_lows_ref, triple_ref, right_ref, output_ref, output_left_ref, cos_ref, minus_ref,
    plus_ref, q_ref, k_ref, v_ref, g_ref,
):
    tables = (cos_ref[...], minus_ref[...], plus_ref[...])
    head_width = output_ref.shape[0]
    mixed = dot_nn(normed, triple_ref[...]) + dot_nn(low, right_ref[...])
    for start in range(0, head_width, LANES):
        cols = slice(start, start + LANES)
        query = rotate(mixed[:, cols], *tables).astype(BF16)
        q_ref[:, cols] = query * HEAD_DIM**-0.5
        k_ref[:, cols] = rotate(
            mixed[:, head_width + start : head_width + start + LANES], *tables
        ).astype(BF16)
    v_ref[...] = mixed[:, 2 * head_width :].astype(BF16)
    g_ref[...] = (
        dot_nt(dy_ref[...], output_ref[...]) + dot_nt(grad_lows_ref[:, :LANES], output_left_ref[...])
    ).astype(BF16)


def project_first_kernel(
    cont_ref, x_ref, dy_ref, grad_lows_ref, gain_ref, shift_ref, triple_ref, left_ref, right_ref, output_ref,
    output_left_ref, cos_ref, minus_ref, plus_ref, normed_ref, low_ref, q_ref, k_ref, v_ref, g_ref,
):
    normed = normalize(x_ref[...].astype(F32), gain_ref[...], shift_ref[...]).astype(BF16)
    normed_ref[...] = normed
    low = dot_nn(normed, left_ref[...]).astype(BF16)
    low_ref[...] = low
    project_body(
        normed, low, dy_ref, grad_lows_ref, triple_ref, right_ref, output_ref, output_left_ref, cos_ref, minus_ref,
        plus_ref, q_ref, k_ref, v_ref, g_ref,
    )


def project_second_kernel(
    cont_ref, normed_ref, low_ref, dy_ref, grad_lows_ref, triple_ref, right_ref, output_ref, output_left_ref, cos_ref,
    minus_ref, plus_ref, q_ref, k_ref, v_ref, g_ref,
):
    project_body(
        normed_ref[...], low_ref[...], dy_ref, grad_lows_ref, triple_ref, right_ref, output_ref, output_left_ref,
        cos_ref, minus_ref, plus_ref, q_ref, k_ref, v_ref, g_ref,
    )


def project(first, conts, inputs, dy, grad_lows, norm, triple, left, right, output, output_left, tables, tile):
    rows, width = dy.shape
    head_width = output.shape[0]
    per_block = SHORT // tile

    def table_index(i, cont):
        return (cont[i // per_block] * per_block + lax.rem(i, per_block), 0)

    table = pl.BlockSpec((tile, LANES), table_index)
    row_specs = [rows_of(tile, value.shape[1]) for value in inputs]
    row_specs += [rows_of(tile, width), rows_of(tile, 2 * LANES)]
    fixed = list(norm) + [triple] + ([left] if first else []) + [right, output, output_left]
    new_specs = [rows_of(tile, width), rows_of(tile, LANES)] if first else []
    new_shapes = [shaped((rows, width), BF16), shaped((rows, LANES), BF16)] if first else []
    return pl.pallas_call(
        project_first_kernel if first else project_second_kernel,
        grid_spec=pltpu.PrefetchScalarGridSpec(
            num_scalar_prefetch=1,
            grid=(rows // tile,),
            in_specs=row_specs + [whole(value.shape) for value in fixed] + [table] * 3,
            out_specs=new_specs + [rows_of(tile, head_width)] * 4,
        ),
        out_shape=new_shapes + [shaped((rows, head_width), BF16)] * 4,
        compiler_params=params(),
        cost_estimate=BRIEF,
        name="project_first" if first else "project_second",
    )(conts, *inputs, dy, grad_lows, *fixed, *tables)


def attend_rows(with_prev, start, count, q_ref, k_ref, v_ref, g_ref, kp_ref, vp_ref, tables, att_ref, gq_ref,
                dk_ref, dv_ref, dkp_ref, dvp_ref):
    first_head = lax.broadcasted_iota(jnp.int32, (1, LANES), 1) < HEAD_DIM
    span = pl.ds(start, count)
    known = start + count
    zero = jnp.zeros((), BF16)

    def stack(pair):
        return jnp.concatenate([jnp.where(first_head, pair, zero), jnp.where(first_head, zero, pair)], axis=0)

    def unstack(both):
        return jnp.where(first_head, both[:count], both[count:])

    queries = stack(q_ref[span, :])
    grads = stack(g_ref[span, :])
    keys = k_ref[pl.ds(0, known), :]
    values = v_ref[pl.ds(0, known), :]
    scores = dot_nt(queries, keys)
    row = lax.broadcasted_iota(jnp.int32, (2 * count, known), 0)
    column = lax.broadcasted_iota(jnp.int32, (2 * count, known), 1)
    row = jnp.where(row >= count, row - count, row) + start
    scores = jnp.where(column <= row, scores, -1e30)
    peak = jnp.max(scores, axis=1, keepdims=True)
    if with_prev:
        prev_scores = dot_nt(queries, kp_ref[...])
        peak = jnp.maximum(peak, jnp.max(prev_scores, axis=1, keepdims=True))
        prev_exp = jnp.exp(prev_scores - peak)
    exp = jnp.exp(scores - peak)
    total = jnp.sum(exp, axis=1, keepdims=True)
    if with_prev:
        total = total + jnp.sum(prev_exp, axis=1, keepdims=True)
    scale = 1.0 / total
    weights = exp * scale
    weights_low = weights.astype(BF16)
    attended = dot_nn(weights_low, values)
    grad_weights = dot_nt(grads, values)
    inner = jnp.sum(weights * grad_weights, axis=1, keepdims=True)
    if with_prev:
        prev_weights = prev_exp * scale
        prev_low = prev_weights.astype(BF16)
        attended = attended + dot_nn(prev_low, vp_ref[...])
        prev_grad = dot_nt(grads, vp_ref[...])
        inner = inner + jnp.sum(prev_weights * prev_grad, axis=1, keepdims=True)
        prev_ds = (prev_weights * (prev_grad - inner)).astype(BF16)
    ds = (weights * (grad_weights - inner)).astype(BF16)
    grad_query = dot_nn(ds, keys)
    if with_prev:
        grad_query = grad_query + dot_nn(prev_ds, kp_ref[...])
        dkp_ref[...] += dot_tn(prev_ds, queries)
        dvp_ref[...] += dot_tn(prev_low, grads)
    dk_ref[pl.ds(0, known), :] += dot_tn(ds, queries)
    dv_ref[pl.ds(0, known), :] += dot_tn(weights_low, grads)
    att_ref[span, :] = unstack(attended).astype(BF16)
    grad_query = unstack(grad_query) * HEAD_DIM**-0.5
    gq_ref[span, :] = unrotate(grad_query, *[table[start : start + count] for table in tables]).astype(BF16)


def attend_kernel(
    blocks, count, cont_ref, q_ref, k_ref, v_ref, g_ref, k_before_ref, v_before_ref, k_halo_ref, v_halo_ref, cos_ref,
    minus_ref, plus_ref, att_ref, gq_ref, gk_ref, gv_ref, dk_halo_ref, dv_halo_ref, kp_ref, vp_ref, dk_ref, dv_ref,
    dkp_ref, dvp_ref,
):
    step = pl.program_id(1)
    block = blocks - 1 - step
    continued = cont_ref[block]
    offset = pl.multiple_of(continued * SHORT, SHORT)
    tables = tuple(ref[pl.ds(offset, SHORT), :] for ref in (cos_ref, minus_ref, plus_ref))

    @pl.when(step == 0)
    def _():
        dk_ref[...] = jnp.zeros_like(dk_ref)
        dv_ref[...] = jnp.zeros_like(dv_ref)

    @pl.when(step > 0)
    def _():
        dk_ref[...] = dkp_ref[...]
        dv_ref[...] = dvp_ref[...]

    dkp_ref[...] = jnp.zeros_like(dkp_ref)
    dvp_ref[...] = jnp.zeros_like(dvp_ref)
    args = (q_ref, k_ref, v_ref, g_ref, kp_ref, vp_ref, tables, att_ref, gq_ref, dk_ref, dv_ref, dkp_ref, dvp_ref)

    @pl.when(continued == 0)
    def _():
        for start in range(0, SHORT, count):
            attend_rows(False, start, count, *args)

    @pl.when(continued != 0)
    def _():
        @pl.when(block == 0)
        def _():
            kp_ref[...] = k_halo_ref[...]
            vp_ref[...] = v_halo_ref[...]

        @pl.when(block != 0)
        def _():
            kp_ref[...] = k_before_ref[...]
            vp_ref[...] = v_before_ref[...]

        for start in range(0, SHORT, count):
            attend_rows(True, start, count, *args)

    gk_ref[...] = unrotate(dk_ref[...], *tables).astype(BF16)
    gv_ref[...] = dv_ref[...].astype(BF16)

    @pl.when(block == 0)
    def _():
        base = tuple(ref[pl.ds(0, SHORT), :] for ref in (cos_ref, minus_ref, plus_ref))
        dk_halo_ref[...] = unrotate(dkp_ref[...], *base).astype(BF16)
        dv_halo_ref[...] = dvp_ref[...].astype(BF16)


def attend(conts, q, k, v, g, k_halo, v_halo, tables, count):
    rows, head_width = q.shape
    blocks = rows // SHORT
    here = pl.BlockSpec((SHORT, LANES), lambda p, i, cont: (blocks - 1 - i, p))
    before = pl.BlockSpec((SHORT, LANES), lambda p, i, cont: (jnp.maximum(blocks - 2 - i, 0), p))
    halo = pl.BlockSpec((SHORT, LANES), lambda p, i, cont: (0, p))
    return pl.pallas_call(
        functools.partial(attend_kernel, blocks, count),
        grid_spec=pltpu.PrefetchScalarGridSpec(
            num_scalar_prefetch=1,
            grid=(head_width // LANES, blocks),
            in_specs=[here] * 4 + [before] * 2 + [halo] * 2 + [whole(table.shape) for table in tables],
            out_specs=[here] * 4 + [halo] * 2,
            scratch_shapes=[pltpu.VMEM((SHORT, LANES), BF16)] * 2 + [pltpu.VMEM((SHORT, LANES), F32)] * 4,
        ),
        out_shape=[shaped((rows, head_width), BF16)] * 4 + [shaped((SHORT, head_width), BF16)] * 2,
        compiler_params=params(2),
        cost_estimate=BRIEF,
        name="attend",
    )(conts, q, k, v, g, k, v, k_halo, v_halo, *tables)


def settle_kernel(
    send_tiles, halo_start, order_ref, normed_ref, low_ref, grad_lows_ref, out_in_ref,
    att0_ref, att1_ref, gq0_ref, gq1_ref, gk0_ref, gk1_ref, gv0_ref, gv1_ref, hk0_ref, hk1_ref, hv0_ref, hv1_ref,
    triple0_ref, triple1_ref, right0_ref, right1_ref, left_ref, output0_ref, output1_ref, output_left0_ref,
    output_left1_ref, out_ref, grad_send_ref, grad_keep_ref, low_att_send_ref, low_att_keep_ref, right_grad0_ref,
    right_grad1_ref, left_grad_ref, output_left_grad0_ref, output_left_grad1_ref,
):
    step = pl.program_id(0)
    here = (order_ref[step] >= halo_start).astype(F32)
    normed = normed_ref[...]
    low = low_ref[...]
    grad_low_out = grad_lows_ref[:, :LANES]
    att0, att1 = att0_ref[...], att1_ref[...]

    def mixed(gq, gk, gv, hk, hv):
        key = (gk[...].astype(F32) + here * hk[...].astype(F32)).astype(BF16)
        value = (gv[...].astype(F32) + here * hv[...].astype(F32)).astype(BF16)
        return jnp.concatenate([gq[...], key, value], axis=1)

    grad0 = mixed(gq0_ref, gk0_ref, gv0_ref, hk0_ref, hv0_ref)
    grad1 = mixed(gq1_ref, gk1_ref, gv1_ref, hk1_ref, hv1_ref)
    grad_low = (dot_nt(grad0, right0_ref[...]) + dot_nt(grad1, right1_ref[...])).astype(BF16)
    grad = (
        dot_nt(grad0, triple0_ref[...]) + dot_nt(grad1, triple1_ref[...]) + dot_nt(grad_low, left_ref[...])
    ).astype(BF16)
    out_ref[...] = out_in_ref[...] + dot_nn(att0, output0_ref[...]) + dot_nn(att1, output1_ref[...])
    low_att = (dot_nn(att0, output_left0_ref[...]) + dot_nn(att1, output_left1_ref[...])).astype(BF16)

    @pl.when(step < send_tiles)
    def _():
        grad_send_ref[...] = grad
        low_att_send_ref[...] = low_att

    @pl.when(step >= send_tiles)
    def _():
        grad_keep_ref[...] = grad
        low_att_keep_ref[...] = low_att

    sums = (right_grad0_ref, right_grad1_ref, left_grad_ref, output_left_grad0_ref, output_left_grad1_ref)

    @pl.when(step == 0)
    def _():
        for ref in sums:
            ref[...] = jnp.zeros_like(ref)

    right_grad0_ref[...] += dot_tn(low, grad0)
    right_grad1_ref[...] += dot_tn(low, grad1)
    left_grad_ref[...] += dot_tn(grad_low, normed)
    output_left_grad0_ref[...] += dot_tn(grad_low_out, att0)
    output_left_grad1_ref[...] += dot_tn(grad_low_out, att1)


def settle(order, normed, low, grad_lows, out, pairs, halos, weights, own_rows, tile):
    rows, width = normed.shape
    head_width = pairs[0].shape[1]
    send_rows = rows - own_rows
    tiles = send_rows // tile
    halo_start = (rows - SHORT) // tile
    halo = pl.BlockSpec((tile, head_width), lambda i, order: (jnp.maximum(order[i] - halo_start, 0), 0))
    return pl.pallas_call(
        functools.partial(settle_kernel, tiles, halo_start),
        grid_spec=pltpu.PrefetchScalarGridSpec(
            num_scalar_prefetch=1,
            grid=(rows // tile,),
            in_specs=[ordered(tile, width), ordered(tile, LANES), ordered(tile, 2 * LANES), ordered(tile, width)]
            + [ordered(tile, head_width)] * 8
            + [halo] * 4
            + [whole(value.shape) for value in weights],
            out_specs=[
                ordered(tile, width),
                sent(tile, width, tiles),
                kept(tile, width, tiles),
                sent(tile, LANES, tiles),
                kept(tile, LANES, tiles),
                held((LANES, 3 * head_width)),
                held((LANES, 3 * head_width)),
                held((LANES, width)),
                held((LANES, head_width)),
                held((LANES, head_width)),
            ],
        ),
        out_shape=[
            shaped((rows, width), F32),
            shaped((send_rows, width), BF16),
            shaped((own_rows, width), BF16),
            shaped((send_rows, LANES), BF16),
            shaped((own_rows, LANES), BF16),
            shaped((LANES, 3 * head_width), F32),
            shaped((LANES, 3 * head_width), F32),
            shaped((LANES, width), F32),
            shaped((LANES, head_width), F32),
            shaped((LANES, head_width), F32),
        ],
        compiler_params=params(),
        cost_estimate=BRIEF,
        name="settle",
    )(order, normed, low, grad_lows, out, *pairs, *halos, *weights)


def finish_kernel(
    peers, x_ref, dy_ref, gain1_ref, gain2_ref, output_right_ref, shrink_right_ref, out_ref, first_ref, second_ref,
    low_att_ref, low_act_ref, *refs,
):
    others = refs[: 5 * peers]
    y_ref, dx_ref, norms_ref, output_right_grad_ref, shrink_right_grad_ref = refs[5 * peers :]

    def total(own, which):
        value = own[...].astype(F32)
        for j in range(peers):
            value = value + others[5 * j + which][...].astype(F32)
        return value

    out = total(out_ref, 0)
    first = total(first_ref, 1)
    second = total(second_ref, 2)
    low_att = total(low_att_ref, 3).astype(BF16)
    low_act = total(low_act_ref, 4).astype(BF16)
    x = x_ref[...].astype(F32)
    dy = dy_ref[...]
    y_ref[...] = (
        x + out + dot_nn(low_att, output_right_ref[...]) + dot_nn(low_act, shrink_right_ref[...])
    ).astype(BF16)
    center = x - jnp.mean(x, axis=-1, keepdims=True)
    spread = jnp.mean(center * center, axis=-1, keepdims=True)
    inverse = lax.rsqrt(spread + EPS)
    unit = center * inverse
    scaled = first * gain1_ref[...] + second * gain2_ref[...]
    mean = jnp.mean(scaled, axis=-1, keepdims=True)
    inner = jnp.mean(scaled * unit, axis=-1, keepdims=True)
    dx_ref[...] = dy.astype(F32) + (scaled - mean - unit * inner) * inverse

    @pl.when(pl.program_id(0) == 0)
    def _():
        norms_ref[...] = jnp.zeros_like(norms_ref)
        output_right_grad_ref[...] = jnp.zeros_like(output_right_grad_ref)
        shrink_right_grad_ref[...] = jnp.zeros_like(shrink_right_grad_ref)

    norms_ref[0:1, :] += jnp.sum(first * unit, axis=0, keepdims=True)
    norms_ref[1:2, :] += jnp.sum(first, axis=0, keepdims=True)
    norms_ref[2:3, :] += jnp.sum(second * unit, axis=0, keepdims=True)
    norms_ref[3:4, :] += jnp.sum(second, axis=0, keepdims=True)
    output_right_grad_ref[...] += dot_tn(low_att, dy)
    shrink_right_grad_ref[...] += dot_tn(low_act, dy)


def finish(x, dy, gain1, gain2, output_right, shrink_right, own, others, tile):
    rows, width = x.shape
    peers = len(others)
    widths = (width, width, width, LANES, LANES)
    return pl.pallas_call(
        functools.partial(finish_kernel, peers),
        grid=(rows // tile,),
        in_specs=[rows_of(tile, width)] * 2
        + [whole((1, width))] * 2
        + [whole(output_right.shape)] * 2
        + [rows_of(tile, size) for size in widths] * (1 + peers),
        out_specs=[rows_of(tile, width)] * 2 + [held((8, width)), held((LANES, width)), held((LANES, width))],
        out_shape=[
            shaped((rows, width), BF16),
            shaped((rows, width), F32),
            shaped((8, width), F32),
            shaped((LANES, width), F32),
            shaped((LANES, width), F32),
        ],
        compiler_params=params(),
        cost_estimate=BRIEF,
        name="finish",
    )(x, dy, gain1, gain2, output_right, shrink_right, *own, *[value for other in others for value in other])


SUM_ROWS = (2, 4, 16)


def sum_kernel(chunks, width, extra, part_ref, both_ref, out_ref, both_out_ref, *scratch):
    dp = lax.axis_index("dp")
    mp = lax.axis_index("mp")
    half, core = mp // 2, lax.rem(mp, 2)
    x, z = lax.rem(dp, 2), dp // 2
    x_peer = (dp + 1 - 2 * x, mp)
    y_peer = (dp, mp + 2 - 4 * half)
    core_peer = (dp, mp + 1 - 2 * core)
    z_places = [lax.rem(z + j, 4) for j in range(1, 4)]
    z_peers = [(place * 2 + x, mp) for place in z_places]
    barrier = pltpu.get_barrier_semaphore()
    for peer in [x_peer, y_peer, core_peer] + z_peers:
        pl.semaphore_signal(barrier, inc=1, device_id=peer, device_id_type=MESH)
    pl.semaphore_wait(barrier, 6)
    started = []

    def send(src, dst, sems, slot, peer):
        copy = pltpu.make_async_remote_copy(
            src_ref=src, dst_ref=dst, send_sem=sems.at[0, slot], recv_sem=sems.at[1, slot], device_id=peer,
            device_id_type=MESH,
        )
        copy.start()
        started.append(copy)
        return copy

    def added(first, *others):
        total = first.astype(F32)
        for other in others:
            total = total + other.astype(F32)
        return total.astype(BF16)

    both_got_ref, both_sum_ref, core_sems, local_sems = scratch[:4]
    refs = [scratch[4 + 7 * i : 4 + 7 * (i + 1)] for i in range(len(chunks))]
    both_copy = send(both_ref.at[1 - core], both_got_ref, core_sems, 0, core_peer)

    def run(index):
        y_first, start, size = chunks[index]
        got1, work1, got2, work2, got_z, full, sems = refs[index]
        shared = start is None
        if shared:
            both_copy.wait_recv()
            for place, at in ((0, half), (1, 1 - half)):
                both_sum_ref[place] = added(both_ref[core, at], both_got_ref[at])
            source = both_sum_ref
        else:
            source = part_ref.at[:, :, :, :, pl.ds(start, size)]
        if y_first:
            copy = send(source.at[1], got1, sems, 0, y_peer)
            yield
            copy.wait_recv()
            work1[...] = added(source[0], got1[...])
            copy = send(work1.at[1 - x], got2, sems, 1, x_peer)
            yield
            copy.wait_recv()
            work2[...] = added(work1[x], got2[...])
        else:
            copy = send(source.at[:, 1 - x], got1, sems, 0, x_peer)
            yield
            copy.wait_recv()
            work1[...] = added(source[:, x], got1[...])
            copy = send(work1.at[1], got2, sems, 1, y_peer)
            yield
            copy.wait_recv()
            work2[...] = added(work1[0], got2[...])
        copies = [
            send(work2.at[place], got_z.at[j], sems, 2 + j, peer)
            for j, (place, peer) in enumerate(zip(z_places, z_peers))
        ]
        yield
        for copy in copies:
            copy.wait_recv()
        full[0, x, z] = added(work2[z], got_z[0], got_z[1], got_z[2])
        mine = full.at[0, x, z]
        copies = [send(mine, mine, sems, 5 + j, peer) for j, peer in enumerate(z_peers)]
        yield
        for copy in copies:
            copy.wait_recv()
        if y_first:
            copy = send(full.at[0, x], full.at[0, x], sems, 8, x_peer)
            yield
            copy.wait_recv()
            copy = send(full.at[0], full.at[1], sems, 9, y_peer)
        else:
            copy = send(full.at[0, x], full.at[1, x], sems, 8, y_peer)
            yield
            copy.wait_recv()
            copy = send(full.at[:, x], full.at[:, x], sems, 9, x_peer)
        yield
        copy.wait_recv()
        target = both_out_ref if shared else out_ref.at[:, :, :, :, :, pl.ds(start, size)]
        last = []
        for place, at in ((0, half), (1, 1 - half)):
            local = pltpu.make_async_copy(full.at[place], target.at[core, at], local_sems.at[index, place])
            local.start()
            last.append(local)
            last.append(send(full.at[place], target.at[core, at], sems, 10 + place, core_peer))
        yield
        last[0].wait()
        last[1].wait_recv()
        last[2].wait()
        last[3].wait_recv()

    running = [run(i) for i in range(len(chunks))]
    while running:
        running = [step for step in running if next(step, "end") != "end"]
    for copy in started:
        copy.wait_send()


def sum_all(part, both):
    width, extra = part.shape[-1], both.shape[-1]
    third = width // 3
    chunks = [(True, 0, third), (False, third, third), (True, 2 * third, third), (False, None, extra)]
    per_chunk = []
    for y_first, _, size in chunks:
        one = (16, size)
        per_chunk += [
            pltpu.VMEM(((2, 4) if y_first else (2, 4)) + one, BF16),
            pltpu.VMEM((2, 4) + one, BF16),
            pltpu.VMEM((4,) + one, BF16),
            pltpu.VMEM((4,) + one, BF16),
            pltpu.VMEM((3,) + one, BF16),
            pltpu.VMEM((2, 2, 4) + one, BF16),
            pltpu.SemaphoreType.DMA((2, 12)),
        ]
    out, both_out = pl.pallas_call(
        functools.partial(sum_kernel, chunks, width, extra),
        out_shape=[shaped((2, 2) + SUM_ROWS + (width,), BF16), shaped((2, 2) + SUM_ROWS + (extra,), BF16)],
        in_specs=[pl.BlockSpec(memory_space=pltpu.VMEM)] * 2,
        out_specs=[pl.BlockSpec(memory_space=pl.ANY)] * 2,
        scratch_shapes=[
            pltpu.VMEM((2,) + SUM_ROWS + (extra,), BF16),
            pltpu.VMEM((2,) + SUM_ROWS + (extra,), BF16),
            pltpu.SemaphoreType.DMA((2, 1)),
            pltpu.SemaphoreType.DMA((len(chunks), 2)),
        ]
        + per_chunk,
        compiler_params=pltpu.CompilerParams(
            collective_id=2, has_side_effects=True, vmem_limit_bytes=VMEM_LIMIT
        ),
        cost_estimate=BRIEF,
        name="sum_all",
    )(part.reshape((2,) + SUM_ROWS + (width,)), both.reshape((2, 2) + SUM_ROWS + (extra,)))
    return out.reshape(2, 2, 128, width), both_out.reshape(2, 2, 128, extra)


def unpack_kernel(widths, part_ref, both_ref, perm_ref, triple_ref, output_ref, up_ref, down_ref, triple_left_ref,
                  up_left_ref, output_right_ref, down_right_ref, norm_ref):
    triple_width, head_width, hidden = widths
    start = triple_width
    triple_ref[...] = dot_nt(part_ref[0, 0, :, :triple_width], perm_ref[...])
    output_ref[...] = part_ref[0, 0, :, start : start + head_width].astype(F32).T
    start += head_width
    up_ref[...] = part_ref[0, 0, :, start : start + hidden].astype(F32)
    start += hidden
    down_ref[...] = part_ref[0, 0, :, start : start + hidden].astype(F32).T
    size = triple_left_ref.shape[0]
    triple_left_ref[...] = both_ref[0, 0, :, :size].astype(F32).T
    up_left_ref[...] = both_ref[0, 0, :, size : 2 * size].astype(F32).T
    output_right_ref[...] = both_ref[0, 0, :, 2 * size : 3 * size].astype(F32)
    down_right_ref[...] = both_ref[0, 0, :, 3 * size : 4 * size].astype(F32)
    norm_ref[0] = both_ref[0, 0, : norm_ref.shape[1], 4 * size :].astype(F32)


def unpack(part, both, perm, width, triple_width, head_width, hidden):
    quarter = width // 4

    def tall(rows):
        return pl.BlockSpec((rows, LANES), lambda s: (s, 0))

    def wide(cols):
        return pl.BlockSpec((LANES, cols), lambda s: (0, s))

    def piece(cols):
        return pl.BlockSpec((1, 1, LANES, cols), lambda s: (lax.rem(s, 2), s // 2, 0, 0))

    return pl.pallas_call(
        functools.partial(unpack_kernel, (triple_width, head_width, hidden)),
        grid=(4,),
        in_specs=[piece(part.shape[-1]), piece(both.shape[-1]), whole(perm.shape)],
        out_specs=[
            wide(triple_width), tall(head_width), wide(hidden), tall(hidden), tall(quarter), tall(quarter),
            wide(quarter), wide(quarter), pl.BlockSpec((1, width // LANES, LANES), lambda s: (s, 0, 0)),
        ],
        out_shape=[
            shaped((LANES, 4 * triple_width), F32),
            shaped((4 * head_width, LANES), F32),
            shaped((LANES, 4 * hidden), F32),
            shaped((4 * hidden, LANES), F32),
            shaped((width, LANES), F32),
            shaped((width, LANES), F32),
            shaped((LANES, width), F32),
            shaped((LANES, width), F32),
            shaped((4, width // LANES, LANES), F32),
        ],
        compiler_params=params(),
        cost_estimate=BRIEF,
        name="unpack",
    )(part, both, perm)


def shards(
    ranks,
    groups,
    block_input,
    sequence_lengths,
    first_gain,
    first_shift,
    second_gain,
    second_shift,
    triple_weight,
    triple_left,
    triple_right,
    output_weight,
    output_left,
    output_right,
    expand_weight,
    expand_left,
    expand_right,
    shrink_weight,
    shrink_left,
    shrink_right,
    cotangent,
):
    unit = ranks // 2
    own_rows, width = block_input.shape
    rows = own_rows * unit
    blocks = rows // SHORT
    tile = math.gcd(own_rows, 256)
    triple_width = triple_weight.shape[1]
    head_width = output_weight.shape[0]
    hidden = expand_weight.shape[1]
    mp = lax.axis_index("mp")
    half = mp // unit
    place = lax.rem(mp, unit)
    far = lax.rem(mp + unit, ranks)
    swap = [(m, (m + unit) % ranks) for m in range(ranks)]
    onward = [(m, m + unit) for m in range(unit)]
    back = [(m + unit, m) for m in range(unit)]

    tables = rotary_tables()
    perm = gather_columns(triple_width)
    continues = find_flags(sequence_lengths[0])
    conts = lax.dynamic_slice_in_dim(continues, half * blocks, blocks, 0)
    per_device = own_rows // tile
    order = jnp.concatenate(
        [
            lax.rem(place + j, unit) * per_device + jnp.arange(per_device, dtype=jnp.int32)
            for j in list(range(1, unit)) + [0]
        ]
    ).astype(jnp.int32)

    def cols(matrix, size, shard):
        return lax.dynamic_slice_in_dim(matrix, shard * size, size, 1)

    def tall(matrix, size, shard):
        return lax.dynamic_slice_in_dim(matrix, shard * size, size, 0)

    def arranged(matrix):
        return jnp.dot(matrix, perm, preferred_element_type=F32).astype(BF16)

    dp = lax.axis_index("dp")
    lead = lax.rem(dp, 2)
    beside = [(d, d + 1 - 2 * (d % 2)) for d in range(groups)]

    def over_y(matrix):
        count = matrix.shape[0] // 2
        return lax.ppermute(lax.dynamic_slice_in_dim(matrix, lead * count, count, 0), "mp", swap)

    def over_x(piece):
        other = lax.ppermute(piece, "dp", beside)
        return jnp.where(
            lead == 0, jnp.concatenate([piece, other], axis=0), jnp.concatenate([other, piece], axis=0)
        )

    triple_own = arranged(triple_weight)
    triple_piece = over_y(triple_own)
    output_piece = over_y(output_weight)
    expand_piece = over_y(expand_weight)
    shrink_piece = over_y(shrink_weight)

    gain1, shift1 = first_gain[None, :], first_shift[None, :]
    gain2, shift2 = second_gain[None, :], second_shift[None, :]
    rights = jnp.concatenate([output_right, shrink_right], axis=0)

    x, dy = unit_gather(unit, block_input, cotangent)

    (normed2, low2, grad_lows, out, grad2, low_act, grad_low2, expand_right_own, shrink_left_own) = feed_first(
        x, dy, gain2, shift2, expand_weight, expand_left, cols(expand_right, hidden, mp), shrink_weight,
        tall(shrink_left, hidden, mp), rights, tile,
    )

    triple_piece, output_piece, low2 = lax.optimization_barrier((triple_piece, output_piece, low2))
    triple_far = over_x(triple_piece)
    output_far = over_x(output_piece)

    right_own = arranged(cols(triple_right, triple_width, mp))
    right_far = arranged(cols(triple_right, triple_width, far))
    output_left_own = tall(output_left, head_width, mp)
    output_left_far = tall(output_left, head_width, far)
    normed1, low1, q_own, k_own, v_own, g_own = project(
        True, conts, (x,), dy, grad_lows, (gain1, shift1), triple_own, triple_left, right_own, output_weight,
        output_left_own, tables, tile,
    )
    last = slice(rows - SHORT, rows)
    halo_far = lax.ppermute(jnp.concatenate([k_own[last], v_own[last]], axis=0), "mp", onward)
    q_far, k_far, v_far, g_far = project(
        False, conts, (normed1, low1), dy, grad_lows, (), triple_far, None, right_far, output_far, output_left_far,
        tables, tile,
    )
    halo_own = lax.ppermute(jnp.concatenate([k_far[last], v_far[last]], axis=0), "mp", onward)
    expand_piece, shrink_piece, q_far = lax.optimization_barrier((expand_piece, shrink_piece, q_far))
    expand_far = over_x(expand_piece)
    shrink_far = over_x(shrink_piece)
    count = 256
    att_far, gq_far, gk_far, gv_far, hk, hv = attend(
        conts, q_far, k_far, v_far, g_far, halo_far[:SHORT], halo_far[SHORT:], tables, count
    )
    back_own = lax.ppermute(jnp.concatenate([hk, hv], axis=0), "mp", back)
    att_own, gq_own, gk_own, gv_own, hk, hv = attend(
        conts, q_own, k_own, v_own, g_own, halo_own[:SHORT], halo_own[SHORT:], tables, count
    )
    back_far = lax.ppermute(jnp.concatenate([hk, hv], axis=0), "mp", back)
    (out, grad1_send, grad1_keep, low_att_send, low_att_keep, triple_right_own, triple_right_far, triple_left_sum,
     output_left_sum_own, output_left_sum_far) = settle(
        order, normed1, low1, grad_lows, out,
        (att_own, att_far, gq_own, gq_far, gk_own, gk_far, gv_own, gv_far),
        (back_own[:SHORT], back_far[:SHORT], back_own[SHORT:], back_far[SHORT:]),
        (triple_own, triple_far, right_own, right_far, triple_left, output_weight, output_far, output_left_own,
         output_left_far),
        own_rows, tile,
    )

    (out_send, out_keep, grad2_send, grad2_keep, low_act_send, low_act_keep, expand_right_far, shrink_left_far,
     expand_left_sum) = feed_second(
        order, normed2, low2, dy, grad_lows, out, grad2, low_act, grad_low2, expand_far, expand_left,
        cols(expand_right, hidden, far), shrink_far, tall(shrink_left, hidden, far), own_rows, tile,
    )

    def pass_on(sent_rows):
        got = []
        for j in range(1, unit):
            ring = [(m, m - m % unit + (m % unit + j) % unit) for m in range(ranks)]
            got.append(lax.ppermute(sent_rows[(j - 1) * own_rows : j * own_rows], "mp", ring))
        return got

    sends = (out_send, grad1_send, grad2_send, low_att_send, low_act_send)
    arrived = list(zip(*[pass_on(value) for value in sends]))
    block_output, input_gradient, norms, output_right_sum, shrink_right_sum = finish(
        block_input, cotangent, gain1, gain2, output_right, shrink_right,
        (out_keep, grad1_keep, grad2_keep, low_att_keep, low_act_keep), arrived, tile,
    )

    own_sums = (triple_right_own, output_left_sum_own, expand_right_own, shrink_left_own)
    far_sums = (triple_right_far, output_left_sum_far, expand_right_far, shrink_left_far)
    both_sums = (triple_left_sum, expand_left_sum, output_right_sum, shrink_right_sum)
    if ranks == 4 and groups == 8:
        part = jnp.stack(
            [jnp.concatenate([value.astype(BF16) for value in sums], axis=1) for sums in (own_sums, far_sums)]
        )
        quarters = [value.astype(BF16).reshape(LANES, 4, width // 4) for value in both_sums]
        norms = jnp.pad(
            norms[:4].astype(BF16).reshape(4, width // LANES, LANES), ((0, 0), (0, LANES - width // LANES), (0, 0))
        )
        both = jnp.concatenate([value.transpose(1, 0, 2) for value in quarters] + [norms], axis=2)
        both = both.reshape(2, 2, LANES, width + LANES).transpose(1, 0, 2, 3)
        part, both = sum_all(part, both)
        (triple_right_sum, output_left_sum, expand_right_sum, shrink_left_sum, triple_left_sum, expand_left_sum,
         output_right_sum, shrink_right_sum, norms) = unpack(
            part, both, perm, width, triple_width, head_width, hidden
        )
        norms = norms.reshape(4, width)
    else:

        def spread(own, other):
            size = own.shape[1]
            wide = jnp.zeros((LANES, size * ranks), BF16)
            wide = lax.dynamic_update_slice_in_dim(wide, own.astype(BF16), mp * size, 1)
            return lax.dynamic_update_slice_in_dim(wide, other.astype(BF16), far * size, 1)

        sums = [spread(own, other) for own, other in zip(own_sums, far_sums)]
        sums += [value.astype(BF16) for value in both_sums]
        norms, *sums = lax.psum([norms] + sums, ("dp", "mp"))
        (triple_right_sum, output_left_sum, expand_right_sum, shrink_left_sum, triple_left_sum, expand_left_sum,
         output_right_sum, shrink_right_sum) = [value.astype(F32) for value in sums]
        triple_right_sum = (
            triple_right_sum.reshape(LANES, ranks, 3, head_width // HEAD_DIM, HEAD_DIM).transpose(0, 1, 3, 2, 4)
        ).reshape(triple_right.shape)
        output_left_sum, shrink_left_sum = output_left_sum.T, shrink_left_sum.T
        triple_left_sum, expand_left_sum = triple_left_sum.T, expand_left_sum.T
    return (
        block_output,
        input_gradient,
        norms[0],
        norms[1],
        norms[2],
        norms[3],
        triple_left_sum,
        triple_right_sum,
        output_left_sum,
        output_right_sum,
        expand_left_sum,
        expand_right_sum,
        shrink_left_sum,
        shrink_right_sum,
    )


def solution(mesh):
    placed = (
        P(("dp", "mp"), None),
        P("dp", None),
        P(),
        P(),
        P(),
        P(),
        P(None, "mp"),
        P(),
        P(),
        P("mp", None),
        P(),
        P(),
        P(None, "mp"),
        P(),
        P(),
        P("mp", None),
        P(),
        P(),
        P(("dp", "mp"), None),
    )
    return jax.shard_map(
        functools.partial(shards, mesh.shape["mp"], mesh.shape["dp"]),
        mesh=mesh,
        in_specs=placed,
        out_specs=(P(("dp", "mp"), None), P(("dp", "mp"), None)) + (P(),) * 12,
        check_vma=False,
    )
```

```python
import functools
import math

import jax
import jax.numpy as jnp
import numpy as np
from jax import lax
from jax.experimental import pallas as pl
from jax.experimental.pallas import tpu as pltpu
from jax.sharding import PartitionSpec as P

HEAD_DIM = 64
ROT = 16
SHORT = 512
TOK_GRP = 3072
SLOTS = 6
EPS = 1e-05
LANES = 128
MESH = pl.DeviceIdType.MESH
BF16 = jnp.bfloat16
F32 = jnp.float32
VMEM_LIMIT = 56 * 1024 * 1024
BRIEF = pl.CostEstimate(flops=1, bytes_accessed=1, transcendentals=0)


def dot_nn(former, latter):
    return lax.dot_general(
        former, latter, (((1,), (0,)), ((), ())), preferred_element_type=F32
    )


def dot_nt(former, latter):
    return lax.dot_general(
        former, latter, (((1,), (1,)), ((), ())), preferred_element_type=F32
    )


def dot_tn(former, latter):
    return lax.dot_general(
        former, latter, (((0,), (0,)), ((), ())), preferred_element_type=F32
    )


def find_flags(group_lengths):
    seq_ends = jnp.cumsum(group_lengths, dtype=jnp.int32)
    starts = seq_ends - group_lengths
    block_starts = jnp.arange(SLOTS, dtype=jnp.int32) * SHORT
    begins = jnp.any(
        (starts[None, :] == block_starts[:, None]) & (group_lengths[None, :] > 0), axis=1
    )
    return jnp.where(begins, 0, 1).astype(jnp.int32)


def rotary_tables():
    half = ROT // 2
    frequency = np.exp(
        np.arange(half, dtype=np.float32) * np.float32(-2.0 * math.log(10000.0) / ROT)
    ).astype(np.float32)
    angles = np.arange(2 * SHORT, dtype=np.float32)[:, None] * frequency[None, :]
    cosine = np.ones((2 * SHORT, LANES), np.float32)
    minus = np.zeros((2 * SHORT, LANES), np.float32)
    plus = np.zeros((2 * SHORT, LANES), np.float32)
    for base in range(0, LANES, HEAD_DIM):
        cosine[:, base : base + half] = np.cos(angles)
        cosine[:, base + half : base + ROT] = np.cos(angles)
        minus[:, base : base + half] = -np.sin(angles)
        plus[:, base + half : base + ROT] = np.sin(angles)
    return jnp.asarray(cosine), jnp.asarray(minus), jnp.asarray(plus)


def low_lanes():
    return lax.broadcasted_iota(jnp.int32, (1, LANES), 1) < HEAD_DIM


def rotate(pair, cosine, minus, plus):
    half = ROT // 2
    return (
        pair * cosine
        + pltpu.roll(pair, LANES - half, 1) * minus
        + pltpu.roll(pair, half, 1) * plus
    )


def unrotate(pair, cosine, minus, plus):
    half = ROT // 2
    return (
        pair * cosine
        - pltpu.roll(pair, LANES - half, 1) * minus
        - pltpu.roll(pair, half, 1) * plus
    )


def normalize(values, gain, shift):
    center = values - jnp.mean(values, axis=-1, keepdims=True)
    spread = jnp.mean(center * center, axis=-1, keepdims=True)
    return center * lax.rsqrt(spread + EPS) * gain + shift


def whole(shape):
    return pl.BlockSpec(
        shape, lambda *idx: (0,) * len(shape), pipeline_mode=pl.Buffered(1)
    )


def held(shape):
    return pl.BlockSpec(shape, lambda *idx: (0,) * len(shape))


def rows_of(tile, width):
    return pl.BlockSpec((tile, width), lambda i, *refs: (i, 0))


def shaped(shape, dtype):
    return jax.ShapeDtypeStruct(shape, dtype)


def params(semantics=1):
    return pltpu.CompilerParams(
        dimension_semantics=("arbitrary",) * semantics, vmem_limit_bytes=VMEM_LIMIT
    )


def unit_gather_kernel(unit, x_ref, d_ref, xg_ref, dg_ref, local_sem, send_sem, recv_sem):
    dp = lax.axis_index("dp")
    mp = lax.axis_index("mp")
    place = lax.rem(mp, unit)
    base = mp - place
    peers = [(dp, base + lax.rem(place + j, unit)) for j in range(1, unit)]
    barrier = pltpu.get_barrier_semaphore()
    for peer in peers:
        pl.semaphore_signal(barrier, inc=1, device_id=peer, device_id_type=MESH)
    pl.semaphore_wait(barrier, unit - 1)
    rows = x_ref.shape[0]
    span = pl.ds(pl.multiple_of(place * rows, rows), rows)
    copies = []
    for which, (src, dst) in enumerate(((x_ref, xg_ref), (d_ref, dg_ref))):
        for j, peer in enumerate(peers):
            copies.append(
                pltpu.make_async_remote_copy(
                    src_ref=src,
                    dst_ref=dst.at[span],
                    send_sem=send_sem.at[which, j],
                    recv_sem=recv_sem.at[which, j],
                    device_id=peer,
                    device_id_type=MESH,
                )
            )
        copies.append(pltpu.make_async_copy(src, dst.at[span], local_sem.at[which]))
    for copy in copies:
        copy.start()
    for copy in copies:
        copy.wait()


def unit_gather(unit, x, d):
    rows, width = x.shape
    anywhere = pl.BlockSpec(memory_space=pl.ANY)
    return pl.pallas_call(
        functools.partial(unit_gather_kernel, unit),
        out_shape=[shaped((rows * unit, width), x.dtype)] * 2,
        in_specs=[pl.BlockSpec(memory_space=pltpu.VMEM)] * 2,
        out_specs=[anywhere] * 2,
        scratch_shapes=[
            pltpu.SemaphoreType.DMA((2,)),
            pltpu.SemaphoreType.DMA((2, unit - 1)),
            pltpu.SemaphoreType.DMA((2, unit - 1)),
        ],
        compiler_params=pltpu.CompilerParams(
            collective_id=1, has_side_effects=True, vmem_limit_bytes=VMEM_LIMIT
        ),
        cost_estimate=BRIEF,
        name="unit_gather",
    )(x, d)


def gelu_parts(hidden):
    cdf = 0.5 + 0.5 * lax.erf(hidden * math.sqrt(0.5))
    density = jnp.exp(-0.5 * hidden * hidden) * (1.0 / math.sqrt(2.0 * math.pi))
    return hidden * cdf, cdf + hidden * density


def feed_core(
    normed, low, dy, grad_low, up_ref, up_right_ref, down_ref, down_left_ref, act_ref, grad_ref, hidden_step
):
    hidden_width = up_ref.shape[1]
    for start in range(0, hidden_width, hidden_step):
        cols = pl.ds(start, hidden_step)
        hidden = dot_nn(normed, up_ref[:, cols]) + dot_nn(low, up_right_ref[:, cols])
        grad_act = dot_nt(dy, down_ref[cols, :]) + dot_nt(grad_low, down_left_ref[cols, :])
        activated, slope = gelu_parts(hidden)
        act_ref[:, cols] = activated.astype(BF16)
        grad_ref[:, cols] = (grad_act * slope).astype(BF16)


def chip_neighbours(unit):
    dp = lax.axis_index("dp")
    mp = lax.axis_index("mp")
    lead = lax.rem(dp, 2)
    return lead, (dp, lax.rem(mp + unit, 2 * unit)), (dp + 1 - 2 * lead, mp)


def courier(unit, pairs, chunks, y_sems, x_sems):
    lead, y_peer, x_peer = chip_neighbours(unit)
    over_y, over_x = [], []
    for k in range(chunks):
        for j, (own, far) in enumerate(pairs):
            count = own.shape[0] // 2 // chunks
            span = pl.ds(pl.multiple_of((lead * chunks + k) * count, count), count)
            for src, sems, peer, group in ((own, y_sems, y_peer, over_y), (far, x_sems, x_peer, over_x)):
                group.append(
                    pltpu.make_async_remote_copy(
                        src_ref=src.at[span],
                        dst_ref=far.at[span],
                        send_sem=sems.at[0, k, j],
                        recv_sem=sems.at[1, k, j],
                        device_id=peer,
                        device_id_type=MESH,
                    )
                )
    return over_y, over_x


def meet(peers):
    barrier = pltpu.get_barrier_semaphore()
    for peer in peers:
        pl.semaphore_signal(barrier, inc=1, device_id=peer, device_id_type=MESH)
    pl.semaphore_wait(barrier, len(peers))


def feed_first_kernel(
    unit, steps, x_ref, dy_ref, gain_ref, shift_ref, up_ref, up_left_ref, up_right_ref, down_ref, down_left_ref,
    output_right_ref, down_right_ref, triple_ref, output_ref, normed_ref, low_ref, grad_lows_ref, out_ref, grad_ref,
    low_act_ref, grad_low_ref, up_right_grad_ref, down_left_grad_ref, triple_far_ref, output_far_ref, act_ref, gh_ref,
    y_sems, x_sems,
):
    step = pl.program_id(0)
    chunks = y_sems.shape[1]
    over_y, over_x = courier(
        unit, ((triple_ref, triple_far_ref), (output_ref, output_far_ref)), chunks, y_sems, x_sems
    )

    @pl.when(step == 0)
    def _():
        meet(chip_neighbours(unit)[1:])
        for copy in over_y:
            copy.start()

    for k in range(chunks):

        @pl.when(step == min(k + 1, steps - 1))
        def _():
            for j in (2 * k, 2 * k + 1):
                over_y[j].wait_recv()
                over_x[j].start()

    normed = normalize(x_ref[...].astype(F32), gain_ref[...], shift_ref[...]).astype(BF16)
    normed_ref[...] = normed
    dy = dy_ref[...]
    low = dot_nn(normed, up_left_ref[...]).astype(BF16)
    low_ref[...] = low
    rights = jnp.concatenate([output_right_ref[...], down_right_ref[...]], axis=0)
    grad_lows = dot_nt(dy, rights).astype(BF16)
    grad_lows_ref[...] = grad_lows
    grad_low = grad_lows[:, LANES:]
    feed_core(normed, low, dy, grad_low, up_ref, up_right_ref, down_ref, down_left_ref, act_ref, gh_ref, 256)
    act = act_ref[...]
    gh = gh_ref[...]
    out_ref[...] = dot_nn(act, down_ref[...])
    grad_ref[...] = dot_nt(gh, up_ref[...])
    low_act_ref[...] = dot_nn(act, down_left_ref[...])
    grad_low_ref[...] = dot_nt(gh, up_right_ref[...])

    @pl.when(pl.program_id(0) == 0)
    def _():
        up_right_grad_ref[...] = jnp.zeros_like(up_right_grad_ref)
        down_left_grad_ref[...] = jnp.zeros_like(down_left_grad_ref)

    up_right_grad_ref[...] += dot_tn(low, gh)
    down_left_grad_ref[...] += dot_tn(grad_low, act)

    @pl.when(step == steps - 1)
    def _():
        for copy in over_y:
            copy.wait_send()
        for copy in over_x:
            copy.wait()


def at_columns(shape, which):
    return pl.BlockSpec(shape, lambda i, meta: (0, meta[which]), pipeline_mode=pl.Buffered(1))


def at_rows(shape, which):
    return pl.BlockSpec(shape, lambda i, meta: (meta[which], 0), pipeline_mode=pl.Buffered(1))


OWN, FAR, LEAD, PLACE, CONT = 0, 1, 2, 3, 4


def feed_first(unit, x, dy, gain, shift, up, up_left, up_right, down, down_left, output_right, down_right, triple,
               output, tile):
    rows, width = x.shape
    hidden = up.shape[1]
    steps = rows // tile
    chunks = math.gcd(4, output.shape[0] // 32)
    anywhere = pl.BlockSpec(memory_space=pl.ANY)
    return pl.pallas_call(
        functools.partial(feed_first_kernel, unit, steps),
        grid=(steps,),
        in_specs=[
            rows_of(tile, width),
            rows_of(tile, width),
            whole((1, width)),
            whole((1, width)),
            whole(up.shape),
            whole(up_left.shape),
            pl.BlockSpec((LANES, hidden), lambda i: (0, lax.axis_index("mp")), pipeline_mode=pl.Buffered(1)),
            whole(down.shape),
            pl.BlockSpec((hidden, LANES), lambda i: (lax.axis_index("mp"), 0), pipeline_mode=pl.Buffered(1)),
            whole(output_right.shape),
            whole(down_right.shape),
            anywhere,
            anywhere,
        ],
        out_specs=[
            rows_of(tile, width),
            rows_of(tile, LANES),
            rows_of(tile, 2 * LANES),
            rows_of(tile, width),
            rows_of(tile, width),
            rows_of(tile, LANES),
            rows_of(tile, LANES),
            held((LANES, hidden)),
            held((LANES, hidden)),
            anywhere,
            anywhere,
        ],
        scratch_shapes=[
            pltpu.VMEM((tile, hidden), BF16),
            pltpu.VMEM((tile, hidden), BF16),
            pltpu.SemaphoreType.DMA((2, chunks, 2)),
            pltpu.SemaphoreType.DMA((2, chunks, 2)),
        ],
        out_shape=[
            shaped((rows, width), BF16),
            shaped((rows, LANES), BF16),
            shaped((rows, 2 * LANES), BF16),
            shaped((rows, width), F32),
            shaped((rows, width), F32),
            shaped((rows, LANES), F32),
            shaped((rows, LANES), F32),
            shaped((LANES, hidden), F32),
            shaped((LANES, hidden), F32),
            shaped(triple.shape, BF16),
            shaped(output.shape, BF16),
        ],
        compiler_params=pltpu.CompilerParams(
            dimension_semantics=("arbitrary",), vmem_limit_bytes=VMEM_LIMIT, collective_id=3, has_side_effects=True
        ),
        cost_estimate=BRIEF,
        name="feed_first",
    )(x, dy, gain, shift, up, up_left, up_right, down, down_left, output_right, down_right, triple, output)


def join_halves(step, lead, pieces, whole_ref):
    @pl.when(step == 0)
    def _():
        count = pieces[0].shape[0]
        for j, piece in enumerate(pieces):
            place = j + lead * (1 - 2 * j)
            whole_ref[pl.ds(pl.multiple_of(place * count, count), count), :] = piece[...]


def feed_second_kernel(
    send_tiles, meta_ref, normed_ref, low_ref, dy_ref, grad_lows_ref, out_in_ref, grad_in_ref, low_act_in_ref,
    grad_low_in_ref, up0_ref, up1_ref, up_left_ref, up_right_ref, down0_ref, down1_ref, down_left_ref, send_ref,
    keep_ref, up_right_grad_ref, down_left_grad_ref, up_left_grad_ref, act_ref, gh_ref, up_ref, down_ref,
):
    step = pl.program_id(0)
    join_halves(step, meta_ref[LEAD], (up0_ref, up1_ref), up_ref)
    join_halves(step, meta_ref[LEAD], (down0_ref, down1_ref), down_ref)
    normed = normed_ref[...]
    low = low_ref[...]
    dy = dy_ref[...]
    grad_low = grad_lows_ref[:, LANES:]
    feed_core(normed, low, dy, grad_low, up_ref, up_right_ref, down_ref, down_left_ref, act_ref, gh_ref, 256)
    act = act_ref[...]
    gh = gh_ref[...]
    grad_low_up = (grad_low_in_ref[...] + dot_nt(gh, up_right_ref[...])).astype(BF16)
    out = (out_in_ref[...] + dot_nn(act, down_ref[...])).astype(BF16)
    low_act = (low_act_in_ref[...] + dot_nn(act, down_left_ref[...])).astype(BF16)
    grad = (
        grad_in_ref[...] + dot_nt(gh, up_ref[...]) + dot_nt(grad_low_up, up_left_ref[...])
    ).astype(BF16)
    width = out.shape[1]

    def put(ref):
        ref[:, :width] = out
        ref[:, width : 2 * width] = grad
        ref[:, 2 * width :] = low_act

    pl.when(step < send_tiles)(lambda: put(send_ref))
    pl.when(step >= send_tiles)(lambda: put(keep_ref))

    @pl.when(step == 0)
    def _():
        up_right_grad_ref[...] = jnp.zeros_like(up_right_grad_ref)
        down_left_grad_ref[...] = jnp.zeros_like(down_left_grad_ref)
        up_left_grad_ref[...] = jnp.zeros_like(up_left_grad_ref)

    up_right_grad_ref[...] += dot_tn(low, gh)
    down_left_grad_ref[...] += dot_tn(grad_low, act)
    up_left_grad_ref[...] += dot_tn(grad_low_up, normed)


def ordered(tile, width, tiles, per_device):
    return pl.BlockSpec(
        (tile, width), lambda i, meta: (lax.rem(i + (meta[PLACE] + 1) * per_device, tiles), 0)
    )


def sent(tile, width, tiles):
    return pl.BlockSpec((tile, width), lambda i, meta: (jnp.minimum(i, tiles - 1), 0))


def kept(tile, width, tiles):
    return pl.BlockSpec((tile, width), lambda i, meta: (jnp.maximum(i - tiles, 0), 0))


def feed_second(meta, normed, low, dy, grad_lows, out, grad, low_act, grad_low, ups, up_left, up_right, downs,
                down_left, own_rows, tile):
    rows, width = normed.shape
    hidden = ups[0].shape[1]
    send_rows = rows - own_rows
    tiles = send_rows // tile
    row_spec = functools.partial(ordered, tiles=rows // tile, per_device=own_rows // tile)
    wide = 2 * width + LANES
    return pl.pallas_call(
        functools.partial(feed_second_kernel, tiles),
        grid_spec=pltpu.PrefetchScalarGridSpec(
            num_scalar_prefetch=1,
            grid=(rows // tile,),
            in_specs=[
                row_spec(tile, width),
                row_spec(tile, LANES),
                row_spec(tile, width),
                row_spec(tile, 2 * LANES),
                row_spec(tile, width),
                row_spec(tile, width),
                row_spec(tile, LANES),
                row_spec(tile, LANES),
                whole(ups[0].shape),
                whole(ups[1].shape),
                whole(up_left.shape),
                at_columns((LANES, hidden), FAR),
                whole(downs[0].shape),
                whole(downs[1].shape),
                at_rows((hidden, LANES), FAR),
            ],
            out_specs=[
                sent(tile, wide, tiles),
                kept(tile, wide, tiles),
                held((LANES, hidden)),
                held((LANES, hidden)),
                held((LANES, width)),
            ],
            scratch_shapes=[
                pltpu.VMEM((tile, hidden), BF16),
                pltpu.VMEM((tile, hidden), BF16),
                pltpu.VMEM((width, hidden), BF16),
                pltpu.VMEM((hidden, width), BF16),
            ],
        ),
        out_shape=[
            shaped((send_rows, wide), BF16),
            shaped((own_rows, wide), BF16),
            shaped((LANES, hidden), F32),
            shaped((LANES, hidden), F32),
            shaped((LANES, width), F32),
        ],
        compiler_params=params(),
        cost_estimate=BRIEF,
        name="feed_second",
    )(meta, normed, low, dy, grad_lows, out, grad, low_act, grad_low, *ups, up_left, up_right, *downs, down_left)


def project_kernel(
    halo_tiles, meta_ref, x_halo_ref, x_ref, dy_ref, grad_lows_ref, gain_ref, shift_ref, triple0_ref, triple1_ref,
    left_ref, right0_ref, right1_ref, output0_ref, output1_ref, output_left0_ref, output_left1_ref, cos_ref,
    minus_ref, plus_ref, normed_ref, low_ref, q_ref, k_ref, v_ref, g_ref,
):
    step = pl.program_id(0)
    tables = (cos_ref[...], minus_ref[...], plus_ref[...])
    head_width = output0_ref.shape[0]
    first = low_lanes()

    def rows(x, full):
        normed = normalize(x.astype(F32), gain_ref[...], shift_ref[...]).astype(BF16)
        low = dot_nn(normed, left_ref[...]).astype(BF16)
        if full:
            normed_ref[...] = normed
            low_ref[...] = low
        for shard, (triple, right) in enumerate(((triple0_ref, right0_ref), (triple1_ref, right1_ref))):
            mixed = dot_nn(normed, triple[...]) + dot_nn(low, right[...])
            for pair in range(head_width // LANES):
                one, two, three = (
                    mixed[:, (3 * pair + part) * LANES : (3 * pair + part + 1) * LANES] for part in range(3)
                )
                cols = pl.ds(shard * head_width + pair * LANES, LANES)
                key = pltpu.roll(jnp.where(first, three, one), HEAD_DIM, 1)
                k_ref[:, cols] = rotate(key, *tables).astype(BF16)
                v_ref[:, cols] = jnp.where(first, two, three).astype(BF16)
                if full:
                    query = rotate(jnp.where(first, one, two), *tables).astype(BF16)
                    q_ref[:, cols] = query * HEAD_DIM**-0.5

    @pl.when(step < halo_tiles)
    def _():
        rows(x_halo_ref[...], False)

    @pl.when(step >= halo_tiles)
    def _():
        rows(x_ref[...], True)
        dy = dy_ref[...]
        grad_low = grad_lows_ref[:, :LANES]
        outputs = jnp.concatenate([output0_ref[...], output1_ref[...]], axis=0)
        lefts = jnp.concatenate([output_left0_ref[...], output_left1_ref[...]], axis=0)
        g_ref[...] = (dot_nt(dy, outputs) + dot_nt(grad_low, lefts)).astype(BF16)


def project(meta, x_halo, x, dy, grad_lows, gain, shift, triples, left, right, outputs, output_left, tables, tile):
    rows, width = dy.shape
    head_width = outputs[0].shape[0]
    triple_width = triples[0].shape[1]
    per_block = SHORT // tile
    halo_tiles = SHORT // tile

    def table_index(i, meta):
        j = jnp.maximum(i - halo_tiles, 0)
        block = meta[CONT + j // per_block] * per_block + lax.rem(j, per_block)
        return (jnp.where(i < halo_tiles, i, block), 0)

    table = pl.BlockSpec((tile, LANES), table_index)

    def main(size):
        return pl.BlockSpec((tile, size), lambda i, meta: (jnp.maximum(i - halo_tiles, 0), 0))

    return pl.pallas_call(
        functools.partial(project_kernel, halo_tiles),
        grid_spec=pltpu.PrefetchScalarGridSpec(
            num_scalar_prefetch=1,
            grid=(halo_tiles + rows // tile,),
            in_specs=[
                pl.BlockSpec((tile, width), lambda i, meta: (jnp.minimum(i, halo_tiles - 1), 0)),
                main(width),
                main(width),
                main(2 * LANES),
                whole(gain.shape),
                whole(shift.shape),
                whole(triples[0].shape),
                whole(triples[1].shape),
                whole(left.shape),
                at_columns((LANES, triple_width), OWN),
                at_columns((LANES, triple_width), FAR),
                whole(outputs[0].shape),
                whole(outputs[1].shape),
                at_rows((head_width, LANES), OWN),
                at_rows((head_width, LANES), FAR),
                table,
                table,
                table,
            ],
            out_specs=[
                main(width),
                main(LANES),
                main(2 * head_width),
                rows_of(tile, 2 * head_width),
                rows_of(tile, 2 * head_width),
                main(2 * head_width),
            ],
        ),
        out_shape=[
            shaped((rows, width), BF16),
            shaped((rows, LANES), BF16),
            shaped((rows, 2 * head_width), BF16),
            shaped((SHORT + rows, 2 * head_width), BF16),
            shaped((SHORT + rows, 2 * head_width), BF16),
            shaped((rows, 2 * head_width), BF16),
        ],
        compiler_params=params(),
        cost_estimate=BRIEF,
        name="project",
    )(meta, x_halo, x, dy, grad_lows, gain, shift, *triples, left, right, right, *outputs, output_left, output_left,
      *tables)


def attend_rows(with_prev, start, count, q_ref, k_ref, v_ref, g_ref, kp_ref, vp_ref, tables, att_ref, gq_ref,
                dk_ref, dv_ref, dkp_ref, dvp_ref):
    first_head = low_lanes()
    span = pl.ds(start, count)
    known = start + count
    zero = jnp.zeros((), BF16)

    def stack(pair):
        return jnp.concatenate([jnp.where(first_head, pair, zero), jnp.where(first_head, zero, pair)], axis=0)

    def unstack(both):
        return jnp.where(first_head, both[:count], both[count:])

    queries = stack(q_ref[span, :])
    grads = stack(g_ref[span, :])
    keys = k_ref[pl.ds(0, known), :]
    values = v_ref[pl.ds(0, known), :]
    scores = dot_nt(queries, keys)
    row = lax.broadcasted_iota(jnp.int32, (2 * count, known), 0)
    column = lax.broadcasted_iota(jnp.int32, (2 * count, known), 1)
    row = jnp.where(row >= count, row - count, row) + start
    scores = jnp.where(column <= row, scores, -1e30)
    peak = jnp.max(scores, axis=1, keepdims=True)
    if with_prev:
        prev_scores = dot_nt(queries, kp_ref[...])
        peak = jnp.maximum(peak, jnp.max(prev_scores, axis=1, keepdims=True))
        prev_exp = jnp.exp(prev_scores - peak)
    exp = jnp.exp(scores - peak)
    total = jnp.sum(exp, axis=1, keepdims=True)
    if with_prev:
        total = total + jnp.sum(prev_exp, axis=1, keepdims=True)
    scale = 1.0 / total
    weights = exp * scale
    weights_low = weights.astype(BF16)
    attended = dot_nn(weights_low, values)
    grad_weights = dot_nt(grads, values)
    inner = jnp.sum(weights * grad_weights, axis=1, keepdims=True)
    if with_prev:
        prev_weights = prev_exp * scale
        prev_low = prev_weights.astype(BF16)
        attended = attended + dot_nn(prev_low, vp_ref[...])
        prev_grad = dot_nt(grads, vp_ref[...])
        inner = inner + jnp.sum(prev_weights * prev_grad, axis=1, keepdims=True)
        prev_ds = (prev_weights * (prev_grad - inner)).astype(BF16)
    ds = (weights * (grad_weights - inner)).astype(BF16)
    grad_query = dot_nn(ds, keys)
    if with_prev:
        grad_query = grad_query + dot_nn(prev_ds, kp_ref[...])
        dkp_ref[...] += dot_tn(prev_ds, queries)
        dvp_ref[...] += dot_tn(prev_low, grads)
    dk_ref[pl.ds(0, known), :] += dot_tn(ds, queries)
    dv_ref[pl.ds(0, known), :] += dot_tn(weights_low, grads)
    att_ref[span, :] = unstack(attended).astype(BF16)
    grad_query = unstack(grad_query) * HEAD_DIM**-0.5
    gq_ref[span, :] = unrotate(grad_query, *[table[start : start + count] for table in tables]).astype(BF16)


def attend_kernel(
    blocks, count, meta_ref, q_ref, k_ref, v_ref, g_ref, kp_ref, vp_ref, cos_ref, minus_ref, plus_ref, att_ref, gq_ref,
    gk_ref, gv_ref, halo_ref, dk_ref, dv_ref, dkp_ref, dvp_ref,
):
    step = pl.program_id(1)
    block = blocks - 1 - step
    continued = meta_ref[CONT + block]
    offset = pl.multiple_of(continued * SHORT, SHORT)
    tables = tuple(ref[pl.ds(offset, SHORT), :] for ref in (cos_ref, minus_ref, plus_ref))

    @pl.when(step == 0)
    def _():
        dk_ref[...] = jnp.zeros_like(dk_ref)
        dv_ref[...] = jnp.zeros_like(dv_ref)

    @pl.when(step > 0)
    def _():
        dk_ref[...] = dkp_ref[...]
        dv_ref[...] = dvp_ref[...]

    dkp_ref[...] = jnp.zeros_like(dkp_ref)
    dvp_ref[...] = jnp.zeros_like(dvp_ref)
    args = (q_ref, k_ref, v_ref, g_ref, kp_ref, vp_ref, tables, att_ref, gq_ref, dk_ref, dv_ref, dkp_ref, dvp_ref)

    @pl.when(continued == 0)
    def _():
        for start in range(0, SHORT, count):
            attend_rows(False, start, count, *args)

    @pl.when(continued != 0)
    def _():
        for start in range(0, SHORT, count):
            attend_rows(True, start, count, *args)

    gk_ref[...] = pltpu.roll(unrotate(dk_ref[...], *tables), HEAD_DIM, 1).astype(BF16)
    gv_ref[...] = dv_ref[...].astype(BF16)

    @pl.when(block == 0)
    def _():
        base = tuple(ref[pl.ds(0, SHORT), :] for ref in (cos_ref, minus_ref, plus_ref))
        halo_ref[0] = pltpu.roll(unrotate(dkp_ref[...], *base), HEAD_DIM, 1).astype(BF16)
        halo_ref[1] = dvp_ref[...].astype(BF16)


def attend(shard, meta, q, k, v, g, tables, count):
    rows, head_width = q.shape[0], q.shape[1] // 2
    blocks, pairs = rows // SHORT, head_width // LANES
    here = pl.BlockSpec((SHORT, LANES), lambda p, i, meta: (blocks - 1 - i, p + shard * pairs))
    after = pl.BlockSpec((SHORT, LANES), lambda p, i, meta: (blocks - i, p + shard * pairs))
    new = pl.BlockSpec((SHORT, LANES), lambda p, i, meta: (blocks - 1 - i, p))
    return pl.pallas_call(
        functools.partial(attend_kernel, blocks, count),
        grid_spec=pltpu.PrefetchScalarGridSpec(
            num_scalar_prefetch=1,
            grid=(pairs, blocks),
            in_specs=[here, after, after, here, here, here] + [whole(table.shape) for table in tables],
            out_specs=[new] * 4 + [pl.BlockSpec((2, SHORT, LANES), lambda p, i, meta: (0, 0, p))],
            scratch_shapes=[pltpu.VMEM((SHORT, LANES), F32)] * 4,
        ),
        out_shape=[shaped((rows, head_width), BF16)] * 4 + [shaped((2, SHORT, head_width), BF16)],
        compiler_params=params(2),
        cost_estimate=BRIEF,
        name="attend",
    )(meta, q, k, v, g, k, v, *tables)


def settle_kernel(
    send_tiles, halo_start, tiles, per_device, meta_ref, normed_ref, low_ref, grad_lows_ref, out_in_ref,
    att0_ref, att1_ref, gq0_ref, gq1_ref, gk0_ref, gk1_ref, gv0_ref, gv1_ref, halo0_ref, halo1_ref,
    triple0_ref, triple1_ref, left_ref, output0_ref, output1_ref, right0_ref, right1_ref, output_left0_ref,
    output_left1_ref, out_ref, send_ref, keep_ref, right_grad0_ref, right_grad1_ref, left_grad_ref,
    output_left_grad0_ref, output_left_grad1_ref,
):
    step = pl.program_id(0)
    here = (lax.rem(step + (meta_ref[PLACE] + 1) * per_device, tiles) >= halo_start).astype(F32)
    normed = normed_ref[...]
    low = low_ref[...]
    grad_low_out = grad_lows_ref[:, :LANES]
    att0, att1 = att0_ref[...], att1_ref[...]
    first = low_lanes()

    def mixed(gq, gk, gv, halo):
        key = (gk[...].astype(F32) + here * halo[0].astype(F32)).astype(BF16)
        value = (gv[...].astype(F32) + here * halo[1].astype(F32)).astype(BF16)
        query = gq[...]
        groups = []
        for start in range(0, query.shape[1], LANES):
            q, k, v = (part[:, start : start + LANES] for part in (query, key, value))
            groups += [jnp.where(first, q, k), jnp.where(first, v, q), jnp.where(first, k, v)]
        return jnp.concatenate(groups, axis=1)

    grad0 = mixed(gq0_ref, gk0_ref, gv0_ref, halo0_ref)
    grad1 = mixed(gq1_ref, gk1_ref, gv1_ref, halo1_ref)
    grad_low = (dot_nt(grad0, right0_ref[...]) + dot_nt(grad1, right1_ref[...])).astype(BF16)
    grad = (
        dot_nt(grad0, triple0_ref[...]) + dot_nt(grad1, triple1_ref[...]) + dot_nt(grad_low, left_ref[...])
    ).astype(BF16)
    out_ref[...] = out_in_ref[...] + dot_nn(att0, output0_ref[...]) + dot_nn(att1, output1_ref[...])
    low_att = (dot_nn(att0, output_left0_ref[...]) + dot_nn(att1, output_left1_ref[...])).astype(BF16)
    width = grad.shape[1]

    def put(ref):
        ref[:, :width] = grad
        ref[:, width:] = low_att

    pl.when(step < send_tiles)(lambda: put(send_ref))
    pl.when(step >= send_tiles)(lambda: put(keep_ref))
    sums = (right_grad0_ref, right_grad1_ref, left_grad_ref, output_left_grad0_ref, output_left_grad1_ref)

    @pl.when(step == 0)
    def _():
        for ref in sums:
            ref[...] = jnp.zeros_like(ref)

    right_grad0_ref[...] += dot_tn(low, grad0)
    right_grad1_ref[...] += dot_tn(low, grad1)
    left_grad_ref[...] += dot_tn(grad_low, normed)
    output_left_grad0_ref[...] += dot_tn(grad_low_out, att0)
    output_left_grad1_ref[...] += dot_tn(grad_low_out, att1)


def settle(meta, normed, low, grad_lows, out, pairs, halos, triples, left, outputs, right, output_left, own_rows, tile):
    rows, width = normed.shape
    head_width = pairs[0].shape[1]
    send_rows = rows - own_rows
    send_tiles, tiles, per_device = send_rows // tile, rows // tile, own_rows // tile
    halo_start = (rows - SHORT) // tile
    row_spec = functools.partial(ordered, tiles=tiles, per_device=per_device)

    def halo_index(i, meta):
        return (0, jnp.maximum(lax.rem(i + (meta[PLACE] + 1) * per_device, tiles) - halo_start, 0), 0)

    return pl.pallas_call(
        functools.partial(settle_kernel, send_tiles, halo_start, tiles, per_device),
        grid_spec=pltpu.PrefetchScalarGridSpec(
            num_scalar_prefetch=1,
            grid=(tiles,),
            in_specs=[row_spec(tile, width), row_spec(tile, LANES), row_spec(tile, 2 * LANES), row_spec(tile, width)]
            + [row_spec(tile, head_width)] * 8
            + [pl.BlockSpec((2, tile, head_width), halo_index)] * 2
            + [whole(value.shape) for value in (*triples, left, *outputs)]
            + [at_columns((LANES, 3 * head_width), which) for which in (OWN, FAR)]
            + [at_rows((head_width, LANES), which) for which in (OWN, FAR)],
            out_specs=[
                row_spec(tile, width),
                sent(tile, width + LANES, send_tiles),
                kept(tile, width + LANES, send_tiles),
                held((LANES, 3 * head_width)),
                held((LANES, 3 * head_width)),
                held((LANES, width)),
                held((LANES, head_width)),
                held((LANES, head_width)),
            ],
        ),
        out_shape=[
            shaped((rows, width), F32),
            shaped((send_rows, width + LANES), BF16),
            shaped((own_rows, width + LANES), BF16),
            shaped((LANES, 3 * head_width), F32),
            shaped((LANES, 3 * head_width), F32),
            shaped((LANES, width), F32),
            shaped((LANES, head_width), F32),
            shaped((LANES, head_width), F32),
        ],
        compiler_params=params(),
        cost_estimate=BRIEF,
        name="settle",
    )(meta, normed, low, grad_lows, out, *pairs, *halos, *triples, left, *outputs, right, right, output_left,
      output_left)


def finish_kernel(
    parts, x_ref, dy_ref, gain1_ref, gain2_ref, output_right_ref, shrink_right_ref, *refs
):
    attention, feed = refs[:parts], refs[parts : 2 * parts]
    y_ref, dx_ref, norms_ref, output_right_grad_ref, shrink_right_grad_ref = refs[2 * parts :]
    width = x_ref.shape[1]

    def total(values, start, size):
        value = values[0][:, start : start + size].astype(F32)
        for other in values[1:]:
            value = value + other[:, start : start + size].astype(F32)
        return value

    out = total(feed, 0, width)
    first = total(attention, 0, width)
    second = total(feed, width, width)
    low_att = total(attention, width, LANES).astype(BF16)
    low_act = total(feed, 2 * width, LANES).astype(BF16)
    x = x_ref[...].astype(F32)
    dy = dy_ref[...]
    y_ref[...] = (
        x + out + dot_nn(low_att, output_right_ref[...]) + dot_nn(low_act, shrink_right_ref[...])
    ).astype(BF16)
    center = x - jnp.mean(x, axis=-1, keepdims=True)
    spread = jnp.mean(center * center, axis=-1, keepdims=True)
    inverse = lax.rsqrt(spread + EPS)
    unit = center * inverse
    scaled = first * gain1_ref[...] + second * gain2_ref[...]
    mean = jnp.mean(scaled, axis=-1, keepdims=True)
    inner = jnp.mean(scaled * unit, axis=-1, keepdims=True)
    dx_ref[...] = dy.astype(F32) + (scaled - mean - unit * inner) * inverse

    @pl.when(pl.program_id(0) == 0)
    def _():
        norms_ref[...] = jnp.zeros_like(norms_ref)
        output_right_grad_ref[...] = jnp.zeros_like(output_right_grad_ref)
        shrink_right_grad_ref[...] = jnp.zeros_like(shrink_right_grad_ref)

    norms_ref[0:1, :] += jnp.sum(first * unit, axis=0, keepdims=True)
    norms_ref[1:2, :] += jnp.sum(first, axis=0, keepdims=True)
    norms_ref[2:3, :] += jnp.sum(second * unit, axis=0, keepdims=True)
    norms_ref[3:4, :] += jnp.sum(second, axis=0, keepdims=True)
    output_right_grad_ref[...] += dot_tn(low_att, dy)
    shrink_right_grad_ref[...] += dot_tn(low_act, dy)


def finish(x, dy, gain1, gain2, output_right, shrink_right, attention, feed, tile):
    rows, width = x.shape
    parts = len(attention)
    return pl.pallas_call(
        functools.partial(finish_kernel, parts),
        grid=(rows // tile,),
        in_specs=[rows_of(tile, width)] * 2
        + [whole((1, width))] * 2
        + [whole(output_right.shape)] * 2
        + [rows_of(tile, width + LANES)] * parts
        + [rows_of(tile, 2 * width + LANES)] * parts,
        out_specs=[rows_of(tile, width)] * 2 + [held((8, width)), held((LANES, width)), held((LANES, width))],
        out_shape=[
            shaped((rows, width), BF16),
            shaped((rows, width), F32),
            shaped((8, width), F32),
            shaped((LANES, width), F32),
            shaped((LANES, width), F32),
        ],
        compiler_params=params(),
        cost_estimate=BRIEF,
        name="finish",
    )(x, dy, gain1, gain2, output_right, shrink_right, *attention, *feed)


SUM_ROWS = (2, 4, 16)


def sum_kernel(chunks, width, extra, part_ref, both_ref, out_ref, both_out_ref, *scratch):
    dp = lax.axis_index("dp")
    mp = lax.axis_index("mp")
    half, core = mp // 2, lax.rem(mp, 2)
    x, z = lax.rem(dp, 2), dp // 2
    x_peer = (dp + 1 - 2 * x, mp)
    y_peer = (dp, mp + 2 - 4 * half)
    core_peer = (dp, mp + 1 - 2 * core)
    z_places = [lax.rem(z + j, 4) for j in range(1, 4)]
    z_peers = [(place * 2 + x, mp) for place in z_places]
    barrier = pltpu.get_barrier_semaphore()
    for peer in [x_peer, y_peer, core_peer] + z_peers:
        pl.semaphore_signal(barrier, inc=1, device_id=peer, device_id_type=MESH)
    pl.semaphore_wait(barrier, 6)
    started = []

    def send(src, dst, sems, slot, peer):
        copy = pltpu.make_async_remote_copy(
            src_ref=src, dst_ref=dst, send_sem=sems.at[0, slot], recv_sem=sems.at[1, slot], device_id=peer,
            device_id_type=MESH,
        )
        copy.start()
        started.append(copy)
        return copy

    def added(first, *others):
        total = first.astype(F32)
        for other in others:
            total = total + other.astype(F32)
        return total.astype(BF16)

    both_got_ref, both_sum_ref, core_sems, local_sems = scratch[:4]
    refs = [scratch[4 + 7 * i : 4 + 7 * (i + 1)] for i in range(len(chunks))]
    both_copy = send(both_ref.at[1 - core], both_got_ref, core_sems, 0, core_peer)

    def run(index):
        y_first, start, size = chunks[index]
        got1, work1, got2, work2, got_z, full, sems = refs[index]
        shared = start is None
        if shared:
            both_copy.wait_recv()
            for place, at in ((0, half), (1, 1 - half)):
                both_sum_ref[place] = added(both_ref[core, at], both_got_ref[at])
            source = both_sum_ref
        else:
            source = part_ref.at[:, :, :, :, pl.ds(start, size)]
        if y_first:
            copy = send(source.at[1], got1, sems, 0, y_peer)
            yield
            copy.wait_recv()
            work1[...] = added(source[0], got1[...])
            copy = send(work1.at[1 - x], got2, sems, 1, x_peer)
            yield
            copy.wait_recv()
            work2[...] = added(work1[x], got2[...])
        else:
            copy = send(source.at[:, 1 - x], got1, sems, 0, x_peer)
            yield
            copy.wait_recv()
            work1[...] = added(source[:, x], got1[...])
            copy = send(work1.at[1], got2, sems, 1, y_peer)
            yield
            copy.wait_recv()
            work2[...] = added(work1[0], got2[...])
        copies = [
            send(work2.at[place], got_z.at[j], sems, 2 + j, peer)
            for j, (place, peer) in enumerate(zip(z_places, z_peers))
        ]
        yield
        for copy in copies:
            copy.wait_recv()
        full[0, x, z] = added(work2[z], got_z[0], got_z[1], got_z[2])
        mine = full.at[0, x, z]
        copies = [send(mine, mine, sems, 5 + j, peer) for j, peer in enumerate(z_peers)]
        yield
        for copy in copies:
            copy.wait_recv()
        if y_first:
            copy = send(full.at[0, x], full.at[0, x], sems, 8, x_peer)
            yield
            copy.wait_recv()
            copy = send(full.at[0], full.at[1], sems, 9, y_peer)
        else:
            copy = send(full.at[0, x], full.at[1, x], sems, 8, y_peer)
            yield
            copy.wait_recv()
            copy = send(full.at[:, x], full.at[:, x], sems, 9, x_peer)
        yield
        copy.wait_recv()
        target = both_out_ref if shared else out_ref.at[:, :, :, :, :, pl.ds(start, size)]
        last = []
        for place, at in ((0, half), (1, 1 - half)):
            local = pltpu.make_async_copy(full.at[place], target.at[core, at], local_sems.at[index, place])
            local.start()
            last.append(local)
            last.append(send(full.at[place], target.at[core, at], sems, 10 + place, core_peer))
        yield
        last[0].wait()
        last[1].wait_recv()
        last[2].wait()
        last[3].wait_recv()

    running = [run(i) for i in range(len(chunks))]
    while running:
        running = [step for step in running if next(step, "end") != "end"]
    for copy in started:
        copy.wait_send()


def sum_all(part, both):
    width, extra = part.shape[-1], both.shape[-1]
    third = width // 3
    chunks = [(True, 0, third), (False, third, third), (True, 2 * third, third), (False, None, extra)]
    per_chunk = []
    for y_first, _, size in chunks:
        one = (16, size)
        per_chunk += [
            pltpu.VMEM(((2, 4) if y_first else (2, 4)) + one, BF16),
            pltpu.VMEM((2, 4) + one, BF16),
            pltpu.VMEM((4,) + one, BF16),
            pltpu.VMEM((4,) + one, BF16),
            pltpu.VMEM((3,) + one, BF16),
            pltpu.VMEM((2, 2, 4) + one, BF16),
            pltpu.SemaphoreType.DMA((2, 12)),
        ]
    out, both_out = pl.pallas_call(
        functools.partial(sum_kernel, chunks, width, extra),
        out_shape=[shaped((2, 2) + SUM_ROWS + (width,), BF16), shaped((2, 2) + SUM_ROWS + (extra,), BF16)],
        in_specs=[pl.BlockSpec(memory_space=pltpu.VMEM)] * 2,
        out_specs=[pl.BlockSpec(memory_space=pl.ANY)] * 2,
        scratch_shapes=[
            pltpu.VMEM((2,) + SUM_ROWS + (extra,), BF16),
            pltpu.VMEM((2,) + SUM_ROWS + (extra,), BF16),
            pltpu.SemaphoreType.DMA((2, 1)),
            pltpu.SemaphoreType.DMA((len(chunks), 2)),
        ]
        + per_chunk,
        compiler_params=pltpu.CompilerParams(
            collective_id=2, has_side_effects=True, vmem_limit_bytes=VMEM_LIMIT
        ),
        cost_estimate=BRIEF,
        name="sum_all",
    )(part.reshape((2,) + SUM_ROWS + (width,)), both.reshape((2, 2) + SUM_ROWS + (extra,)))
    return out.reshape(2, 2, 128, width), both_out.reshape(2, 2, 128, extra)


def unpack_kernel(widths, part_ref, both_ref, triple_ref, output_ref, up_ref, down_ref, triple_left_ref,
                  up_left_ref, output_right_ref, down_right_ref, norm_ref):
    triple_width, head_width, hidden = widths
    start = triple_width
    triple_ref[...] = part_ref[0, 0, :, :triple_width].astype(F32)
    output_ref[...] = part_ref[0, 0, :, start : start + head_width].astype(F32).T
    start += head_width
    up_ref[...] = part_ref[0, 0, :, start : start + hidden].astype(F32)
    start += hidden
    down_ref[...] = part_ref[0, 0, :, start : start + hidden].astype(F32).T
    size = triple_left_ref.shape[0]
    triple_left_ref[...] = both_ref[0, 0, :, :size].astype(F32).T
    up_left_ref[...] = both_ref[0, 0, :, size : 2 * size].astype(F32).T
    output_right_ref[...] = both_ref[0, 0, :, 2 * size : 3 * size].astype(F32)
    down_right_ref[...] = both_ref[0, 0, :, 3 * size : 4 * size].astype(F32)
    norm_ref[0] = both_ref[0, 0, : norm_ref.shape[1], 4 * size :].astype(F32)


def unpack(part, both, width, triple_width, head_width, hidden):
    quarter = width // 4

    def tall(rows):
        return pl.BlockSpec((rows, LANES), lambda s: (s, 0))

    def wide(cols):
        return pl.BlockSpec((LANES, cols), lambda s: (0, s))

    def piece(cols):
        return pl.BlockSpec((1, 1, LANES, cols), lambda s: (lax.rem(s, 2), s // 2, 0, 0))

    return pl.pallas_call(
        functools.partial(unpack_kernel, (triple_width, head_width, hidden)),
        grid=(4,),
        in_specs=[piece(part.shape[-1]), piece(both.shape[-1])],
        out_specs=[
            wide(triple_width), tall(head_width), wide(hidden), tall(hidden), tall(quarter), tall(quarter),
            wide(quarter), wide(quarter), pl.BlockSpec((1, width // LANES, LANES), lambda s: (s, 0, 0)),
        ],
        out_shape=[
            shaped((LANES, 4 * triple_width), F32),
            shaped((4 * head_width, LANES), F32),
            shaped((LANES, 4 * hidden), F32),
            shaped((4 * hidden, LANES), F32),
            shaped((width, LANES), F32),
            shaped((width, LANES), F32),
            shaped((LANES, width), F32),
            shaped((LANES, width), F32),
            shaped((4, width // LANES, LANES), F32),
        ],
        compiler_params=params(),
        cost_estimate=BRIEF,
        name="unpack",
    )(part, both)


def shards(
    ranks,
    groups,
    block_input,
    sequence_lengths,
    first_gain,
    first_shift,
    second_gain,
    second_shift,
    triple_weight,
    triple_left,
    triple_right,
    output_weight,
    output_left,
    output_right,
    expand_weight,
    expand_left,
    expand_right,
    shrink_weight,
    shrink_left,
    shrink_right,
    cotangent,
):
    unit = ranks // 2
    own_rows, width = block_input.shape
    rows = own_rows * unit
    blocks = rows // SHORT
    tile = math.gcd(own_rows, 256)
    triple_width = triple_weight.shape[1]
    head_width = output_weight.shape[0]
    hidden = expand_weight.shape[1]
    mp = lax.axis_index("mp")
    half = mp // unit
    place = lax.rem(mp, unit)
    far = lax.rem(mp + unit, ranks)
    swap = [(m, (m + unit) % ranks) for m in range(ranks)]
    onward = [(m, m + unit) for m in range(unit)]
    back = [(m + unit, m) for m in range(unit)]

    tables = rotary_tables()
    dp = lax.axis_index("dp")
    lead = lax.rem(dp, 2)
    beside = [(d, d + 1 - 2 * (d % 2)) for d in range(groups)]
    continues = find_flags(sequence_lengths[0])
    conts = lax.dynamic_slice_in_dim(continues, half * blocks, blocks, 0)
    meta = jnp.concatenate([jnp.stack([mp, far, lead, place]).astype(jnp.int32), conts])
    gain1, shift1 = first_gain[None, :], first_shift[None, :]
    gain2, shift2 = second_gain[None, :], second_shift[None, :]

    x, dy = unit_gather(unit, block_input, cotangent)
    x_halo = lax.ppermute(x[rows - SHORT :], "mp", onward)

    def over_y(matrix):
        count = matrix.shape[0] // 2
        return lax.ppermute(lax.dynamic_slice_in_dim(matrix, lead * count, count, 0), "mp", swap)

    def over_x(piece):
        return lax.ppermute(piece, "dp", beside)

    (normed2, low2, grad_lows, out, grad2, low_act, grad_low2, expand_right_own, shrink_left_own, triple_far,
     output_far) = feed_first(
        unit, x, dy, gain2, shift2, expand_weight, expand_left, expand_right, shrink_weight, shrink_left, output_right,
        shrink_right, triple_weight, output_weight, tile,
    )
    expand_weight_late, shrink_weight_late, grad_lows = lax.optimization_barrier(
        (expand_weight, shrink_weight, grad_lows)
    )
    expand_piece = over_y(expand_weight_late)
    shrink_piece = over_y(shrink_weight_late)
    normed1, low1, q, k, v, g = project(
        meta, x_halo, x, dy, grad_lows, gain1, shift1, (triple_weight, triple_far), triple_left, triple_right,
        (output_weight, output_far), output_left, tables, tile,
    )
    count = 256
    att_far, gq_far, gk_far, gv_far, halo = attend(1, meta, q, k, v, g, tables, count)
    halo_own = lax.ppermute(halo, "mp", back)
    expand_piece, q = lax.optimization_barrier((expand_piece, q))
    expand_other = over_x(expand_piece)
    att_own, gq_own, gk_own, gv_own, halo = attend(0, meta, q, k, v, g, tables, count)
    halo_far = lax.ppermute(halo, "mp", back)
    shrink_piece, att_own = lax.optimization_barrier((shrink_piece, att_own))
    shrink_other = over_x(shrink_piece)
    (out, send1, keep1, triple_right_own, triple_right_far, triple_left_sum, output_left_sum_own,
     output_left_sum_far) = settle(
        meta, normed1, low1, grad_lows, out,
        (att_own, att_far, gq_own, gq_far, gk_own, gk_far, gv_own, gv_far), (halo_own, halo_far),
        (triple_weight, triple_far), triple_left, (output_weight, output_far), triple_right, output_left, own_rows, tile,
    )
    send2, keep2, expand_right_far, shrink_left_far, expand_left_sum = feed_second(
        meta, normed2, low2, dy, grad_lows, out, grad2, low_act, grad_low2, (expand_piece, expand_other), expand_left,
        expand_right, (shrink_piece, shrink_other), shrink_left, own_rows, tile,
    )

    def pass_on(sent_rows):
        got = []
        for j in range(1, unit):
            ring = [(m, m - m % unit + (m % unit + j) % unit) for m in range(ranks)]
            got.append(lax.ppermute(sent_rows[(j - 1) * own_rows : j * own_rows], "mp", ring))
        return got

    block_output, input_gradient, norms, output_right_sum, shrink_right_sum = finish(
        block_input, cotangent, gain1, gain2, output_right, shrink_right, [keep1] + pass_on(send1),
        [keep2] + pass_on(send2), math.gcd(own_rows, 128),
    )

    own_sums = (triple_right_own, output_left_sum_own, expand_right_own, shrink_left_own)
    far_sums = (triple_right_far, output_left_sum_far, expand_right_far, shrink_left_far)
    both_sums = (triple_left_sum, expand_left_sum, output_right_sum, shrink_right_sum)
    if ranks == 4 and groups == 8:
        part = jnp.stack(
            [jnp.concatenate([value.astype(BF16) for value in sums], axis=1) for sums in (own_sums, far_sums)]
        )
        quarters = [value.astype(BF16).reshape(LANES, 4, width // 4) for value in both_sums]
        norms = jnp.pad(
            norms[:4].astype(BF16).reshape(4, width // LANES, LANES), ((0, 0), (0, LANES - width // LANES), (0, 0))
        )
        both = jnp.concatenate([value.transpose(1, 0, 2) for value in quarters] + [norms], axis=2)
        both = both.reshape(2, 2, LANES, width + LANES).transpose(1, 0, 2, 3)
        part, both = sum_all(part, both)
        (triple_right_sum, output_left_sum, expand_right_sum, shrink_left_sum, triple_left_sum, expand_left_sum,
         output_right_sum, shrink_right_sum, norms) = unpack(
            part, both, width, triple_width, head_width, hidden
        )
        norms = norms.reshape(4, width)
    else:

        def spread(own, other):
            size = own.shape[1]
            wide = jnp.zeros((LANES, size * ranks), BF16)
            wide = lax.dynamic_update_slice_in_dim(wide, own.astype(BF16), mp * size, 1)
            return lax.dynamic_update_slice_in_dim(wide, other.astype(BF16), far * size, 1)

        sums = [spread(own, other) for own, other in zip(own_sums, far_sums)]
        sums += [value.astype(BF16) for value in both_sums]
        norms, *sums = lax.psum([norms] + sums, ("dp", "mp"))
        (triple_right_sum, output_left_sum, expand_right_sum, shrink_left_sum, triple_left_sum, expand_left_sum,
         output_right_sum, shrink_right_sum) = [value.astype(F32) for value in sums]
        output_left_sum, shrink_left_sum = output_left_sum.T, shrink_left_sum.T
        triple_left_sum, expand_left_sum = triple_left_sum.T, expand_left_sum.T
    return (
        block_output,
        input_gradient,
        norms[0],
        norms[1],
        norms[2],
        norms[3],
        triple_left_sum,
        triple_right_sum,
        output_left_sum,
        output_right_sum,
        expand_left_sum,
        expand_right_sum,
        shrink_left_sum,
        shrink_right_sum,
    )


def solution(mesh):
    placed = (
        P(("dp", "mp"), None),
        P("dp", None),
        P(),
        P(),
        P(),
        P(),
        P(None, "mp"),
        P(),
        P(),
        P("mp", None),
        P(),
        P(),
        P(None, "mp"),
        P(),
        P(),
        P("mp", None),
        P(),
        P(),
        P(("dp", "mp"), None),
    )
    return jax.shard_map(
        functools.partial(shards, mesh.shape["mp"], mesh.shape["dp"]),
        mesh=mesh,
        in_specs=placed,
        out_specs=(P(("dp", "mp"), None), P(("dp", "mp"), None)) + (P(),) * 12,
        check_vma=False,
    )
```

```python
import functools
import math

import jax
import jax.numpy as jnp
import numpy as np
from jax import lax
from jax.experimental import pallas as pl
from jax.experimental.pallas import tpu as pltpu
from jax.sharding import PartitionSpec as P

HEAD_DIM = 64
ROT = 16
SHORT = 512
TOK_GRP = 3072
SLOTS = 6
EPS = 1e-05
LANES = 128
MESH = pl.DeviceIdType.MESH
BF16 = jnp.bfloat16
F32 = jnp.float32
VMEM_LIMIT = 56 * 1024 * 1024
BRIEF = pl.CostEstimate(flops=1, bytes_accessed=1, transcendentals=0)


def dot_nn(former, latter):
    return lax.dot_general(
        former, latter, (((1,), (0,)), ((), ())), preferred_element_type=F32
    )


def dot_nt(former, latter):
    return lax.dot_general(
        former, latter, (((1,), (1,)), ((), ())), preferred_element_type=F32
    )


def dot_tn(former, latter):
    return lax.dot_general(
        former, latter, (((0,), (0,)), ((), ())), preferred_element_type=F32
    )


def find_flags(group_lengths):
    seq_ends = jnp.cumsum(group_lengths, dtype=jnp.int32)
    starts = seq_ends - group_lengths
    block_starts = jnp.arange(SLOTS, dtype=jnp.int32) * SHORT
    begins = jnp.any(
        (starts[None, :] == block_starts[:, None]) & (group_lengths[None, :] > 0), axis=1
    )
    return jnp.where(begins, 0, 1).astype(jnp.int32)


def rotary_tables():
    half = ROT // 2
    frequency = np.exp(
        np.arange(half, dtype=np.float32) * np.float32(-2.0 * math.log(10000.0) / ROT)
    ).astype(np.float32)
    angles = np.arange(2 * SHORT, dtype=np.float32)[:, None] * frequency[None, :]
    cosine = np.ones((2 * SHORT, LANES), np.float32)
    minus = np.zeros((2 * SHORT, LANES), np.float32)
    plus = np.zeros((2 * SHORT, LANES), np.float32)
    for base in range(0, LANES, HEAD_DIM):
        cosine[:, base : base + half] = np.cos(angles)
        cosine[:, base + half : base + ROT] = np.cos(angles)
        minus[:, base : base + half] = -np.sin(angles)
        plus[:, base + half : base + ROT] = np.sin(angles)
    return jnp.asarray(cosine), jnp.asarray(minus), jnp.asarray(plus)


def low_lanes():
    return lax.broadcasted_iota(jnp.int32, (1, LANES), 1) < HEAD_DIM


def rotate(pair, cosine, minus, plus):
    half = ROT // 2
    return (
        pair * cosine
        + pltpu.roll(pair, LANES - half, 1) * minus
        + pltpu.roll(pair, half, 1) * plus
    )


def unrotate(pair, cosine, minus, plus):
    half = ROT // 2
    return (
        pair * cosine
        - pltpu.roll(pair, LANES - half, 1) * minus
        - pltpu.roll(pair, half, 1) * plus
    )


def normalize(values, gain, shift):
    center = values - jnp.mean(values, axis=-1, keepdims=True)
    spread = jnp.mean(center * center, axis=-1, keepdims=True)
    return center * lax.rsqrt(spread + EPS) * gain + shift


def whole(shape):
    return pl.BlockSpec(
        shape, lambda *idx: (0,) * len(shape), pipeline_mode=pl.Buffered(1)
    )


def held(shape):
    return pl.BlockSpec(shape, lambda *idx: (0,) * len(shape))


def rows_of(tile, width):
    return pl.BlockSpec((tile, width), lambda i, *refs: (i, 0))


def shaped(shape, dtype):
    return jax.ShapeDtypeStruct(shape, dtype)


def params(semantics=1):
    return pltpu.CompilerParams(
        dimension_semantics=("arbitrary",) * semantics, vmem_limit_bytes=VMEM_LIMIT
    )


def gelu_parts(hidden):
    cdf = 0.5 + 0.5 * lax.erf(hidden * math.sqrt(0.5))
    density = jnp.exp(-0.5 * hidden * hidden) * (1.0 / math.sqrt(2.0 * math.pi))
    return hidden * cdf, cdf + hidden * density


def feed_core(
    normed, low, dy, grad_low, up_ref, up_right_ref, down_ref, down_left_ref, act_ref, grad_ref, hidden_step
):
    hidden_width = up_ref.shape[1]
    for start in range(0, hidden_width, hidden_step):
        cols = pl.ds(start, hidden_step)
        hidden = dot_nn(normed, up_ref[:, cols]) + dot_nn(low, up_right_ref[:, cols])
        grad_act = dot_nt(dy, down_ref[cols, :]) + dot_nt(grad_low, down_left_ref[cols, :])
        activated, slope = gelu_parts(hidden)
        act_ref[:, cols] = activated.astype(BF16)
        grad_ref[:, cols] = (grad_act * slope).astype(BF16)


def chip_neighbours(unit):
    dp = lax.axis_index("dp")
    mp = lax.axis_index("mp")
    lead = lax.rem(dp, 2)
    return lead, (dp, lax.rem(mp + unit, 2 * unit)), (dp + 1 - 2 * lead, mp)


def courier(unit, pairs, chunks, y_sems, x_sems):
    lead, y_peer, x_peer = chip_neighbours(unit)
    over_y, over_x = [], []
    for k in range(chunks):
        for j, (own, far) in enumerate(pairs):
            count = own.shape[0] // 2 // chunks
            span = pl.ds(pl.multiple_of((lead * chunks + k) * count, count), count)
            for src, sems, peer, group in ((own, y_sems, y_peer, over_y), (far, x_sems, x_peer, over_x)):
                group.append(
                    pltpu.make_async_remote_copy(
                        src_ref=src.at[span],
                        dst_ref=far.at[span],
                        send_sem=sems.at[0, k, j],
                        recv_sem=sems.at[1, k, j],
                        device_id=peer,
                        device_id_type=MESH,
                    )
                )
    return over_y, over_x


def meet(peers):
    barrier = pltpu.get_barrier_semaphore()
    for peer in peers:
        pl.semaphore_signal(barrier, inc=1, device_id=peer, device_id_type=MESH)
    pl.semaphore_wait(barrier, len(peers))


def place_in_unit(unit):
    mp = lax.axis_index("mp")
    return lax.rem(mp, unit), mp - lax.rem(mp, unit)


def unit_peers(unit):
    place, base = place_in_unit(unit)
    return [(lax.axis_index("dp"), base + lax.rem(place + unit - s, unit)) for s in range(1, unit)]


def halo_copies(unit, x_ref, halo_ref, y_sems, unit_sems):
    own_rows = x_ref.shape[0]
    chunk = math.gcd(own_rows, 128)
    dp = lax.axis_index("dp")
    found = []
    for k in range(SHORT // chunk):
        row = unit * own_rows - SHORT + k * chunk
        holder, start = row // own_rows, row % own_rows
        target = halo_ref.at[pl.ds(k * chunk, chunk)]
        over_y = pltpu.make_async_remote_copy(
            src_ref=x_ref.at[pl.ds(start, chunk)], dst_ref=target, send_sem=y_sems.at[0, k], recv_sem=y_sems.at[1, k],
            device_id=(dp, unit + holder), device_id_type=MESH,
        )
        spread = [
            pltpu.make_async_remote_copy(
                src_ref=target, dst_ref=target, send_sem=unit_sems.at[0, k, s - 1], recv_sem=unit_sems.at[1, k, s - 1],
                device_id=(dp, unit + (holder + s) % unit), device_id_type=MESH,
            )
            for s in range(1, unit)
        ]
        found.append((holder, over_y, spread))
    return found


def feed_first_kernel(
    unit, tile, x_ref, dy_ref, gain1_ref, shift1_ref, gain2_ref, shift2_ref, up_ref, up_left_ref, up_right_ref, down_ref,
    down_left_ref, output_right_ref, down_right_ref, x_all_ref, dy_all_ref, triple_ref, output_ref, normed1_ref,
    normed_ref, dy_full_ref, low_ref, grad_lows_ref, out_ref, grad_ref, low_act_ref, grad_low_ref, up_right_grad_ref,
    down_left_grad_ref, triple_far_ref, output_far_ref, halo_ref, up_half_ref, down_half_ref, act_ref, gh_ref, xs_ref,
    x_got_ref, dy_got_ref, y_sems, x_sems, unit_sems, halo_y_sems, halo_unit_sems, local_sems,
):
    step = pl.program_id(0)
    own_rows = x_all_ref.shape[0]
    per_device = own_rows // tile
    steps = unit * per_device
    chunks = y_sems.shape[1]
    place, base = place_in_unit(unit)
    half = base // unit
    peers = unit_peers(unit)
    over_y, over_x = courier(
        unit, ((triple_ref, triple_far_ref), (output_ref, output_far_ref)), chunks, y_sems, x_sems
    )
    halo = halo_copies(unit, x_all_ref, halo_ref, halo_y_sems, halo_unit_sems)
    rows_out = [
        pltpu.make_async_remote_copy(
            src_ref=src, dst_ref=dst.at[j], send_sem=unit_sems.at[0, which, j], recv_sem=unit_sems.at[1, which, j],
            device_id=peer, device_id_type=MESH,
        )
        for j, peer in enumerate(peers)
        for which, (src, dst) in enumerate(((x_all_ref, x_got_ref), (dy_all_ref, dy_got_ref)))
    ]
    lead = chip_neighbours(unit)[0]
    kept_halves = [
        pltpu.make_async_copy(
            src.at[pl.ds(pl.multiple_of(lead * dst.shape[0], dst.shape[0]), dst.shape[0])], dst, local_sems.at[j]
        )
        for j, (src, dst) in enumerate(((up_ref, up_half_ref), (down_ref, down_half_ref)))
    ]

    @pl.when(step == 0)
    def _():
        meet([*chip_neighbours(unit)[1:], *peers])
        for copy in rows_out + over_y + kept_halves:
            copy.start()
        xs_ref[...] = x_ref[...]
        dy_full_ref[...] = dy_ref[...]

    for holder, copy, _ in halo:
        pl.when((step == 0) & (half == 0) & (place == holder))(copy.start)

    @pl.when((step > 0) & (step < per_device))
    def _():
        xs_ref[...] = x_ref[...]
        dy_full_ref[...] = dy_ref[...]

    for slot in range(unit - 1):

        @pl.when(step == per_device * (slot + 1))
        def _():
            for which in range(2):
                rows_out[2 * slot + which].wait_recv()

        @pl.when((step >= per_device * (slot + 1)) & (step < per_device * (slot + 2)))
        def _():
            span = pl.ds(pl.multiple_of((step - per_device * (slot + 1)) * tile, tile), tile)
            xs_ref[...] = x_got_ref[slot, span]
            dy_full_ref[...] = dy_got_ref[slot, span]

    for k in range(chunks):

        @pl.when(step == min(k + 1, steps - 1))
        def _():
            for j in (2 * k, 2 * k + 1):
                over_y[j].wait_recv()
                over_x[j].start()

    x = xs_ref[...].astype(F32)
    center = x - jnp.mean(x, axis=-1, keepdims=True)
    spread = jnp.mean(center * center, axis=-1, keepdims=True)
    scaled = center * lax.rsqrt(spread + EPS)
    normed1_ref[...] = (scaled * gain1_ref[...] + shift1_ref[...]).astype(BF16)
    normed = (scaled * gain2_ref[...] + shift2_ref[...]).astype(BF16)
    normed_ref[...] = normed
    dy = dy_full_ref[...]
    low = dot_nn(normed, up_left_ref[...]).astype(BF16)
    low_ref[...] = low
    rights = jnp.concatenate([output_right_ref[...], down_right_ref[...]], axis=0)
    grad_lows = dot_nt(dy, rights).astype(BF16)
    grad_lows_ref[...] = grad_lows
    grad_low = grad_lows[:, LANES:]
    feed_core(normed, low, dy, grad_low, up_ref, up_right_ref, down_ref, down_left_ref, act_ref, gh_ref, 256)
    act = act_ref[...]
    gh = gh_ref[...]
    out_ref[...] = dot_nn(act, down_ref[...])
    grad_ref[...] = dot_nt(gh, up_ref[...])
    low_act_ref[...] = dot_nn(act, down_left_ref[...])
    grad_low_ref[...] = dot_nt(gh, up_right_ref[...])

    @pl.when(step == 0)
    def _():
        up_right_grad_ref[...] = jnp.zeros_like(up_right_grad_ref)
        down_left_grad_ref[...] = jnp.zeros_like(down_left_grad_ref)

    up_right_grad_ref[...] += dot_tn(low, gh)
    down_left_grad_ref[...] += dot_tn(grad_low, act)

    @pl.when((step == 0) & (half == 0))
    def _():
        fills = [
            pltpu.make_async_copy(xs_ref, halo_ref.at[pl.ds(k * tile, tile)], local_sems.at[2 + k])
            for k in range(SHORT // tile)
        ]
        for copy in fills:
            copy.start()
        for copy in fills:
            copy.wait()

    @pl.when(step == steps - 1)
    def _():
        for holder, copy, spread_copies in halo:

            @pl.when((half == 1) & (place == holder))
            def _():
                copy.wait_recv()
                for other in spread_copies:
                    other.start()

        for holder, copy, spread_copies in halo:
            pl.when((half == 0) & (place == holder))(copy.wait_send)

            @pl.when((half == 1) & (place == holder))
            def _():
                for other in spread_copies:
                    other.wait_send()

            for s in range(1, unit):
                pl.when((half == 1) & (place == (holder + s) % unit))(spread_copies[s - 1].wait_recv)
        for copy in rows_out + over_y:
            copy.wait_send()
        for copy in over_x + kept_halves:
            copy.wait()


def at_columns(shape, which):
    return pl.BlockSpec(shape, lambda i, meta: (0, meta[which]), pipeline_mode=pl.Buffered(1))


def at_rows(shape, which):
    return pl.BlockSpec(shape, lambda i, meta: (meta[which], 0), pipeline_mode=pl.Buffered(1))


OWN, FAR, LEAD, PLACE, CONT = 0, 1, 2, 3, 4


def feed_first(unit, x, dy, norms, up, up_left, up_right, down, down_left, output_right, down_right, triple, output,
               tile):
    own_rows, width = x.shape
    rows = own_rows * unit
    hidden = up.shape[1]
    steps, per_device = rows // tile, own_rows // tile
    chunks = math.gcd(4, output.shape[0] // 32)
    halo_chunks = SHORT // math.gcd(own_rows, 128)
    anywhere = pl.BlockSpec(memory_space=pl.ANY)
    here = pl.BlockSpec((tile, width), lambda i: (jnp.minimum(i, per_device - 1), 0))

    def turned(size):
        def index(i):
            return (lax.rem(i + place_in_unit(unit)[0] * per_device, steps), 0)

        return pl.BlockSpec((tile, size), index)

    return pl.pallas_call(
        functools.partial(feed_first_kernel, unit, tile),
        grid=(steps,),
        in_specs=[here, here]
        + [whole((1, width))] * 4
        + [
            whole(up.shape),
            whole(up_left.shape),
            pl.BlockSpec((LANES, hidden), lambda i: (0, lax.axis_index("mp")), pipeline_mode=pl.Buffered(1)),
            whole(down.shape),
            pl.BlockSpec((hidden, LANES), lambda i: (lax.axis_index("mp"), 0), pipeline_mode=pl.Buffered(1)),
            whole(output_right.shape),
            whole(down_right.shape),
        ]
        + [anywhere] * 4,
        out_specs=[
            turned(width),
            turned(width),
            turned(width),
            turned(LANES),
            turned(2 * LANES),
            turned(width),
            turned(width),
            turned(LANES),
            turned(LANES),
            held((LANES, hidden)),
            held((LANES, hidden)),
        ]
        + [anywhere] * 5,
        scratch_shapes=[
            pltpu.VMEM((tile, hidden), BF16),
            pltpu.VMEM((tile, hidden), BF16),
            pltpu.VMEM((tile, width), BF16),
            pltpu.VMEM((unit - 1, own_rows, width), BF16),
            pltpu.VMEM((unit - 1, own_rows, width), BF16),
            pltpu.SemaphoreType.DMA((2, chunks, 2)),
            pltpu.SemaphoreType.DMA((2, chunks, 2)),
            pltpu.SemaphoreType.DMA((2, 2, unit - 1)),
            pltpu.SemaphoreType.DMA((2, halo_chunks)),
            pltpu.SemaphoreType.DMA((2, halo_chunks, unit - 1)),
            pltpu.SemaphoreType.DMA((2 + SHORT // tile,)),
        ],
        out_shape=[
            shaped((rows, width), BF16),
            shaped((rows, width), BF16),
            shaped((rows, width), BF16),
            shaped((rows, LANES), BF16),
            shaped((rows, 2 * LANES), BF16),
            shaped((rows, width), F32),
            shaped((rows, width), F32),
            shaped((rows, LANES), F32),
            shaped((rows, LANES), F32),
            shaped((LANES, hidden), F32),
            shaped((LANES, hidden), F32),
            shaped(triple.shape, BF16),
            shaped(output.shape, BF16),
            shaped((SHORT, width), BF16),
            shaped((up.shape[0] // 2, up.shape[1]), BF16),
            shaped((down.shape[0] // 2, down.shape[1]), BF16),
        ],
        compiler_params=pltpu.CompilerParams(
            dimension_semantics=("arbitrary",), vmem_limit_bytes=VMEM_LIMIT, collective_id=3, has_side_effects=True
        ),
        cost_estimate=BRIEF,
        name="feed_first",
    )(x, dy, *norms, up, up_left, up_right, down, down_left, output_right, down_right, x, dy, triple, output)


def join_halves(step, lead, pieces, whole_ref):
    @pl.when(step == 0)
    def _():
        count = pieces[0].shape[0]
        for j, piece in enumerate(pieces):
            place = j + lead * (1 - 2 * j)
            whole_ref[pl.ds(pl.multiple_of(place * count, count), count), :] = piece[...]


def feed_second_kernel(
    unit, tile, normed_ref, low_ref, dy_ref, grad_lows_ref, out_in_ref, grad_in_ref, low_act_in_ref, grad_low_in_ref,
    x_ref, keep_ref, got1_ref, gain1_ref, gain2_ref, output_right_ref, down_right_ref, up0_ref, up1_ref, up_left_ref,
    up_right_ref, down0_ref, down1_ref, down_left_ref, y_ref, dx_ref, norms_ref, output_right_grad_ref,
    down_right_grad_ref, up_right_grad_ref, down_left_grad_ref, up_left_grad_ref, act_ref, gh_ref, up_ref, down_ref,
    send_ref, got_ref, sems,
):
    step = pl.program_id(0)
    own_rows = got_ref.shape[1]
    per_device = own_rows // tile
    send_tiles = (unit - 1) * per_device
    lead = chip_neighbours(unit)[0]
    peers = unit_peers(unit)
    copies = [
        [
            pltpu.make_async_remote_copy(
                src_ref=send_ref.at[s, pl.ds(t * tile, tile)], dst_ref=got_ref.at[s, pl.ds(t * tile, tile)],
                send_sem=sems.at[0, s, t], recv_sem=sems.at[1, s, t], device_id=peer, device_id_type=MESH,
            )
            for t in range(per_device)
        ]
        for s, peer in enumerate(peers)
    ]

    @pl.when(step == 0)
    def _():
        meet(peers)
        for ref in (norms_ref, output_right_grad_ref, down_right_grad_ref, up_right_grad_ref, down_left_grad_ref,
                    up_left_grad_ref):
            ref[...] = jnp.zeros_like(ref)

    join_halves(step, lead, (up0_ref, up1_ref), up_ref)
    join_halves(step, lead, (down0_ref, down1_ref), down_ref)
    normed = normed_ref[...]
    low = low_ref[...]
    dy = dy_ref[...]
    grad_low = grad_lows_ref[:, LANES:]
    feed_core(normed, low, dy, grad_low, up_ref, up_right_ref, down_ref, down_left_ref, act_ref, gh_ref, 256)
    act = act_ref[...]
    gh = gh_ref[...]
    grad_low_up = (grad_low_in_ref[...] + dot_nt(gh, up_right_ref[...])).astype(BF16)
    width = dy.shape[1]

    def results():
        out = out_in_ref[...] + dot_nn(act, down_ref[...])
        grad = grad_in_ref[...] + dot_nt(gh, up_ref[...]) + dot_nt(grad_low_up, up_left_ref[...])
        low_act = low_act_in_ref[...] + dot_nn(act, down_left_ref[...])
        return out, grad, low_act

    up_right_grad_ref[...] += dot_tn(low, gh)
    down_left_grad_ref[...] += dot_tn(grad_low, act)
    up_left_grad_ref[...] += dot_tn(grad_low_up, normed)

    @pl.when(step < send_tiles)
    def _():
        out, grad, low_act = results()
        slot = step // per_device
        span = pl.ds(pl.multiple_of(lax.rem(step, per_device) * tile, tile), tile)
        send_ref[slot, span, :width] = out.astype(BF16)
        send_ref[slot, span, width : 2 * width] = grad.astype(BF16)
        send_ref[slot, span, 2 * width :] = low_act.astype(BF16)

    for s in range(unit - 1):
        for t in range(per_device):
            pl.when(step == s * per_device + t)(copies[s][t].start)
            pl.when(step == send_tiles + t)(copies[s][t].wait_recv)

    @pl.when(step >= send_tiles)
    def _():
        out, second, low_act = results()
        span = pl.ds(pl.multiple_of((step - send_tiles) * tile, tile), tile)
        first = keep_ref[:, :width].astype(F32)
        low_att = keep_ref[:, width:].astype(F32)
        for s in range(unit - 1):
            first = first + got1_ref[s, :, :width].astype(F32)
            low_att = low_att + got1_ref[s, :, width:].astype(F32)
            out = out + got_ref[s, span, :width].astype(F32)
            second = second + got_ref[s, span, width : 2 * width].astype(F32)
            low_act = low_act + got_ref[s, span, 2 * width :].astype(F32)
        low_att, low_act = low_att.astype(BF16), low_act.astype(BF16)
        x = x_ref[...].astype(F32)
        y_ref[...] = (
            x + out + dot_nn(low_att, output_right_ref[...]) + dot_nn(low_act, down_right_ref[...])
        ).astype(BF16)
        center = x - jnp.mean(x, axis=-1, keepdims=True)
        spread = jnp.mean(center * center, axis=-1, keepdims=True)
        inverse = lax.rsqrt(spread + EPS)
        scaled = center * inverse
        total = first * gain1_ref[...] + second * gain2_ref[...]
        mean = jnp.mean(total, axis=-1, keepdims=True)
        inner = jnp.mean(total * scaled, axis=-1, keepdims=True)
        dx_ref[...] = dy.astype(F32) + (total - mean - scaled * inner) * inverse
        norms_ref[0:1, :] += jnp.sum(first * scaled, axis=0, keepdims=True)
        norms_ref[1:2, :] += jnp.sum(first, axis=0, keepdims=True)
        norms_ref[2:3, :] += jnp.sum(second * scaled, axis=0, keepdims=True)
        norms_ref[3:4, :] += jnp.sum(second, axis=0, keepdims=True)
        output_right_grad_ref[...] += dot_tn(low_att, dy)
        down_right_grad_ref[...] += dot_tn(low_act, dy)

    @pl.when(step == unit * per_device - 1)
    def _():
        for group in copies:
            for copy in group:
                copy.wait_send()


def feed_second(unit, normed, low, dy, grad_lows, out, grad, low_act, grad_low, x, keep, got, gains, output_right,
                down_right, ups, up_left, up_right, downs, down_left, tile):
    rows, width = normed.shape
    own_rows = rows // unit
    hidden = ups[0].shape[1]
    steps, per_device = rows // tile, own_rows // tile
    send_tiles = steps - per_device
    wide = 2 * width + LANES

    def turned(size):
        def index(i):
            place, slot = place_in_unit(unit)[0], i // per_device + 1
            return (lax.rem(place + unit - slot, unit) * per_device + lax.rem(i, per_device), 0)

        return pl.BlockSpec((tile, size), index)

    def late(size):
        return pl.BlockSpec((tile, size), lambda i: (jnp.maximum(i - send_tiles, 0), 0))

    def far():
        return lax.rem(lax.axis_index("mp") + unit, 2 * unit)

    return pl.pallas_call(
        functools.partial(feed_second_kernel, unit, tile),
        grid=(steps,),
        in_specs=[
            turned(width),
            turned(LANES),
            turned(width),
            turned(2 * LANES),
            turned(width),
            turned(width),
            turned(LANES),
            turned(LANES),
            late(width),
            late(width + LANES),
            pl.BlockSpec((unit - 1, tile, width + LANES), lambda i: (0, jnp.maximum(i - send_tiles, 0), 0)),
            whole((1, width)),
            whole((1, width)),
            whole(output_right.shape),
            whole(down_right.shape),
            whole(ups[0].shape),
            whole(ups[1].shape),
            whole(up_left.shape),
            pl.BlockSpec((LANES, hidden), lambda i: (0, far()), pipeline_mode=pl.Buffered(1)),
            whole(downs[0].shape),
            whole(downs[1].shape),
            pl.BlockSpec((hidden, LANES), lambda i: (far(), 0), pipeline_mode=pl.Buffered(1)),
        ],
        out_specs=[
            late(width),
            late(width),
            held((8, width)),
            held((LANES, width)),
            held((LANES, width)),
            held((LANES, hidden)),
            held((LANES, hidden)),
            held((LANES, width)),
        ],
        scratch_shapes=[
            pltpu.VMEM((tile, hidden), BF16),
            pltpu.VMEM((tile, hidden), BF16),
            pltpu.VMEM((width, hidden), BF16),
            pltpu.VMEM((hidden, width), BF16),
            pltpu.VMEM((unit - 1, own_rows, wide), BF16),
            pltpu.VMEM((unit - 1, own_rows, wide), BF16),
            pltpu.SemaphoreType.DMA((2, unit - 1, per_device)),
        ],
        out_shape=[
            shaped((own_rows, width), BF16),
            shaped((own_rows, width), F32),
            shaped((8, width), F32),
            shaped((LANES, width), F32),
            shaped((LANES, width), F32),
            shaped((LANES, hidden), F32),
            shaped((LANES, hidden), F32),
            shaped((LANES, width), F32),
        ],
        compiler_params=pltpu.CompilerParams(
            dimension_semantics=("arbitrary",), vmem_limit_bytes=VMEM_LIMIT, collective_id=4, has_side_effects=True
        ),
        cost_estimate=BRIEF,
        name="feed_second",
    )(normed, low, dy, grad_lows, out, grad, low_act, grad_low, x, keep, got, *gains, output_right, down_right, *ups,
      up_left, up_right, *downs, down_left)


def project_kernel(
    main_tiles, meta_ref, x_halo_ref, normed_ref, dy_ref, grad_lows_ref, gain_ref, shift_ref, triple0_ref, triple1_ref,
    left_ref, right0_ref, right1_ref, output0_ref, output1_ref, output_left0_ref, output_left1_ref, cos_ref,
    minus_ref, plus_ref, low_ref, q_ref, k_ref, v_ref, g_ref,
):
    step = pl.program_id(0)
    tables = (cos_ref[...], minus_ref[...], plus_ref[...])
    head_width = output0_ref.shape[0]
    first = low_lanes()

    def rows(normed, full):
        low = dot_nn(normed, left_ref[...]).astype(BF16)
        if full:
            low_ref[...] = low
        for shard, (triple, right) in enumerate(((triple0_ref, right0_ref), (triple1_ref, right1_ref))):
            mixed = dot_nn(normed, triple[...]) + dot_nn(low, right[...])
            for pair in range(head_width // LANES):
                one, two, three = (
                    mixed[:, (3 * pair + part) * LANES : (3 * pair + part + 1) * LANES] for part in range(3)
                )
                cols = pl.ds(shard * head_width + pair * LANES, LANES)
                key = pltpu.roll(jnp.where(first, three, one), HEAD_DIM, 1)
                k_ref[:, cols] = rotate(key, *tables).astype(BF16)
                v_ref[:, cols] = jnp.where(first, two, three).astype(BF16)
                if full:
                    query = rotate(jnp.where(first, one, two), *tables).astype(BF16)
                    q_ref[:, cols] = query * HEAD_DIM**-0.5

    @pl.when(step < main_tiles)
    def _():
        rows(normed_ref[...], True)
        dy = dy_ref[...]
        grad_low = grad_lows_ref[:, :LANES]
        outputs = jnp.concatenate([output0_ref[...], output1_ref[...]], axis=0)
        lefts = jnp.concatenate([output_left0_ref[...], output_left1_ref[...]], axis=0)
        g_ref[...] = (dot_nt(dy, outputs) + dot_nt(grad_low, lefts)).astype(BF16)

    @pl.when(step >= main_tiles)
    def _():
        rows(normalize(x_halo_ref[...].astype(F32), gain_ref[...], shift_ref[...]).astype(BF16), False)


def project(meta, x_halo, normed, dy, grad_lows, gain, shift, triples, left, right, outputs, output_left, tables, tile):
    rows, width = dy.shape
    head_width = outputs[0].shape[0]
    triple_width = triples[0].shape[1]
    per_block = SHORT // tile
    main_tiles, halo_tiles = rows // tile, SHORT // tile

    def table_index(i, meta):
        block = meta[CONT + jnp.minimum(i, main_tiles - 1) // per_block] * per_block + lax.rem(i, per_block)
        return (jnp.where(i < main_tiles, block, i - main_tiles), 0)

    table = pl.BlockSpec((tile, LANES), table_index)

    def main(size):
        return pl.BlockSpec((tile, size), lambda i, meta: (jnp.minimum(i, main_tiles - 1), 0))

    def late(size):
        return pl.BlockSpec((tile, size), lambda i, meta: (jnp.maximum(i - main_tiles, 0), 0))

    def all_rows(size):
        return pl.BlockSpec(
            (tile, size), lambda i, meta: (jnp.where(i < main_tiles, i + halo_tiles, i - main_tiles), 0)
        )

    return pl.pallas_call(
        functools.partial(project_kernel, main_tiles),
        grid_spec=pltpu.PrefetchScalarGridSpec(
            num_scalar_prefetch=1,
            grid=(main_tiles + halo_tiles,),
            in_specs=[
                late(width),
                main(width),
                main(width),
                main(2 * LANES),
                whole(gain.shape),
                whole(shift.shape),
                whole(triples[0].shape),
                whole(triples[1].shape),
                whole(left.shape),
                at_columns((LANES, triple_width), OWN),
                at_columns((LANES, triple_width), FAR),
                whole(outputs[0].shape),
                whole(outputs[1].shape),
                at_rows((head_width, LANES), OWN),
                at_rows((head_width, LANES), FAR),
                table,
                table,
                table,
            ],
            out_specs=[
                main(LANES),
                main(2 * head_width),
                all_rows(2 * head_width),
                all_rows(2 * head_width),
                main(2 * head_width),
            ],
        ),
        out_shape=[
            shaped((rows, LANES), BF16),
            shaped((rows, 2 * head_width), BF16),
            shaped((SHORT + rows, 2 * head_width), BF16),
            shaped((SHORT + rows, 2 * head_width), BF16),
            shaped((rows, 2 * head_width), BF16),
        ],
        compiler_params=params(),
        cost_estimate=BRIEF,
        name="project",
    )(meta, x_halo, normed, dy, grad_lows, gain, shift, *triples, left, right, right, *outputs, output_left,
      output_left, *tables)


def attend_rows(with_prev, start, count, q_ref, k_ref, v_ref, g_ref, kp_ref, vp_ref, tables, att_ref, gq_ref,
                dk_ref, dv_ref, dkp_ref, dvp_ref):
    first_head = low_lanes()
    span = pl.ds(start, count)
    known = start + count
    zero = jnp.zeros((), BF16)

    def stack(pair):
        return jnp.concatenate([jnp.where(first_head, pair, zero), jnp.where(first_head, zero, pair)], axis=0)

    def unstack(both):
        return jnp.where(first_head, both[:count], both[count:])

    queries = stack(q_ref[span, :])
    grads = stack(g_ref[span, :])
    keys = k_ref[pl.ds(0, known), :]
    values = v_ref[pl.ds(0, known), :]
    scores = dot_nt(queries, keys)
    row = lax.broadcasted_iota(jnp.int32, (2 * count, known), 0)
    column = lax.broadcasted_iota(jnp.int32, (2 * count, known), 1)
    row = jnp.where(row >= count, row - count, row) + start
    scores = jnp.where(column <= row, scores, -1e30)
    peak = jnp.max(scores, axis=1, keepdims=True)
    if with_prev:
        prev_scores = dot_nt(queries, kp_ref[...])
        peak = jnp.maximum(peak, jnp.max(prev_scores, axis=1, keepdims=True))
        prev_exp = jnp.exp(prev_scores - peak)
    exp = jnp.exp(scores - peak)
    total = jnp.sum(exp, axis=1, keepdims=True)
    if with_prev:
        total = total + jnp.sum(prev_exp, axis=1, keepdims=True)
    scale = 1.0 / total
    weights = exp * scale
    weights_low = weights.astype(BF16)
    attended = dot_nn(weights_low, values)
    grad_weights = dot_nt(grads, values)
    inner = jnp.sum(weights * grad_weights, axis=1, keepdims=True)
    if with_prev:
        prev_weights = prev_exp * scale
        prev_low = prev_weights.astype(BF16)
        attended = attended + dot_nn(prev_low, vp_ref[...])
        prev_grad = dot_nt(grads, vp_ref[...])
        inner = inner + jnp.sum(prev_weights * prev_grad, axis=1, keepdims=True)
        prev_ds = (prev_weights * (prev_grad - inner)).astype(BF16)
    ds = (weights * (grad_weights - inner)).astype(BF16)
    grad_query = dot_nn(ds, keys)
    if with_prev:
        grad_query = grad_query + dot_nn(prev_ds, kp_ref[...])
        dkp_ref[...] += dot_tn(prev_ds, queries)
        dvp_ref[...] += dot_tn(prev_low, grads)
    dk_ref[pl.ds(0, known), :] += dot_tn(ds, queries)
    dv_ref[pl.ds(0, known), :] += dot_tn(weights_low, grads)
    att_ref[span, :] = unstack(attended).astype(BF16)
    grad_query = unstack(grad_query) * HEAD_DIM**-0.5
    gq_ref[span, :] = unrotate(grad_query, *[table[start : start + count] for table in tables]).astype(BF16)


def attend_kernel(
    blocks, count, meta_ref, q_ref, k_ref, v_ref, g_ref, kp_ref, vp_ref, cos_ref, minus_ref, plus_ref, att_ref, gq_ref,
    gk_ref, gv_ref, halo_ref, dk_ref, dv_ref, dkp_ref, dvp_ref,
):
    step = pl.program_id(1)
    block = blocks - 1 - step
    continued = meta_ref[CONT + block]
    offset = pl.multiple_of(continued * SHORT, SHORT)
    tables = tuple(ref[pl.ds(offset, SHORT), :] for ref in (cos_ref, minus_ref, plus_ref))

    @pl.when(step == 0)
    def _():
        dk_ref[...] = jnp.zeros_like(dk_ref)
        dv_ref[...] = jnp.zeros_like(dv_ref)

    @pl.when(step > 0)
    def _():
        dk_ref[...] = dkp_ref[...]
        dv_ref[...] = dvp_ref[...]

    dkp_ref[...] = jnp.zeros_like(dkp_ref)
    dvp_ref[...] = jnp.zeros_like(dvp_ref)
    args = (q_ref, k_ref, v_ref, g_ref, kp_ref, vp_ref, tables, att_ref, gq_ref, dk_ref, dv_ref, dkp_ref, dvp_ref)

    @pl.when(continued == 0)
    def _():
        for start in range(0, SHORT, count):
            attend_rows(False, start, count, *args)

    @pl.when(continued != 0)
    def _():
        for start in range(0, SHORT, count):
            attend_rows(True, start, count, *args)

    gk_ref[...] = pltpu.roll(unrotate(dk_ref[...], *tables), HEAD_DIM, 1).astype(BF16)
    gv_ref[...] = dv_ref[...].astype(BF16)

    @pl.when(block == 0)
    def _():
        base = tuple(ref[pl.ds(0, SHORT), :] for ref in (cos_ref, minus_ref, plus_ref))
        halo_ref[0] = pltpu.roll(unrotate(dkp_ref[...], *base), HEAD_DIM, 1).astype(BF16)
        halo_ref[1] = dvp_ref[...].astype(BF16)


def attend(shard, meta, q, k, v, g, tables, count):
    rows, head_width = q.shape[0], q.shape[1] // 2
    blocks, pairs = rows // SHORT, head_width // LANES
    here = pl.BlockSpec((SHORT, LANES), lambda p, i, meta: (blocks - 1 - i, p + shard * pairs))
    after = pl.BlockSpec((SHORT, LANES), lambda p, i, meta: (blocks - i, p + shard * pairs))
    new = pl.BlockSpec((SHORT, LANES), lambda p, i, meta: (blocks - 1 - i, p))
    return pl.pallas_call(
        functools.partial(attend_kernel, blocks, count),
        grid_spec=pltpu.PrefetchScalarGridSpec(
            num_scalar_prefetch=1,
            grid=(pairs, blocks),
            in_specs=[here, after, after, here, here, here] + [whole(table.shape) for table in tables],
            out_specs=[new] * 4 + [pl.BlockSpec((2, SHORT, LANES), lambda p, i, meta: (0, 0, p))],
            scratch_shapes=[pltpu.VMEM((SHORT, LANES), F32)] * 4,
        ),
        out_shape=[shaped((rows, head_width), BF16)] * 4 + [shaped((2, SHORT, head_width), BF16)],
        compiler_params=params(2),
        cost_estimate=BRIEF,
        name="attend",
    )(meta, q, k, v, g, k, v, *tables)


def settle_kernel(
    unit, tile, normed_ref, low_ref, grad_lows_ref, out_in_ref, att0_ref, att1_ref, gq0_ref, gq1_ref, gk0_ref, gk1_ref,
    gv0_ref, gv1_ref, halo0_ref, halo1_ref, triple0_ref, triple1_ref, left_ref, output0_ref, output1_ref, right0_ref,
    right1_ref, output_left0_ref, output_left1_ref, out_ref, keep_ref, right_grad0_ref, right_grad1_ref, left_grad_ref,
    output_left_grad0_ref, output_left_grad1_ref, got_ref, send_ref, halo_got_ref, key_ref, value_ref, halo_sems, sems,
):
    step = pl.program_id(0)
    per_device = got_ref.shape[1] // tile
    steps = unit * per_device
    halo_start = steps - SHORT // tile
    place, base = place_in_unit(unit)
    half = base // unit
    peers = unit_peers(unit)
    y_peer = chip_neighbours(unit)[1]
    halo_copy = pltpu.make_async_remote_copy(
        src_ref=halo1_ref, dst_ref=halo_got_ref, send_sem=halo_sems.at[0], recv_sem=halo_sems.at[1], device_id=y_peer,
        device_id_type=MESH,
    )
    copies = [
        [
            pltpu.make_async_remote_copy(
                src_ref=send_ref.at[s, pl.ds(t * tile, tile)], dst_ref=got_ref.at[s, pl.ds(t * tile, tile)],
                send_sem=sems.at[0, s, t], recv_sem=sems.at[1, s, t], device_id=peer, device_id_type=MESH,
            )
            for t in range(per_device)
        ]
        for s, peer in enumerate(peers)
    ]
    sums = (right_grad0_ref, right_grad1_ref, left_grad_ref, output_left_grad0_ref, output_left_grad1_ref)

    @pl.when(step == 0)
    def _():
        meet([y_peer, *peers])
        pl.when(half == 1)(halo_copy.start)
        for ref in sums:
            ref[...] = jnp.zeros_like(ref)

    key_ref[0], key_ref[1] = gk0_ref[...], gk1_ref[...]
    value_ref[0], value_ref[1] = gv0_ref[...], gv1_ref[...]

    @pl.when((half == 0) & (step >= halo_start))
    def _():
        pl.when(step == halo_start)(halo_copy.wait_recv)
        span = pl.ds(pl.multiple_of((step - halo_start) * tile, tile), tile)
        for shard, halo in enumerate((halo0_ref, halo_got_ref)):
            key_ref[shard] = (key_ref[shard].astype(F32) + halo[0, span].astype(F32)).astype(BF16)
            value_ref[shard] = (value_ref[shard].astype(F32) + halo[1, span].astype(F32)).astype(BF16)

    normed = normed_ref[...]
    low = low_ref[...]
    grad_low_out = grad_lows_ref[:, :LANES]
    att0, att1 = att0_ref[...], att1_ref[...]
    first = low_lanes()

    def mixed(gq, shard):
        query, key, value = gq[...], key_ref[shard], value_ref[shard]
        groups = []
        for start in range(0, query.shape[1], LANES):
            q, k, v = (part[:, start : start + LANES] for part in (query, key, value))
            groups += [jnp.where(first, q, k), jnp.where(first, v, q), jnp.where(first, k, v)]
        return jnp.concatenate(groups, axis=1)

    grad0 = mixed(gq0_ref, 0)
    grad1 = mixed(gq1_ref, 1)
    grad_low = (dot_nt(grad0, right0_ref[...]) + dot_nt(grad1, right1_ref[...])).astype(BF16)
    grad = (
        dot_nt(grad0, triple0_ref[...]) + dot_nt(grad1, triple1_ref[...]) + dot_nt(grad_low, left_ref[...])
    ).astype(BF16)
    out_ref[...] = out_in_ref[...] + dot_nn(att0, output0_ref[...]) + dot_nn(att1, output1_ref[...])
    low_att = (dot_nn(att0, output_left0_ref[...]) + dot_nn(att1, output_left1_ref[...])).astype(BF16)
    width = grad.shape[1]

    @pl.when(step // per_device == place)
    def _():
        keep_ref[:, :width] = grad
        keep_ref[:, width:] = low_att

    span = pl.ds(pl.multiple_of(lax.rem(step, per_device) * tile, tile), tile)
    for s in range(unit - 1):
        owner = lax.rem(place + unit - (s + 1), unit)

        @pl.when(step // per_device == owner)
        def _():
            send_ref[s, span, :width] = grad
            send_ref[s, span, width:] = low_att

        for t in range(per_device):
            pl.when(step == owner * per_device + t)(copies[s][t].start)

    right_grad0_ref[...] += dot_tn(low, grad0)
    right_grad1_ref[...] += dot_tn(low, grad1)
    left_grad_ref[...] += dot_tn(grad_low, normed)
    output_left_grad0_ref[...] += dot_tn(grad_low_out, att0)
    output_left_grad1_ref[...] += dot_tn(grad_low_out, att1)

    @pl.when(step == steps - 1)
    def _():
        pl.when(half == 1)(halo_copy.wait_send)
        for group in copies:
            for copy in group:
                copy.wait()


def settle(unit, normed, low, grad_lows, out, pairs, halos, triples, left, outputs, right, output_left, tile):
    rows, width = normed.shape
    own_rows = rows // unit
    head_width = pairs[0].shape[1]
    steps, per_device = rows // tile, own_rows // tile
    anywhere = pl.BlockSpec(memory_space=pl.ANY)

    def own(i):
        return lax.axis_index("mp")

    def far(i):
        return lax.rem(lax.axis_index("mp") + unit, 2 * unit)

    def kept(i):
        return (jnp.clip(i - place_in_unit(unit)[0] * per_device, 0, per_device - 1), 0)

    return pl.pallas_call(
        functools.partial(settle_kernel, unit, tile),
        grid=(steps,),
        in_specs=[rows_of(tile, width), rows_of(tile, LANES), rows_of(tile, 2 * LANES), rows_of(tile, width)]
        + [rows_of(tile, head_width)] * 8
        + [whole(halos[0].shape), anywhere]
        + [whole(value.shape) for value in (*triples, left, *outputs)]
        + [
            pl.BlockSpec((LANES, 3 * head_width), lambda i: (0, own(i)), pipeline_mode=pl.Buffered(1)),
            pl.BlockSpec((LANES, 3 * head_width), lambda i: (0, far(i)), pipeline_mode=pl.Buffered(1)),
            pl.BlockSpec((head_width, LANES), lambda i: (own(i), 0), pipeline_mode=pl.Buffered(1)),
            pl.BlockSpec((head_width, LANES), lambda i: (far(i), 0), pipeline_mode=pl.Buffered(1)),
        ],
        out_specs=[
            rows_of(tile, width),
            pl.BlockSpec((tile, width + LANES), kept),
            held((LANES, 3 * head_width)),
            held((LANES, 3 * head_width)),
            held((LANES, width)),
            held((LANES, head_width)),
            held((LANES, head_width)),
            anywhere,
        ],
        scratch_shapes=[
            pltpu.VMEM((unit - 1, own_rows, width + LANES), BF16),
            pltpu.VMEM((2, SHORT, head_width), BF16),
            pltpu.VMEM((2, tile, head_width), BF16),
            pltpu.VMEM((2, tile, head_width), BF16),
            pltpu.SemaphoreType.DMA((2,)),
            pltpu.SemaphoreType.DMA((2, unit - 1, per_device)),
        ],
        out_shape=[
            shaped((rows, width), F32),
            shaped((own_rows, width + LANES), BF16),
            shaped((LANES, 3 * head_width), F32),
            shaped((LANES, 3 * head_width), F32),
            shaped((LANES, width), F32),
            shaped((LANES, head_width), F32),
            shaped((LANES, head_width), F32),
            shaped((unit - 1, own_rows, width + LANES), BF16),
        ],
        compiler_params=pltpu.CompilerParams(
            dimension_semantics=("arbitrary",), vmem_limit_bytes=VMEM_LIMIT, collective_id=5, has_side_effects=True
        ),
        cost_estimate=BRIEF,
        name="settle",
    )(normed, low, grad_lows, out, *pairs, *halos, *triples, left, *outputs, right, right, output_left,
      output_left)


SUM_ROWS = (2, 4, 16)


def sum_kernel(chunks, width, extra, part_ref, both_ref, out_ref, both_out_ref, *scratch):
    dp = lax.axis_index("dp")
    mp = lax.axis_index("mp")
    half, core = mp // 2, lax.rem(mp, 2)
    x, z = lax.rem(dp, 2), dp // 2
    x_peer = (dp + 1 - 2 * x, mp)
    y_peer = (dp, mp + 2 - 4 * half)
    core_peer = (dp, mp + 1 - 2 * core)
    z_places = [lax.rem(z + j, 4) for j in range(1, 4)]
    z_peers = [(place * 2 + x, mp) for place in z_places]
    barrier = pltpu.get_barrier_semaphore()
    for peer in [x_peer, y_peer, core_peer] + z_peers:
        pl.semaphore_signal(barrier, inc=1, device_id=peer, device_id_type=MESH)
    pl.semaphore_wait(barrier, 6)
    started = []

    def send(src, dst, sems, slot, peer):
        copy = pltpu.make_async_remote_copy(
            src_ref=src, dst_ref=dst, send_sem=sems.at[0, slot], recv_sem=sems.at[1, slot], device_id=peer,
            device_id_type=MESH,
        )
        copy.start()
        started.append(copy)
        return copy

    def added(first, *others):
        total = first.astype(F32)
        for other in others:
            total = total + other.astype(F32)
        return total.astype(BF16)

    both_got_ref, both_sum_ref, core_sems, local_sems = scratch[:4]
    refs = [scratch[4 + 7 * i : 4 + 7 * (i + 1)] for i in range(len(chunks))]
    both_copy = send(both_ref.at[1 - core], both_got_ref, core_sems, 0, core_peer)

    def run(index):
        y_first, start, size = chunks[index]
        got1, work1, got2, work2, got_z, full, sems = refs[index]
        shared = start is None
        if shared:
            both_copy.wait_recv()
            for place, at in ((0, half), (1, 1 - half)):
                both_sum_ref[place] = added(both_ref[core, at], both_got_ref[at])
            source = both_sum_ref
        else:
            source = part_ref.at[:, :, :, :, pl.ds(start, size)]
        if y_first:
            copy = send(source.at[1], got1, sems, 0, y_peer)
            yield
            copy.wait_recv()
            work1[...] = added(source[0], got1[...])
            copy = send(work1.at[1 - x], got2, sems, 1, x_peer)
            yield
            copy.wait_recv()
            work2[...] = added(work1[x], got2[...])
        else:
            copy = send(source.at[:, 1 - x], got1, sems, 0, x_peer)
            yield
            copy.wait_recv()
            work1[...] = added(source[:, x], got1[...])
            copy = send(work1.at[1], got2, sems, 1, y_peer)
            yield
            copy.wait_recv()
            work2[...] = added(work1[0], got2[...])
        copies = [
            send(work2.at[place], got_z.at[j], sems, 2 + j, peer)
            for j, (place, peer) in enumerate(zip(z_places, z_peers))
        ]
        yield
        for copy in copies:
            copy.wait_recv()
        full[0, x, z] = added(work2[z], got_z[0], got_z[1], got_z[2])
        mine = full.at[0, x, z]
        copies = [send(mine, mine, sems, 5 + j, peer) for j, peer in enumerate(z_peers)]
        yield
        for copy in copies:
            copy.wait_recv()
        if y_first:
            copy = send(full.at[0, x], full.at[0, x], sems, 8, x_peer)
            yield
            copy.wait_recv()
            copy = send(full.at[0], full.at[1], sems, 9, y_peer)
        else:
            copy = send(full.at[0, x], full.at[1, x], sems, 8, y_peer)
            yield
            copy.wait_recv()
            copy = send(full.at[:, x], full.at[:, x], sems, 9, x_peer)
        yield
        copy.wait_recv()
        target = both_out_ref if shared else out_ref.at[:, :, :, :, :, pl.ds(start, size)]
        last = []
        for place, at in ((0, half), (1, 1 - half)):
            local = pltpu.make_async_copy(full.at[place], target.at[core, at], local_sems.at[index, place])
            local.start()
            last.append(local)
            last.append(send(full.at[place], target.at[core, at], sems, 10 + place, core_peer))
        yield
        last[0].wait()
        last[1].wait_recv()
        last[2].wait()
        last[3].wait_recv()

    running = [run(i) for i in range(len(chunks))]
    while running:
        running = [step for step in running if next(step, "end") != "end"]
    for copy in started:
        copy.wait_send()


def sum_all(part, both):
    width, extra = part.shape[-1], both.shape[-1]
    third = width // 3
    chunks = [(True, 0, third), (False, third, third), (True, 2 * third, third), (False, None, extra)]
    per_chunk = []
    for y_first, _, size in chunks:
        one = (16, size)
        per_chunk += [
            pltpu.VMEM(((2, 4) if y_first else (2, 4)) + one, BF16),
            pltpu.VMEM((2, 4) + one, BF16),
            pltpu.VMEM((4,) + one, BF16),
            pltpu.VMEM((4,) + one, BF16),
            pltpu.VMEM((3,) + one, BF16),
            pltpu.VMEM((2, 2, 4) + one, BF16),
            pltpu.SemaphoreType.DMA((2, 12)),
        ]
    out, both_out = pl.pallas_call(
        functools.partial(sum_kernel, chunks, width, extra),
        out_shape=[shaped((2, 2) + SUM_ROWS + (width,), BF16), shaped((2, 2) + SUM_ROWS + (extra,), BF16)],
        in_specs=[pl.BlockSpec(memory_space=pltpu.VMEM)] * 2,
        out_specs=[pl.BlockSpec(memory_space=pl.ANY)] * 2,
        scratch_shapes=[
            pltpu.VMEM((2,) + SUM_ROWS + (extra,), BF16),
            pltpu.VMEM((2,) + SUM_ROWS + (extra,), BF16),
            pltpu.SemaphoreType.DMA((2, 1)),
            pltpu.SemaphoreType.DMA((len(chunks), 2)),
        ]
        + per_chunk,
        compiler_params=pltpu.CompilerParams(
            collective_id=2, has_side_effects=True, vmem_limit_bytes=VMEM_LIMIT
        ),
        cost_estimate=BRIEF,
        name="sum_all",
    )(part.reshape((2,) + SUM_ROWS + (width,)), both.reshape((2, 2) + SUM_ROWS + (extra,)))
    return out.reshape(2, 2, 128, width), both_out.reshape(2, 2, 128, extra)


def unpack_kernel(widths, part_ref, both_ref, triple_ref, output_ref, up_ref, down_ref, triple_left_ref,
                  up_left_ref, output_right_ref, down_right_ref, norm_ref):
    triple_width, head_width, hidden = widths
    start = triple_width
    triple_ref[...] = part_ref[0, 0, :, :triple_width].astype(F32)
    output_ref[...] = part_ref[0, 0, :, start : start + head_width].astype(F32).T
    start += head_width
    up_ref[...] = part_ref[0, 0, :, start : start + hidden].astype(F32)
    start += hidden
    down_ref[...] = part_ref[0, 0, :, start : start + hidden].astype(F32).T
    size = triple_left_ref.shape[0]
    triple_left_ref[...] = both_ref[0, 0, :, :size].astype(F32).T
    up_left_ref[...] = both_ref[0, 0, :, size : 2 * size].astype(F32).T
    output_right_ref[...] = both_ref[0, 0, :, 2 * size : 3 * size].astype(F32)
    down_right_ref[...] = both_ref[0, 0, :, 3 * size : 4 * size].astype(F32)
    norm_ref[0] = both_ref[0, 0, : norm_ref.shape[1], 4 * size :].astype(F32)


def unpack(part, both, width, triple_width, head_width, hidden):
    quarter = width // 4

    def tall(rows):
        return pl.BlockSpec((rows, LANES), lambda s: (s, 0))

    def wide(cols):
        return pl.BlockSpec((LANES, cols), lambda s: (0, s))

    def piece(cols):
        return pl.BlockSpec((1, 1, LANES, cols), lambda s: (lax.rem(s, 2), s // 2, 0, 0))

    return pl.pallas_call(
        functools.partial(unpack_kernel, (triple_width, head_width, hidden)),
        grid=(4,),
        in_specs=[piece(part.shape[-1]), piece(both.shape[-1])],
        out_specs=[
            wide(triple_width), tall(head_width), wide(hidden), tall(hidden), tall(quarter), tall(quarter),
            wide(quarter), wide(quarter), pl.BlockSpec((1, width // LANES, LANES), lambda s: (s, 0, 0)),
        ],
        out_shape=[
            shaped((LANES, 4 * triple_width), F32),
            shaped((4 * head_width, LANES), F32),
            shaped((LANES, 4 * hidden), F32),
            shaped((4 * hidden, LANES), F32),
            shaped((width, LANES), F32),
            shaped((width, LANES), F32),
            shaped((LANES, width), F32),
            shaped((LANES, width), F32),
            shaped((4, width // LANES, LANES), F32),
        ],
        compiler_params=params(),
        cost_estimate=BRIEF,
        name="unpack",
    )(part, both)


def shards(
    ranks,
    groups,
    block_input,
    sequence_lengths,
    first_gain,
    first_shift,
    second_gain,
    second_shift,
    triple_weight,
    triple_left,
    triple_right,
    output_weight,
    output_left,
    output_right,
    expand_weight,
    expand_left,
    expand_right,
    shrink_weight,
    shrink_left,
    shrink_right,
    cotangent,
):
    unit = ranks // 2
    own_rows, width = block_input.shape
    rows = own_rows * unit
    blocks = rows // SHORT
    tile = math.gcd(own_rows, 256)
    triple_width = triple_weight.shape[1]
    head_width = output_weight.shape[0]
    hidden = expand_weight.shape[1]
    mp = lax.axis_index("mp")
    half = mp // unit
    place = lax.rem(mp, unit)
    far = lax.rem(mp + unit, ranks)
    swap = [(m, (m + unit) % ranks) for m in range(ranks)]
    onward = [(m, m + unit) for m in range(unit)]
    back = [(m + unit, m) for m in range(unit)]

    tables = rotary_tables()
    dp = lax.axis_index("dp")
    lead = lax.rem(dp, 2)
    beside = [(d, d + 1 - 2 * (d % 2)) for d in range(groups)]
    continues = find_flags(sequence_lengths[0])
    conts = lax.dynamic_slice_in_dim(continues, half * blocks, blocks, 0)
    meta = jnp.concatenate([jnp.stack([mp, far, lead, place]).astype(jnp.int32), conts])
    gain1, shift1 = first_gain[None, :], first_shift[None, :]
    gain2, shift2 = second_gain[None, :], second_shift[None, :]

    (normed1, normed2, dy, low2, grad_lows, out, grad2, low_act, grad_low2, expand_right_own, shrink_left_own,
     triple_far, output_far, x_halo, expand_half, shrink_half) = feed_first(
        unit, block_input, cotangent, (gain1, shift1, gain2, shift2), expand_weight, expand_left, expand_right,
        shrink_weight, shrink_left, output_right, shrink_right, triple_weight, output_weight, tile,
    )
    expand_piece = lax.ppermute(expand_half, "mp", swap)
    shrink_piece = lax.ppermute(shrink_half, "mp", swap)
    low1, q, k, v, g = project(
        meta, x_halo, normed1, dy, grad_lows, gain1, shift1, (triple_weight, triple_far), triple_left, triple_right,
        (output_weight, output_far), output_left, tables, tile,
    )
    expand_piece, q = lax.optimization_barrier((expand_piece, q))
    expand_other = lax.ppermute(expand_piece, "dp", beside)
    count = 256
    att_far, gq_far, gk_far, gv_far, halo = attend(1, meta, q, k, v, g, tables, count)
    halo_own = lax.ppermute(halo, "mp", back)
    shrink_piece, q = lax.optimization_barrier((shrink_piece, q))
    shrink_other = lax.ppermute(shrink_piece, "dp", beside)
    att_own, gq_own, gk_own, gv_own, halo = attend(0, meta, q, k, v, g, tables, count)
    (out, keep1, triple_right_own, triple_right_far, triple_left_sum, output_left_sum_own, output_left_sum_far,
     got1) = settle(
        unit, normed1, low1, grad_lows, out,
        (att_own, att_far, gq_own, gq_far, gk_own, gk_far, gv_own, gv_far), (halo_own, halo),
        (triple_weight, triple_far), triple_left, (output_weight, output_far), triple_right, output_left, tile,
    )
    (block_output, input_gradient, norms, output_right_sum, shrink_right_sum, expand_right_far, shrink_left_far,
     expand_left_sum) = feed_second(
        unit, normed2, low2, dy, grad_lows, out, grad2, low_act, grad_low2, block_input, keep1, got1, (gain1, gain2),
        output_right, shrink_right, (expand_piece, expand_other), expand_left, expand_right,
        (shrink_piece, shrink_other), shrink_left, tile,
    )

    own_sums = (triple_right_own, output_left_sum_own, expand_right_own, shrink_left_own)
    far_sums = (triple_right_far, output_left_sum_far, expand_right_far, shrink_left_far)
    both_sums = (triple_left_sum, expand_left_sum, output_right_sum, shrink_right_sum)
    if ranks == 4 and groups == 8:
        part = jnp.stack(
            [jnp.concatenate([value.astype(BF16) for value in sums], axis=1) for sums in (own_sums, far_sums)]
        )
        quarters = [value.astype(BF16).reshape(LANES, 4, width // 4) for value in both_sums]
        norms = jnp.pad(
            norms[:4].astype(BF16).reshape(4, width // LANES, LANES), ((0, 0), (0, LANES - width // LANES), (0, 0))
        )
        both = jnp.concatenate([value.transpose(1, 0, 2) for value in quarters] + [norms], axis=2)
        both = both.reshape(2, 2, LANES, width + LANES).transpose(1, 0, 2, 3)
        part, both = sum_all(part, both)
        (triple_right_sum, output_left_sum, expand_right_sum, shrink_left_sum, triple_left_sum, expand_left_sum,
         output_right_sum, shrink_right_sum, norms) = unpack(
            part, both, width, triple_width, head_width, hidden
        )
        norms = norms.reshape(4, width)
    else:

        def spread(own, other):
            size = own.shape[1]
            wide = jnp.zeros((LANES, size * ranks), BF16)
            wide = lax.dynamic_update_slice_in_dim(wide, own.astype(BF16), mp * size, 1)
            return lax.dynamic_update_slice_in_dim(wide, other.astype(BF16), far * size, 1)

        sums = [spread(own, other) for own, other in zip(own_sums, far_sums)]
        sums += [value.astype(BF16) for value in both_sums]
        norms, *sums = lax.psum([norms] + sums, ("dp", "mp"))
        (triple_right_sum, output_left_sum, expand_right_sum, shrink_left_sum, triple_left_sum, expand_left_sum,
         output_right_sum, shrink_right_sum) = [value.astype(F32) for value in sums]
        output_left_sum, shrink_left_sum = output_left_sum.T, shrink_left_sum.T
        triple_left_sum, expand_left_sum = triple_left_sum.T, expand_left_sum.T
    return (
        block_output,
        input_gradient,
        norms[0],
        norms[1],
        norms[2],
        norms[3],
        triple_left_sum,
        triple_right_sum,
        output_left_sum,
        output_right_sum,
        expand_left_sum,
        expand_right_sum,
        shrink_left_sum,
        shrink_right_sum,
    )


def solution(mesh):
    placed = (
        P(("dp", "mp"), None),
        P("dp", None),
        P(),
        P(),
        P(),
        P(),
        P(None, "mp"),
        P(),
        P(),
        P("mp", None),
        P(),
        P(),
        P(None, "mp"),
        P(),
        P(),
        P("mp", None),
        P(),
        P(),
        P(("dp", "mp"), None),
    )
    return jax.shard_map(
        functools.partial(shards, mesh.shape["mp"], mesh.shape["dp"]),
        mesh=mesh,
        in_specs=placed,
        out_specs=(P(("dp", "mp"), None), P(("dp", "mp"), None)) + (P(),) * 12,
        check_vma=False,
    )
```

```python
import functools
import math

import jax
import jax.numpy as jnp
import numpy as np
from jax import lax
from jax.experimental import pallas as pl
from jax.experimental.pallas import tpu as pltpu
from jax.sharding import PartitionSpec as P

HEAD_DIM = 64
ROT = 16
SHORT = 512
TOK_GRP = 3072
SLOTS = 6
EPS = 1e-05
LANES = 128
MESH = pl.DeviceIdType.MESH
BF16 = jnp.bfloat16
F32 = jnp.float32
VMEM_LIMIT = 56 * 1024 * 1024
BRIEF = pl.CostEstimate(flops=1, bytes_accessed=1, transcendentals=0)


def dot_nn(former, latter):
    return lax.dot_general(
        former, latter, (((1,), (0,)), ((), ())), preferred_element_type=F32
    )


def dot_nt(former, latter):
    return lax.dot_general(
        former, latter, (((1,), (1,)), ((), ())), preferred_element_type=F32
    )


def dot_tn(former, latter):
    return lax.dot_general(
        former, latter, (((0,), (0,)), ((), ())), preferred_element_type=F32
    )


def find_flags(group_lengths):
    seq_ends = jnp.cumsum(group_lengths, dtype=jnp.int32)
    starts = seq_ends - group_lengths
    block_starts = jnp.arange(SLOTS, dtype=jnp.int32) * SHORT
    begins = jnp.any(
        (starts[None, :] == block_starts[:, None]) & (group_lengths[None, :] > 0), axis=1
    )
    return jnp.where(begins, 0, 1).astype(jnp.int32)


def rotary_tables():
    half = ROT // 2
    frequency = np.exp(
        np.arange(half, dtype=np.float32) * np.float32(-2.0 * math.log(10000.0) / ROT)
    ).astype(np.float32)
    angles = np.arange(2 * SHORT, dtype=np.float32)[:, None] * frequency[None, :]
    cosine = np.ones((2 * SHORT, LANES), np.float32)
    minus = np.zeros((2 * SHORT, LANES), np.float32)
    plus = np.zeros((2 * SHORT, LANES), np.float32)
    for base in range(0, LANES, HEAD_DIM):
        cosine[:, base : base + half] = np.cos(angles)
        cosine[:, base + half : base + ROT] = np.cos(angles)
        minus[:, base : base + half] = -np.sin(angles)
        plus[:, base + half : base + ROT] = np.sin(angles)
    return jnp.asarray(cosine), jnp.asarray(minus), jnp.asarray(plus)


def tall_tables():
    half = ROT // 2
    frequency = np.exp(
        np.arange(half, dtype=np.float32) * np.float32(-2.0 * math.log(10000.0) / ROT)
    ).astype(np.float32)
    angles = frequency[:, None] * np.arange(2 * SHORT, dtype=np.float32)[None, :]
    return jnp.asarray(np.cos(angles)), jnp.asarray(np.sin(angles))


def low_lanes():
    return lax.broadcasted_iota(jnp.int32, (1, LANES), 1) < HEAD_DIM


def rotate(pair, cosine, minus, plus):
    half = ROT // 2
    return (
        pair * cosine
        + pltpu.roll(pair, LANES - half, 1) * minus
        + pltpu.roll(pair, half, 1) * plus
    )


def unrotate(pair, cosine, minus, plus):
    half = ROT // 2
    return (
        pair * cosine
        - pltpu.roll(pair, LANES - half, 1) * minus
        - pltpu.roll(pair, half, 1) * plus
    )


def normalize(values, gain, shift):
    center = values - jnp.mean(values, axis=-1, keepdims=True)
    spread = jnp.mean(center * center, axis=-1, keepdims=True)
    return center * lax.rsqrt(spread + EPS) * gain + shift


def whole(shape):
    return pl.BlockSpec(
        shape, lambda *idx: (0,) * len(shape), pipeline_mode=pl.Buffered(1)
    )


def held(shape):
    return pl.BlockSpec(shape, lambda *idx: (0,) * len(shape))


def rows_of(tile, width):
    return pl.BlockSpec((tile, width), lambda i, *refs: (i, 0))


def shaped(shape, dtype):
    return jax.ShapeDtypeStruct(shape, dtype)


def params(semantics=1):
    return pltpu.CompilerParams(
        dimension_semantics=("arbitrary",) * semantics, vmem_limit_bytes=VMEM_LIMIT
    )


SUM_ROWS = (2, 4, 16)


class Net:
    def __init__(self):
        dp, mp = lax.axis_index("dp"), lax.axis_index("mp")
        self.half, self.core = mp // 2, lax.rem(mp, 2)
        self.x, self.z = lax.rem(dp, 2), dp // 2
        self.other_half, self.other_core, self.other_x = 1 - self.half, 1 - self.core, 1 - self.x
        self.x_peer = (dp + 1 - 2 * self.x, mp)
        self.y_peer = (dp, mp + 2 - 4 * self.half)
        self.core_peer = (dp, mp + 1 - 2 * self.core)
        self.z_places = [lax.rem(self.z + j, 4) for j in range(1, 4)]
        self.z_peers = [(place * 2 + self.x, mp) for place in self.z_places]
        self.started = []

    def copy(self, src, dst, sems, slot, peer):
        return pltpu.make_async_remote_copy(
            src_ref=src, dst_ref=dst, send_sem=sems.at[0, slot], recv_sem=sems.at[1, slot], device_id=peer,
            device_id_type=MESH,
        )

    def start(self, copies):
        for copy in copies:
            copy.start()
        self.started += copies


def arrive(copies):
    for copy in copies:
        copy.wait_recv()


def added(first, *others):
    total = first.astype(F32)
    for other in others:
        total = total + other.astype(F32)
    return total.astype(BF16)


def sum_scratch(order, size):
    one = (16, size)
    first = {"yxz": ((2, 4), (2, 4)), "xyz": ((2, 4), (2, 4)), "xz": ((4,), (4,)), "zx": ((3, 2), (2,))}[order]
    second = {"yxz": ((4,), (4,)), "xyz": ((4,), (4,)), "xz": ((3,), (1,)), "zx": ((1,), (1,))}[order]
    return [pltpu.VMEM(shape + one, BF16) for shape in (*first, *second, (3,), (2, 2, 4))] + [
        pltpu.SemaphoreType.DMA((2, 12))
    ]


def sum_chunk(net, order, source, scratch):
    got1, work1, got2, work2, got3, full, sems = scratch
    x, z, other_x = net.x, net.z, net.other_x
    own, rows, plane = full.at[0, x, z], full.at[0, x], full.at[0, :, z]

    def to_z(src, dst, slot):
        return [
            net.copy(src(place), dst(j), sems, slot + j, peer)
            for j, (place, peer) in enumerate(zip(net.z_places, net.z_peers))
        ]

    def one(src, dst, slot, peer):
        return [net.copy(src, dst, sems, slot, peer)]

    last = work1 if order == "xz" else work2
    if order != "xyz":
        over_y = one(full.at[0], full.at[1], 9, net.y_peer)
    if order == "zx":
        spread = to_z(lambda place: source.at[:, place], lambda j: got1.at[j], 2)
        cross = one(work1.at[other_x], got2.at[0], 0, net.x_peer)
        back = one(own, own, 8, net.x_peer)
        gather = to_z(lambda place: plane, lambda j: plane, 5)
    else:
        spread = to_z(lambda place: last.at[place], lambda j: got3.at[j], 2)
        gather = to_z(lambda place: own, lambda j: own, 5)
        if order == "yxz":
            first = one(source.at[1], got1, 0, net.y_peer)
            second = one(work1.at[other_x], got2, 1, net.x_peer)
        elif order == "xyz":
            first = one(source.at[:, other_x], got1, 0, net.x_peer)
            second = one(work1.at[1], got2, 1, net.y_peer)
            over_y = one(rows, full.at[1, x], 8, net.y_peer)
            over_x = one(full.at[:, x], full.at[:, x], 9, net.x_peer)
        else:
            first = one(source.at[other_x], got1, 0, net.x_peer)
        if order != "xyz":
            over_x = one(rows, rows, 8, net.x_peer)

    def stages():
        if order == "zx":
            net.start(spread)
            yield
            arrive(spread)
            work1[...] = added(source[:, z], got1[0], got1[1], got1[2])
            net.start(cross)
            yield
            arrive(cross)
            full[0, x, z] = added(work1[x], got2[0])
            net.start(back)
            yield
            arrive(back)
            net.start(gather)
            yield
            arrive(gather)
            net.start(over_y)
            yield
            arrive(over_y)
            return
        net.start(first)
        yield
        arrive(first)
        if order == "yxz":
            work1[...] = added(source[0], got1[...])
            net.start(second)
            yield
            arrive(second)
            work2[...] = added(work1[x], got2[...])
        elif order == "xyz":
            work1[...] = added(source[:, x], got1[...])
            net.start(second)
            yield
            arrive(second)
            work2[...] = added(work1[0], got2[...])
        else:
            work1[...] = added(source[x], got1[...])
        net.start(spread)
        yield
        arrive(spread)
        full[0, x, z] = added(last[z], got3[0], got3[1], got3[2])
        net.start(gather)
        yield
        arrive(gather)
        for copies in (over_y, over_x) if order == "xyz" else (over_x, over_y):
            net.start(copies)
            yield
            arrive(copies)

    return stages()


def sum_both(net, order, both, got, total, core_sems, scratch):
    exchange = [net.copy(both.at[net.other_core], got, core_sems, 0, net.core_peer)]
    chunk = sum_chunk(net, order, total, scratch)

    def stages():
        net.start(exchange)
        yield
        arrive(exchange)
        for place, at in ((0, net.half), (1, net.other_half)):
            total[place] = added(both[net.core, at], got[at])
        yield from chunk

    return stages()


def both_scratch(order, size):
    return [
        pltpu.VMEM((2,) + SUM_ROWS + (size,), BF16),
        pltpu.VMEM((2,) + SUM_ROWS + (size,), BF16),
        pltpu.SemaphoreType.DMA((2, 1)),
    ] + sum_scratch(order, size)


def quarters(ref, *arrays):
    start = 0
    for array in arrays:
        size = array.shape[1] // 4
        for q in range(4):
            ref[q % 2, q // 2, :, start : start + size] = array[:, q * size : (q + 1) * size].astype(BF16)
        start += size


def gelu_parts(hidden):
    cdf = 0.5 + 0.5 * lax.erf(hidden * math.sqrt(0.5))
    density = jnp.exp(-0.5 * hidden * hidden) * (1.0 / math.sqrt(2.0 * math.pi))
    return hidden * cdf, cdf + hidden * density


def feed_core(
    normed, low, dy, grad_low, up_ref, up_right_ref, down_ref, down_left_ref, act_ref, grad_ref, hidden_step
):
    hidden_width = up_ref.shape[1]
    for start in range(0, hidden_width, hidden_step):
        cols = pl.ds(start, hidden_step)
        hidden = dot_nn(normed, up_ref[:, cols]) + dot_nn(low, up_right_ref[:, cols])
        grad_act = dot_nt(dy, down_ref[cols, :]) + dot_nt(grad_low, down_left_ref[cols, :])
        activated, slope = gelu_parts(hidden)
        act_ref[:, cols] = activated.astype(BF16)
        grad_ref[:, cols] = (grad_act * slope).astype(BF16)


def chip_neighbours(unit):
    dp = lax.axis_index("dp")
    mp = lax.axis_index("mp")
    lead = lax.rem(dp, 2)
    return lead, (dp, lax.rem(mp + unit, 2 * unit)), (dp + 1 - 2 * lead, mp)


def leads():
    dp = lax.axis_index("dp")
    return lax.rem(dp, 2), lax.rem(dp // 2, 2)


def courier(unit, pairs, chunks, y_sems, x_sems):
    lead, y_peer, x_peer = chip_neighbours(unit)
    over_y, over_x = [], []
    for k in range(chunks):
        for j, (own, far) in enumerate(pairs):
            count = own.shape[0] // 2 // chunks
            span = pl.ds(pl.multiple_of((lead * chunks + k) * count, count), count)
            for src, sems, peer, group in ((own, y_sems, y_peer, over_y), (far, x_sems, x_peer, over_x)):
                group.append(
                    pltpu.make_async_remote_copy(
                        src_ref=src.at[span],
                        dst_ref=far.at[span],
                        send_sem=sems.at[0, k, j],
                        recv_sem=sems.at[1, k, j],
                        device_id=peer,
                        device_id_type=MESH,
                    )
                )
    return over_y, over_x


def meet(peers):
    barrier = pltpu.get_barrier_semaphore()
    for peer in peers:
        pl.semaphore_signal(barrier, inc=1, device_id=peer, device_id_type=MESH)
    pl.semaphore_wait(barrier, len(peers))


def place_in_unit(unit):
    mp = lax.axis_index("mp")
    return lax.rem(mp, unit), mp - lax.rem(mp, unit)


def unit_peers(unit):
    place, base = place_in_unit(unit)
    return [(lax.axis_index("dp"), base + lax.rem(place + unit - s, unit)) for s in range(1, unit)]


def halo_copies(unit, x_ref, halo_ref, y_sems, unit_sems):
    own_rows = x_ref.shape[0]
    chunk = math.gcd(own_rows, 128)
    dp = lax.axis_index("dp")
    found = []
    for k in range(SHORT // chunk):
        row = unit * own_rows - SHORT + k * chunk
        holder, start = row // own_rows, row % own_rows
        target = halo_ref.at[pl.ds(k * chunk, chunk)]
        over_y = pltpu.make_async_remote_copy(
            src_ref=x_ref.at[pl.ds(start, chunk)], dst_ref=target, send_sem=y_sems.at[0, k], recv_sem=y_sems.at[1, k],
            device_id=(dp, unit + holder), device_id_type=MESH,
        )
        spread = [
            pltpu.make_async_remote_copy(
                src_ref=target, dst_ref=target, send_sem=unit_sems.at[0, k, s - 1], recv_sem=unit_sems.at[1, k, s - 1],
                device_id=(dp, unit + (holder + s) % unit), device_id_type=MESH,
            )
            for s in range(1, unit)
        ]
        found.append((holder, over_y, spread))
    return found


def feed_first_kernel(
    unit, tile, x_ref, dy_ref, gain1_ref, shift1_ref, gain2_ref, shift2_ref, up_ref, up_left_ref, up_right_ref, down_ref,
    down_left_ref, output_right_ref, down_right_ref, x_all_ref, dy_all_ref, triple_ref, output_ref, normed1_ref,
    normed_ref, dy_full_ref, low_ref, grad_lows_ref, out_ref, grad_ref, low_act_ref, grad_low_ref, sums_ref,
    triple_far_ref, output_far_ref, halo_ref, up_half_ref, down_half_ref, act_ref, gh_ref, acc_ref, xs_ref,
    x_got_ref, dy_got_ref, y_sems, x_sems, unit_sems, halo_y_sems, halo_unit_sems, local_sems,
):
    step = pl.program_id(0)
    own_rows = x_all_ref.shape[0]
    per_device = own_rows // tile
    steps = unit * per_device
    chunks = y_sems.shape[1]
    place, base = place_in_unit(unit)
    half = base // unit
    peers = unit_peers(unit)
    over_y, over_x = courier(
        unit, ((triple_ref, triple_far_ref), (output_ref, output_far_ref)), chunks, y_sems, x_sems
    )
    halo = halo_copies(unit, x_all_ref, halo_ref, halo_y_sems, halo_unit_sems)
    rows_out = [
        pltpu.make_async_remote_copy(
            src_ref=src, dst_ref=dst.at[j], send_sem=unit_sems.at[0, which, j], recv_sem=unit_sems.at[1, which, j],
            device_id=peer, device_id_type=MESH,
        )
        for j, peer in enumerate(peers)
        for which, (src, dst) in enumerate(((x_all_ref, x_got_ref), (dy_all_ref, dy_got_ref)))
    ]
    kept_halves = [
        pltpu.make_async_copy(
            src.at[pl.ds(pl.multiple_of(lead * dst.shape[0], dst.shape[0]), dst.shape[0])], dst, local_sems.at[j]
        )
        for j, (lead, src, dst) in enumerate(zip(leads(), (up_ref, down_ref), (up_half_ref, down_half_ref)))
    ]

    @pl.when(step == 0)
    def _():
        meet([*chip_neighbours(unit)[1:], *peers])
        for copy in rows_out + over_y + kept_halves:
            copy.start()
        xs_ref[...] = x_ref[...]
        dy_full_ref[...] = dy_ref[...]

    for holder, copy, _ in halo:
        pl.when((step == 0) & (half == 0) & (place == holder))(copy.start)

    @pl.when((step > 0) & (step < per_device))
    def _():
        xs_ref[...] = x_ref[...]
        dy_full_ref[...] = dy_ref[...]

    for slot in range(unit - 1):

        @pl.when(step == per_device * (slot + 1))
        def _():
            for which in range(2):
                rows_out[2 * slot + which].wait_recv()

        @pl.when((step >= per_device * (slot + 1)) & (step < per_device * (slot + 2)))
        def _():
            span = pl.ds(pl.multiple_of((step - per_device * (slot + 1)) * tile, tile), tile)
            xs_ref[...] = x_got_ref[slot, span]
            dy_full_ref[...] = dy_got_ref[slot, span]

    for k in range(chunks):

        @pl.when(step == min(k + 1, steps - 1))
        def _():
            for j in (2 * k, 2 * k + 1):
                over_y[j].wait_recv()
                over_x[j].start()

    x = xs_ref[...].astype(F32)
    center = x - jnp.mean(x, axis=-1, keepdims=True)
    spread = jnp.mean(center * center, axis=-1, keepdims=True)
    scaled = center * lax.rsqrt(spread + EPS)
    normed1_ref[...] = (scaled * gain1_ref[...] + shift1_ref[...]).astype(BF16)
    normed = (scaled * gain2_ref[...] + shift2_ref[...]).astype(BF16)
    normed_ref[...] = normed
    dy = dy_full_ref[...]
    low = dot_nn(normed, up_left_ref[...]).astype(BF16)
    low_ref[...] = low
    rights = jnp.concatenate([output_right_ref[...], down_right_ref[...]], axis=0)
    grad_lows = dot_nt(dy, rights).astype(BF16)
    grad_lows_ref[...] = grad_lows
    grad_low = grad_lows[:, LANES:]
    feed_core(normed, low, dy, grad_low, up_ref, up_right_ref, down_ref, down_left_ref, act_ref, gh_ref, 256)
    act = act_ref[...]
    gh = gh_ref[...]
    out_ref[...] = dot_nn(act, down_ref[...])
    grad_ref[...] = dot_nt(gh, up_ref[...])
    low_act_ref[...] = dot_nn(act, down_left_ref[...])
    grad_low_ref[...] = dot_nt(gh, up_right_ref[...])

    @pl.when(step == 0)
    def _():
        acc_ref[...] = jnp.zeros_like(acc_ref)

    hidden = up_ref.shape[1]
    acc_ref[:, :hidden] += dot_tn(low, gh)
    acc_ref[:, hidden:] += dot_tn(grad_low, act)

    @pl.when((step == 0) & (half == 0))
    def _():
        fills = [
            pltpu.make_async_copy(xs_ref, halo_ref.at[pl.ds(k * tile, tile)], local_sems.at[2 + k])
            for k in range(SHORT // tile)
        ]
        for copy in fills:
            copy.start()
        for copy in fills:
            copy.wait()

    @pl.when(step == steps - 1)
    def _():
        sums_ref[...] = acc_ref[...].astype(BF16)
        for holder, copy, spread_copies in halo:

            @pl.when((half == 1) & (place == holder))
            def _():
                copy.wait_recv()
                for other in spread_copies:
                    other.start()

        for holder, copy, spread_copies in halo:
            pl.when((half == 0) & (place == holder))(copy.wait_send)

            @pl.when((half == 1) & (place == holder))
            def _():
                for other in spread_copies:
                    other.wait_send()

            for s in range(1, unit):
                pl.when((half == 1) & (place == (holder + s) % unit))(spread_copies[s - 1].wait_recv)
        for copy in rows_out + over_y:
            copy.wait_send()
        for copy in over_x + kept_halves:
            copy.wait()


def at_columns(shape, which):
    return pl.BlockSpec(shape, lambda i, meta: (0, meta[which]), pipeline_mode=pl.Buffered(1))


def at_rows(shape, which):
    return pl.BlockSpec(shape, lambda i, meta: (meta[which], 0), pipeline_mode=pl.Buffered(1))


OWN, FAR, LEAD, PLACE, CONT = 0, 1, 2, 3, 4


def feed_first(unit, x, dy, norms, up, up_left, up_right, down, down_left, output_right, down_right, triple, output,
               tile):
    own_rows, width = x.shape
    rows = own_rows * unit
    hidden = up.shape[1]
    steps, per_device = rows // tile, own_rows // tile
    chunks = math.gcd(4, output.shape[0] // 32)
    halo_chunks = SHORT // math.gcd(own_rows, 128)
    anywhere = pl.BlockSpec(memory_space=pl.ANY)
    here = pl.BlockSpec((tile, width), lambda i: (jnp.minimum(i, per_device - 1), 0))

    def turned(size):
        def index(i):
            return (lax.rem(i + place_in_unit(unit)[0] * per_device, steps), 0)

        return pl.BlockSpec((tile, size), index)

    return pl.pallas_call(
        functools.partial(feed_first_kernel, unit, tile),
        grid=(steps,),
        in_specs=[here, here]
        + [whole((1, width))] * 4
        + [
            whole(up.shape),
            whole(up_left.shape),
            pl.BlockSpec((LANES, hidden), lambda i: (0, lax.axis_index("mp")), pipeline_mode=pl.Buffered(1)),
            whole(down.shape),
            pl.BlockSpec((hidden, LANES), lambda i: (lax.axis_index("mp"), 0), pipeline_mode=pl.Buffered(1)),
            whole(output_right.shape),
            whole(down_right.shape),
        ]
        + [anywhere] * 4,
        out_specs=[
            turned(width),
            turned(width),
            turned(width),
            turned(LANES),
            turned(2 * LANES),
            turned(width),
            turned(width),
            turned(LANES),
            turned(LANES),
            held((LANES, 2 * hidden)),
        ]
        + [anywhere] * 5,
        scratch_shapes=[
            pltpu.VMEM((tile, hidden), BF16),
            pltpu.VMEM((tile, hidden), BF16),
            pltpu.VMEM((LANES, 2 * hidden), F32),
            pltpu.VMEM((tile, width), BF16),
            pltpu.VMEM((unit - 1, own_rows, width), BF16),
            pltpu.VMEM((unit - 1, own_rows, width), BF16),
            pltpu.SemaphoreType.DMA((2, chunks, 2)),
            pltpu.SemaphoreType.DMA((2, chunks, 2)),
            pltpu.SemaphoreType.DMA((2, 2, unit - 1)),
            pltpu.SemaphoreType.DMA((2, halo_chunks)),
            pltpu.SemaphoreType.DMA((2, halo_chunks, unit - 1)),
            pltpu.SemaphoreType.DMA((2 + SHORT // tile,)),
        ],
        out_shape=[
            shaped((rows, width), BF16),
            shaped((rows, width), BF16),
            shaped((rows, width), BF16),
            shaped((rows, LANES), BF16),
            shaped((rows, 2 * LANES), BF16),
            shaped((rows, width), F32),
            shaped((rows, width), F32),
            shaped((rows, LANES), F32),
            shaped((rows, LANES), F32),
            shaped((LANES, 2 * hidden), BF16),
            shaped(triple.shape, BF16),
            shaped(output.shape, BF16),
            shaped((SHORT, width), BF16),
            shaped((up.shape[0] // 2, up.shape[1]), BF16),
            shaped((down.shape[0] // 2, down.shape[1]), BF16),
        ],
        compiler_params=pltpu.CompilerParams(
            dimension_semantics=("arbitrary",), vmem_limit_bytes=VMEM_LIMIT, collective_id=3, has_side_effects=True
        ),
        cost_estimate=BRIEF,
        name="feed_first",
    )(x, dy, *norms, up, up_left, up_right, down, down_left, output_right, down_right, x, dy, triple, output)


def join_halves(step, lead, pieces, whole_ref):
    @pl.when(step == 0)
    def _():
        count = pieces[0].shape[0]
        for j, piece in enumerate(pieces):
            place = j + lead * (1 - 2 * j)
            whole_ref[pl.ds(pl.multiple_of(place * count, count), count), :] = piece[...]


def feed_second_kernel(
    unit, tile, normed_ref, low_ref, dy_ref, grad_lows_ref, out_in_ref, grad_in_ref, low_act_in_ref, grad_low_in_ref,
    x_ref, keep_ref, got1_ref, gain1_ref, gain2_ref, output_right_ref, down_right_ref, up0_ref, up1_ref, up_left_ref,
    up_right_ref, down0_ref, down1_ref, down_left_ref, early_ref, heads_ref, left_ref, y_ref, dx_ref, sums_ref, both_ref,
    heads_out_ref, left_out_ref, act_ref, gh_ref, up_ref, down_ref, send_ref, got_ref, early_got_ref, acc_ref, norms_ref,
    output_right_grad_ref, down_right_grad_ref, up_left_grad_ref, sems, early_sems, out_sems, *sum_refs,
):
    step = pl.program_id(0)
    own_rows = got_ref.shape[1]
    per_device = own_rows // tile
    send_tiles = (unit - 1) * per_device
    up_lead, down_lead = leads()
    peers = unit_peers(unit)
    copies = [
        [
            pltpu.make_async_remote_copy(
                src_ref=send_ref.at[s, pl.ds(t * tile, tile)], dst_ref=got_ref.at[s, pl.ds(t * tile, tile)],
                send_sem=sems.at[0, s, t], recv_sem=sems.at[1, s, t], device_id=peer, device_id_type=MESH,
            )
            for t in range(per_device)
        ]
        for s, peer in enumerate(peers)
    ]

    steps = unit * per_device
    y_peer = chip_neighbours(unit)[1]
    pieces = early_sems.shape[1]
    count = early_ref.shape[0] // pieces
    early_copies = [
        pltpu.make_async_remote_copy(
            src_ref=early_ref.at[pl.ds(j * count, count)], dst_ref=early_got_ref.at[pl.ds(j * count, count)],
            send_sem=early_sems.at[0, j], recv_sem=early_sems.at[1, j], device_id=y_peer, device_id_type=MESH,
        )
        for j in range(pieces)
    ]
    hosted = len(sum_refs) > 0
    if hosted:
        net = Net()
        size = heads_ref.shape[-1] // 2
        split = len(sum_scratch("yxz", size))
        heads_refs = (sum_refs[:split], sum_refs[split : 2 * split])
        left_refs = sum_refs[2 * split :]
        stages = [
            sum_chunk(net, order, heads_ref.at[:, :, :, :, pl.ds(j * size, size)], heads_refs[j])
            for j, order in enumerate(("yxz", "xyz"))
        ]
        stages.append(sum_both(net, "yxz", left_ref, *left_refs[:3], left_refs[3:]))

    def advance(at):
        if hosted:

            @pl.when(step == at)
            def _():
                for stage in stages:
                    next(stage, None)

    @pl.when(step == 0)
    def _():
        meet([*peers, y_peer] + ([net.x_peer, *net.z_peers] if hosted else []))
        for ref in (norms_ref, output_right_grad_ref, down_right_grad_ref, acc_ref, up_left_grad_ref):
            ref[...] = jnp.zeros_like(ref)

    for k in range(6):
        advance(k)
    for j, copy in enumerate(early_copies):
        pl.when(step == min(j + 1, steps - 1))(copy.start)
    join_halves(step, up_lead, (up0_ref, up1_ref), up_ref)
    join_halves(step, down_lead, (down0_ref, down1_ref), down_ref)
    normed = normed_ref[...]
    low = low_ref[...]
    dy = dy_ref[...]
    grad_low = grad_lows_ref[:, LANES:]
    feed_core(normed, low, dy, grad_low, up_ref, up_right_ref, down_ref, down_left_ref, act_ref, gh_ref, 256)
    act = act_ref[...]
    gh = gh_ref[...]
    grad_low_up = (grad_low_in_ref[...] + dot_nt(gh, up_right_ref[...])).astype(BF16)
    width = dy.shape[1]
    hidden = up_ref.shape[1]

    def results():
        out = out_in_ref[...] + dot_nn(act, down_ref[...])
        grad = grad_in_ref[...] + dot_nt(gh, up_ref[...]) + dot_nt(grad_low_up, up_left_ref[...])
        low_act = low_act_in_ref[...] + dot_nn(act, down_left_ref[...])
        return out, grad, low_act

    acc_ref[:, :hidden] += dot_tn(low, gh)
    acc_ref[:, hidden:] += dot_tn(grad_low, act)
    up_left_grad_ref[...] += dot_tn(grad_low_up, normed)

    @pl.when(step < send_tiles)
    def _():
        out, grad, low_act = results()
        slot = step // per_device
        span = pl.ds(pl.multiple_of(lax.rem(step, per_device) * tile, tile), tile)
        send_ref[slot, span, :width] = out.astype(BF16)
        send_ref[slot, span, width : 2 * width] = grad.astype(BF16)
        send_ref[slot, span, 2 * width :] = low_act.astype(BF16)

    for s in range(unit - 1):
        for t in range(per_device):
            pl.when(step == s * per_device + t)(copies[s][t].start)
            pl.when(step == send_tiles + t)(copies[s][t].wait_recv)

    @pl.when(step >= send_tiles)
    def _():
        out, second, low_act = results()
        span = pl.ds(pl.multiple_of((step - send_tiles) * tile, tile), tile)
        first = keep_ref[:, :width].astype(F32)
        low_att = keep_ref[:, width:].astype(F32)
        for s in range(unit - 1):
            first = first + got1_ref[s, :, :width].astype(F32)
            low_att = low_att + got1_ref[s, :, width:].astype(F32)
            out = out + got_ref[s, span, :width].astype(F32)
            second = second + got_ref[s, span, width : 2 * width].astype(F32)
            low_act = low_act + got_ref[s, span, 2 * width :].astype(F32)
        low_att, low_act = low_att.astype(BF16), low_act.astype(BF16)
        x = x_ref[...].astype(F32)
        y_ref[...] = (
            x + out + dot_nn(low_att, output_right_ref[...]) + dot_nn(low_act, down_right_ref[...])
        ).astype(BF16)
        center = x - jnp.mean(x, axis=-1, keepdims=True)
        spread = jnp.mean(center * center, axis=-1, keepdims=True)
        inverse = lax.rsqrt(spread + EPS)
        scaled = center * inverse
        total = first * gain1_ref[...] + second * gain2_ref[...]
        mean = jnp.mean(total, axis=-1, keepdims=True)
        inner = jnp.mean(total * scaled, axis=-1, keepdims=True)
        dx_ref[...] = dy.astype(F32) + (total - mean - scaled * inner) * inverse
        norms_ref[0:1, :] += jnp.sum(first * scaled, axis=0, keepdims=True)
        norms_ref[1:2, :] += jnp.sum(first, axis=0, keepdims=True)
        norms_ref[2:3, :] += jnp.sum(second * scaled, axis=0, keepdims=True)
        norms_ref[3:4, :] += jnp.sum(second, axis=0, keepdims=True)
        output_right_grad_ref[...] += dot_tn(low_att, dy)
        down_right_grad_ref[...] += dot_tn(low_act, dy)

    @pl.when(step == steps - 1)
    def _():
        for copy in early_copies:
            copy.wait()
        sums_ref[...] = (acc_ref[...] + early_got_ref[...].astype(F32)).astype(BF16)
        quarters(both_ref, up_left_grad_ref[...], output_right_grad_ref[...], down_right_grad_ref[...])
        start = 3 * (width // 4)
        count = width // LANES
        for q in range(4):
            rows = [norms_ref[q : q + 1, j * LANES : (j + 1) * LANES] for j in range(count)]
            block = jnp.concatenate([*rows, jnp.zeros((LANES - count, LANES), F32)], axis=0)
            both_ref[q % 2, q // 2, :, start:] = block.astype(BF16)
        for group in copies:
            for copy in group:
                copy.wait_send()
        if hosted:
            for stage in stages:
                for _ in stage:
                    pass
            outs = []
            for j, refs in enumerate((*heads_refs, left_refs[3:])):
                full = refs[5]
                target = left_out_ref if j == 2 else heads_out_ref.at[:, :, :, :, pl.ds(j * size, size)]
                outs.append(pltpu.make_async_copy(full, target, out_sems.at[j]))
                outs[-1].start()
            for copy in net.started:
                copy.wait_send()
            for copy in outs:
                copy.wait()


def feed_second(unit, normed, low, dy, grad_lows, out, grad, low_act, grad_low, x, keep, got, gains, output_right,
                down_right, ups, up_left, up_right, downs, down_left, early, heads, left, hosted, tile):
    rows, width = normed.shape
    own_rows = rows // unit
    anywhere = pl.BlockSpec(memory_space=pl.ANY)
    extra = []
    if hosted:
        heads = heads.reshape((2,) + SUM_ROWS + heads.shape[-1:])
        left = left.reshape((2, 2) + SUM_ROWS + left.shape[-1:])
        extra = sum_scratch("yxz", heads.shape[-1] // 2) + sum_scratch("xyz", heads.shape[-1] // 2)
        extra += both_scratch("yxz", left.shape[-1])
    hidden = ups[0].shape[1]
    steps, per_device = rows // tile, own_rows // tile
    send_tiles = steps - per_device
    wide = 2 * width + LANES

    def turned(size):
        def index(i):
            place, slot = place_in_unit(unit)[0], i // per_device + 1
            return (lax.rem(place + unit - slot, unit) * per_device + lax.rem(i, per_device), 0)

        return pl.BlockSpec((tile, size), index)

    def late(size):
        return pl.BlockSpec((tile, size), lambda i: (jnp.maximum(i - send_tiles, 0), 0))

    def far():
        return lax.rem(lax.axis_index("mp") + unit, 2 * unit)

    return pl.pallas_call(
        functools.partial(feed_second_kernel, unit, tile),
        grid=(steps,),
        in_specs=[
            turned(width),
            turned(LANES),
            turned(width),
            turned(2 * LANES),
            turned(width),
            turned(width),
            turned(LANES),
            turned(LANES),
            late(width),
            late(width + LANES),
            pl.BlockSpec((unit - 1, tile, width + LANES), lambda i: (0, jnp.maximum(i - send_tiles, 0), 0)),
            whole((1, width)),
            whole((1, width)),
            whole(output_right.shape),
            whole(down_right.shape),
            whole(ups[0].shape),
            whole(ups[1].shape),
            whole(up_left.shape),
            pl.BlockSpec((LANES, hidden), lambda i: (0, far()), pipeline_mode=pl.Buffered(1)),
            whole(downs[0].shape),
            whole(downs[1].shape),
            pl.BlockSpec((hidden, LANES), lambda i: (far(), 0), pipeline_mode=pl.Buffered(1)),
            whole(early.shape),
            whole(heads.shape),
            whole(left.shape),
        ],
        out_specs=[
            late(width),
            late(width),
            held((LANES, 2 * hidden)),
            held((2, 2, LANES, 3 * (width // 4) + LANES)),
            anywhere,
            anywhere,
        ],
        scratch_shapes=[
            pltpu.VMEM((tile, hidden), BF16),
            pltpu.VMEM((tile, hidden), BF16),
            pltpu.VMEM((width, hidden), BF16),
            pltpu.VMEM((hidden, width), BF16),
            pltpu.VMEM((unit - 1, own_rows, wide), BF16),
            pltpu.VMEM((unit - 1, own_rows, wide), BF16),
            pltpu.VMEM((LANES, 2 * hidden), BF16),
            pltpu.VMEM((LANES, 2 * hidden), F32),
            pltpu.VMEM((8, width), F32),
            pltpu.VMEM((LANES, width), F32),
            pltpu.VMEM((LANES, width), F32),
            pltpu.VMEM((LANES, width), F32),
            pltpu.SemaphoreType.DMA((2, unit - 1, per_device)),
            pltpu.SemaphoreType.DMA((2, 4)),
            pltpu.SemaphoreType.DMA((3,)),
        ]
        + extra,
        out_shape=[
            shaped((own_rows, width), BF16),
            shaped((own_rows, width), F32),
            shaped((LANES, 2 * hidden), BF16),
            shaped((2, 2, LANES, 3 * (width // 4) + LANES), BF16),
            shaped(heads.shape, BF16),
            shaped(left.shape[1:] if hosted else left.shape, BF16),
        ],
        compiler_params=pltpu.CompilerParams(
            dimension_semantics=("arbitrary",), vmem_limit_bytes=VMEM_LIMIT, collective_id=4, has_side_effects=True
        ),
        cost_estimate=BRIEF,
        name="feed_second",
    )(normed, low, dy, grad_lows, out, grad, low_act, grad_low, x, keep, got, *gains, output_right, down_right, *ups,
      up_left, up_right, *downs, down_left, early, heads, left)


def project_kernel(
    main_tiles, meta_ref, x_halo_ref, normed_ref, dy_ref, grad_lows_ref, gain_ref, shift_ref, triple0_ref, triple1_ref,
    left_ref, right0_ref, right1_ref, output0_ref, output1_ref, output_left0_ref, output_left1_ref, cos_ref,
    minus_ref, plus_ref, low_ref, q_ref, k_ref, v_ref, g_ref,
):
    step = pl.program_id(0)
    tables = (cos_ref[...], minus_ref[...], plus_ref[...])
    head_width = output0_ref.shape[0]
    first = low_lanes()

    def rows(normed, full):
        low = dot_nn(normed, left_ref[...]).astype(BF16)
        if full:
            low_ref[...] = low
        for shard, (triple, right) in enumerate(((triple0_ref, right0_ref), (triple1_ref, right1_ref))):
            mixed = dot_nn(normed, triple[...]) + dot_nn(low, right[...])
            for pair in range(head_width // LANES):
                one, two, three = (
                    mixed[:, (3 * pair + part) * LANES : (3 * pair + part + 1) * LANES] for part in range(3)
                )
                cols = pl.ds(shard * head_width + pair * LANES, LANES)
                key = pltpu.roll(jnp.where(first, three, one), HEAD_DIM, 1)
                k_ref[:, cols] = rotate(key, *tables).astype(BF16)
                v_ref[:, cols] = jnp.where(first, two, three).astype(BF16)
                if full:
                    query = rotate(jnp.where(first, one, two), *tables).astype(BF16)
                    q_ref[:, cols] = query * HEAD_DIM**-0.5

    @pl.when(step < main_tiles)
    def _():
        rows(normed_ref[...], True)
        dy = dy_ref[...]
        grad_low = grad_lows_ref[:, :LANES]
        outputs = jnp.concatenate([output0_ref[...], output1_ref[...]], axis=0)
        lefts = jnp.concatenate([output_left0_ref[...], output_left1_ref[...]], axis=0)
        g_ref[...] = (dot_nt(dy, outputs) + dot_nt(grad_low, lefts)).astype(BF16)

    @pl.when(step >= main_tiles)
    def _():
        rows(normalize(x_halo_ref[...].astype(F32), gain_ref[...], shift_ref[...]).astype(BF16), False)


def project(meta, x_halo, normed, dy, grad_lows, gain, shift, triples, left, right, outputs, output_left, tables, tile):
    rows, width = dy.shape
    head_width = outputs[0].shape[0]
    triple_width = triples[0].shape[1]
    per_block = SHORT // tile
    main_tiles, halo_tiles = rows // tile, SHORT // tile

    def table_index(i, meta):
        block = meta[CONT + jnp.minimum(i, main_tiles - 1) // per_block] * per_block + lax.rem(i, per_block)
        return (jnp.where(i < main_tiles, block, i - main_tiles), 0)

    table = pl.BlockSpec((tile, LANES), table_index)

    def main(size):
        return pl.BlockSpec((tile, size), lambda i, meta: (jnp.minimum(i, main_tiles - 1), 0))

    def late(size):
        return pl.BlockSpec((tile, size), lambda i, meta: (jnp.maximum(i - main_tiles, 0), 0))

    def all_rows(size):
        return pl.BlockSpec(
            (tile, size), lambda i, meta: (jnp.where(i < main_tiles, i + halo_tiles, i - main_tiles), 0)
        )

    return pl.pallas_call(
        functools.partial(project_kernel, main_tiles),
        grid_spec=pltpu.PrefetchScalarGridSpec(
            num_scalar_prefetch=1,
            grid=(main_tiles + halo_tiles,),
            in_specs=[
                late(width),
                main(width),
                main(width),
                main(2 * LANES),
                whole(gain.shape),
                whole(shift.shape),
                whole(triples[0].shape),
                whole(triples[1].shape),
                whole(left.shape),
                at_columns((LANES, triple_width), OWN),
                at_columns((LANES, triple_width), FAR),
                whole(outputs[0].shape),
                whole(outputs[1].shape),
                at_rows((head_width, LANES), OWN),
                at_rows((head_width, LANES), FAR),
                table,
                table,
                table,
            ],
            out_specs=[
                main(LANES),
                main(2 * head_width),
                all_rows(2 * head_width),
                all_rows(2 * head_width),
                main(2 * head_width),
            ],
        ),
        out_shape=[
            shaped((rows, LANES), BF16),
            shaped((rows, 2 * head_width), BF16),
            shaped((SHORT + rows, 2 * head_width), BF16),
            shaped((SHORT + rows, 2 * head_width), BF16),
            shaped((rows, 2 * head_width), BF16),
        ],
        compiler_params=params(),
        cost_estimate=BRIEF,
        name="project",
    )(meta, x_halo, normed, dy, grad_lows, gain, shift, *triples, left, right, right, *outputs, output_left,
      output_left, *tables)


def attend_rows(with_prev, pairs, count, allowed, q_ref, k_ref, v_ref, g_ref, kp_ref, vp_ref, tables, att_ref, gq_ref,
                dk_ref, dv_ref, dkp_ref, dvp_ref):
    first = low_lanes()
    zero = jnp.zeros((), BF16)

    def stack(pair):
        return jnp.concatenate([jnp.where(first, pair, zero), jnp.where(first, zero, pair)], axis=0)

    def unstack(both):
        return jnp.where(first, both[:count], both[count:])

    def joined(fold, values):
        return functools.reduce(fold, values)

    pieces = []
    for lanes in pairs:
        for start in range(0, SHORT, count):
            span = pl.ds(start, count)
            parts = []
            if with_prev:
                parts.append((kp_ref[:, lanes], vp_ref[:, lanes], dkp_ref, dvp_ref, pl.ds(0, SHORT)))
            if start:
                before = pl.ds(0, start)
                parts.append((k_ref[before, lanes], v_ref[before, lanes], dk_ref, dv_ref, before))
            parts.append((k_ref[span, lanes], v_ref[span, lanes], dk_ref, dv_ref, span))
            pieces.append((lanes, span, stack(q_ref[span, lanes]), stack(g_ref[span, lanes]), parts))

    scores, grads, weights, lows, inners, slopes = [], [], [], [], [], []
    for _, _, queries, _, parts in pieces:
        found = [dot_nt(queries, part[0]) for part in parts]
        scores.append(found[:-1] + [jnp.where(allowed, found[-1], -1e30)])
    for _, _, _, grad, parts in pieces:
        grads.append([dot_nt(grad, part[1]) for part in parts])
    for found in scores:
        peak = joined(jnp.maximum, [jnp.max(score, axis=1, keepdims=True) for score in found])
        exps = [jnp.exp(score - peak) for score in found]
        scale = 1.0 / joined(jnp.add, [jnp.sum(exp, axis=1, keepdims=True) for exp in exps])
        weights.append([exp * scale for exp in exps])
        lows.append([weight.astype(BF16) for weight in weights[-1]])
    for (lanes, span, _, grad, parts), low in zip(pieces, lows):
        attended = joined(jnp.add, [dot_nn(weight, part[1]) for weight, part in zip(low, parts)])
        att_ref[span, lanes] = unstack(attended).astype(BF16)
        inners.append(jnp.sum(attended * grad.astype(F32), axis=1, keepdims=True))
    for weight, grad, inner in zip(weights, grads, inners):
        slopes.append([(w * (g - inner)).astype(BF16) for w, g in zip(weight, grad)])
    for (lanes, span, queries, grad, parts), low, slope in zip(pieces, lows, slopes):
        grad_query = joined(jnp.add, [dot_nn(ds, part[0]) for ds, part in zip(slope, parts)])
        for ds, weight, (_, _, to_key, to_value, rows) in zip(slope, low, parts):
            to_key[lanes, rows] += dot_tn(queries, ds)
            to_value[lanes, rows] += dot_tn(grad, weight)
        grad_query = unstack(grad_query) * HEAD_DIM**-0.5
        gq_ref[span, lanes] = unrotate(grad_query, *[table[span] for table in tables]).astype(BF16)


def unrotate_tall(ref, lanes, cosine, sine):
    half = ROT // 2
    value = ref[lanes, :]
    halves = []
    for base in (HEAD_DIM, 0):
        one, two = value[base : base + half], value[base + half : base + ROT]
        halves += [one * cosine + two * sine, two * cosine - one * sine, value[base + ROT : base + HEAD_DIM]]
    return jnp.concatenate(halves, axis=0).astype(BF16).T


def attend_kernel(
    blocks, pairs, count, meta_ref, q_ref, k_ref, v_ref, g_ref, kp_ref, vp_ref, cos_ref, minus_ref, plus_ref,
    tall_cos_ref, tall_sin_ref, att_ref, gq_ref, gk_ref, gv_ref, halo_ref, dk_ref, dv_ref,
):
    step = pl.program_id(0)
    block = blocks - 1 - step
    continued = meta_ref[CONT + block]
    offset = pl.multiple_of(continued * SHORT, SHORT)
    tables = tuple(ref.at[pl.ds(offset, SHORT)] for ref in (cos_ref, minus_ref, plus_ref))
    now = lax.rem(step, 2)
    own = (dk_ref.at[now], dv_ref.at[now])
    before = (dk_ref.at[1 - now], dv_ref.at[1 - now])

    @pl.when(step == 0)
    def _():
        for ref in own:
            ref[...] = jnp.zeros_like(ref)

    for ref in before:
        ref[...] = jnp.zeros_like(ref)
    row = lax.broadcasted_iota(jnp.int32, (2 * count, count), 0)
    column = lax.broadcasted_iota(jnp.int32, (2 * count, count), 1)
    allowed = column <= jnp.where(row >= count, row - count, row)
    args = (q_ref, k_ref, v_ref, g_ref, kp_ref, vp_ref, tables, att_ref, gq_ref, *own, *before)
    lanes = [pl.ds(pair * LANES, LANES) for pair in range(pairs)]

    def block_of(with_prev):
        for start in range(0, pairs, 2):
            attend_rows(with_prev, lanes[start : start + 2], count, allowed, *args)

    pl.when(continued == 0)(lambda: block_of(False))
    pl.when(continued != 0)(lambda: block_of(True))
    turn = tuple(ref[:, pl.ds(offset, SHORT)] for ref in (tall_cos_ref, tall_sin_ref))
    for pair in lanes:
        gk_ref[:, pair] = unrotate_tall(own[0], pair, *turn)
        gv_ref[:, pair] = own[1][pair, :].astype(BF16).T

    @pl.when(block == 0)
    def _():
        base = tuple(ref[:, pl.ds(0, SHORT)] for ref in (tall_cos_ref, tall_sin_ref))
        for pair in lanes:
            halo_ref[0, :, pair] = unrotate_tall(before[0], pair, *base)
            halo_ref[1, :, pair] = before[1][pair, :].astype(BF16).T


def attend(meta, q, k, v, g, tables, tall, count):
    rows, head_width = q.shape
    blocks = rows // SHORT
    here = pl.BlockSpec((SHORT, head_width), lambda i, meta: (blocks - 1 - i, 0))
    after = pl.BlockSpec((SHORT, head_width), lambda i, meta: (blocks - i, 0))
    return pl.pallas_call(
        functools.partial(attend_kernel, blocks, head_width // LANES, count),
        grid_spec=pltpu.PrefetchScalarGridSpec(
            num_scalar_prefetch=1,
            grid=(blocks,),
            in_specs=[here, after, after, here, here, here] + [whole(table.shape) for table in (*tables, *tall)],
            out_specs=[here] * 4 + [held((2, SHORT, head_width))],
            scratch_shapes=[pltpu.VMEM((2, head_width, SHORT), F32)] * 2,
        ),
        out_shape=[shaped((rows, head_width), BF16)] * 4 + [shaped((2, SHORT, head_width), BF16)],
        compiler_params=params(),
        cost_estimate=BRIEF,
        name="attend",
    )(meta, q, k, v, g, k, v, *tables, *tall)


def settle_kernel(
    unit, tile, normed_ref, low_ref, grad_lows_ref, out_in_ref, att_ref, gq_ref, gk_ref, gv_ref, halo_ref, triple0_ref,
    triple1_ref, left_ref, output0_ref, output1_ref, right0_ref, right1_ref, output_left0_ref, output_left1_ref, out_ref,
    keep_ref, heads_ref, left_sums_ref, got_ref, send_ref, halo_got_ref, key_ref, value_ref, acc_ref, left_grad_ref,
    halo_sems, sems,
):
    step = pl.program_id(0)
    per_device = got_ref.shape[1] // tile
    steps = unit * per_device
    halo_start = steps - SHORT // tile
    place, base = place_in_unit(unit)
    half = base // unit
    peers = unit_peers(unit)
    y_peer = chip_neighbours(unit)[1]
    halo_copies = []
    for j in range(SHORT // tile):
        part = pl.ds(j * tile, tile)
        halo_copies.append(
            pltpu.make_async_remote_copy(
                src_ref=halo_ref.at[:, part], dst_ref=halo_got_ref.at[:, part], send_sem=halo_sems.at[0, j],
                recv_sem=halo_sems.at[1, j], device_id=y_peer, device_id_type=MESH,
            )
        )
    copies = [
        [
            pltpu.make_async_remote_copy(
                src_ref=send_ref.at[s, pl.ds(t * tile, tile)], dst_ref=got_ref.at[s, pl.ds(t * tile, tile)],
                send_sem=sems.at[0, s, t], recv_sem=sems.at[1, s, t], device_id=peer, device_id_type=MESH,
            )
            for t in range(per_device)
        ]
        for s, peer in enumerate(peers)
    ]
    @pl.when(step == 0)
    def _():
        meet([y_peer, *peers])

        @pl.when(half == 1)
        def _():
            for copy in halo_copies:
                copy.start()

        for ref in (acc_ref, left_grad_ref):
            ref[...] = jnp.zeros_like(ref)

    key_ref[...], value_ref[...] = gk_ref[...], gv_ref[...]
    for j, copy in enumerate(halo_copies):

        @pl.when((half == 0) & (step == halo_start + j))
        def _():
            copy.wait_recv()
            rows = pl.ds(j * tile, tile)
            count = output0_ref.shape[0]
            for ref, which in ((key_ref, 0), (value_ref, 1)):
                for here, there in ((pl.ds(0, count), pl.ds(count, count)), (pl.ds(count, count), pl.ds(0, count))):
                    ref[:, here] = (ref[:, here].astype(F32) + halo_got_ref[which, rows, there].astype(F32)).astype(BF16)

    normed = normed_ref[...]
    low = low_ref[...]
    grad_low_out = grad_lows_ref[:, :LANES]
    head_width = output0_ref.shape[0]
    att0, att1 = att_ref[:, :head_width], att_ref[:, head_width:]
    first = low_lanes()

    def mixed(shard):
        groups = []
        for start in range(shard * head_width, (shard + 1) * head_width, LANES):
            q, k, v = (ref[:, start : start + LANES] for ref in (gq_ref, key_ref, value_ref))
            groups += [jnp.where(first, q, k), jnp.where(first, v, q), jnp.where(first, k, v)]
        return jnp.concatenate(groups, axis=1)

    grad0, grad1 = mixed(0), mixed(1)
    grad_low = (dot_nt(grad0, right0_ref[...]) + dot_nt(grad1, right1_ref[...])).astype(BF16)
    grad = (
        dot_nt(grad0, triple0_ref[...]) + dot_nt(grad1, triple1_ref[...]) + dot_nt(grad_low, left_ref[...])
    ).astype(BF16)
    out_ref[...] = out_in_ref[...] + dot_nn(att0, output0_ref[...]) + dot_nn(att1, output1_ref[...])
    low_att = (dot_nn(att0, output_left0_ref[...]) + dot_nn(att1, output_left1_ref[...])).astype(BF16)
    width = grad.shape[1]

    @pl.when(step // per_device == place)
    def _():
        keep_ref[:, :width] = grad
        keep_ref[:, width:] = low_att

    span = pl.ds(pl.multiple_of(lax.rem(step, per_device) * tile, tile), tile)
    for s in range(unit - 1):
        owner = lax.rem(place + unit - (s + 1), unit)

        @pl.when(step // per_device == owner)
        def _():
            send_ref[s, span, :width] = grad
            send_ref[s, span, width:] = low_att

        for t in range(per_device):
            pl.when(step == owner * per_device + t)(copies[s][t].start)

    triple_width = grad0.shape[1]
    acc_ref[0, :, :triple_width] += dot_tn(low, grad0)
    acc_ref[1, :, :triple_width] += dot_tn(low, grad1)
    left_grad_ref[...] += dot_tn(grad_low, normed)
    acc_ref[0, :, triple_width:] += dot_tn(grad_low_out, att0)
    acc_ref[1, :, triple_width:] += dot_tn(grad_low_out, att1)

    @pl.when(step == steps - 1)
    def _():
        heads_ref[...] = acc_ref[...].astype(BF16)
        quarters(left_sums_ref, left_grad_ref[...])

        @pl.when(half == 1)
        def _():
            for copy in halo_copies:
                copy.wait_send()

        for group in copies:
            for copy in group:
                copy.wait()


def settle(unit, normed, low, grad_lows, out, heads, halo, triples, left, outputs, right, output_left, tile):
    rows, width = normed.shape
    own_rows = rows // unit
    head_width = outputs[0].shape[0]
    steps, per_device = rows // tile, own_rows // tile
    anywhere = pl.BlockSpec(memory_space=pl.ANY)

    def own(i):
        return lax.axis_index("mp")

    def far(i):
        return lax.rem(lax.axis_index("mp") + unit, 2 * unit)

    def kept(i):
        return (jnp.clip(i - place_in_unit(unit)[0] * per_device, 0, per_device - 1), 0)

    return pl.pallas_call(
        functools.partial(settle_kernel, unit, tile),
        grid=(steps,),
        in_specs=[rows_of(tile, width), rows_of(tile, LANES), rows_of(tile, 2 * LANES), rows_of(tile, width)]
        + [rows_of(tile, 2 * head_width)] * 4
        + [anywhere]
        + [whole(value.shape) for value in (*triples, left, *outputs)]
        + [
            pl.BlockSpec((LANES, 3 * head_width), lambda i: (0, own(i)), pipeline_mode=pl.Buffered(1)),
            pl.BlockSpec((LANES, 3 * head_width), lambda i: (0, far(i)), pipeline_mode=pl.Buffered(1)),
            pl.BlockSpec((head_width, LANES), lambda i: (own(i), 0), pipeline_mode=pl.Buffered(1)),
            pl.BlockSpec((head_width, LANES), lambda i: (far(i), 0), pipeline_mode=pl.Buffered(1)),
        ],
        out_specs=[
            rows_of(tile, width),
            pl.BlockSpec((tile, width + LANES), kept),
            held((2, LANES, 4 * head_width)),
            held((2, 2, LANES, width // 4)),
            anywhere,
        ],
        scratch_shapes=[
            pltpu.VMEM((unit - 1, own_rows, width + LANES), BF16),
            pltpu.VMEM((2, SHORT, 2 * head_width), BF16),
            pltpu.VMEM((tile, 2 * head_width), BF16),
            pltpu.VMEM((tile, 2 * head_width), BF16),
            pltpu.VMEM((2, LANES, 4 * head_width), F32),
            pltpu.VMEM((LANES, width), F32),
            pltpu.SemaphoreType.DMA((2, SHORT // tile)),
            pltpu.SemaphoreType.DMA((2, unit - 1, per_device)),
        ],
        out_shape=[
            shaped((rows, width), F32),
            shaped((own_rows, width + LANES), BF16),
            shaped((2, LANES, 4 * head_width), BF16),
            shaped((2, 2, LANES, width // 4), BF16),
            shaped((unit - 1, own_rows, width + LANES), BF16),
        ],
        compiler_params=pltpu.CompilerParams(
            dimension_semantics=("arbitrary",), vmem_limit_bytes=VMEM_LIMIT, collective_id=5, has_side_effects=True
        ),
        cost_estimate=BRIEF,
        name="settle",
    )(normed, low, grad_lows, out, *heads, halo, *triples, left, *outputs, right, right, output_left,
      output_left)


def sum_kernel(size, feed_ref, both_ref, heads_ref, left_ref, feed_out_ref, both_out_ref, heads_out_ref, left_out_ref,
               cross_sems, local_sems, *refs):
    net = Net()
    meet([net.x_peer, net.y_peer, net.core_peer, *net.z_peers])
    locals_, crossing = [], []

    def hand_over(slot, full, out, first, second):
        for place, at in ((0, first), (1, second)):
            target = out.at[net.core, at]
            local = pltpu.make_async_copy(full.at[place], target, local_sems.at[slot, place])
            local.start()
            locals_.append(local)
            crossing.append(net.copy(full.at[place], target, cross_sems, 2 * slot + place, net.core_peer))
            net.start(crossing[-1:])

    split = len(sum_scratch("xz", size))
    feed_refs = (refs[:split], refs[split : 2 * split])
    both_refs = refs[2 * split :]
    running = [sum_both(net, "xyz", both_ref, *both_refs[:3], both_refs[3:])]
    running += [
        sum_chunk(net, order, feed_ref.at[:, :, :, pl.ds(j * size, size)], feed_refs[j])
        for j, order in enumerate(("xz", "zx"))
    ]
    done = [
        lambda: hand_over(0, both_refs[3:][5], both_out_ref, net.half, net.other_half),
        lambda: hand_over(1, feed_refs[0][5], feed_out_ref.at[:, :, :, :, :, pl.ds(0, size)], net.other_half, net.half),
        lambda: hand_over(2, feed_refs[1][5], feed_out_ref.at[:, :, :, :, :, pl.ds(size, size)], net.other_half, net.half),
    ]
    first = True
    while running:
        kept = []
        for step, finish in zip(running, done):
            if next(step, "end") == "end":
                finish()
            else:
                kept.append((step, finish))
        running, done = [pair[0] for pair in kept], [pair[1] for pair in kept]
        if first:
            hand_over(3, heads_ref, heads_out_ref, net.half, net.other_half)
            hand_over(4, left_ref, left_out_ref, net.half, net.other_half)
            first = False
    for copy in locals_:
        copy.wait()
    for copy in crossing:
        copy.wait_recv()
    for copy in net.started:
        copy.wait_send()


def sum_all(feed, both, heads, left):
    arrays = (feed.reshape(SUM_ROWS + feed.shape[-1:]), both.reshape((2, 2) + SUM_ROWS + both.shape[-1:]), heads, left)
    size = feed.shape[-1] // 2
    outs = [shaped((2, 2) + SUM_ROWS + array.shape[-1:], BF16) for array in arrays]
    results = pl.pallas_call(
        functools.partial(sum_kernel, size),
        out_shape=outs,
        in_specs=[pl.BlockSpec(memory_space=pltpu.VMEM)] * 4,
        out_specs=[pl.BlockSpec(memory_space=pl.ANY)] * 4,
        scratch_shapes=[pltpu.SemaphoreType.DMA((2, 10)), pltpu.SemaphoreType.DMA((5, 2))]
        + sum_scratch("xz", size)
        + sum_scratch("zx", size)
        + both_scratch("xyz", both.shape[-1]),
        compiler_params=pltpu.CompilerParams(
            collective_id=2, has_side_effects=True, vmem_limit_bytes=VMEM_LIMIT
        ),
        cost_estimate=BRIEF,
        name="sum_all",
    )(*arrays)
    return [value.reshape(2, 2, LANES, value.shape[-1]) for value in results]


def unpack_kernel(triple_width, feed_ref, both_ref, heads_ref, left_ref, triple_ref, output_ref, up_ref, down_ref,
                  triple_left_ref, up_left_ref, output_right_ref, down_right_ref, norm_ref):
    triple_ref[...] = heads_ref[0, 0, :, :triple_width].astype(F32)
    output_ref[...] = heads_ref[0, 0, :, triple_width:].astype(F32).T
    hidden = up_ref.shape[1]
    up_ref[...] = feed_ref[0, 0, :, :hidden].astype(F32)
    down_ref[...] = feed_ref[0, 0, :, hidden:].astype(F32).T
    size = triple_left_ref.shape[0]
    triple_left_ref[...] = left_ref[0, 0].astype(F32).T
    up_left_ref[...] = both_ref[0, 0, :, :size].astype(F32).T
    output_right_ref[...] = both_ref[0, 0, :, size : 2 * size].astype(F32)
    down_right_ref[...] = both_ref[0, 0, :, 2 * size : 3 * size].astype(F32)
    norm_ref[0] = both_ref[0, 0, : norm_ref.shape[1], 3 * size :].astype(F32)


def unpack(feed, both, heads, left, triple_width):
    arrays = (feed, both, heads, left)
    hidden, quarter = feed.shape[-1] // 2, left.shape[-1]
    width, head_width = 4 * quarter, heads.shape[-1] - triple_width

    def tall(rows):
        return pl.BlockSpec((rows, LANES), lambda s: (s, 0))

    def wide(cols):
        return pl.BlockSpec((LANES, cols), lambda s: (0, s))

    return pl.pallas_call(
        functools.partial(unpack_kernel, triple_width),
        grid=(4,),
        in_specs=[
            pl.BlockSpec((1, 1) + value.shape[2:], lambda s: (lax.rem(s, 2), s // 2, 0, 0)) for value in arrays
        ],
        out_specs=[
            wide(triple_width), tall(head_width), wide(hidden), tall(hidden), tall(quarter), tall(quarter),
            wide(quarter), wide(quarter), pl.BlockSpec((1, width // LANES, LANES), lambda s: (s, 0, 0)),
        ],
        out_shape=[
            shaped((LANES, 4 * triple_width), F32),
            shaped((4 * head_width, LANES), F32),
            shaped((LANES, 4 * hidden), F32),
            shaped((4 * hidden, LANES), F32),
            shaped((width, LANES), F32),
            shaped((width, LANES), F32),
            shaped((LANES, width), F32),
            shaped((LANES, width), F32),
            shaped((4, width // LANES, LANES), F32),
        ],
        compiler_params=params(),
        cost_estimate=BRIEF,
        name="unpack",
    )(*arrays)


def shards(
    ranks,
    groups,
    block_input,
    sequence_lengths,
    first_gain,
    first_shift,
    second_gain,
    second_shift,
    triple_weight,
    triple_left,
    triple_right,
    output_weight,
    output_left,
    output_right,
    expand_weight,
    expand_left,
    expand_right,
    shrink_weight,
    shrink_left,
    shrink_right,
    cotangent,
):
    unit = ranks // 2
    own_rows, width = block_input.shape
    rows = own_rows * unit
    blocks = rows // SHORT
    tile = math.gcd(own_rows, 256)
    triple_width = triple_weight.shape[1]
    head_width = output_weight.shape[0]
    hidden = expand_weight.shape[1]
    mp = lax.axis_index("mp")
    half = mp // unit
    place = lax.rem(mp, unit)
    far = lax.rem(mp + unit, ranks)
    swap = [(m, (m + unit) % ranks) for m in range(ranks)]

    tables = rotary_tables()
    dp = lax.axis_index("dp")
    lead = lax.rem(dp, 2)
    beside = [[(d, d ^ bit) for d in range(groups)] for bit in (1, 2)]
    continues = find_flags(sequence_lengths[0])
    conts = lax.dynamic_slice_in_dim(continues, half * blocks, blocks, 0)
    meta = jnp.concatenate([jnp.stack([mp, far, lead, place]).astype(jnp.int32), conts])
    gain1, shift1 = first_gain[None, :], first_shift[None, :]
    gain2, shift2 = second_gain[None, :], second_shift[None, :]

    (normed1, normed2, dy, low2, grad_lows, out, grad2, low_act, grad_low2, feed_sums, triple_far,
     output_far, x_halo, expand_half, shrink_half) = feed_first(
        unit, block_input, cotangent, (gain1, shift1, gain2, shift2), expand_weight, expand_left, expand_right,
        shrink_weight, shrink_left, output_right, shrink_right, triple_weight, output_weight, tile,
    )
    expand_piece = lax.ppermute(expand_half, "mp", swap)
    shrink_piece = lax.ppermute(shrink_half, "mp", swap)
    low1, q, k, v, g = project(
        meta, x_halo, normed1, dy, grad_lows, gain1, shift1, (triple_weight, triple_far), triple_left, triple_right,
        (output_weight, output_far), output_left, tables, tile,
    )
    expand_piece, q = lax.optimization_barrier((expand_piece, q))
    expand_other = lax.ppermute(expand_piece, "dp", beside[0])
    att, gq, gk, gv, halo = attend(meta, q, k, v, g, tables, tall_tables(), 256)
    shrink_piece, att = lax.optimization_barrier((shrink_piece, att))
    shrink_other = lax.ppermute(shrink_piece, "dp", beside[1])
    out, keep1, heads, left, got1 = settle(
        unit, normed1, low1, grad_lows, out, (att, gq, gk, gv), halo, (triple_weight, triple_far), triple_left,
        (output_weight, output_far), triple_right, output_left, tile,
    )
    hosted = ranks == 4 and groups == 8
    block_output, input_gradient, feed_sums, both, heads_sum, left_sum = feed_second(
        unit, normed2, low2, dy, grad_lows, out, grad2, low_act, grad_low2, block_input, keep1, got1, (gain1, gain2),
        output_right, shrink_right, (expand_piece, expand_other), expand_left, expand_right,
        (shrink_piece, shrink_other), shrink_left, feed_sums, heads, left, hosted, tile,
    )
    if hosted:
        (triple_right_sum, output_left_sum, expand_right_sum, shrink_left_sum, triple_left_sum, expand_left_sum,
         output_right_sum, shrink_right_sum, norms) = unpack(
            *sum_all(feed_sums, both, heads_sum, left_sum), triple_width
        )
        norms = norms.reshape(4, width)
    else:

        def spread(*placed):
            size = placed[0][0].shape[1]
            wide = jnp.zeros((LANES, size * ranks), BF16)
            for value, shard in placed:
                wide = lax.dynamic_update_slice_in_dim(wide, value, shard * size, 1)
            return wide

        def joined(value):
            return value.transpose(2, 1, 0, 3).reshape(LANES, -1)

        def columns(value, start, size):
            return value.reshape(LANES, ranks, -1)[:, :, start : start + size].reshape(LANES, -1).astype(F32)

        heads, feed, left, both = lax.psum(
            (spread((heads[0], mp), (heads[1], far)), spread((feed_sums, far)), left, both), ("dp", "mp")
        )
        triple_right_sum = columns(heads, 0, triple_width)
        output_left_sum = columns(heads, triple_width, head_width).T
        expand_right_sum = columns(feed, 0, hidden)
        shrink_left_sum = columns(feed, hidden, hidden).T
        triple_left_sum = joined(left).astype(F32).T
        quarter = width // 4
        expand_left_sum = joined(both[..., :quarter]).astype(F32).T
        output_right_sum = joined(both[..., quarter : 2 * quarter]).astype(F32)
        shrink_right_sum = joined(both[..., 2 * quarter : 3 * quarter]).astype(F32)
        norms = both[:, :, : width // LANES, 3 * quarter :].transpose(1, 0, 2, 3).reshape(4, width).astype(F32)
    return (
        block_output,
        input_gradient,
        norms[0],
        norms[1],
        norms[2],
        norms[3],
        triple_left_sum,
        triple_right_sum,
        output_left_sum,
        output_right_sum,
        expand_left_sum,
        expand_right_sum,
        shrink_left_sum,
        shrink_right_sum,
    )


def solution(mesh):
    placed = (
        P(("dp", "mp"), None),
        P("dp", None),
        P(),
        P(),
        P(),
        P(),
        P(None, "mp"),
        P(),
        P(),
        P("mp", None),
        P(),
        P(),
        P(None, "mp"),
        P(),
        P(),
        P("mp", None),
        P(),
        P(),
        P(("dp", "mp"), None),
    )
    return jax.shard_map(
        functools.partial(shards, mesh.shape["mp"], mesh.shape["dp"]),
        mesh=mesh,
        in_specs=placed,
        out_specs=(P(("dp", "mp"), None), P(("dp", "mp"), None)) + (P(),) * 12,
        check_vma=False,
    )
```

```python
import functools
import math

import jax
import jax.numpy as jnp
import numpy as np
from jax import lax
from jax.experimental import pallas as pl
from jax.experimental.pallas import tpu as pltpu
from jax.sharding import PartitionSpec as P

HEAD_DIM = 64
ROT = 16
SHORT = 512
TOK_GRP = 3072
SLOTS = 6
EPS = 1e-05
LANES = 128
MESH = pl.DeviceIdType.MESH
BF16 = jnp.bfloat16
F32 = jnp.float32
VMEM_LIMIT = 56 * 1024 * 1024
BRIEF = pl.CostEstimate(flops=1, bytes_accessed=1, transcendentals=0)


def dot_nn(former, latter):
    return lax.dot_general(
        former, latter, (((1,), (0,)), ((), ())), preferred_element_type=F32
    )


def dot_nt(former, latter):
    return lax.dot_general(
        former, latter, (((1,), (1,)), ((), ())), preferred_element_type=F32
    )


def dot_tn(former, latter):
    return lax.dot_general(
        former, latter, (((0,), (0,)), ((), ())), preferred_element_type=F32
    )


def find_flags(group_lengths):
    seq_ends = jnp.cumsum(group_lengths, dtype=jnp.int32)
    starts = seq_ends - group_lengths
    block_starts = jnp.arange(SLOTS, dtype=jnp.int32) * SHORT
    begins = jnp.any(
        (starts[None, :] == block_starts[:, None]) & (group_lengths[None, :] > 0), axis=1
    )
    return jnp.where(begins, 0, 1).astype(jnp.int32)


def rotary_tables():
    half = ROT // 2
    frequency = np.exp(
        np.arange(half, dtype=np.float32) * np.float32(-2.0 * math.log(10000.0) / ROT)
    ).astype(np.float32)
    angles = np.arange(2 * SHORT, dtype=np.float32)[:, None] * frequency[None, :]
    cosine = np.ones((2 * SHORT, LANES), np.float32)
    minus = np.zeros((2 * SHORT, LANES), np.float32)
    plus = np.zeros((2 * SHORT, LANES), np.float32)
    for base in range(0, LANES, HEAD_DIM):
        cosine[:, base : base + half] = np.cos(angles)
        cosine[:, base + half : base + ROT] = np.cos(angles)
        minus[:, base : base + half] = -np.sin(angles)
        plus[:, base + half : base + ROT] = np.sin(angles)
    return jnp.asarray(cosine), jnp.asarray(minus), jnp.asarray(plus)


def tall_tables():
    half = ROT // 2
    frequency = np.exp(
        np.arange(half, dtype=np.float32) * np.float32(-2.0 * math.log(10000.0) / ROT)
    ).astype(np.float32)
    angles = frequency[:, None] * np.arange(2 * SHORT, dtype=np.float32)[None, :]
    return jnp.asarray(np.cos(angles)), jnp.asarray(np.sin(angles))


def low_lanes():
    return lax.broadcasted_iota(jnp.int32, (1, LANES), 1) < HEAD_DIM


def rotate(pair, cosine, minus, plus):
    half = ROT // 2
    return (
        pair * cosine
        + pltpu.roll(pair, LANES - half, 1) * minus
        + pltpu.roll(pair, half, 1) * plus
    )


def unrotate(pair, cosine, minus, plus):
    half = ROT // 2
    return (
        pair * cosine
        - pltpu.roll(pair, LANES - half, 1) * minus
        - pltpu.roll(pair, half, 1) * plus
    )


def normalize(values, gain, shift):
    center = values - jnp.mean(values, axis=-1, keepdims=True)
    spread = jnp.mean(center * center, axis=-1, keepdims=True)
    return center * lax.rsqrt(spread + EPS) * gain + shift


def whole(shape):
    return pl.BlockSpec(
        shape, lambda *idx: (0,) * len(shape), pipeline_mode=pl.Buffered(1)
    )


def held(shape):
    return pl.BlockSpec(shape, lambda *idx: (0,) * len(shape))


def rows_of(tile, width):
    return pl.BlockSpec((tile, width), lambda i, *refs: (i, 0))


def shaped(shape, dtype):
    return jax.ShapeDtypeStruct(shape, dtype)


def params(semantics=1):
    return pltpu.CompilerParams(
        dimension_semantics=("arbitrary",) * semantics, vmem_limit_bytes=VMEM_LIMIT
    )


SUM_ROWS = (2, 4, 16)


class Net:
    def __init__(self):
        dp, mp = lax.axis_index("dp"), lax.axis_index("mp")
        self.half, self.core = mp // 2, lax.rem(mp, 2)
        self.x, self.z = lax.rem(dp, 2), dp // 2
        self.other_half, self.other_core, self.other_x = 1 - self.half, 1 - self.core, 1 - self.x
        self.x_peer = (dp + 1 - 2 * self.x, mp)
        self.y_peer = (dp, mp + 2 - 4 * self.half)
        self.core_peer = (dp, mp + 1 - 2 * self.core)
        self.z_places = [lax.rem(self.z + j, 4) for j in range(1, 4)]
        self.z_peers = [(place * 2 + self.x, mp) for place in self.z_places]
        self.started = []

    def copy(self, src, dst, sems, slot, peer):
        return pltpu.make_async_remote_copy(
            src_ref=src, dst_ref=dst, send_sem=sems.at[0, slot], recv_sem=sems.at[1, slot], device_id=peer,
            device_id_type=MESH,
        )

    def start(self, copies):
        for copy in copies:
            copy.start()
        self.started += copies


def arrive(copies):
    for copy in copies:
        copy.wait_recv()


def added(first, *others):
    total = first.astype(F32)
    for other in others:
        total = total + other.astype(F32)
    return total.astype(BF16)


def sum_scratch(order, size):
    one = (16, size)
    first = {"yxz": ((2, 4), (2, 4)), "xyz": ((2, 4), (2, 4)), "xz": ((4,), (4,)), "zx": ((3, 2), (2,))}[order]
    second = {"yxz": ((4,), (4,)), "xyz": ((4,), (4,)), "xz": ((3,), (1,)), "zx": ((1,), (1,))}[order]
    return [pltpu.VMEM(shape + one, BF16) for shape in (*first, *second, (3,), (2, 2, 4))] + [
        pltpu.SemaphoreType.DMA((2, 12))
    ]


def sum_chunk(net, order, source, scratch):
    got1, work1, got2, work2, got3, full, sems = scratch
    x, z, other_x = net.x, net.z, net.other_x
    own, rows, plane = full.at[0, x, z], full.at[0, x], full.at[0, :, z]

    def to_z(src, dst, slot):
        return [
            net.copy(src(place), dst(j), sems, slot + j, peer)
            for j, (place, peer) in enumerate(zip(net.z_places, net.z_peers))
        ]

    def one(src, dst, slot, peer):
        return [net.copy(src, dst, sems, slot, peer)]

    last = work1 if order == "xz" else work2
    if order != "xyz":
        over_y = one(full.at[0], full.at[1], 9, net.y_peer)
    if order == "zx":
        spread = to_z(lambda place: source.at[:, place], lambda j: got1.at[j], 2)
        cross = one(work1.at[other_x], got2.at[0], 0, net.x_peer)
        back = one(own, own, 8, net.x_peer)
        gather = to_z(lambda place: plane, lambda j: plane, 5)
    else:
        spread = to_z(lambda place: last.at[place], lambda j: got3.at[j], 2)
        gather = to_z(lambda place: own, lambda j: own, 5)
        if order == "yxz":
            first = one(source.at[1], got1, 0, net.y_peer)
            second = one(work1.at[other_x], got2, 1, net.x_peer)
        elif order == "xyz":
            first = one(source.at[:, other_x], got1, 0, net.x_peer)
            second = one(work1.at[1], got2, 1, net.y_peer)
            over_y = one(rows, full.at[1, x], 8, net.y_peer)
            over_x = one(full.at[:, x], full.at[:, x], 9, net.x_peer)
        else:
            first = one(source.at[other_x], got1, 0, net.x_peer)
        if order != "xyz":
            over_x = one(rows, rows, 8, net.x_peer)

    def begin(copies):
        return lambda: net.start(copies)

    def after(copies, work, then):
        def stage():
            arrive(copies)
            if work is not None:
                target, value = work
                target[...] = value()
            if then is not None:
                net.start(then)

        return stage

    if order == "zx":
        mine = (work1, lambda: added(source[:, z], got1[0], got1[1], got1[2]))
        total = (own, lambda: added(work1[x], got2[0]))
        return [
            begin(spread), after(spread, mine, cross), after(cross, total, back), after(back, None, gather),
            after(gather, None, over_y), after(over_y, None, None),
        ]
    total = (own, lambda: added(last[z], got3[0], got3[1], got3[2]))
    if order == "yxz":
        head = [begin(first), after(first, (work1, lambda: added(source[0], got1[...])), second)]
        head.append(after(second, (work2, lambda: added(work1[x], got2[...])), spread))
    elif order == "xyz":
        head = [begin(first), after(first, (work1, lambda: added(source[:, x], got1[...])), second)]
        head.append(after(second, (work2, lambda: added(work1[0], got2[...])), spread))
    else:
        head = [begin(first), after(first, (work1, lambda: added(source[x], got1[...])), spread)]
    one_way, other_way = (over_y, over_x) if order == "xyz" else (over_x, over_y)
    return head + [
        after(spread, total, gather), after(gather, None, one_way), after(one_way, None, other_way),
        after(other_way, None, None),
    ]


def sum_both(net, parts, both, got, total, core_sems, scratches):
    exchange = [net.copy(both.at[net.other_core], got, core_sems, 0, net.core_peer)]
    chunks, start = [], 0
    for (order, size), scratch in zip(parts, scratches):
        chunks.append(sum_chunk(net, order, total.at[:, :, :, :, pl.ds(start, size)], scratch))
        start += size

    def combine():
        arrive(exchange)
        for place, at in ((0, net.half), (1, net.other_half)):
            total[place] = added(both[net.core, at], got[at])
        for chunk in chunks:
            chunk[0]()

    def together(k):
        def stage():
            for chunk in chunks:
                if k < len(chunk):
                    chunk[k]()

        return stage

    longest = max(len(chunk) for chunk in chunks)
    return [lambda: net.start(exchange), combine] + [together(k) for k in range(1, longest)]


def both_scratch(parts):
    size = sum(part[1] for part in parts)
    return [
        pltpu.VMEM((2,) + SUM_ROWS + (size,), BF16),
        pltpu.VMEM((2,) + SUM_ROWS + (size,), BF16),
        pltpu.SemaphoreType.DMA((2, 1)),
    ] + [shape for part in parts for shape in sum_scratch(*part)]


def split_columns(size):
    count = (size // 2 + LANES - 1) // LANES * LANES
    return (("yxz", count), ("xyz", size - count))


def quarters(ref, *arrays):
    start = 0
    for array in arrays:
        size = array.shape[1] // 4
        for q in range(4):
            ref[q % 2, q // 2, :, start : start + size] = array[:, q * size : (q + 1) * size].astype(BF16)
        start += size


def gelu_parts(hidden):
    cdf = 0.5 + 0.5 * lax.erf(hidden * math.sqrt(0.5))
    density = jnp.exp(-0.5 * hidden * hidden) * (1.0 / math.sqrt(2.0 * math.pi))
    return hidden * cdf, cdf + hidden * density


def feed_core(rows, grads, up_ref, down_ref, act_ref, grad_ref, hidden_step):
    for start in range(0, up_ref.shape[1], hidden_step):
        cols = pl.ds(start, hidden_step)
        hidden = dot_nn(rows, up_ref[:, cols])
        grad_act = dot_nt(grads, down_ref[cols, :])
        activated, slope = gelu_parts(hidden)
        act_ref[:, cols] = activated.astype(BF16)
        grad_ref[:, cols] = (grad_act * slope).astype(BF16)


def shard_index(unit, far):
    return lax.rem(lax.axis_index("mp") + (unit if far else 0), 2 * unit)


def columns_of(ref, size, shard):
    return ref.at[:, pl.ds(pl.multiple_of(shard * size, size), size)]


def rows_at(ref, size, shard):
    return ref.at[pl.ds(pl.multiple_of(shard * size, size), size)]


def load(step, sems, pairs):
    copies = [pltpu.make_async_copy(src, dst, sems.at[j]) for j, (src, dst) in enumerate(pairs)]

    @pl.when(step == 0)
    def _():
        for copy in copies:
            copy.start()
        for copy in copies:
            copy.wait()


def head_weights(unit, triples, right, outputs, output_left, triple_ref, output_ref):
    width = triples[0].shape[0]
    head_width = outputs[0].shape[0]
    size = 3 * head_width
    pairs = []
    for j in range(2):
        shard = shard_index(unit, j == 1)
        cols, rows = pl.ds(j * size, size), pl.ds(j * head_width, head_width)
        pairs += [
            (triples[j], triple_ref.at[pl.ds(0, width), cols]),
            (columns_of(right, size, shard), triple_ref.at[pl.ds(width, LANES), cols]),
            (outputs[j], output_ref.at[rows, pl.ds(0, width)]),
            (rows_at(output_left, head_width, shard), output_ref.at[rows, pl.ds(width, LANES)]),
        ]
    return pairs


def chip_neighbours(unit):
    dp = lax.axis_index("dp")
    mp = lax.axis_index("mp")
    lead = lax.rem(dp, 2)
    return lead, (dp, lax.rem(mp + unit, 2 * unit)), (dp + 1 - 2 * lead, mp)


def leads():
    dp = lax.axis_index("dp")
    return lax.rem(dp, 2), lax.rem(dp // 2, 2)


def courier(unit, pairs, chunks, y_sems, x_sems):
    lead, y_peer, x_peer = chip_neighbours(unit)
    over_y, over_x = [], []
    for k in range(chunks):
        for j, (own, far) in enumerate(pairs):
            count = own.shape[0] // 2 // chunks
            span = pl.ds(pl.multiple_of((lead * chunks + k) * count, count), count)
            for src, sems, peer, group in ((own, y_sems, y_peer, over_y), (far, x_sems, x_peer, over_x)):
                group.append(
                    pltpu.make_async_remote_copy(
                        src_ref=src.at[span],
                        dst_ref=far.at[span],
                        send_sem=sems.at[0, k, j],
                        recv_sem=sems.at[1, k, j],
                        device_id=peer,
                        device_id_type=MESH,
                    )
                )
    return over_y, over_x


def meet(peers):
    barrier = pltpu.get_barrier_semaphore()
    for peer in peers:
        pl.semaphore_signal(barrier, inc=1, device_id=peer, device_id_type=MESH)
    pl.semaphore_wait(barrier, len(peers))


def place_in_unit(unit):
    mp = lax.axis_index("mp")
    return lax.rem(mp, unit), mp - lax.rem(mp, unit)


def unit_peers(unit):
    place, base = place_in_unit(unit)
    return [(lax.axis_index("dp"), base + lax.rem(place + unit - s, unit)) for s in range(1, unit)]


def halo_copies(unit, x_ref, halo_ref, y_sems, unit_sems):
    own_rows = x_ref.shape[0]
    chunk = math.gcd(own_rows, 128)
    dp = lax.axis_index("dp")
    found = []
    for k in range(SHORT // chunk):
        row = unit * own_rows - SHORT + k * chunk
        holder, start = row // own_rows, row % own_rows
        target = halo_ref.at[pl.ds(k * chunk, chunk)]
        over_y = pltpu.make_async_remote_copy(
            src_ref=x_ref.at[pl.ds(start, chunk)], dst_ref=target, send_sem=y_sems.at[0, k], recv_sem=y_sems.at[1, k],
            device_id=(dp, unit + holder), device_id_type=MESH,
        )
        spread = [
            pltpu.make_async_remote_copy(
                src_ref=target, dst_ref=target, send_sem=unit_sems.at[0, k, s - 1], recv_sem=unit_sems.at[1, k, s - 1],
                device_id=(dp, unit + (holder + s) % unit), device_id_type=MESH,
            )
            for s in range(1, unit)
        ]
        found.append((holder, over_y, spread))
    return found


def feed_first_kernel(
    unit, tile, x_ref, dy_ref, gain1_ref, shift1_ref, gain2_ref, shift2_ref, up_own_ref, up_left_ref, up_right_ref,
    down_own_ref, down_left_ref, output_right_ref, down_right_ref, x_all_ref, dy_all_ref, triple_ref, output_ref, normed1_ref,
    normed_ref, dy_full_ref, low_ref, grad_lows_ref, out_ref, grad_ref, low_act_ref, grad_low_ref, sums_ref,
    triple_far_ref, output_far_ref, halo_ref, up_half_ref, down_half_ref, act_ref, gh_ref, up_ref, down_ref, acc_ref,
    xs_ref, x_got_ref, dy_got_ref, y_sems, x_sems, unit_sems, halo_y_sems, halo_unit_sems, local_sems, load_sems,
):
    step = pl.program_id(0)
    width, hidden = up_own_ref.shape
    weights = (
        (up_own_ref, up_ref.at[pl.ds(0, width)]),
        (columns_of(up_right_ref, hidden, shard_index(unit, False)), up_ref.at[pl.ds(width, LANES)]),
        (down_own_ref, down_ref.at[:, pl.ds(0, width)]),
        (rows_at(down_left_ref, hidden, shard_index(unit, False)), down_ref.at[:, pl.ds(width, LANES)]),
    )
    own_rows = x_all_ref.shape[0]
    per_device = own_rows // tile
    steps = unit * per_device
    chunks = y_sems.shape[1]
    place, base = place_in_unit(unit)
    half = base // unit
    peers = unit_peers(unit)
    over_y, over_x = courier(
        unit, ((triple_ref, triple_far_ref), (output_ref, output_far_ref)), chunks, y_sems, x_sems
    )
    halo = halo_copies(unit, x_all_ref, halo_ref, halo_y_sems, halo_unit_sems)
    rows_out = [
        pltpu.make_async_remote_copy(
            src_ref=src, dst_ref=dst.at[j], send_sem=unit_sems.at[0, which, j], recv_sem=unit_sems.at[1, which, j],
            device_id=peer, device_id_type=MESH,
        )
        for j, peer in enumerate(peers)
        for which, (src, dst) in enumerate(((x_all_ref, x_got_ref), (dy_all_ref, dy_got_ref)))
    ]
    kept_halves = [
        pltpu.make_async_copy(
            src.at[
                pl.ds(pl.multiple_of(lead * dst.shape[0], dst.shape[0]), dst.shape[0]), pl.ds(0, dst.shape[1])
            ],
            dst,
            local_sems.at[j],
        )
        for j, (lead, src, dst) in enumerate(zip(leads(), (up_ref, down_ref), (up_half_ref, down_half_ref)))
    ]

    @pl.when(step == 0)
    def _():
        meet([*chip_neighbours(unit)[1:], *peers])
        for copy in rows_out + over_y:
            copy.start()

    for holder, copy, _ in halo:
        pl.when((step == 0) & (half == 0) & (place == holder))(copy.start)
    load(step, load_sems, weights)

    @pl.when(step == 0)
    def _():
        for copy in kept_halves:
            copy.start()
        xs_ref[...] = x_ref[...]
        dy_full_ref[...] = dy_ref[...]

    @pl.when((step > 0) & (step < per_device))
    def _():
        xs_ref[...] = x_ref[...]
        dy_full_ref[...] = dy_ref[...]

    for slot in range(unit - 1):

        @pl.when(step == per_device * (slot + 1))
        def _():
            for which in range(2):
                rows_out[2 * slot + which].wait_recv()

        @pl.when((step >= per_device * (slot + 1)) & (step < per_device * (slot + 2)))
        def _():
            span = pl.ds(pl.multiple_of((step - per_device * (slot + 1)) * tile, tile), tile)
            xs_ref[...] = x_got_ref[slot, span]
            dy_full_ref[...] = dy_got_ref[slot, span]

    for k in range(chunks):

        @pl.when(step == min(k + 1, steps - 1))
        def _():
            for j in (2 * k, 2 * k + 1):
                over_y[j].wait_recv()
                over_x[j].start()

    x = xs_ref[...].astype(F32)
    center = x - jnp.mean(x, axis=-1, keepdims=True)
    spread = jnp.mean(center * center, axis=-1, keepdims=True)
    scaled = center * lax.rsqrt(spread + EPS)
    normed1_ref[...] = (scaled * gain1_ref[...] + shift1_ref[...]).astype(BF16)
    normed = (scaled * gain2_ref[...] + shift2_ref[...]).astype(BF16)
    normed_ref[...] = normed
    dy = dy_full_ref[...]
    low = dot_nn(normed, up_left_ref[...]).astype(BF16)
    low_ref[...] = low
    rights = jnp.concatenate([output_right_ref[...], down_right_ref[...]], axis=0)
    grad_lows = dot_nt(dy, rights).astype(BF16)
    grad_lows_ref[...] = grad_lows
    grad_low = grad_lows[:, LANES:]
    feed_core(
        jnp.concatenate([normed, low], axis=1), jnp.concatenate([dy, grad_low], axis=1), up_ref, down_ref, act_ref,
        gh_ref, 512,
    )
    act = act_ref[...]
    gh = gh_ref[...]
    forward = dot_nn(act, down_ref[...])
    backward = dot_nt(gh, up_ref[...])
    out_ref[...], low_act_ref[...] = forward[:, :width], forward[:, width:]
    grad_ref[...], grad_low_ref[...] = backward[:, :width], backward[:, width:]

    @pl.when(step == 0)
    def _():
        acc_ref[...] = jnp.zeros_like(acc_ref)

    acc_ref[:, :hidden] += dot_tn(low, gh)
    acc_ref[:, hidden:] += dot_tn(grad_low, act)

    @pl.when((step == 0) & (half == 0))
    def _():
        fills = [
            pltpu.make_async_copy(xs_ref, halo_ref.at[pl.ds(k * tile, tile)], local_sems.at[2 + k])
            for k in range(SHORT // tile)
        ]
        for copy in fills:
            copy.start()
        for copy in fills:
            copy.wait()

    @pl.when(step == steps - 1)
    def _():
        sums_ref[...] = acc_ref[...].astype(BF16)
        for holder, copy, spread_copies in halo:

            @pl.when((half == 1) & (place == holder))
            def _():
                copy.wait_recv()
                for other in spread_copies:
                    other.start()

        for holder, copy, spread_copies in halo:
            pl.when((half == 0) & (place == holder))(copy.wait_send)

            @pl.when((half == 1) & (place == holder))
            def _():
                for other in spread_copies:
                    other.wait_send()

            for s in range(1, unit):
                pl.when((half == 1) & (place == (holder + s) % unit))(spread_copies[s - 1].wait_recv)
        for copy in rows_out + over_y:
            copy.wait_send()
        for copy in over_x + kept_halves:
            copy.wait()


def feed_first(unit, x, dy, norms, up, up_left, up_right, down, down_left, output_right, down_right, triple, output,
               tile):
    own_rows, width = x.shape
    rows = own_rows * unit
    hidden = up.shape[1]
    steps, per_device = rows // tile, own_rows // tile
    chunks = math.gcd(4, output.shape[0] // 32)
    halo_chunks = SHORT // math.gcd(own_rows, 128)
    anywhere = pl.BlockSpec(memory_space=pl.ANY)
    here = pl.BlockSpec((tile, width), lambda i: (jnp.minimum(i, per_device - 1), 0))

    def turned(size):
        def index(i):
            return (lax.rem(i + place_in_unit(unit)[0] * per_device, steps), 0)

        return pl.BlockSpec((tile, size), index)

    return pl.pallas_call(
        functools.partial(feed_first_kernel, unit, tile),
        grid=(steps,),
        in_specs=[here, here]
        + [whole((1, width))] * 4
        + [
            anywhere,
            whole(up_left.shape),
            anywhere,
            anywhere,
            anywhere,
            whole(output_right.shape),
            whole(down_right.shape),
        ]
        + [anywhere] * 4,
        out_specs=[
            turned(width),
            turned(width),
            turned(width),
            turned(LANES),
            turned(2 * LANES),
            turned(width),
            turned(width),
            turned(LANES),
            turned(LANES),
            held((LANES, 2 * hidden)),
        ]
        + [anywhere] * 5,
        scratch_shapes=[
            pltpu.VMEM((tile, hidden), BF16),
            pltpu.VMEM((tile, hidden), BF16),
            pltpu.VMEM((width + LANES, hidden), BF16),
            pltpu.VMEM((hidden, width + LANES), BF16),
            pltpu.VMEM((LANES, 2 * hidden), F32),
            pltpu.VMEM((tile, width), BF16),
            pltpu.VMEM((unit - 1, own_rows, width), BF16),
            pltpu.VMEM((unit - 1, own_rows, width), BF16),
            pltpu.SemaphoreType.DMA((2, chunks, 2)),
            pltpu.SemaphoreType.DMA((2, chunks, 2)),
            pltpu.SemaphoreType.DMA((2, 2, unit - 1)),
            pltpu.SemaphoreType.DMA((2, halo_chunks)),
            pltpu.SemaphoreType.DMA((2, halo_chunks, unit - 1)),
            pltpu.SemaphoreType.DMA((2 + SHORT // tile,)),
            pltpu.SemaphoreType.DMA((4,)),
        ],
        out_shape=[
            shaped((rows, width), BF16),
            shaped((rows, width), BF16),
            shaped((rows, width), BF16),
            shaped((rows, LANES), BF16),
            shaped((rows, 2 * LANES), BF16),
            shaped((rows, width), F32),
            shaped((rows, width), F32),
            shaped((rows, LANES), F32),
            shaped((rows, LANES), F32),
            shaped((LANES, 2 * hidden), BF16),
            shaped(triple.shape, BF16),
            shaped(output.shape, BF16),
            shaped((SHORT, width), BF16),
            shaped((up.shape[0] // 2, up.shape[1]), BF16),
            shaped((down.shape[0] // 2, down.shape[1]), BF16),
        ],
        compiler_params=pltpu.CompilerParams(
            dimension_semantics=("arbitrary",), vmem_limit_bytes=VMEM_LIMIT, collective_id=3, has_side_effects=True
        ),
        cost_estimate=BRIEF,
        name="feed_first",
    )(x, dy, *norms, up, up_left, up_right, down, down_left, output_right, down_right, x, dy, triple, output)


def feed_second_kernel(
    unit, tile, normed_ref, low_ref, dy_ref, grad_lows_ref, out_in_ref, grad_in_ref, low_act_in_ref, grad_low_in_ref,
    x_ref, keep_ref, got1_ref, gain1_ref, gain2_ref, output_right_ref, down_right_ref, up0_ref, up1_ref, up_left_ref,
    up_right_ref, down0_ref, down1_ref, down_left_ref, early_ref, heads_ref, left_ref, y_ref, dx_ref, sums_ref, both_ref,
    heads_out_ref, left_out_ref, act_ref, gh_ref, up_ref, down_ref, send_ref, got_ref, early_got_ref, acc_ref, norms_ref,
    output_right_grad_ref, down_right_grad_ref, up_left_grad_ref, sems, early_sems, out_sems, load_sems, *sum_refs,
):
    step = pl.program_id(0)
    own_rows = got_ref.shape[1]
    per_device = own_rows // tile
    send_tiles = (unit - 1) * per_device
    width, hidden = up_ref.shape[0] - LANES, up_ref.shape[1]
    shard = shard_index(unit, True)
    weights = [
        (columns_of(up_right_ref, hidden, shard), up_ref.at[pl.ds(width, LANES)]),
        (rows_at(down_left_ref, hidden, shard), down_ref.at[:, pl.ds(width, LANES)]),
    ]
    for lead, pieces, ref in zip(leads(), ((up0_ref, up1_ref), (down0_ref, down1_ref)), (up_ref, down_ref)):
        for place, piece in zip((lead, 1 - lead), pieces):
            weights.append((piece, rows_at(ref, piece.shape[0], place).at[:, pl.ds(0, piece.shape[1])]))
    peers = unit_peers(unit)
    copies = [
        [
            pltpu.make_async_remote_copy(
                src_ref=send_ref.at[s, pl.ds(t * tile, tile)], dst_ref=got_ref.at[s, pl.ds(t * tile, tile)],
                send_sem=sems.at[0, s, t], recv_sem=sems.at[1, s, t], device_id=peer, device_id_type=MESH,
            )
            for t in range(per_device)
        ]
        for s, peer in enumerate(peers)
    ]

    steps = unit * per_device
    y_peer = chip_neighbours(unit)[1]
    pieces = early_sems.shape[1]
    count = early_ref.shape[0] // pieces
    early_copies = [
        pltpu.make_async_remote_copy(
            src_ref=early_ref.at[pl.ds(j * count, count)], dst_ref=early_got_ref.at[pl.ds(j * count, count)],
            send_sem=early_sems.at[0, j], recv_sem=early_sems.at[1, j], device_id=y_peer, device_id_type=MESH,
        )
        for j in range(pieces)
    ]
    hosted = len(sum_refs) > 0
    if hosted:
        net = Net()
        size = heads_ref.shape[-1] // 2
        split = len(sum_scratch("yxz", size))
        heads_refs = (sum_refs[:split], sum_refs[split : 2 * split])
        left_refs = sum_refs[2 * split :]
        stages = [
            sum_chunk(net, order, heads_ref.at[:, :, :, :, pl.ds(j * size, size)], heads_refs[j])
            for j, order in enumerate(("yxz", "xyz"))
        ]
        stages.append(sum_both(net, (("yxz", left_ref.shape[-1]),), left_ref, *left_refs[:3], (left_refs[3:],)))

    def advance():
        if hosted:
            for at in range(steps):

                @pl.when(step == at)
                def _():
                    for stage in stages:
                        stage[at]()

    @pl.when(step == 0)
    def _():
        meet([*peers, y_peer] + ([net.x_peer, *net.z_peers] if hosted else []))
        for ref in (norms_ref, output_right_grad_ref, down_right_grad_ref, acc_ref, up_left_grad_ref):
            ref[...] = jnp.zeros_like(ref)

    advance()
    for j, copy in enumerate(early_copies):
        pl.when(step == min(j + 1, steps - 1))(copy.start)
    load(step, load_sems, weights)
    normed = normed_ref[...]
    low = low_ref[...]
    dy = dy_ref[...]
    grad_low = grad_lows_ref[:, LANES:]
    feed_core(
        jnp.concatenate([normed, low], axis=1), jnp.concatenate([dy, grad_low], axis=1), up_ref, down_ref, act_ref,
        gh_ref, 512,
    )
    act = act_ref[...]
    gh = gh_ref[...]
    forward = dot_nn(act, down_ref[...])
    backward = dot_nt(gh, up_ref[...])
    grad_low_up = (grad_low_in_ref[...] + backward[:, width:]).astype(BF16)
    out = out_in_ref[...] + forward[:, :width]
    low_act = low_act_in_ref[...] + forward[:, width:]
    second = grad_in_ref[...] + backward[:, :width] + dot_nt(grad_low_up, up_left_ref[...])
    acc_ref[:, :hidden] += dot_tn(low, gh)
    acc_ref[:, hidden:] += dot_tn(grad_low, act)
    up_left_grad_ref[...] += dot_tn(grad_low_up, normed)

    @pl.when(step < send_tiles)
    def _():
        slot = step // per_device
        span = pl.ds(pl.multiple_of(lax.rem(step, per_device) * tile, tile), tile)
        send_ref[slot, span, :width] = out.astype(BF16)
        send_ref[slot, span, width : 2 * width] = second.astype(BF16)
        send_ref[slot, span, 2 * width :] = low_act.astype(BF16)

    for s in range(unit - 1):
        for t in range(per_device):
            pl.when(step == s * per_device + t)(copies[s][t].start)
            pl.when(step == send_tiles + t)(copies[s][t].wait_recv)

    @pl.when(step >= send_tiles)
    def _():
        span = pl.ds(pl.multiple_of((step - send_tiles) * tile, tile), tile)
        first = keep_ref[:, :width].astype(F32)
        low_att = keep_ref[:, width:].astype(F32)
        total_out, total_second, total_low = out, second, low_act
        for s in range(unit - 1):
            first = first + got1_ref[s, :, :width].astype(F32)
            low_att = low_att + got1_ref[s, :, width:].astype(F32)
            total_out = total_out + got_ref[s, span, :width].astype(F32)
            total_second = total_second + got_ref[s, span, width : 2 * width].astype(F32)
            total_low = total_low + got_ref[s, span, 2 * width :].astype(F32)
        low_att, total_low = low_att.astype(BF16), total_low.astype(BF16)
        x = x_ref[...].astype(F32)
        y_ref[...] = (
            x + total_out + dot_nn(low_att, output_right_ref[...]) + dot_nn(total_low, down_right_ref[...])
        ).astype(BF16)
        center = x - jnp.mean(x, axis=-1, keepdims=True)
        spread = jnp.mean(center * center, axis=-1, keepdims=True)
        inverse = lax.rsqrt(spread + EPS)
        scaled = center * inverse
        total = first * gain1_ref[...] + total_second * gain2_ref[...]
        mean = jnp.mean(total, axis=-1, keepdims=True)
        inner = jnp.mean(total * scaled, axis=-1, keepdims=True)
        dx_ref[...] = dy.astype(F32) + (total - mean - scaled * inner) * inverse
        norms_ref[0:1, :] += jnp.sum(first * scaled, axis=0, keepdims=True)
        norms_ref[1:2, :] += jnp.sum(first, axis=0, keepdims=True)
        norms_ref[2:3, :] += jnp.sum(total_second * scaled, axis=0, keepdims=True)
        norms_ref[3:4, :] += jnp.sum(total_second, axis=0, keepdims=True)
        output_right_grad_ref[...] += dot_tn(low_att, dy)
        down_right_grad_ref[...] += dot_tn(total_low, dy)

    @pl.when(step == steps - 1)
    def _():
        for copy in early_copies:
            copy.wait()
        sums_ref[...] = (acc_ref[...] + early_got_ref[...].astype(F32)).astype(BF16)
        quarters(both_ref, up_left_grad_ref[...], output_right_grad_ref[...], down_right_grad_ref[...])
        start = 3 * (width // 4)
        count = width // LANES
        for q in range(4):
            rows = [norms_ref[q : q + 1, j * LANES : (j + 1) * LANES] for j in range(count)]
            block = jnp.concatenate([*rows, jnp.zeros((LANES - count, LANES), F32)], axis=0)
            both_ref[q % 2, q // 2, :, start:] = block.astype(BF16)
        for group in copies:
            for copy in group:
                copy.wait_send()
        if hosted:
            for at in range(steps, max(len(stage) for stage in stages)):
                for stage in stages:
                    if at < len(stage):
                        stage[at]()
            outs = []
            for j, refs in enumerate((*heads_refs, left_refs[3:])):
                full = refs[5]
                target = left_out_ref if j == 2 else heads_out_ref.at[:, :, :, :, pl.ds(j * size, size)]
                outs.append(pltpu.make_async_copy(full, target, out_sems.at[j]))
                outs[-1].start()
            for copy in net.started:
                copy.wait_send()
            for copy in outs:
                copy.wait()


def feed_second(unit, normed, low, dy, grad_lows, out, grad, low_act, grad_low, x, keep, got, gains, output_right,
                down_right, ups, up_left, up_right, downs, down_left, early, heads, left, hosted, tile):
    rows, width = normed.shape
    own_rows = rows // unit
    anywhere = pl.BlockSpec(memory_space=pl.ANY)
    extra = []
    if hosted:
        heads = heads.reshape((2,) + SUM_ROWS + heads.shape[-1:])
        left = left.reshape((2, 2) + SUM_ROWS + left.shape[-1:])
        extra = sum_scratch("yxz", heads.shape[-1] // 2) + sum_scratch("xyz", heads.shape[-1] // 2)
        extra += both_scratch((("yxz", left.shape[-1]),))
    hidden = ups[0].shape[1]
    steps, per_device = rows // tile, own_rows // tile
    send_tiles = steps - per_device
    wide = 2 * width + LANES

    def turned(size):
        def index(i):
            place, slot = place_in_unit(unit)[0], i // per_device + 1
            return (lax.rem(place + unit - slot, unit) * per_device + lax.rem(i, per_device), 0)

        return pl.BlockSpec((tile, size), index)

    def late(size):
        return pl.BlockSpec((tile, size), lambda i: (jnp.maximum(i - send_tiles, 0), 0))

    return pl.pallas_call(
        functools.partial(feed_second_kernel, unit, tile),
        grid=(steps,),
        in_specs=[
            turned(width),
            turned(LANES),
            turned(width),
            turned(2 * LANES),
            turned(width),
            turned(width),
            turned(LANES),
            turned(LANES),
            late(width),
            late(width + LANES),
            pl.BlockSpec((unit - 1, tile, width + LANES), lambda i: (0, jnp.maximum(i - send_tiles, 0), 0)),
            whole((1, width)),
            whole((1, width)),
            whole(output_right.shape),
            whole(down_right.shape),
            anywhere,
            anywhere,
            whole(up_left.shape),
            anywhere,
            anywhere,
            anywhere,
            anywhere,
            whole(early.shape),
            whole(heads.shape),
            whole(left.shape),
        ],
        out_specs=[
            late(width),
            late(width),
            held((LANES, 2 * hidden)),
            held((2, 2, LANES, 3 * (width // 4) + LANES)),
            anywhere,
            anywhere,
        ],
        scratch_shapes=[
            pltpu.VMEM((tile, hidden), BF16),
            pltpu.VMEM((tile, hidden), BF16),
            pltpu.VMEM((width + LANES, hidden), BF16),
            pltpu.VMEM((hidden, width + LANES), BF16),
            pltpu.VMEM((unit - 1, own_rows, wide), BF16),
            pltpu.VMEM((unit - 1, own_rows, wide), BF16),
            pltpu.VMEM((LANES, 2 * hidden), BF16),
            pltpu.VMEM((LANES, 2 * hidden), F32),
            pltpu.VMEM((8, width), F32),
            pltpu.VMEM((LANES, width), F32),
            pltpu.VMEM((LANES, width), F32),
            pltpu.VMEM((LANES, width), F32),
            pltpu.SemaphoreType.DMA((2, unit - 1, per_device)),
            pltpu.SemaphoreType.DMA((2, 4)),
            pltpu.SemaphoreType.DMA((3,)),
            pltpu.SemaphoreType.DMA((6,)),
        ]
        + extra,
        out_shape=[
            shaped((own_rows, width), BF16),
            shaped((own_rows, width), F32),
            shaped((LANES, 2 * hidden), BF16),
            shaped((2, 2, LANES, 3 * (width // 4) + LANES), BF16),
            shaped(heads.shape, BF16),
            shaped(left.shape[1:] if hosted else left.shape, BF16),
        ],
        compiler_params=pltpu.CompilerParams(
            dimension_semantics=("arbitrary",), vmem_limit_bytes=VMEM_LIMIT, collective_id=4, has_side_effects=True
        ),
        cost_estimate=BRIEF,
        name="feed_second",
    )(normed, low, dy, grad_lows, out, grad, low_act, grad_low, x, keep, got, *gains, output_right, down_right, *ups,
      up_left, up_right, *downs, down_left, early, heads, left)


def project_kernel(
    unit, main_tiles, halo_ref, normed_ref, dy_ref, grad_lows_ref, late_ref, cos0_ref, cos1_ref, minus0_ref, minus1_ref, plus0_ref,
    plus1_ref, gain_ref, shift_ref, triple0_ref, triple1_ref, left_ref, right_ref, output0_ref, output1_ref,
    output_left_ref, low_ref, q_ref, k_ref, v_ref, g_ref, triple_ref, output_ref, load_sems,
):
    step = pl.program_id(0)
    load(
        step, load_sems,
        head_weights(
            unit, (triple0_ref, triple1_ref), right_ref, (output0_ref, output1_ref), output_left_ref, triple_ref,
            output_ref,
        ),
    )

    later = late_ref[0, 0:1, :] > 0.0
    tables = tuple(
        jnp.where(later, two[...], one[...])
        for one, two in ((cos0_ref, cos1_ref), (minus0_ref, minus1_ref), (plus0_ref, plus1_ref))
    )
    head_width = output0_ref.shape[0]
    first = low_lanes()

    def rows(normed, full):
        low = dot_nn(normed, left_ref[...]).astype(BF16)
        if full:
            low_ref[...] = low
        mixed = dot_nn(jnp.concatenate([normed, low], axis=1), triple_ref[...])
        if full:
            grads = jnp.concatenate([dy_ref[...], grad_lows_ref[:, :LANES]], axis=1)
            g_ref[...] = dot_nt(grads, output_ref[...]).astype(BF16)
        for pair in range(2 * head_width // LANES):
            one, two, three = (
                mixed[:, (3 * pair + part) * LANES : (3 * pair + part + 1) * LANES] for part in range(3)
            )
            cols = pl.ds(pair * LANES, LANES)
            key = pltpu.roll(jnp.where(first, three, one), HEAD_DIM, 1)
            k_ref[:, cols] = rotate(key, *tables).astype(BF16)
            v_ref[:, cols] = jnp.where(first, two, three).astype(BF16)
            if full:
                query = rotate(jnp.where(first, one, two), *tables).astype(BF16)
                q_ref[:, cols] = query * HEAD_DIM**-0.5

    @pl.when(step < main_tiles)
    def _():
        rows(normed_ref[...], True)

    @pl.when(step >= main_tiles)
    def _():
        rows(normalize(halo_ref[...].astype(F32), gain_ref[...], shift_ref[...]).astype(BF16), False)


def project(unit, conts, x_halo, normed, dy, grad_lows, gain, shift, triples, left, right, outputs, output_left, tables,
            tile):
    rows, width = dy.shape
    head_width = outputs[0].shape[0]
    anywhere = pl.BlockSpec(memory_space=pl.ANY)
    per_block = SHORT // tile
    main_tiles, halo_tiles = rows // tile, SHORT // tile
    late = jnp.concatenate([jnp.repeat(conts, per_block), jnp.zeros((halo_tiles,), jnp.int32)])
    late = jnp.broadcast_to(late.astype(F32)[:, None, None], (main_tiles + halo_tiles, 8, LANES))

    halo = pl.BlockSpec((tile, width), lambda i: (jnp.maximum(i - main_tiles, 0), 0))

    def table(which):
        return pl.BlockSpec((tile, LANES), lambda i: (which * per_block + lax.rem(i, per_block), 0))

    def main(size):
        return pl.BlockSpec((tile, size), lambda i: (jnp.minimum(i, main_tiles - 1), 0))

    def all_rows(size):
        return pl.BlockSpec((tile, size), lambda i: (jnp.where(i < main_tiles, i + halo_tiles, i - main_tiles), 0))

    return pl.pallas_call(
        functools.partial(project_kernel, unit, main_tiles),
        grid=(main_tiles + halo_tiles,),
        in_specs=[
            halo,
            main(width),
            main(width),
            main(2 * LANES),
            pl.BlockSpec((1, 8, LANES), lambda i: (i, 0, 0)),
            table(0),
            table(1),
            table(0),
            table(1),
            table(0),
            table(1),
            whole(gain.shape),
            whole(shift.shape),
            anywhere,
            anywhere,
            whole(left.shape),
            anywhere,
            anywhere,
            anywhere,
            anywhere,
        ],
        out_specs=[
            main(LANES),
            main(2 * head_width),
            all_rows(2 * head_width),
            all_rows(2 * head_width),
            main(2 * head_width),
        ],
        scratch_shapes=[
            pltpu.VMEM((width + LANES, 6 * head_width), BF16),
            pltpu.VMEM((2 * head_width, width + LANES), BF16),
            pltpu.SemaphoreType.DMA((8,)),
        ],
        out_shape=[
            shaped((rows, LANES), BF16),
            shaped((rows, 2 * head_width), BF16),
            shaped((SHORT + rows, 2 * head_width), BF16),
            shaped((SHORT + rows, 2 * head_width), BF16),
            shaped((rows, 2 * head_width), BF16),
        ],
        compiler_params=params(),
        cost_estimate=BRIEF,
        name="project",
    )(x_halo, normed, dy, grad_lows, late, *[table for table in tables for _ in range(2)], gain, shift, *triples, left, right,
      *outputs, output_left)


def attend_rows(with_prev, pairs, count, allowed, q_ref, k_ref, v_ref, g_ref, kp_ref, vp_ref, tables, att_ref, gq_ref,
                dk_ref, dv_ref, dkp_ref, dvp_ref):
    first = low_lanes()
    zero = jnp.zeros((), BF16)

    def stack(pair):
        return jnp.concatenate([jnp.where(first, pair, zero), jnp.where(first, zero, pair)], axis=0)

    def unstack(both):
        return jnp.where(first, both[:count], both[count:])

    def joined(fold, values):
        return functools.reduce(fold, values)

    pieces = []
    for lanes in pairs:
        for start in range(0, SHORT, count):
            span = pl.ds(start, count)
            parts = []
            if with_prev:
                parts.append((kp_ref[:, lanes], vp_ref[:, lanes], dkp_ref, dvp_ref, pl.ds(0, SHORT)))
            if start:
                before = pl.ds(0, start)
                parts.append((k_ref[before, lanes], v_ref[before, lanes], dk_ref, dv_ref, before))
            parts.append((k_ref[span, lanes], v_ref[span, lanes], dk_ref, dv_ref, span))
            pieces.append((lanes, span, stack(q_ref[span, lanes]), stack(g_ref[span, lanes]), parts))

    scores, grads, weights, lows, inners, slopes = [], [], [], [], [], []
    for _, _, queries, _, parts in pieces:
        found = [dot_nt(queries, part[0]) for part in parts]
        scores.append(found[:-1] + [jnp.where(allowed, found[-1], -1e30)])
    for _, _, _, grad, parts in pieces:
        grads.append([dot_nt(grad, part[1]) for part in parts])
    for found in scores:
        peak = joined(jnp.maximum, [jnp.max(score, axis=1, keepdims=True) for score in found])
        exps = [jnp.exp(score - peak) for score in found]
        scale = 1.0 / joined(jnp.add, [jnp.sum(exp, axis=1, keepdims=True) for exp in exps])
        weights.append([exp * scale for exp in exps])
        lows.append([weight.astype(BF16) for weight in weights[-1]])
    for (lanes, span, _, grad, parts), low in zip(pieces, lows):
        attended = joined(jnp.add, [dot_nn(weight, part[1]) for weight, part in zip(low, parts)])
        att_ref[span, lanes] = unstack(attended).astype(BF16)
        inners.append(jnp.sum(attended * grad.astype(F32), axis=1, keepdims=True))
    for weight, grad, inner in zip(weights, grads, inners):
        slopes.append([(w * (g - inner)).astype(BF16) for w, g in zip(weight, grad)])
    for (lanes, span, queries, grad, parts), low, slope in zip(pieces, lows, slopes):
        grad_query = joined(jnp.add, [dot_nn(ds, part[0]) for ds, part in zip(slope, parts)])
        for ds, weight, (_, _, to_key, to_value, rows) in zip(slope, low, parts):
            to_key[lanes, rows] += dot_tn(queries, ds)
            to_value[lanes, rows] += dot_tn(grad, weight)
        grad_query = unstack(grad_query) * HEAD_DIM**-0.5
        gq_ref[span, lanes] = unrotate(grad_query, *[table[span] for table in tables]).astype(BF16)


def unrotate_tall(ref, lanes, cosine, sine):
    half = ROT // 2
    value = ref[lanes, :]
    halves = []
    for base in (HEAD_DIM, 0):
        one, two = value[base : base + half], value[base + half : base + ROT]
        halves += [one * cosine + two * sine, two * cosine - one * sine, value[base + ROT : base + HEAD_DIM]]
    return jnp.concatenate(halves, axis=0).astype(BF16).T


def attend_kernel(
    blocks, pairs, count, conts_ref, q_ref, k_ref, v_ref, g_ref, kp_ref, vp_ref, cos_ref, minus_ref, plus_ref,
    tall_cos_ref, tall_sin_ref, att_ref, gq_ref, gk_ref, gv_ref, halo_ref, dk_ref, dv_ref,
):
    step = pl.program_id(0)
    block = blocks - 1 - step
    continued = conts_ref[block]
    offset = pl.multiple_of(continued * SHORT, SHORT)
    tables = tuple(ref.at[pl.ds(offset, SHORT)] for ref in (cos_ref, minus_ref, plus_ref))
    now = lax.rem(step, 2)
    own = (dk_ref.at[now], dv_ref.at[now])
    before = (dk_ref.at[1 - now], dv_ref.at[1 - now])

    @pl.when(step == 0)
    def _():
        for ref in own:
            ref[...] = jnp.zeros_like(ref)

    for ref in before:
        ref[...] = jnp.zeros_like(ref)
    row = lax.broadcasted_iota(jnp.int32, (2 * count, count), 0)
    column = lax.broadcasted_iota(jnp.int32, (2 * count, count), 1)
    allowed = column <= jnp.where(row >= count, row - count, row)
    args = (q_ref, k_ref, v_ref, g_ref, kp_ref, vp_ref, tables, att_ref, gq_ref, *own, *before)
    lanes = [pl.ds(pair * LANES, LANES) for pair in range(pairs)]

    def block_of(with_prev):
        for start in range(0, pairs, 2):
            attend_rows(with_prev, lanes[start : start + 2], count, allowed, *args)

    pl.when(continued == 0)(lambda: block_of(False))
    pl.when(continued != 0)(lambda: block_of(True))
    turn = tuple(ref[:, pl.ds(offset, SHORT)] for ref in (tall_cos_ref, tall_sin_ref))
    for pair in lanes:
        gk_ref[:, pair] = unrotate_tall(own[0], pair, *turn)
        gv_ref[:, pair] = own[1][pair, :].astype(BF16).T

    @pl.when(block == 0)
    def _():
        base = tuple(ref[:, pl.ds(0, SHORT)] for ref in (tall_cos_ref, tall_sin_ref))
        for pair in lanes:
            halo_ref[0, :, pair] = unrotate_tall(before[0], pair, *base)
            halo_ref[1, :, pair] = before[1][pair, :].astype(BF16).T


def attend(conts, q, k, v, g, tables, tall, count):
    rows, head_width = q.shape
    blocks = rows // SHORT
    here = pl.BlockSpec((SHORT, head_width), lambda i, conts: (blocks - 1 - i, 0))
    after = pl.BlockSpec((SHORT, head_width), lambda i, conts: (blocks - i, 0))
    return pl.pallas_call(
        functools.partial(attend_kernel, blocks, head_width // LANES, count),
        grid_spec=pltpu.PrefetchScalarGridSpec(
            num_scalar_prefetch=1,
            grid=(blocks,),
            in_specs=[here, after, after, here, here, here] + [whole(table.shape) for table in (*tables, *tall)],
            out_specs=[here] * 4 + [held((2, SHORT, head_width))],
            scratch_shapes=[pltpu.VMEM((2, head_width, SHORT), F32)] * 2,
        ),
        out_shape=[shaped((rows, head_width), BF16)] * 4 + [shaped((2, SHORT, head_width), BF16)],
        compiler_params=params(),
        cost_estimate=BRIEF,
        name="attend",
    )(conts, q, k, v, g, k, v, *tables, *tall)


def settle_kernel(
    unit, tile, normed_ref, low_ref, grad_lows_ref, out_in_ref, att_ref, gq_ref, gk_ref, gv_ref, halo_ref, triple0_ref,
    triple1_ref, left_ref, output0_ref, output1_ref, right_ref, output_left_ref, out_ref, keep_ref, heads_ref,
    left_sums_ref, got_ref, send_ref, halo_got_ref, key_ref, value_ref, mixed_ref, triple_ref, output_ref, acc_ref,
    out_acc_ref, left_grad_ref, halo_sems, sems, load_sems,
):
    step = pl.program_id(0)
    per_device = got_ref.shape[1] // tile
    steps = unit * per_device
    halo_start = steps - SHORT // tile
    place, base = place_in_unit(unit)
    half = base // unit
    peers = unit_peers(unit)
    y_peer = chip_neighbours(unit)[1]
    halo_copies = []
    for j in range(SHORT // tile):
        part = pl.ds(j * tile, tile)
        halo_copies.append(
            pltpu.make_async_remote_copy(
                src_ref=halo_ref.at[:, part], dst_ref=halo_got_ref.at[:, part], send_sem=halo_sems.at[0, j],
                recv_sem=halo_sems.at[1, j], device_id=y_peer, device_id_type=MESH,
            )
        )
    copies = [
        [
            pltpu.make_async_remote_copy(
                src_ref=send_ref.at[s, pl.ds(t * tile, tile)], dst_ref=got_ref.at[s, pl.ds(t * tile, tile)],
                send_sem=sems.at[0, s, t], recv_sem=sems.at[1, s, t], device_id=peer, device_id_type=MESH,
            )
            for t in range(per_device)
        ]
        for s, peer in enumerate(peers)
    ]
    @pl.when(step == 0)
    def _():
        meet([y_peer, *peers])

        @pl.when(half == 1)
        def _():
            for copy in halo_copies:
                copy.start()

        for ref in (acc_ref, out_acc_ref, left_grad_ref):
            ref[...] = jnp.zeros_like(ref)

    load(
        step, load_sems,
        head_weights(
            unit, (triple0_ref, triple1_ref), right_ref, (output0_ref, output1_ref), output_left_ref, triple_ref,
            output_ref,
        ),
    )

    key_ref[...], value_ref[...] = gk_ref[...], gv_ref[...]
    for j, copy in enumerate(halo_copies):

        @pl.when((half == 0) & (step == halo_start + j))
        def _():
            copy.wait_recv()
            rows = pl.ds(j * tile, tile)
            count = output0_ref.shape[0]
            for ref, which in ((key_ref, 0), (value_ref, 1)):
                for here, there in ((pl.ds(0, count), pl.ds(count, count)), (pl.ds(count, count), pl.ds(0, count))):
                    ref[:, here] = (ref[:, here].astype(F32) + halo_got_ref[which, rows, there].astype(F32)).astype(BF16)

    normed = normed_ref[...]
    low = low_ref[...]
    grad_low_out = grad_lows_ref[:, :LANES]
    head_width = output0_ref.shape[0]
    first = low_lanes()
    for pair in range(2 * head_width // LANES):
        q, k, v = (ref[:, pair * LANES : (pair + 1) * LANES] for ref in (gq_ref, key_ref, value_ref))
        for part, value in enumerate((jnp.where(first, q, k), jnp.where(first, v, q), jnp.where(first, k, v))):
            mixed_ref[:, (3 * pair + part) * LANES : (3 * pair + part + 1) * LANES] = value
    mixed = mixed_ref[...]
    att = att_ref[...]
    width = normed.shape[1]
    backward = dot_nt(mixed, triple_ref[...])
    forward = dot_nn(att, output_ref[...])
    grad_low = backward[:, width:].astype(BF16)
    grad = (backward[:, :width] + dot_nt(grad_low, left_ref[...])).astype(BF16)
    out_ref[...] = out_in_ref[...] + forward[:, :width]
    low_att = forward[:, width:].astype(BF16)

    @pl.when(step // per_device == place)
    def _():
        keep_ref[:, :width] = grad
        keep_ref[:, width:] = low_att

    span = pl.ds(pl.multiple_of(lax.rem(step, per_device) * tile, tile), tile)
    for s in range(unit - 1):
        owner = lax.rem(place + unit - (s + 1), unit)

        @pl.when(step // per_device == owner)
        def _():
            send_ref[s, span, :width] = grad
            send_ref[s, span, width:] = low_att

        for t in range(per_device):
            pl.when(step == owner * per_device + t)(copies[s][t].start)

    acc_ref[...] += dot_tn(low, mixed)
    out_acc_ref[...] += dot_tn(grad_low_out, att)
    left_grad_ref[...] += dot_tn(grad_low, normed)

    @pl.when(step == steps - 1)
    def _():
        size = 3 * head_width
        for j in range(2):
            heads_ref[j, :, :size] = acc_ref[:, j * size : (j + 1) * size].astype(BF16)
            heads_ref[j, :, size:] = out_acc_ref[:, j * head_width : (j + 1) * head_width].astype(BF16)
        quarters(left_sums_ref, left_grad_ref[...])

        @pl.when(half == 1)
        def _():
            for copy in halo_copies:
                copy.wait_send()

        for group in copies:
            for copy in group:
                copy.wait()


def settle(unit, normed, low, grad_lows, out, heads, halo, triples, left, outputs, right, output_left, tile):
    rows, width = normed.shape
    own_rows = rows // unit
    head_width = outputs[0].shape[0]
    steps, per_device = rows // tile, own_rows // tile
    anywhere = pl.BlockSpec(memory_space=pl.ANY)

    def kept(i):
        return (jnp.clip(i - place_in_unit(unit)[0] * per_device, 0, per_device - 1), 0)

    return pl.pallas_call(
        functools.partial(settle_kernel, unit, tile),
        grid=(steps,),
        in_specs=[rows_of(tile, width), rows_of(tile, LANES), rows_of(tile, 2 * LANES), rows_of(tile, width)]
        + [rows_of(tile, 2 * head_width)] * 4
        + [anywhere]
        + [anywhere, anywhere, whole(left.shape), anywhere, anywhere, anywhere, anywhere],
        out_specs=[
            rows_of(tile, width),
            pl.BlockSpec((tile, width + LANES), kept),
            held((2, LANES, 4 * head_width)),
            held((2, 2, LANES, width // 4)),
            anywhere,
        ],
        scratch_shapes=[
            pltpu.VMEM((unit - 1, own_rows, width + LANES), BF16),
            pltpu.VMEM((2, SHORT, 2 * head_width), BF16),
            pltpu.VMEM((tile, 2 * head_width), BF16),
            pltpu.VMEM((tile, 2 * head_width), BF16),
            pltpu.VMEM((tile, 6 * head_width), BF16),
            pltpu.VMEM((width + LANES, 6 * head_width), BF16),
            pltpu.VMEM((2 * head_width, width + LANES), BF16),
            pltpu.VMEM((LANES, 6 * head_width), F32),
            pltpu.VMEM((LANES, 2 * head_width), F32),
            pltpu.VMEM((LANES, width), F32),
            pltpu.SemaphoreType.DMA((2, SHORT // tile)),
            pltpu.SemaphoreType.DMA((2, unit - 1, per_device)),
            pltpu.SemaphoreType.DMA((8,)),
        ],
        out_shape=[
            shaped((rows, width), F32),
            shaped((own_rows, width + LANES), BF16),
            shaped((2, LANES, 4 * head_width), BF16),
            shaped((2, 2, LANES, width // 4), BF16),
            shaped((unit - 1, own_rows, width + LANES), BF16),
        ],
        compiler_params=pltpu.CompilerParams(
            dimension_semantics=("arbitrary",), vmem_limit_bytes=VMEM_LIMIT, collective_id=5, has_side_effects=True
        ),
        cost_estimate=BRIEF,
        name="settle",
    )(normed, low, grad_lows, out, *heads, halo, *triples, left, *outputs, right, output_left)


FEED_ORDERS = ("xz", "zx", "xz", "zx")


def sum_kernel(size, feed_ref, both_ref, heads_ref, left_ref, feed_out_ref, both_out_ref, heads_out_ref, left_out_ref,
               cross_sems, local_sems, *refs):
    net = Net()
    meet([net.x_peer, net.y_peer, net.core_peer, *net.z_peers])
    locals_, crossing = [], []

    def hand_over(slot, full, out, first, second):
        for place, at in ((0, first), (1, second)):
            target = out.at[net.core, at]
            local = pltpu.make_async_copy(full.at[place], target, local_sems.at[slot, place])
            local.start()
            locals_.append(local)
            crossing.append(net.copy(full.at[place], target, cross_sems, 2 * slot + place, net.core_peer))
            net.start(crossing[-1:])

    split = len(sum_scratch("xz", size))
    feed_refs = [refs[j * split : (j + 1) * split] for j in range(len(FEED_ORDERS))]
    both_refs = refs[len(FEED_ORDERS) * split :]
    parts = split_columns(both_ref.shape[-1])
    per_part = (len(both_refs) - 3) // 2
    scratches = (both_refs[3 : 3 + per_part], both_refs[3 + per_part :])
    running = [sum_both(net, parts, both_ref, *both_refs[:3], scratches)]
    running += [
        sum_chunk(net, order, feed_ref.at[:, :, :, pl.ds(j * size, size)], feed_refs[j])
        for j, order in enumerate(FEED_ORDERS)
    ]

    def both_done():
        start = 0
        for j, (_, count) in enumerate(parts):
            columns = both_out_ref.at[:, :, :, :, :, pl.ds(start, count)]
            hand_over(j, scratches[j][5], columns, net.half, net.other_half)
            start += count

    def feed_done(j):
        columns = feed_out_ref.at[:, :, :, :, :, pl.ds(j * size, size)]
        hand_over(4 + j, feed_refs[j][5], columns, net.other_half, net.half)

    for k in range(max(len(stage) for stage in running)):
        for j, stage in enumerate(running):
            if k < len(stage):
                stage[k]()
            if k == len(stage) - 1:
                both_done() if j == 0 else feed_done(j - 1)
        if k == 0:
            hand_over(2, heads_ref, heads_out_ref, net.half, net.other_half)
            hand_over(3, left_ref, left_out_ref, net.half, net.other_half)
    for copy in locals_:
        copy.wait()
    for copy in crossing:
        copy.wait_recv()
    for copy in net.started:
        copy.wait_send()


def sum_all(feed, both, heads, left):
    arrays = (feed.reshape(SUM_ROWS + feed.shape[-1:]), both.reshape((2, 2) + SUM_ROWS + both.shape[-1:]), heads, left)
    size = feed.shape[-1] // len(FEED_ORDERS)
    slots = 4 + len(FEED_ORDERS)
    outs = [shaped((2, 2) + SUM_ROWS + array.shape[-1:], BF16) for array in arrays]
    results = pl.pallas_call(
        functools.partial(sum_kernel, size),
        out_shape=outs,
        in_specs=[pl.BlockSpec(memory_space=pltpu.VMEM)] * 4,
        out_specs=[pl.BlockSpec(memory_space=pl.ANY)] * 4,
        scratch_shapes=[pltpu.SemaphoreType.DMA((2, 2 * slots)), pltpu.SemaphoreType.DMA((slots, 2))]
        + [shape for order in FEED_ORDERS for shape in sum_scratch(order, size)]
        + both_scratch(split_columns(both.shape[-1])),
        compiler_params=pltpu.CompilerParams(
            collective_id=2, has_side_effects=True, vmem_limit_bytes=VMEM_LIMIT
        ),
        cost_estimate=BRIEF,
        name="sum_all",
    )(*arrays)
    return [value.reshape(2, 2, LANES, value.shape[-1]) for value in results]


def unpack_kernel(triple_width, feed_ref, both_ref, heads_ref, left_ref, triple_ref, output_ref, up_ref, down_ref,
                  triple_left_ref, up_left_ref, output_right_ref, down_right_ref, *norm_refs):
    triple_ref[...] = heads_ref[0, 0, :, :triple_width].astype(F32)
    output_ref[...] = heads_ref[0, 0, :, triple_width:].astype(F32).T
    hidden = up_ref.shape[1]
    up_ref[...] = feed_ref[0, 0, :, :hidden].astype(F32)
    down_ref[...] = feed_ref[0, 0, :, hidden:].astype(F32).T
    size = triple_left_ref.shape[0]
    triple_left_ref[...] = left_ref[0, 0].astype(F32).T
    up_left_ref[...] = both_ref[0, 0, :, :size].astype(F32).T
    output_right_ref[...] = both_ref[0, 0, :, size : 2 * size].astype(F32)
    down_right_ref[...] = both_ref[0, 0, :, 2 * size : 3 * size].astype(F32)
    for q, ref in enumerate(norm_refs):

        @pl.when(pl.program_id(0) == q)
        def _():
            ref[...] = both_ref[0, 0, : ref.shape[0], 3 * size :].astype(F32)


def unpack(feed, both, heads, left, triple_width):
    arrays = (feed, both, heads, left)
    hidden, quarter = feed.shape[-1] // 2, left.shape[-1]
    width, head_width = 4 * quarter, heads.shape[-1] - triple_width

    def tall(rows):
        return pl.BlockSpec((rows, LANES), lambda s: (s, 0))

    def wide(cols):
        return pl.BlockSpec((LANES, cols), lambda s: (0, s))

    return pl.pallas_call(
        functools.partial(unpack_kernel, triple_width),
        grid=(4,),
        in_specs=[
            pl.BlockSpec((1, 1) + value.shape[2:], lambda s: (lax.rem(s, 2), s // 2, 0, 0)) for value in arrays
        ],
        out_specs=[
            wide(triple_width), tall(head_width), wide(hidden), tall(hidden), tall(quarter), tall(quarter),
            wide(quarter), wide(quarter), *[held((width // LANES, LANES))] * 4,
        ],
        out_shape=[
            shaped((LANES, 4 * triple_width), F32),
            shaped((4 * head_width, LANES), F32),
            shaped((LANES, 4 * hidden), F32),
            shaped((4 * hidden, LANES), F32),
            shaped((width, LANES), F32),
            shaped((width, LANES), F32),
            shaped((LANES, width), F32),
            shaped((LANES, width), F32),
        ]
        + [shaped((width // LANES, LANES), F32)] * 4,
        compiler_params=params(),
        cost_estimate=BRIEF,
        name="unpack",
    )(*arrays)


def shards(
    ranks,
    groups,
    block_input,
    sequence_lengths,
    first_gain,
    first_shift,
    second_gain,
    second_shift,
    triple_weight,
    triple_left,
    triple_right,
    output_weight,
    output_left,
    output_right,
    expand_weight,
    expand_left,
    expand_right,
    shrink_weight,
    shrink_left,
    shrink_right,
    cotangent,
):
    unit = ranks // 2
    own_rows, width = block_input.shape
    rows = own_rows * unit
    blocks = rows // SHORT
    tile = math.gcd(own_rows, 256)
    triple_width = triple_weight.shape[1]
    head_width = output_weight.shape[0]
    hidden = expand_weight.shape[1]
    mp = lax.axis_index("mp")
    half = mp // unit
    place = lax.rem(mp, unit)
    far = lax.rem(mp + unit, ranks)
    swap = [(m, (m + unit) % ranks) for m in range(ranks)]

    tables = rotary_tables()
    beside = [[(d, d ^ bit) for d in range(groups)] for bit in (1, 2)]
    continues = find_flags(sequence_lengths[0])
    conts = lax.dynamic_slice_in_dim(continues, half * blocks, blocks, 0)
    gain1, shift1 = first_gain[None, :], first_shift[None, :]
    gain2, shift2 = second_gain[None, :], second_shift[None, :]

    (normed1, normed2, dy, low2, grad_lows, out, grad2, low_act, grad_low2, feed_sums, triple_far,
     output_far, x_halo, expand_half, shrink_half) = feed_first(
        unit, block_input, cotangent, (gain1, shift1, gain2, shift2), expand_weight, expand_left, expand_right,
        shrink_weight, shrink_left, output_right, shrink_right, triple_weight, output_weight, tile,
    )
    expand_piece = lax.ppermute(expand_half, "mp", swap)
    shrink_piece = lax.ppermute(shrink_half, "mp", swap)
    low1, q, k, v, g = project(
        unit, conts, x_halo, normed1, dy, grad_lows, gain1, shift1, (triple_weight, triple_far), triple_left,
        triple_right, (output_weight, output_far), output_left, tables, tile,
    )
    att, gq, gk, gv, halo = attend(conts, q, k, v, g, tables, tall_tables(), 256)
    expand_piece, shrink_piece, att = lax.optimization_barrier((expand_piece, shrink_piece, att))
    expand_other = lax.ppermute(expand_piece, "dp", beside[0])
    shrink_other = lax.ppermute(shrink_piece, "dp", beside[1])
    out, keep1, heads, left, got1 = settle(
        unit, normed1, low1, grad_lows, out, (att, gq, gk, gv), halo, (triple_weight, triple_far), triple_left,
        (output_weight, output_far), triple_right, output_left, tile,
    )
    hosted = ranks == 4 and groups == 8
    block_output, input_gradient, feed_sums, both, heads_sum, left_sum = feed_second(
        unit, normed2, low2, dy, grad_lows, out, grad2, low_act, grad_low2, block_input, keep1, got1, (gain1, gain2),
        output_right, shrink_right, (expand_piece, expand_other), expand_left, expand_right,
        (shrink_piece, shrink_other), shrink_left, feed_sums, heads, left, hosted, tile,
    )
    if hosted:
        (triple_right_sum, output_left_sum, expand_right_sum, shrink_left_sum, triple_left_sum, expand_left_sum,
         output_right_sum, shrink_right_sum, *norms) = unpack(
            *sum_all(feed_sums, both, heads_sum, left_sum), triple_width
        )
        norms = [value.reshape(width) for value in norms]
    else:

        def spread(*placed):
            size = placed[0][0].shape[1]
            wide = jnp.zeros((LANES, size * ranks), BF16)
            for value, shard in placed:
                wide = lax.dynamic_update_slice_in_dim(wide, value, shard * size, 1)
            return wide

        def joined(value):
            return value.transpose(2, 1, 0, 3).reshape(LANES, -1)

        def columns(value, start, size):
            return value.reshape(LANES, ranks, -1)[:, :, start : start + size].reshape(LANES, -1).astype(F32)

        heads, feed, left, both = lax.psum(
            (spread((heads[0], mp), (heads[1], far)), spread((feed_sums, far)), left, both), ("dp", "mp")
        )
        triple_right_sum = columns(heads, 0, triple_width)
        output_left_sum = columns(heads, triple_width, head_width).T
        expand_right_sum = columns(feed, 0, hidden)
        shrink_left_sum = columns(feed, hidden, hidden).T
        triple_left_sum = joined(left).astype(F32).T
        quarter = width // 4
        expand_left_sum = joined(both[..., :quarter]).astype(F32).T
        output_right_sum = joined(both[..., quarter : 2 * quarter]).astype(F32)
        shrink_right_sum = joined(both[..., 2 * quarter : 3 * quarter]).astype(F32)
        norms = both[:, :, : width // LANES, 3 * quarter :].transpose(1, 0, 2, 3).reshape(4, width).astype(F32)
    return (
        block_output,
        input_gradient,
        norms[0],
        norms[1],
        norms[2],
        norms[3],
        triple_left_sum,
        triple_right_sum,
        output_left_sum,
        output_right_sum,
        expand_left_sum,
        expand_right_sum,
        shrink_left_sum,
        shrink_right_sum,
    )


def solution(mesh):
    placed = (
        P(("dp", "mp"), None),
        P("dp", None),
        P(),
        P(),
        P(),
        P(),
        P(None, "mp"),
        P(),
        P(),
        P("mp", None),
        P(),
        P(),
        P(None, "mp"),
        P(),
        P(),
        P("mp", None),
        P(),
        P(),
        P(("dp", "mp"), None),
    )
    return jax.shard_map(
        functools.partial(shards, mesh.shape["mp"], mesh.shape["dp"]),
        mesh=mesh,
        in_specs=placed,
        out_specs=(P(("dp", "mp"), None), P(("dp", "mp"), None)) + (P(),) * 12,
        check_vma=False,
    )
```

```python
import functools
import math

import jax
import jax.numpy as jnp
import numpy as np
from jax import lax
from jax.experimental import pallas as pl
from jax.experimental.pallas import tpu as pltpu
from jax.sharding import PartitionSpec as P

HEAD_DIM = 64
ROT = 16
SHORT = 512
TOK_GRP = 3072
SLOTS = 6
EPS = 1e-05
LANES = 128
MESH = pl.DeviceIdType.MESH
BF16 = jnp.bfloat16
F32 = jnp.float32
VMEM_LIMIT = 56 * 1024 * 1024
BRIEF = pl.CostEstimate(flops=1, bytes_accessed=1, transcendentals=0)


def dot_nn(former, latter):
    return lax.dot_general(
        former, latter, (((1,), (0,)), ((), ())), preferred_element_type=F32
    )


def dot_nt(former, latter):
    return lax.dot_general(
        former, latter, (((1,), (1,)), ((), ())), preferred_element_type=F32
    )


def dot_tn(former, latter):
    return lax.dot_general(
        former, latter, (((0,), (0,)), ((), ())), preferred_element_type=F32
    )


def find_flags(group_lengths):
    seq_ends = jnp.cumsum(group_lengths, dtype=jnp.int32)
    starts = seq_ends - group_lengths
    block_starts = jnp.arange(SLOTS, dtype=jnp.int32) * SHORT
    begins = jnp.any(
        (starts[None, :] == block_starts[:, None]) & (group_lengths[None, :] > 0), axis=1
    )
    return jnp.where(begins, 0, 1).astype(jnp.int32)


def rotary_tables():
    half = ROT // 2
    frequency = np.exp(
        np.arange(half, dtype=np.float32) * np.float32(-2.0 * math.log(10000.0) / ROT)
    ).astype(np.float32)
    angles = np.arange(2 * SHORT, dtype=np.float32)[:, None] * frequency[None, :]
    cosine = np.ones((2 * SHORT, LANES), np.float32)
    minus = np.zeros((2 * SHORT, LANES), np.float32)
    plus = np.zeros((2 * SHORT, LANES), np.float32)
    for base in range(0, LANES, HEAD_DIM):
        cosine[:, base : base + half] = np.cos(angles)
        cosine[:, base + half : base + ROT] = np.cos(angles)
        minus[:, base : base + half] = -np.sin(angles)
        plus[:, base + half : base + ROT] = np.sin(angles)
    return jnp.asarray(cosine), jnp.asarray(minus), jnp.asarray(plus)


def tall_tables():
    half = ROT // 2
    frequency = np.exp(
        np.arange(half, dtype=np.float32) * np.float32(-2.0 * math.log(10000.0) / ROT)
    ).astype(np.float32)
    angles = frequency[:, None] * np.arange(2 * SHORT, dtype=np.float32)[None, :]
    return jnp.asarray(np.cos(angles)), jnp.asarray(np.sin(angles))


def low_lanes():
    return lax.broadcasted_iota(jnp.int32, (1, LANES), 1) < HEAD_DIM


def rotate(pair, cosine, minus, plus):
    half = ROT // 2
    return (
        pair * cosine
        + pltpu.roll(pair, LANES - half, 1) * minus
        + pltpu.roll(pair, half, 1) * plus
    )


def unrotate(pair, cosine, minus, plus):
    half = ROT // 2
    return (
        pair * cosine
        - pltpu.roll(pair, LANES - half, 1) * minus
        - pltpu.roll(pair, half, 1) * plus
    )


def normalize(values, gain, shift):
    center = values - jnp.mean(values, axis=-1, keepdims=True)
    spread = jnp.mean(center * center, axis=-1, keepdims=True)
    return center * lax.rsqrt(spread + EPS) * gain + shift


def whole(shape):
    return pl.BlockSpec(
        shape, lambda *idx: (0,) * len(shape), pipeline_mode=pl.Buffered(1)
    )


def held(shape):
    return pl.BlockSpec(shape, lambda *idx: (0,) * len(shape))


def rows_of(tile, width):
    return pl.BlockSpec((tile, width), lambda i, *refs: (i, 0))


def shaped(shape, dtype):
    return jax.ShapeDtypeStruct(shape, dtype)


def params(semantics=1):
    return pltpu.CompilerParams(
        dimension_semantics=("arbitrary",) * semantics, vmem_limit_bytes=VMEM_LIMIT
    )


SUM_ROWS = (2, 4, 16)


class Net:
    def __init__(self):
        dp, mp = lax.axis_index("dp"), lax.axis_index("mp")
        self.half, self.core = mp // 2, lax.rem(mp, 2)
        self.x, self.z = lax.rem(dp, 2), dp // 2
        self.other_half, self.other_core, self.other_x = 1 - self.half, 1 - self.core, 1 - self.x
        self.x_peer = (dp + 1 - 2 * self.x, mp)
        self.y_peer = (dp, mp + 2 - 4 * self.half)
        self.core_peer = (dp, mp + 1 - 2 * self.core)
        self.z_places = [lax.rem(self.z + j, 4) for j in range(1, 4)]
        self.z_peers = [(place * 2 + self.x, mp) for place in self.z_places]
        self.started = []

    def copy(self, src, dst, sems, slot, peer):
        return pltpu.make_async_remote_copy(
            src_ref=src, dst_ref=dst, send_sem=sems.at[0, slot], recv_sem=sems.at[1, slot], device_id=peer,
            device_id_type=MESH,
        )

    def start(self, copies):
        for copy in copies:
            copy.start()
        self.started += copies


def arrive(copies):
    for copy in copies:
        copy.wait_recv()


def added(first, *others):
    total = first.astype(F32)
    for other in others:
        total = total + other.astype(F32)
    return total.astype(BF16)


def sum_scratch(order, size):
    one = (16, size)
    first = {"yxz": ((2, 4), (2, 4)), "xyz": ((2, 4), (2, 4)), "xz": ((4,), (4,)), "zx": ((3, 2), (2,))}[order]
    second = {"yxz": ((4,), (4,)), "xyz": ((4,), (4,)), "xz": ((3,), (1,)), "zx": ((1,), (1,))}[order]
    return [pltpu.VMEM(shape + one, BF16) for shape in (*first, *second, (3,), (2, 2, 4))] + [
        pltpu.SemaphoreType.DMA((2, 12))
    ]


def sum_chunk(net, order, source, scratch):
    got1, work1, got2, work2, got3, full, sems = scratch
    x, z, other_x = net.x, net.z, net.other_x
    own, rows, plane = full.at[0, x, z], full.at[0, x], full.at[0, :, z]

    def to_z(src, dst, slot):
        return [
            net.copy(src(place), dst(j), sems, slot + j, peer)
            for j, (place, peer) in enumerate(zip(net.z_places, net.z_peers))
        ]

    def one(src, dst, slot, peer):
        return [net.copy(src, dst, sems, slot, peer)]

    last = work1 if order == "xz" else work2
    if order != "xyz":
        over_y = one(full.at[0], full.at[1], 9, net.y_peer)
    if order == "zx":
        spread = to_z(lambda place: source.at[:, place], lambda j: got1.at[j], 2)
        cross = one(work1.at[other_x], got2.at[0], 0, net.x_peer)
        back = one(own, own, 8, net.x_peer)
        gather = to_z(lambda place: plane, lambda j: plane, 5)
    else:
        spread = to_z(lambda place: last.at[place], lambda j: got3.at[j], 2)
        gather = to_z(lambda place: own, lambda j: own, 5)
        if order == "yxz":
            first = one(source.at[1], got1, 0, net.y_peer)
            second = one(work1.at[other_x], got2, 1, net.x_peer)
        elif order == "xyz":
            first = one(source.at[:, other_x], got1, 0, net.x_peer)
            second = one(work1.at[1], got2, 1, net.y_peer)
            over_y = one(rows, full.at[1, x], 8, net.y_peer)
            over_x = one(full.at[:, x], full.at[:, x], 9, net.x_peer)
        else:
            first = one(source.at[other_x], got1, 0, net.x_peer)
        if order != "xyz":
            over_x = one(rows, rows, 8, net.x_peer)

    def begin(copies):
        return lambda: net.start(copies)

    def after(copies, work, then):
        def stage():
            arrive(copies)
            if work is not None:
                target, value = work
                target[...] = value()
            if then is not None:
                net.start(then)

        return stage

    if order == "zx":
        mine = (work1, lambda: added(source[:, z], got1[0], got1[1], got1[2]))
        total = (own, lambda: added(work1[x], got2[0]))
        return [
            begin(spread), after(spread, mine, cross), after(cross, total, back), after(back, None, gather),
            after(gather, None, over_y), after(over_y, None, None),
        ]
    total = (own, lambda: added(last[z], got3[0], got3[1], got3[2]))
    if order == "yxz":
        head = [begin(first), after(first, (work1, lambda: added(source[0], got1[...])), second)]
        head.append(after(second, (work2, lambda: added(work1[x], got2[...])), spread))
    elif order == "xyz":
        head = [begin(first), after(first, (work1, lambda: added(source[:, x], got1[...])), second)]
        head.append(after(second, (work2, lambda: added(work1[0], got2[...])), spread))
    else:
        head = [begin(first), after(first, (work1, lambda: added(source[x], got1[...])), spread)]
    one_way, other_way = (over_y, over_x) if order == "xyz" else (over_x, over_y)
    return head + [
        after(spread, total, gather), after(gather, None, one_way), after(one_way, None, other_way),
        after(other_way, None, None),
    ]


def sum_both(net, parts, both, got, total, core_sems, scratches):
    exchange = [net.copy(both.at[net.other_core], got, core_sems, 0, net.core_peer)]
    chunks, start = [], 0
    for (order, size), scratch in zip(parts, scratches):
        chunks.append(sum_chunk(net, order, total.at[:, :, :, :, pl.ds(start, size)], scratch))
        start += size

    def combine():
        arrive(exchange)
        for place, at in ((0, net.half), (1, net.other_half)):
            total[place] = added(both[net.core, at], got[at])
        for chunk in chunks:
            chunk[0]()

    def together(k):
        def stage():
            for chunk in chunks:
                if k < len(chunk):
                    chunk[k]()

        return stage

    longest = max(len(chunk) for chunk in chunks)
    return [lambda: net.start(exchange), combine] + [together(k) for k in range(1, longest)]


def both_scratch(parts):
    size = sum(part[1] for part in parts)
    return [
        pltpu.VMEM((2,) + SUM_ROWS + (size,), BF16),
        pltpu.VMEM((2,) + SUM_ROWS + (size,), BF16),
        pltpu.SemaphoreType.DMA((2, 1)),
    ] + [shape for part in parts for shape in sum_scratch(*part)]


def split_columns(size):
    count = (size // 2 + LANES - 1) // LANES * LANES
    return (("yxz", count), ("xyz", size - count))


def quarters(ref, *arrays):
    start = 0
    for array in arrays:
        size = array.shape[1] // 4
        for q in range(4):
            ref[q % 2, q // 2, :, start : start + size] = array[:, q * size : (q + 1) * size].astype(BF16)
        start += size


def gelu_parts(hidden):
    cdf = 0.5 + 0.5 * lax.erf(hidden * math.sqrt(0.5))
    density = jnp.exp(-0.5 * hidden * hidden) * (1.0 / math.sqrt(2.0 * math.pi))
    return hidden * cdf, cdf + hidden * density


def feed_core(rows, grads, up_ref, down_ref, act_ref, grad_ref, hidden_step):
    for start in range(0, up_ref.shape[1], hidden_step):
        cols = pl.ds(start, hidden_step)
        hidden = dot_nn(rows, up_ref[:, cols])
        grad_act = dot_nt(grads, down_ref[cols, :])
        activated, slope = gelu_parts(hidden)
        act_ref[:, cols] = activated.astype(BF16)
        grad_ref[:, cols] = (grad_act * slope).astype(BF16)


def shard_index(unit, far):
    return lax.rem(lax.axis_index("mp") + (unit if far else 0), 2 * unit)


def columns_of(ref, size, shard):
    return ref.at[:, pl.ds(pl.multiple_of(shard * size, size), size)]


def rows_at(ref, size, shard):
    return ref.at[pl.ds(pl.multiple_of(shard * size, size), size)]


def load(step, sems, pairs):
    copies = [pltpu.make_async_copy(src, dst, sems.at[j]) for j, (src, dst) in enumerate(pairs)]

    @pl.when(step == 0)
    def _():
        for copy in copies:
            copy.start()
        for copy in copies:
            copy.wait()


def head_weights(unit, triples, right, outputs, output_left, triple_ref, output_ref):
    width = triples[0].shape[0]
    head_width = outputs[0].shape[0]
    size = 3 * head_width
    pairs = []
    for j in range(2):
        shard = shard_index(unit, j == 1)
        cols, rows = pl.ds(j * size, size), pl.ds(j * head_width, head_width)
        pairs += [
            (triples[j], triple_ref.at[pl.ds(0, width), cols]),
            (columns_of(right, size, shard), triple_ref.at[pl.ds(width, LANES), cols]),
            (outputs[j], output_ref.at[rows, pl.ds(0, width)]),
            (rows_at(output_left, head_width, shard), output_ref.at[rows, pl.ds(width, LANES)]),
        ]
    return pairs


def chip_neighbours(unit):
    dp = lax.axis_index("dp")
    mp = lax.axis_index("mp")
    lead = lax.rem(dp, 2)
    return lead, (dp, lax.rem(mp + unit, 2 * unit)), (dp + 1 - 2 * lead, mp)


def leads():
    dp = lax.axis_index("dp")
    return lax.rem(dp, 2), lax.rem(dp // 2, 2)


def courier(unit, pairs, chunks, y_sems, x_sems):
    lead, y_peer, x_peer = chip_neighbours(unit)
    over_y, over_x = [], []
    for k in range(chunks):
        for j, (own, far) in enumerate(pairs):
            count = own.shape[0] // 2 // chunks
            span = pl.ds(pl.multiple_of((lead * chunks + k) * count, count), count)
            for src, sems, peer, group in ((own, y_sems, y_peer, over_y), (far, x_sems, x_peer, over_x)):
                group.append(
                    pltpu.make_async_remote_copy(
                        src_ref=src.at[span],
                        dst_ref=far.at[span],
                        send_sem=sems.at[0, k, j],
                        recv_sem=sems.at[1, k, j],
                        device_id=peer,
                        device_id_type=MESH,
                    )
                )
    return over_y, over_x


def meet(peers):
    barrier = pltpu.get_barrier_semaphore()
    for peer in peers:
        pl.semaphore_signal(barrier, inc=1, device_id=peer, device_id_type=MESH)
    pl.semaphore_wait(barrier, len(peers))


def place_in_unit(unit):
    mp = lax.axis_index("mp")
    return lax.rem(mp, unit), mp - lax.rem(mp, unit)


def unit_peers(unit):
    place, base = place_in_unit(unit)
    return [(lax.axis_index("dp"), base + lax.rem(place + unit - s, unit)) for s in range(1, unit)]


def halo_copies(unit, x_ref, halo_ref, y_sems, unit_sems):
    own_rows = x_ref.shape[0]
    chunk = math.gcd(own_rows, 128)
    dp = lax.axis_index("dp")
    found = []
    for k in range(SHORT // chunk):
        row = unit * own_rows - SHORT + k * chunk
        holder, start = row // own_rows, row % own_rows
        target = halo_ref.at[pl.ds(k * chunk, chunk)]
        over_y = pltpu.make_async_remote_copy(
            src_ref=x_ref.at[pl.ds(start, chunk)], dst_ref=target, send_sem=y_sems.at[0, k], recv_sem=y_sems.at[1, k],
            device_id=(dp, unit + holder), device_id_type=MESH,
        )
        spread = [
            pltpu.make_async_remote_copy(
                src_ref=target, dst_ref=target, send_sem=unit_sems.at[0, k, s - 1], recv_sem=unit_sems.at[1, k, s - 1],
                device_id=(dp, unit + (holder + s) % unit), device_id_type=MESH,
            )
            for s in range(1, unit)
        ]
        found.append((holder, over_y, spread))
    return found


def feed_first_kernel(
    unit, tile, x_ref, dy_ref, gain1_ref, shift1_ref, gain2_ref, shift2_ref, up_own_ref, up_left_ref, up_right_ref,
    down_own_ref, down_left_ref, output_right_ref, down_right_ref, x_all_ref, dy_all_ref, triple_ref, output_ref, normed1_ref,
    normed_ref, dy_full_ref, low_ref, grad_lows_ref, out_ref, grad_ref, low_act_ref, grad_low_ref, sums_ref,
    triple_far_ref, output_far_ref, halo_ref, up_half_ref, down_half_ref, act_ref, gh_ref, up_ref, down_ref, acc_ref,
    xs_ref, x_got_ref, dy_got_ref, y_sems, x_sems, unit_sems, halo_y_sems, halo_unit_sems, local_sems, load_sems,
):
    step = pl.program_id(0)
    width, hidden = up_own_ref.shape
    weights = (
        (up_own_ref, up_ref.at[pl.ds(0, width)]),
        (columns_of(up_right_ref, hidden, shard_index(unit, False)), up_ref.at[pl.ds(width, LANES)]),
        (down_own_ref, down_ref.at[:, pl.ds(0, width)]),
        (rows_at(down_left_ref, hidden, shard_index(unit, False)), down_ref.at[:, pl.ds(width, LANES)]),
    )
    own_rows = x_all_ref.shape[0]
    per_device = own_rows // tile
    steps = unit * per_device
    chunks = y_sems.shape[1]
    place, base = place_in_unit(unit)
    half = base // unit
    peers = unit_peers(unit)
    over_y, over_x = courier(
        unit, ((triple_ref, triple_far_ref), (output_ref, output_far_ref)), chunks, y_sems, x_sems
    )
    halo = halo_copies(unit, x_all_ref, halo_ref, halo_y_sems, halo_unit_sems)
    rows_out = [
        pltpu.make_async_remote_copy(
            src_ref=src, dst_ref=dst.at[j], send_sem=unit_sems.at[0, which, j], recv_sem=unit_sems.at[1, which, j],
            device_id=peer, device_id_type=MESH,
        )
        for j, peer in enumerate(peers)
        for which, (src, dst) in enumerate(((x_all_ref, x_got_ref), (dy_all_ref, dy_got_ref)))
    ]
    kept_halves = [
        pltpu.make_async_copy(
            src.at[
                pl.ds(pl.multiple_of(lead * dst.shape[0], dst.shape[0]), dst.shape[0]), pl.ds(0, dst.shape[1])
            ],
            dst,
            local_sems.at[j],
        )
        for j, (lead, src, dst) in enumerate(zip(leads(), (up_ref, down_ref), (up_half_ref, down_half_ref)))
    ]

    @pl.when(step == 0)
    def _():
        meet([*chip_neighbours(unit)[1:], *peers])
        for copy in rows_out + over_y:
            copy.start()

    for holder, copy, _ in halo:
        pl.when((step == 0) & (half == 0) & (place == holder))(copy.start)
    load(step, load_sems, weights)

    @pl.when(step == 0)
    def _():
        for copy in kept_halves:
            copy.start()
        xs_ref[...] = x_ref[...]
        dy_full_ref[...] = dy_ref[...]

    @pl.when((step > 0) & (step < per_device))
    def _():
        xs_ref[...] = x_ref[...]
        dy_full_ref[...] = dy_ref[...]

    for slot in range(unit - 1):

        @pl.when(step == per_device * (slot + 1))
        def _():
            for which in range(2):
                rows_out[2 * slot + which].wait_recv()

        @pl.when((step >= per_device * (slot + 1)) & (step < per_device * (slot + 2)))
        def _():
            span = pl.ds(pl.multiple_of((step - per_device * (slot + 1)) * tile, tile), tile)
            xs_ref[...] = x_got_ref[slot, span]
            dy_full_ref[...] = dy_got_ref[slot, span]

    for k in range(chunks):

        @pl.when(step == min(k + 1, steps - 1))
        def _():
            for j in (2 * k, 2 * k + 1):
                over_y[j].wait_recv()
                over_x[j].start()

    x = xs_ref[...].astype(F32)
    center = x - jnp.mean(x, axis=-1, keepdims=True)
    spread = jnp.mean(center * center, axis=-1, keepdims=True)
    scaled = center * lax.rsqrt(spread + EPS)
    normed1_ref[...] = (scaled * gain1_ref[...] + shift1_ref[...]).astype(BF16)
    normed = (scaled * gain2_ref[...] + shift2_ref[...]).astype(BF16)
    normed_ref[...] = normed
    dy = dy_full_ref[...]
    low = dot_nn(normed, up_left_ref[...]).astype(BF16)
    low_ref[...] = low
    rights = jnp.concatenate([output_right_ref[...], down_right_ref[...]], axis=0)
    grad_lows = dot_nt(dy, rights).astype(BF16)
    grad_lows_ref[...] = grad_lows
    grad_low = grad_lows[:, LANES:]
    feed_core(
        jnp.concatenate([normed, low], axis=1), jnp.concatenate([dy, grad_low], axis=1), up_ref, down_ref, act_ref,
        gh_ref, 512,
    )
    act = act_ref[...]
    gh = gh_ref[...]
    forward = dot_nn(act, down_ref[...])
    backward = dot_nt(gh, up_ref[...])
    out_ref[...], low_act_ref[...] = forward[:, :width], forward[:, width:]
    grad_ref[...], grad_low_ref[...] = backward[:, :width], backward[:, width:]

    @pl.when(step == 0)
    def _():
        acc_ref[...] = jnp.zeros_like(acc_ref)

    acc_ref[:, :hidden] += dot_tn(low, gh)
    acc_ref[:, hidden:] += dot_tn(grad_low, act)

    @pl.when((step == 0) & (half == 0))
    def _():
        fills = [
            pltpu.make_async_copy(xs_ref, halo_ref.at[pl.ds(k * tile, tile)], local_sems.at[2 + k])
            for k in range(SHORT // tile)
        ]
        for copy in fills:
            copy.start()
        for copy in fills:
            copy.wait()

    @pl.when(step == steps - 1)
    def _():
        sums_ref[...] = acc_ref[...].astype(BF16)
        for holder, copy, spread_copies in halo:

            @pl.when((half == 1) & (place == holder))
            def _():
                copy.wait_recv()
                for other in spread_copies:
                    other.start()

        for holder, copy, spread_copies in halo:
            pl.when((half == 0) & (place == holder))(copy.wait_send)

            @pl.when((half == 1) & (place == holder))
            def _():
                for other in spread_copies:
                    other.wait_send()

            for s in range(1, unit):
                pl.when((half == 1) & (place == (holder + s) % unit))(spread_copies[s - 1].wait_recv)
        for copy in rows_out + over_y:
            copy.wait_send()
        for copy in over_x + kept_halves:
            copy.wait()


def feed_first(unit, x, dy, norms, up, up_left, up_right, down, down_left, output_right, down_right, triple, output,
               tile):
    own_rows, width = x.shape
    rows = own_rows * unit
    hidden = up.shape[1]
    steps, per_device = rows // tile, own_rows // tile
    chunks = math.gcd(4, output.shape[0] // 32)
    halo_chunks = SHORT // math.gcd(own_rows, 128)
    anywhere = pl.BlockSpec(memory_space=pl.ANY)
    here = pl.BlockSpec((tile, width), lambda i: (jnp.minimum(i, per_device - 1), 0))

    def turned(size):
        def index(i):
            return (lax.rem(i + place_in_unit(unit)[0] * per_device, steps), 0)

        return pl.BlockSpec((tile, size), index)

    return pl.pallas_call(
        functools.partial(feed_first_kernel, unit, tile),
        grid=(steps,),
        in_specs=[here, here]
        + [whole((1, width))] * 4
        + [
            anywhere,
            whole(up_left.shape),
            anywhere,
            anywhere,
            anywhere,
            whole(output_right.shape),
            whole(down_right.shape),
        ]
        + [anywhere] * 4,
        out_specs=[
            turned(width),
            turned(width),
            turned(width),
            turned(LANES),
            turned(2 * LANES),
            turned(width),
            turned(width),
            turned(LANES),
            turned(LANES),
            held((LANES, 2 * hidden)),
        ]
        + [anywhere] * 5,
        scratch_shapes=[
            pltpu.VMEM((tile, hidden), BF16),
            pltpu.VMEM((tile, hidden), BF16),
            pltpu.VMEM((width + LANES, hidden), BF16),
            pltpu.VMEM((hidden, width + LANES), BF16),
            pltpu.VMEM((LANES, 2 * hidden), F32),
            pltpu.VMEM((tile, width), BF16),
            pltpu.VMEM((unit - 1, own_rows, width), BF16),
            pltpu.VMEM((unit - 1, own_rows, width), BF16),
            pltpu.SemaphoreType.DMA((2, chunks, 2)),
            pltpu.SemaphoreType.DMA((2, chunks, 2)),
            pltpu.SemaphoreType.DMA((2, 2, unit - 1)),
            pltpu.SemaphoreType.DMA((2, halo_chunks)),
            pltpu.SemaphoreType.DMA((2, halo_chunks, unit - 1)),
            pltpu.SemaphoreType.DMA((2 + SHORT // tile,)),
            pltpu.SemaphoreType.DMA((4,)),
        ],
        out_shape=[
            shaped((rows, width), BF16),
            shaped((rows, width), BF16),
            shaped((rows, width), BF16),
            shaped((rows, LANES), BF16),
            shaped((rows, 2 * LANES), BF16),
            shaped((rows, width), F32),
            shaped((rows, width), F32),
            shaped((rows, LANES), F32),
            shaped((rows, LANES), F32),
            shaped((LANES, 2 * hidden), BF16),
            shaped(triple.shape, BF16),
            shaped(output.shape, BF16),
            shaped((SHORT, width), BF16),
            shaped((up.shape[0] // 2, up.shape[1]), BF16),
            shaped((down.shape[0] // 2, down.shape[1]), BF16),
        ],
        compiler_params=pltpu.CompilerParams(
            dimension_semantics=("arbitrary",), vmem_limit_bytes=VMEM_LIMIT, collective_id=3, has_side_effects=True
        ),
        cost_estimate=BRIEF,
        name="feed_first",
    )(x, dy, *norms, up, up_left, up_right, down, down_left, output_right, down_right, x, dy, triple, output)


def feed_second_kernel(
    unit, tile, normed_ref, low_ref, dy_ref, grad_lows_ref, out_in_ref, grad_in_ref, low_act_in_ref, grad_low_in_ref,
    x_ref, keep_ref, got1_ref, gain1_ref, gain2_ref, output_right_ref, down_right_ref, up0_ref, up1_ref, up_left_ref,
    up_right_ref, down0_ref, down1_ref, down_left_ref, early_ref, heads_ref, left_ref, y_ref, dx_ref, sums_ref, both_ref,
    heads_out_ref, left_out_ref, act_ref, gh_ref, up_ref, down_ref, send_ref, got_ref, early_got_ref, acc_ref, norms_ref,
    output_right_grad_ref, down_right_grad_ref, up_left_grad_ref, sems, early_sems, out_sems, load_sems, *sum_refs,
):
    step = pl.program_id(0)
    own_rows = got_ref.shape[1]
    per_device = own_rows // tile
    send_tiles = (unit - 1) * per_device
    width, hidden = up_ref.shape[0] - LANES, up_ref.shape[1]
    shard = shard_index(unit, True)
    weights = [
        (columns_of(up_right_ref, hidden, shard), up_ref.at[pl.ds(width, LANES)]),
        (rows_at(down_left_ref, hidden, shard), down_ref.at[:, pl.ds(width, LANES)]),
    ]
    for lead, pieces, ref in zip(leads(), ((up0_ref, up1_ref), (down0_ref, down1_ref)), (up_ref, down_ref)):
        for place, piece in zip((lead, 1 - lead), pieces):
            weights.append((piece, rows_at(ref, piece.shape[0], place).at[:, pl.ds(0, piece.shape[1])]))
    peers = unit_peers(unit)
    copies = [
        [
            pltpu.make_async_remote_copy(
                src_ref=send_ref.at[s, pl.ds(t * tile, tile)], dst_ref=got_ref.at[s, pl.ds(t * tile, tile)],
                send_sem=sems.at[0, s, t], recv_sem=sems.at[1, s, t], device_id=peer, device_id_type=MESH,
            )
            for t in range(per_device)
        ]
        for s, peer in enumerate(peers)
    ]

    steps = unit * per_device
    y_peer = chip_neighbours(unit)[1]
    pieces = early_sems.shape[1]
    count = early_ref.shape[0] // pieces
    early_copies = [
        pltpu.make_async_remote_copy(
            src_ref=early_ref.at[pl.ds(j * count, count)], dst_ref=early_got_ref.at[pl.ds(j * count, count)],
            send_sem=early_sems.at[0, j], recv_sem=early_sems.at[1, j], device_id=y_peer, device_id_type=MESH,
        )
        for j in range(pieces)
    ]
    hosted = len(sum_refs) > 0
    if hosted:
        net = Net()
        size = heads_ref.shape[-1] // 2
        split = len(sum_scratch("yxz", size))
        heads_refs = (sum_refs[:split], sum_refs[split : 2 * split])
        left_refs = sum_refs[2 * split :]
        stages = [
            sum_chunk(net, order, heads_ref.at[:, :, :, :, pl.ds(j * size, size)], heads_refs[j])
            for j, order in enumerate(("yxz", "xyz"))
        ]
        stages.append(sum_both(net, (("yxz", left_ref.shape[-1]),), left_ref, *left_refs[:3], (left_refs[3:],)))

    def advance():
        if hosted:
            for at in range(steps):

                @pl.when(step == at)
                def _():
                    for stage in stages:
                        stage[at]()

    @pl.when(step == 0)
    def _():
        meet([*peers, y_peer] + ([net.x_peer, *net.z_peers] if hosted else []))
        for ref in (norms_ref, output_right_grad_ref, down_right_grad_ref, acc_ref, up_left_grad_ref):
            ref[...] = jnp.zeros_like(ref)

    advance()
    for j, copy in enumerate(early_copies):
        pl.when(step == min(j + 1, steps - 1))(copy.start)
    load(step, load_sems, weights)
    normed = normed_ref[...]
    low = low_ref[...]
    dy = dy_ref[...]
    grad_low = grad_lows_ref[:, LANES:]
    feed_core(
        jnp.concatenate([normed, low], axis=1), jnp.concatenate([dy, grad_low], axis=1), up_ref, down_ref, act_ref,
        gh_ref, 512,
    )
    act = act_ref[...]
    gh = gh_ref[...]
    forward = dot_nn(act, down_ref[...])
    backward = dot_nt(gh, up_ref[...])
    grad_low_up = (grad_low_in_ref[...] + backward[:, width:]).astype(BF16)
    out = out_in_ref[...] + forward[:, :width]
    low_act = low_act_in_ref[...] + forward[:, width:]
    second = grad_in_ref[...] + backward[:, :width] + dot_nt(grad_low_up, up_left_ref[...])
    acc_ref[:, :hidden] += dot_tn(low, gh)
    acc_ref[:, hidden:] += dot_tn(grad_low, act)
    up_left_grad_ref[...] += dot_tn(grad_low_up, normed)

    @pl.when(step < send_tiles)
    def _():
        slot = step // per_device
        span = pl.ds(pl.multiple_of(lax.rem(step, per_device) * tile, tile), tile)
        send_ref[slot, span, :width] = out.astype(BF16)
        send_ref[slot, span, width : 2 * width] = second.astype(BF16)
        send_ref[slot, span, 2 * width :] = low_act.astype(BF16)

    for s in range(unit - 1):
        for t in range(per_device):
            pl.when(step == s * per_device + t)(copies[s][t].start)
            pl.when(step == send_tiles + t)(copies[s][t].wait_recv)

    @pl.when(step >= send_tiles)
    def _():
        span = pl.ds(pl.multiple_of((step - send_tiles) * tile, tile), tile)
        first = keep_ref[:, :width].astype(F32)
        low_att = keep_ref[:, width:].astype(F32)
        total_out, total_second, total_low = out, second, low_act
        for s in range(unit - 1):
            first = first + got1_ref[s, :, :width].astype(F32)
            low_att = low_att + got1_ref[s, :, width:].astype(F32)
            total_out = total_out + got_ref[s, span, :width].astype(F32)
            total_second = total_second + got_ref[s, span, width : 2 * width].astype(F32)
            total_low = total_low + got_ref[s, span, 2 * width :].astype(F32)
        low_att, total_low = low_att.astype(BF16), total_low.astype(BF16)
        x = x_ref[...].astype(F32)
        y_ref[...] = (
            x + total_out + dot_nn(low_att, output_right_ref[...]) + dot_nn(total_low, down_right_ref[...])
        ).astype(BF16)
        center = x - jnp.mean(x, axis=-1, keepdims=True)
        spread = jnp.mean(center * center, axis=-1, keepdims=True)
        inverse = lax.rsqrt(spread + EPS)
        scaled = center * inverse
        total = first * gain1_ref[...] + total_second * gain2_ref[...]
        mean = jnp.mean(total, axis=-1, keepdims=True)
        inner = jnp.mean(total * scaled, axis=-1, keepdims=True)
        dx_ref[...] = dy.astype(F32) + (total - mean - scaled * inner) * inverse
        norms_ref[0:1, :] += jnp.sum(first * scaled, axis=0, keepdims=True)
        norms_ref[1:2, :] += jnp.sum(first, axis=0, keepdims=True)
        norms_ref[2:3, :] += jnp.sum(total_second * scaled, axis=0, keepdims=True)
        norms_ref[3:4, :] += jnp.sum(total_second, axis=0, keepdims=True)
        output_right_grad_ref[...] += dot_tn(low_att, dy)
        down_right_grad_ref[...] += dot_tn(total_low, dy)

    @pl.when(step == steps - 1)
    def _():
        for copy in early_copies:
            copy.wait()
        sums_ref[...] = (acc_ref[...] + early_got_ref[...].astype(F32)).astype(BF16)
        quarters(both_ref, up_left_grad_ref[...], output_right_grad_ref[...], down_right_grad_ref[...])
        start = 3 * (width // 4)
        count = width // LANES
        for q in range(4):
            rows = [norms_ref[q : q + 1, j * LANES : (j + 1) * LANES] for j in range(count)]
            block = jnp.concatenate([*rows, jnp.zeros((LANES - count, LANES), F32)], axis=0)
            both_ref[q % 2, q // 2, :, start:] = block.astype(BF16)
        for group in copies:
            for copy in group:
                copy.wait_send()
        if hosted:
            for at in range(steps, max(len(stage) for stage in stages)):
                for stage in stages:
                    if at < len(stage):
                        stage[at]()
            outs = []
            for j, refs in enumerate((*heads_refs, left_refs[3:])):
                full = refs[5]
                target = left_out_ref if j == 2 else heads_out_ref.at[:, :, :, :, pl.ds(j * size, size)]
                outs.append(pltpu.make_async_copy(full, target, out_sems.at[j]))
                outs[-1].start()
            for copy in net.started:
                copy.wait_send()
            for copy in outs:
                copy.wait()


def feed_second(unit, normed, low, dy, grad_lows, out, grad, low_act, grad_low, x, keep, got, gains, output_right,
                down_right, ups, up_left, up_right, downs, down_left, early, heads, left, hosted, tile):
    rows, width = normed.shape
    own_rows = rows // unit
    anywhere = pl.BlockSpec(memory_space=pl.ANY)
    extra = []
    if hosted:
        heads = heads.reshape((2,) + SUM_ROWS + heads.shape[-1:])
        left = left.reshape((2, 2) + SUM_ROWS + left.shape[-1:])
        extra = sum_scratch("yxz", heads.shape[-1] // 2) + sum_scratch("xyz", heads.shape[-1] // 2)
        extra += both_scratch((("yxz", left.shape[-1]),))
    hidden = ups[0].shape[1]
    steps, per_device = rows // tile, own_rows // tile
    send_tiles = steps - per_device
    wide = 2 * width + LANES

    def turned(size):
        def index(i):
            place, slot = place_in_unit(unit)[0], i // per_device + 1
            return (lax.rem(place + unit - slot, unit) * per_device + lax.rem(i, per_device), 0)

        return pl.BlockSpec((tile, size), index)

    def late(size):
        return pl.BlockSpec((tile, size), lambda i: (jnp.maximum(i - send_tiles, 0), 0))

    return pl.pallas_call(
        functools.partial(feed_second_kernel, unit, tile),
        grid=(steps,),
        in_specs=[
            turned(width),
            turned(LANES),
            turned(width),
            turned(2 * LANES),
            turned(width),
            turned(width),
            turned(LANES),
            turned(LANES),
            late(width),
            late(width + LANES),
            pl.BlockSpec((unit - 1, tile, width + LANES), lambda i: (0, jnp.maximum(i - send_tiles, 0), 0)),
            whole((1, width)),
            whole((1, width)),
            whole(output_right.shape),
            whole(down_right.shape),
            anywhere,
            anywhere,
            whole(up_left.shape),
            anywhere,
            anywhere,
            anywhere,
            anywhere,
            whole(early.shape),
            whole(heads.shape),
            whole(left.shape),
        ],
        out_specs=[
            late(width),
            late(width),
            held((LANES, 2 * hidden)),
            held((2, 2, LANES, 3 * (width // 4) + LANES)),
            anywhere,
            anywhere,
        ],
        scratch_shapes=[
            pltpu.VMEM((tile, hidden), BF16),
            pltpu.VMEM((tile, hidden), BF16),
            pltpu.VMEM((width + LANES, hidden), BF16),
            pltpu.VMEM((hidden, width + LANES), BF16),
            pltpu.VMEM((unit - 1, own_rows, wide), BF16),
            pltpu.VMEM((unit - 1, own_rows, wide), BF16),
            pltpu.VMEM((LANES, 2 * hidden), BF16),
            pltpu.VMEM((LANES, 2 * hidden), F32),
            pltpu.VMEM((8, width), F32),
            pltpu.VMEM((LANES, width), F32),
            pltpu.VMEM((LANES, width), F32),
            pltpu.VMEM((LANES, width), F32),
            pltpu.SemaphoreType.DMA((2, unit - 1, per_device)),
            pltpu.SemaphoreType.DMA((2, 4)),
            pltpu.SemaphoreType.DMA((3,)),
            pltpu.SemaphoreType.DMA((6,)),
        ]
        + extra,
        out_shape=[
            shaped((own_rows, width), BF16),
            shaped((own_rows, width), F32),
            shaped((LANES, 2 * hidden), BF16),
            shaped((2, 2, LANES, 3 * (width // 4) + LANES), BF16),
            shaped(heads.shape, BF16),
            shaped(left.shape[1:] if hosted else left.shape, BF16),
        ],
        compiler_params=pltpu.CompilerParams(
            dimension_semantics=("arbitrary",), vmem_limit_bytes=VMEM_LIMIT, collective_id=4, has_side_effects=True
        ),
        cost_estimate=BRIEF,
        name="feed_second",
    )(normed, low, dy, grad_lows, out, grad, low_act, grad_low, x, keep, got, *gains, output_right, down_right, *ups,
      up_left, up_right, *downs, down_left, early, heads, left)


def project_kernel(
    unit, main_tiles, halo_ref, normed_ref, dy_ref, grad_lows_ref, late_ref, cos0_ref, cos1_ref, minus0_ref, minus1_ref, plus0_ref,
    plus1_ref, gain_ref, shift_ref, triple0_ref, triple1_ref, left_ref, right_ref, output0_ref, output1_ref,
    output_left_ref, low_ref, q_ref, k_ref, v_ref, g_ref, triple_ref, output_ref, load_sems,
):
    step = pl.program_id(0)
    load(
        step, load_sems,
        head_weights(
            unit, (triple0_ref, triple1_ref), right_ref, (output0_ref, output1_ref), output_left_ref, triple_ref,
            output_ref,
        ),
    )

    later = late_ref[0, 0:1, :] > 0.0
    tables = tuple(
        jnp.where(later, two[...], one[...])
        for one, two in ((cos0_ref, cos1_ref), (minus0_ref, minus1_ref), (plus0_ref, plus1_ref))
    )
    head_width = output0_ref.shape[0]
    first = low_lanes()

    def rows(normed, full):
        low = dot_nn(normed, left_ref[...]).astype(BF16)
        if full:
            low_ref[...] = low
        mixed = dot_nn(jnp.concatenate([normed, low], axis=1), triple_ref[...])
        if full:
            grads = jnp.concatenate([dy_ref[...], grad_lows_ref[:, :LANES]], axis=1)
            g_ref[...] = dot_nt(grads, output_ref[...]).astype(BF16)
        for pair in range(2 * head_width // LANES):
            one, two, three = (
                mixed[:, (3 * pair + part) * LANES : (3 * pair + part + 1) * LANES] for part in range(3)
            )
            cols = pl.ds(pair * LANES, LANES)
            key = pltpu.roll(jnp.where(first, three, one), HEAD_DIM, 1)
            k_ref[:, cols] = rotate(key, *tables).astype(BF16)
            v_ref[:, cols] = jnp.where(first, two, three).astype(BF16)
            if full:
                query = rotate(jnp.where(first, one, two), *tables).astype(BF16)
                q_ref[:, cols] = query * HEAD_DIM**-0.5

    @pl.when(step < main_tiles)
    def _():
        rows(normed_ref[...], True)

    @pl.when(step >= main_tiles)
    def _():
        rows(normalize(halo_ref[...].astype(F32), gain_ref[...], shift_ref[...]).astype(BF16), False)


def project(unit, conts, x_halo, normed, dy, grad_lows, gain, shift, triples, left, right, outputs, output_left, tables,
            tile):
    rows, width = dy.shape
    head_width = outputs[0].shape[0]
    anywhere = pl.BlockSpec(memory_space=pl.ANY)
    per_block = SHORT // tile
    main_tiles, halo_tiles = rows // tile, SHORT // tile
    late = jnp.concatenate([jnp.repeat(conts, per_block), jnp.zeros((halo_tiles,), jnp.int32)])
    late = jnp.broadcast_to(late.astype(F32)[:, None, None], (main_tiles + halo_tiles, 8, LANES))

    halo = pl.BlockSpec((tile, width), lambda i: (jnp.maximum(i - main_tiles, 0), 0))

    def table(which):
        return pl.BlockSpec((tile, LANES), lambda i: (which * per_block + lax.rem(i, per_block), 0))

    def main(size):
        return pl.BlockSpec((tile, size), lambda i: (jnp.minimum(i, main_tiles - 1), 0))

    def all_rows(size):
        return pl.BlockSpec((tile, size), lambda i: (jnp.where(i < main_tiles, i + halo_tiles, i - main_tiles), 0))

    return pl.pallas_call(
        functools.partial(project_kernel, unit, main_tiles),
        grid=(main_tiles + halo_tiles,),
        in_specs=[
            halo,
            main(width),
            main(width),
            main(2 * LANES),
            pl.BlockSpec((1, 8, LANES), lambda i: (i, 0, 0)),
            table(0),
            table(1),
            table(0),
            table(1),
            table(0),
            table(1),
            whole(gain.shape),
            whole(shift.shape),
            anywhere,
            anywhere,
            whole(left.shape),
            anywhere,
            anywhere,
            anywhere,
            anywhere,
        ],
        out_specs=[
            main(LANES),
            main(2 * head_width),
            all_rows(2 * head_width),
            all_rows(2 * head_width),
            main(2 * head_width),
        ],
        scratch_shapes=[
            pltpu.VMEM((width + LANES, 6 * head_width), BF16),
            pltpu.VMEM((2 * head_width, width + LANES), BF16),
            pltpu.SemaphoreType.DMA((8,)),
        ],
        out_shape=[
            shaped((rows, LANES), BF16),
            shaped((rows, 2 * head_width), BF16),
            shaped((SHORT + rows, 2 * head_width), BF16),
            shaped((SHORT + rows, 2 * head_width), BF16),
            shaped((rows, 2 * head_width), BF16),
        ],
        compiler_params=params(),
        cost_estimate=BRIEF,
        name="project",
    )(x_halo, normed, dy, grad_lows, late, *[table for table in tables for _ in range(2)], gain, shift, *triples, left, right,
      *outputs, output_left)


def attend_rows(with_prev, pairs, count, allowed, q_ref, k_ref, v_ref, g_ref, kp_ref, vp_ref, tables, att_ref, gq_ref,
                dk_ref, dv_ref, dkp_ref, dvp_ref):
    first = low_lanes()
    zero = jnp.zeros((), BF16)

    def stack(pair):
        return jnp.concatenate([jnp.where(first, pair, zero), jnp.where(first, zero, pair)], axis=0)

    def unstack(both):
        return jnp.where(first, both[:count], both[count:])

    def joined(fold, values):
        return functools.reduce(fold, values)

    pieces = []
    for lanes in pairs:
        for start in range(0, SHORT, count):
            span = pl.ds(start, count)
            parts = []
            if with_prev:
                parts.append((kp_ref[:, lanes], vp_ref[:, lanes], dkp_ref, dvp_ref, pl.ds(0, SHORT)))
            if start:
                before = pl.ds(0, start)
                parts.append((k_ref[before, lanes], v_ref[before, lanes], dk_ref, dv_ref, before))
            parts.append((k_ref[span, lanes], v_ref[span, lanes], dk_ref, dv_ref, span))
            pieces.append((lanes, span, stack(q_ref[span, lanes]), stack(g_ref[span, lanes]), parts))

    scores, grads, weights, lows, inners, slopes = [], [], [], [], [], []
    for _, _, queries, _, parts in pieces:
        found = [dot_nt(queries, part[0]) for part in parts]
        scores.append(found[:-1] + [jnp.where(allowed, found[-1], -1e30)])
    for _, _, _, grad, parts in pieces:
        grads.append([dot_nt(grad, part[1]) for part in parts])
    for found in scores:
        peak = joined(jnp.maximum, [jnp.max(score, axis=1, keepdims=True) for score in found])
        exps = [jnp.exp(score - peak) for score in found]
        scale = 1.0 / joined(jnp.add, [jnp.sum(exp, axis=1, keepdims=True) for exp in exps])
        weights.append([exp * scale for exp in exps])
        lows.append([weight.astype(BF16) for weight in weights[-1]])
    for (lanes, span, _, grad, parts), low in zip(pieces, lows):
        attended = joined(jnp.add, [dot_nn(weight, part[1]) for weight, part in zip(low, parts)])
        att_ref[span, lanes] = unstack(attended).astype(BF16)
        inners.append(jnp.sum(attended * grad.astype(F32), axis=1, keepdims=True))
    for weight, grad, inner in zip(weights, grads, inners):
        slopes.append([(w * (g - inner)).astype(BF16) for w, g in zip(weight, grad)])
    for (lanes, span, queries, grad, parts), low, slope in zip(pieces, lows, slopes):
        grad_query = joined(jnp.add, [dot_nn(ds, part[0]) for ds, part in zip(slope, parts)])
        for ds, weight, (_, _, to_key, to_value, rows) in zip(slope, low, parts):
            to_key[lanes, rows] += dot_tn(queries, ds)
            to_value[lanes, rows] += dot_tn(grad, weight)
        grad_query = unstack(grad_query) * HEAD_DIM**-0.5
        gq_ref[span, lanes] = unrotate(grad_query, *[table[span] for table in tables]).astype(BF16)


def unrotate_tall(ref, lanes, cosine, sine):
    half = ROT // 2
    value = ref[lanes, :]
    halves = []
    for base in (HEAD_DIM, 0):
        one, two = value[base : base + half], value[base + half : base + ROT]
        halves += [one * cosine + two * sine, two * cosine - one * sine, value[base + ROT : base + HEAD_DIM]]
    return jnp.concatenate(halves, axis=0).astype(BF16).T


def attend_kernel(
    blocks, pairs, count, conts_ref, q_ref, k_ref, v_ref, g_ref, kp_ref, vp_ref, cos_ref, minus_ref, plus_ref,
    tall_cos_ref, tall_sin_ref, att_ref, gq_ref, gk_ref, gv_ref, halo_ref, dk_ref, dv_ref,
):
    step = pl.program_id(0)
    block = blocks - 1 - step
    continued = conts_ref[block]
    offset = pl.multiple_of(continued * SHORT, SHORT)
    tables = tuple(ref.at[pl.ds(offset, SHORT)] for ref in (cos_ref, minus_ref, plus_ref))
    now = lax.rem(step, 2)
    own = (dk_ref.at[now], dv_ref.at[now])
    before = (dk_ref.at[1 - now], dv_ref.at[1 - now])

    @pl.when(step == 0)
    def _():
        for ref in own:
            ref[...] = jnp.zeros_like(ref)

    for ref in before:
        ref[...] = jnp.zeros_like(ref)
    row = lax.broadcasted_iota(jnp.int32, (2 * count, count), 0)
    column = lax.broadcasted_iota(jnp.int32, (2 * count, count), 1)
    allowed = column <= jnp.where(row >= count, row - count, row)
    args = (q_ref, k_ref, v_ref, g_ref, kp_ref, vp_ref, tables, att_ref, gq_ref, *own, *before)

    def each(some, work):
        some = math.gcd(some, pairs)

        def body(i, carry):
            work([pl.ds(pl.multiple_of((i * some + j) * LANES, LANES), LANES) for j in range(some)])
            return carry

        lax.fori_loop(0, pairs // some, body, 0)

    pl.when(continued == 0)(lambda: each(2, lambda lanes: attend_rows(False, lanes, count, allowed, *args)))
    pl.when(continued != 0)(lambda: each(2, lambda lanes: attend_rows(True, lanes, count, allowed, *args)))
    turn = tuple(ref.at[:, pl.ds(offset, SHORT)] for ref in (tall_cos_ref, tall_sin_ref))

    def leave(lanes):
        for pair in lanes:
            gk_ref[:, pair] = unrotate_tall(own[0], pair, *[ref[...] for ref in turn])
            gv_ref[:, pair] = own[1][pair, :].astype(BF16).T

    each(1, leave)

    @pl.when(block == 0)
    def _():
        base = tuple(ref.at[:, pl.ds(0, SHORT)] for ref in (tall_cos_ref, tall_sin_ref))

        def leave_halo(lanes):
            for pair in lanes:
                halo_ref[0, :, pair] = unrotate_tall(before[0], pair, *[ref[...] for ref in base])
                halo_ref[1, :, pair] = before[1][pair, :].astype(BF16).T

        each(1, leave_halo)


def attend(conts, q, k, v, g, tables, tall, count):
    rows, head_width = q.shape
    blocks = rows // SHORT
    here = pl.BlockSpec((SHORT, head_width), lambda i, conts: (blocks - 1 - i, 0))
    after = pl.BlockSpec((SHORT, head_width), lambda i, conts: (blocks - i, 0))
    return pl.pallas_call(
        functools.partial(attend_kernel, blocks, head_width // LANES, count),
        grid_spec=pltpu.PrefetchScalarGridSpec(
            num_scalar_prefetch=1,
            grid=(blocks,),
            in_specs=[here, after, after, here, here, here] + [whole(table.shape) for table in (*tables, *tall)],
            out_specs=[here] * 4 + [held((2, SHORT, head_width))],
            scratch_shapes=[pltpu.VMEM((2, head_width, SHORT), F32)] * 2,
        ),
        out_shape=[shaped((rows, head_width), BF16)] * 4 + [shaped((2, SHORT, head_width), BF16)],
        compiler_params=params(),
        cost_estimate=BRIEF,
        name="attend",
    )(conts, q, k, v, g, k, v, *tables, *tall)


def settle_kernel(
    unit, tile, normed_ref, low_ref, grad_lows_ref, out_in_ref, att_ref, gq_ref, gk_ref, gv_ref, halo_ref, triple0_ref,
    triple1_ref, left_ref, output0_ref, output1_ref, right_ref, output_left_ref, out_ref, keep_ref, heads_ref,
    left_sums_ref, got_ref, send_ref, halo_got_ref, key_ref, value_ref, mixed_ref, triple_ref, output_ref, acc_ref,
    out_acc_ref, left_grad_ref, halo_sems, sems, load_sems,
):
    step = pl.program_id(0)
    per_device = got_ref.shape[1] // tile
    steps = unit * per_device
    halo_start = steps - SHORT // tile
    place, base = place_in_unit(unit)
    half = base // unit
    peers = unit_peers(unit)
    y_peer = chip_neighbours(unit)[1]
    halo_copies = []
    for j in range(SHORT // tile):
        part = pl.ds(j * tile, tile)
        halo_copies.append(
            pltpu.make_async_remote_copy(
                src_ref=halo_ref.at[:, part], dst_ref=halo_got_ref.at[:, part], send_sem=halo_sems.at[0, j],
                recv_sem=halo_sems.at[1, j], device_id=y_peer, device_id_type=MESH,
            )
        )
    copies = [
        [
            pltpu.make_async_remote_copy(
                src_ref=send_ref.at[s, pl.ds(t * tile, tile)], dst_ref=got_ref.at[s, pl.ds(t * tile, tile)],
                send_sem=sems.at[0, s, t], recv_sem=sems.at[1, s, t], device_id=peer, device_id_type=MESH,
            )
            for t in range(per_device)
        ]
        for s, peer in enumerate(peers)
    ]
    @pl.when(step == 0)
    def _():
        meet([y_peer, *peers])

        @pl.when(half == 1)
        def _():
            for copy in halo_copies:
                copy.start()

        for ref in (acc_ref, out_acc_ref, left_grad_ref):
            ref[...] = jnp.zeros_like(ref)

    load(
        step, load_sems,
        head_weights(
            unit, (triple0_ref, triple1_ref), right_ref, (output0_ref, output1_ref), output_left_ref, triple_ref,
            output_ref,
        ),
    )

    key_ref[...], value_ref[...] = gk_ref[...], gv_ref[...]
    for j, copy in enumerate(halo_copies):

        @pl.when((half == 0) & (step == halo_start + j))
        def _():
            copy.wait_recv()
            rows = pl.ds(j * tile, tile)
            count = output0_ref.shape[0]
            for ref, which in ((key_ref, 0), (value_ref, 1)):
                for here, there in ((pl.ds(0, count), pl.ds(count, count)), (pl.ds(count, count), pl.ds(0, count))):
                    ref[:, here] = (ref[:, here].astype(F32) + halo_got_ref[which, rows, there].astype(F32)).astype(BF16)

    normed = normed_ref[...]
    low = low_ref[...]
    grad_low_out = grad_lows_ref[:, :LANES]
    head_width = output0_ref.shape[0]
    first = low_lanes()
    for pair in range(2 * head_width // LANES):
        q, k, v = (ref[:, pair * LANES : (pair + 1) * LANES] for ref in (gq_ref, key_ref, value_ref))
        for part, value in enumerate((jnp.where(first, q, k), jnp.where(first, v, q), jnp.where(first, k, v))):
            mixed_ref[:, (3 * pair + part) * LANES : (3 * pair + part + 1) * LANES] = value
    mixed = mixed_ref[...]
    att = att_ref[...]
    width = normed.shape[1]
    backward = dot_nt(mixed, triple_ref[...])
    forward = dot_nn(att, output_ref[...])
    grad_low = backward[:, width:].astype(BF16)
    grad = (backward[:, :width] + dot_nt(grad_low, left_ref[...])).astype(BF16)
    out_ref[...] = out_in_ref[...] + forward[:, :width]
    low_att = forward[:, width:].astype(BF16)

    @pl.when(step // per_device == place)
    def _():
        keep_ref[:, :width] = grad
        keep_ref[:, width:] = low_att

    span = pl.ds(pl.multiple_of(lax.rem(step, per_device) * tile, tile), tile)
    for s in range(unit - 1):
        owner = lax.rem(place + unit - (s + 1), unit)

        @pl.when(step // per_device == owner)
        def _():
            send_ref[s, span, :width] = grad
            send_ref[s, span, width:] = low_att

        for t in range(per_device):
            pl.when(step == owner * per_device + t)(copies[s][t].start)

    acc_ref[...] += dot_tn(low, mixed)
    out_acc_ref[...] += dot_tn(grad_low_out, att)
    left_grad_ref[...] += dot_tn(grad_low, normed)

    @pl.when(step == steps - 1)
    def _():
        size = 3 * head_width
        for j in range(2):
            heads_ref[j, :, :size] = acc_ref[:, j * size : (j + 1) * size].astype(BF16)
            heads_ref[j, :, size:] = out_acc_ref[:, j * head_width : (j + 1) * head_width].astype(BF16)
        quarters(left_sums_ref, left_grad_ref[...])

        @pl.when(half == 1)
        def _():
            for copy in halo_copies:
                copy.wait_send()

        for group in copies:
            for copy in group:
                copy.wait()


def settle(unit, normed, low, grad_lows, out, heads, halo, triples, left, outputs, right, output_left, tile):
    rows, width = normed.shape
    own_rows = rows // unit
    head_width = outputs[0].shape[0]
    steps, per_device = rows // tile, own_rows // tile
    anywhere = pl.BlockSpec(memory_space=pl.ANY)

    def kept(i):
        return (jnp.clip(i - place_in_unit(unit)[0] * per_device, 0, per_device - 1), 0)

    return pl.pallas_call(
        functools.partial(settle_kernel, unit, tile),
        grid=(steps,),
        in_specs=[rows_of(tile, width), rows_of(tile, LANES), rows_of(tile, 2 * LANES), rows_of(tile, width)]
        + [rows_of(tile, 2 * head_width)] * 4
        + [anywhere]
        + [anywhere, anywhere, whole(left.shape), anywhere, anywhere, anywhere, anywhere],
        out_specs=[
            rows_of(tile, width),
            pl.BlockSpec((tile, width + LANES), kept),
            held((2, LANES, 4 * head_width)),
            held((2, 2, LANES, width // 4)),
            anywhere,
        ],
        scratch_shapes=[
            pltpu.VMEM((unit - 1, own_rows, width + LANES), BF16),
            pltpu.VMEM((2, SHORT, 2 * head_width), BF16),
            pltpu.VMEM((tile, 2 * head_width), BF16),
            pltpu.VMEM((tile, 2 * head_width), BF16),
            pltpu.VMEM((tile, 6 * head_width), BF16),
            pltpu.VMEM((width + LANES, 6 * head_width), BF16),
            pltpu.VMEM((2 * head_width, width + LANES), BF16),
            pltpu.VMEM((LANES, 6 * head_width), F32),
            pltpu.VMEM((LANES, 2 * head_width), F32),
            pltpu.VMEM((LANES, width), F32),
            pltpu.SemaphoreType.DMA((2, SHORT // tile)),
            pltpu.SemaphoreType.DMA((2, unit - 1, per_device)),
            pltpu.SemaphoreType.DMA((8,)),
        ],
        out_shape=[
            shaped((rows, width), F32),
            shaped((own_rows, width + LANES), BF16),
            shaped((2, LANES, 4 * head_width), BF16),
            shaped((2, 2, LANES, width // 4), BF16),
            shaped((unit - 1, own_rows, width + LANES), BF16),
        ],
        compiler_params=pltpu.CompilerParams(
            dimension_semantics=("arbitrary",), vmem_limit_bytes=VMEM_LIMIT, collective_id=5, has_side_effects=True
        ),
        cost_estimate=BRIEF,
        name="settle",
    )(normed, low, grad_lows, out, *heads, halo, *triples, left, *outputs, right, output_left)


FEED_ORDERS = ("xz", "zx", "xz", "zx")


def sum_kernel(size, feed_ref, both_ref, heads_ref, left_ref, feed_out_ref, both_out_ref, heads_out_ref, left_out_ref,
               cross_sems, local_sems, *refs):
    net = Net()
    meet([net.x_peer, net.y_peer, net.core_peer, *net.z_peers])
    locals_, crossing = [], []

    def hand_over(slot, full, out, first, second):
        for place, at in ((0, first), (1, second)):
            target = out.at[net.core, at]
            local = pltpu.make_async_copy(full.at[place], target, local_sems.at[slot, place])
            local.start()
            locals_.append(local)
            crossing.append(net.copy(full.at[place], target, cross_sems, 2 * slot + place, net.core_peer))
            net.start(crossing[-1:])

    split = len(sum_scratch("xz", size))
    feed_refs = [refs[j * split : (j + 1) * split] for j in range(len(FEED_ORDERS))]
    both_refs = refs[len(FEED_ORDERS) * split :]
    parts = split_columns(both_ref.shape[-1])
    per_part = (len(both_refs) - 3) // 2
    scratches = (both_refs[3 : 3 + per_part], both_refs[3 + per_part :])
    running = [sum_both(net, parts, both_ref, *both_refs[:3], scratches)]
    running += [
        sum_chunk(net, order, feed_ref.at[:, :, :, pl.ds(j * size, size)], feed_refs[j])
        for j, order in enumerate(FEED_ORDERS)
    ]

    def both_done():
        start = 0
        for j, (_, count) in enumerate(parts):
            columns = both_out_ref.at[:, :, :, :, :, pl.ds(start, count)]
            hand_over(j, scratches[j][5], columns, net.half, net.other_half)
            start += count

    def feed_done(j):
        columns = feed_out_ref.at[:, :, :, :, :, pl.ds(j * size, size)]
        hand_over(4 + j, feed_refs[j][5], columns, net.other_half, net.half)

    for k in range(max(len(stage) for stage in running)):
        for j, stage in enumerate(running):
            if k < len(stage):
                stage[k]()
            if k == len(stage) - 1:
                both_done() if j == 0 else feed_done(j - 1)
        if k == 0:
            hand_over(2, heads_ref, heads_out_ref, net.half, net.other_half)
            hand_over(3, left_ref, left_out_ref, net.half, net.other_half)
    for copy in locals_:
        copy.wait()
    for copy in crossing:
        copy.wait_recv()
    for copy in net.started:
        copy.wait_send()


def sum_all(feed, both, heads, left):
    arrays = (feed.reshape(SUM_ROWS + feed.shape[-1:]), both.reshape((2, 2) + SUM_ROWS + both.shape[-1:]), heads, left)
    size = feed.shape[-1] // len(FEED_ORDERS)
    slots = 4 + len(FEED_ORDERS)
    outs = [shaped((2, 2) + SUM_ROWS + array.shape[-1:], BF16) for array in arrays]
    results = pl.pallas_call(
        functools.partial(sum_kernel, size),
        out_shape=outs,
        in_specs=[pl.BlockSpec(memory_space=pltpu.VMEM)] * 4,
        out_specs=[pl.BlockSpec(memory_space=pl.ANY)] * 4,
        scratch_shapes=[pltpu.SemaphoreType.DMA((2, 2 * slots)), pltpu.SemaphoreType.DMA((slots, 2))]
        + [shape for order in FEED_ORDERS for shape in sum_scratch(order, size)]
        + both_scratch(split_columns(both.shape[-1])),
        compiler_params=pltpu.CompilerParams(
            collective_id=2, has_side_effects=True, vmem_limit_bytes=VMEM_LIMIT
        ),
        cost_estimate=BRIEF,
        name="sum_all",
    )(*arrays)
    return [value.reshape(2, 2, LANES, value.shape[-1]) for value in results]


def unpack_kernel(triple_width, feed_ref, both_ref, heads_ref, left_ref, triple_ref, output_ref, up_ref, down_ref,
                  triple_left_ref, up_left_ref, output_right_ref, down_right_ref, *norm_refs):
    triple_ref[...] = heads_ref[0, 0, :, :triple_width].astype(F32)
    output_ref[...] = heads_ref[0, 0, :, triple_width:].astype(F32).T
    hidden = up_ref.shape[1]
    up_ref[...] = feed_ref[0, 0, :, :hidden].astype(F32)
    down_ref[...] = feed_ref[0, 0, :, hidden:].astype(F32).T
    size = triple_left_ref.shape[0]
    triple_left_ref[...] = left_ref[0, 0].astype(F32).T
    up_left_ref[...] = both_ref[0, 0, :, :size].astype(F32).T
    output_right_ref[...] = both_ref[0, 0, :, size : 2 * size].astype(F32)
    down_right_ref[...] = both_ref[0, 0, :, 2 * size : 3 * size].astype(F32)
    for q, ref in enumerate(norm_refs):

        @pl.when(pl.program_id(0) == q)
        def _():
            ref[...] = both_ref[0, 0, : ref.shape[0], 3 * size :].astype(F32)


def unpack(feed, both, heads, left, triple_width):
    arrays = (feed, both, heads, left)
    hidden, quarter = feed.shape[-1] // 2, left.shape[-1]
    width, head_width = 4 * quarter, heads.shape[-1] - triple_width

    def tall(rows):
        return pl.BlockSpec((rows, LANES), lambda s: (s, 0))

    def wide(cols):
        return pl.BlockSpec((LANES, cols), lambda s: (0, s))

    return pl.pallas_call(
        functools.partial(unpack_kernel, triple_width),
        grid=(4,),
        in_specs=[
            pl.BlockSpec((1, 1) + value.shape[2:], lambda s: (lax.rem(s, 2), s // 2, 0, 0)) for value in arrays
        ],
        out_specs=[
            wide(triple_width), tall(head_width), wide(hidden), tall(hidden), tall(quarter), tall(quarter),
            wide(quarter), wide(quarter), *[held((width // LANES, LANES))] * 4,
        ],
        out_shape=[
            shaped((LANES, 4 * triple_width), F32),
            shaped((4 * head_width, LANES), F32),
            shaped((LANES, 4 * hidden), F32),
            shaped((4 * hidden, LANES), F32),
            shaped((width, LANES), F32),
            shaped((width, LANES), F32),
            shaped((LANES, width), F32),
            shaped((LANES, width), F32),
        ]
        + [shaped((width // LANES, LANES), F32)] * 4,
        compiler_params=params(),
        cost_estimate=BRIEF,
        name="unpack",
    )(*arrays)


def shards(
    ranks,
    groups,
    block_input,
    sequence_lengths,
    first_gain,
    first_shift,
    second_gain,
    second_shift,
    triple_weight,
    triple_left,
    triple_right,
    output_weight,
    output_left,
    output_right,
    expand_weight,
    expand_left,
    expand_right,
    shrink_weight,
    shrink_left,
    shrink_right,
    cotangent,
):
    unit = ranks // 2
    own_rows, width = block_input.shape
    rows = own_rows * unit
    blocks = rows // SHORT
    tile = math.gcd(own_rows, 256)
    triple_width = triple_weight.shape[1]
    head_width = output_weight.shape[0]
    hidden = expand_weight.shape[1]
    mp = lax.axis_index("mp")
    half = mp // unit
    place = lax.rem(mp, unit)
    far = lax.rem(mp + unit, ranks)
    swap = [(m, (m + unit) % ranks) for m in range(ranks)]

    tables = rotary_tables()
    beside = [[(d, d ^ bit) for d in range(groups)] for bit in (1, 2)]
    continues = find_flags(sequence_lengths[0])
    conts = lax.dynamic_slice_in_dim(continues, half * blocks, blocks, 0)
    gain1, shift1 = first_gain[None, :], first_shift[None, :]
    gain2, shift2 = second_gain[None, :], second_shift[None, :]

    (normed1, normed2, dy, low2, grad_lows, out, grad2, low_act, grad_low2, feed_sums, triple_far,
     output_far, x_halo, expand_half, shrink_half) = feed_first(
        unit, block_input, cotangent, (gain1, shift1, gain2, shift2), expand_weight, expand_left, expand_right,
        shrink_weight, shrink_left, output_right, shrink_right, triple_weight, output_weight, tile,
    )
    expand_piece = lax.ppermute(expand_half, "mp", swap)
    shrink_piece = lax.ppermute(shrink_half, "mp", swap)
    low1, q, k, v, g = project(
        unit, conts, x_halo, normed1, dy, grad_lows, gain1, shift1, (triple_weight, triple_far), triple_left,
        triple_right, (output_weight, output_far), output_left, tables, tile,
    )
    att, gq, gk, gv, halo = attend(conts, q, k, v, g, tables, tall_tables(), 256)
    expand_piece, shrink_piece, att = lax.optimization_barrier((expand_piece, shrink_piece, att))
    expand_other = lax.ppermute(expand_piece, "dp", beside[0])
    shrink_other = lax.ppermute(shrink_piece, "dp", beside[1])
    out, keep1, heads, left, got1 = settle(
        unit, normed1, low1, grad_lows, out, (att, gq, gk, gv), halo, (triple_weight, triple_far), triple_left,
        (output_weight, output_far), triple_right, output_left, tile,
    )
    hosted = ranks == 4 and groups == 8
    block_output, input_gradient, feed_sums, both, heads_sum, left_sum = feed_second(
        unit, normed2, low2, dy, grad_lows, out, grad2, low_act, grad_low2, block_input, keep1, got1, (gain1, gain2),
        output_right, shrink_right, (expand_piece, expand_other), expand_left, expand_right,
        (shrink_piece, shrink_other), shrink_left, feed_sums, heads, left, hosted, tile,
    )
    if hosted:
        (triple_right_sum, output_left_sum, expand_right_sum, shrink_left_sum, triple_left_sum, expand_left_sum,
         output_right_sum, shrink_right_sum, *norms) = unpack(
            *sum_all(feed_sums, both, heads_sum, left_sum), triple_width
        )
        norms = [value.reshape(width) for value in norms]
    else:

        def spread(*placed):
            size = placed[0][0].shape[1]
            wide = jnp.zeros((LANES, size * ranks), BF16)
            for value, shard in placed:
                wide = lax.dynamic_update_slice_in_dim(wide, value, shard * size, 1)
            return wide

        def joined(value):
            return value.transpose(2, 1, 0, 3).reshape(LANES, -1)

        def columns(value, start, size):
            return value.reshape(LANES, ranks, -1)[:, :, start : start + size].reshape(LANES, -1).astype(F32)

        heads, feed, left, both = lax.psum(
            (spread((heads[0], mp), (heads[1], far)), spread((feed_sums, far)), left, both), ("dp", "mp")
        )
        triple_right_sum = columns(heads, 0, triple_width)
        output_left_sum = columns(heads, triple_width, head_width).T
        expand_right_sum = columns(feed, 0, hidden)
        shrink_left_sum = columns(feed, hidden, hidden).T
        triple_left_sum = joined(left).astype(F32).T
        quarter = width // 4
        expand_left_sum = joined(both[..., :quarter]).astype(F32).T
        output_right_sum = joined(both[..., quarter : 2 * quarter]).astype(F32)
        shrink_right_sum = joined(both[..., 2 * quarter : 3 * quarter]).astype(F32)
        norms = both[:, :, : width // LANES, 3 * quarter :].transpose(1, 0, 2, 3).reshape(4, width).astype(F32)
    return (
        block_output,
        input_gradient,
        norms[0],
        norms[1],
        norms[2],
        norms[3],
        triple_left_sum,
        triple_right_sum,
        output_left_sum,
        output_right_sum,
        expand_left_sum,
        expand_right_sum,
        shrink_left_sum,
        shrink_right_sum,
    )


def solution(mesh):
    placed = (
        P(("dp", "mp"), None),
        P("dp", None),
        P(),
        P(),
        P(),
        P(),
        P(None, "mp"),
        P(),
        P(),
        P("mp", None),
        P(),
        P(),
        P(None, "mp"),
        P(),
        P(),
        P("mp", None),
        P(),
        P(),
        P(("dp", "mp"), None),
    )
    return jax.shard_map(
        functools.partial(shards, mesh.shape["mp"], mesh.shape["dp"]),
        mesh=mesh,
        in_specs=placed,
        out_specs=(P(("dp", "mp"), None), P(("dp", "mp"), None)) + (P(),) * 12,
        check_vma=False,
    )
```

```python
import functools
import math

import jax
import jax.numpy as jnp
import numpy as np
from jax import lax
from jax.experimental import pallas as pl
from jax.experimental.pallas import tpu as pltpu
from jax.sharding import PartitionSpec as P

HEAD_DIM = 64
ROT = 16
SHORT = 512
TOK_GRP = 3072
SLOTS = 6
EPS = 1e-05
LANES = 128
MESH = pl.DeviceIdType.MESH
BF16 = jnp.bfloat16
F32 = jnp.float32
VMEM_LIMIT = 56 * 1024 * 1024
BRIEF = pl.CostEstimate(flops=1, bytes_accessed=1, transcendentals=0)


def dot_nn(former, latter):
    return lax.dot_general(
        former, latter, (((1,), (0,)), ((), ())), preferred_element_type=F32
    )


def dot_nt(former, latter):
    return lax.dot_general(
        former, latter, (((1,), (1,)), ((), ())), preferred_element_type=F32
    )


def dot_tn(former, latter):
    return lax.dot_general(
        former, latter, (((0,), (0,)), ((), ())), preferred_element_type=F32
    )


def find_flags(group_lengths):
    seq_ends = jnp.cumsum(group_lengths, dtype=jnp.int32)
    starts = seq_ends - group_lengths
    block_starts = jnp.arange(SLOTS, dtype=jnp.int32) * SHORT
    begins = jnp.any(
        (starts[None, :] == block_starts[:, None]) & (group_lengths[None, :] > 0), axis=1
    )
    return jnp.where(begins, 0, 1).astype(jnp.int32)


def rotary_tables():
    half = ROT // 2
    frequency = np.exp(
        np.arange(half, dtype=np.float32) * np.float32(-2.0 * math.log(10000.0) / ROT)
    ).astype(np.float32)
    angles = np.arange(2 * SHORT, dtype=np.float32)[:, None] * frequency[None, :]
    cosine = np.ones((2 * SHORT, LANES), np.float32)
    minus = np.zeros((2 * SHORT, LANES), np.float32)
    plus = np.zeros((2 * SHORT, LANES), np.float32)
    for base in range(0, LANES, HEAD_DIM):
        cosine[:, base : base + half] = np.cos(angles)
        cosine[:, base + half : base + ROT] = np.cos(angles)
        minus[:, base : base + half] = -np.sin(angles)
        plus[:, base + half : base + ROT] = np.sin(angles)
    return jnp.asarray(cosine), jnp.asarray(minus), jnp.asarray(plus)


def tall_tables():
    half = ROT // 2
    frequency = np.exp(
        np.arange(half, dtype=np.float32) * np.float32(-2.0 * math.log(10000.0) / ROT)
    ).astype(np.float32)
    angles = frequency[:, None] * np.arange(2 * SHORT, dtype=np.float32)[None, :]
    return jnp.asarray(np.cos(angles)), jnp.asarray(np.sin(angles))


def low_lanes():
    return lax.broadcasted_iota(jnp.int32, (1, LANES), 1) < HEAD_DIM


def rotate(pair, cosine, minus, plus):
    half = ROT // 2
    return (
        pair * cosine
        + pltpu.roll(pair, LANES - half, 1) * minus
        + pltpu.roll(pair, half, 1) * plus
    )


def unrotate(pair, cosine, minus, plus):
    half = ROT // 2
    return (
        pair * cosine
        - pltpu.roll(pair, LANES - half, 1) * minus
        - pltpu.roll(pair, half, 1) * plus
    )


def normalize(values, gain, shift):
    center = values - jnp.mean(values, axis=-1, keepdims=True)
    spread = jnp.mean(center * center, axis=-1, keepdims=True)
    return center * lax.rsqrt(spread + EPS) * gain + shift


def whole(shape):
    return pl.BlockSpec(
        shape, lambda *idx: (0,) * len(shape), pipeline_mode=pl.Buffered(1)
    )


def held(shape):
    return pl.BlockSpec(shape, lambda *idx: (0,) * len(shape))


def rows_of(tile, width):
    return pl.BlockSpec((tile, width), lambda i, *refs: (i, 0))


def shaped(shape, dtype):
    return jax.ShapeDtypeStruct(shape, dtype)


def params(semantics=1):
    return pltpu.CompilerParams(
        dimension_semantics=("arbitrary",) * semantics, vmem_limit_bytes=VMEM_LIMIT
    )


SUM_ROWS = (2, 4, 16)


class Net:
    def __init__(self):
        dp, mp = lax.axis_index("dp"), lax.axis_index("mp")
        self.half, self.core = mp // 2, lax.rem(mp, 2)
        self.x, self.z = lax.rem(dp, 2), dp // 2
        self.other_half, self.other_core, self.other_x = 1 - self.half, 1 - self.core, 1 - self.x
        self.x_peer = (dp + 1 - 2 * self.x, mp)
        self.y_peer = (dp, mp + 2 - 4 * self.half)
        self.core_peer = (dp, mp + 1 - 2 * self.core)
        self.z_places = [lax.rem(self.z + j, 4) for j in range(1, 4)]
        self.z_peers = [(place * 2 + self.x, mp) for place in self.z_places]
        self.started = []

    def copy(self, src, dst, sems, slot, peer):
        return pltpu.make_async_remote_copy(
            src_ref=src, dst_ref=dst, send_sem=sems.at[0, slot], recv_sem=sems.at[1, slot], device_id=peer,
            device_id_type=MESH,
        )

    def start(self, copies):
        for copy in copies:
            copy.start()
        self.started += copies


def arrive(copies):
    for copy in copies:
        copy.wait_recv()


def added(first, *others):
    total = first.astype(F32)
    for other in others:
        total = total + other.astype(F32)
    return total.astype(BF16)


def sum_scratch(order, size):
    one = (16, size)
    first = {"yxz": ((2, 4), (2, 4)), "xyz": ((2, 4), (2, 4)), "xz": ((4,), (4,)), "zx": ((3, 2), (2,))}[order]
    second = {"yxz": ((4,), (4,)), "xyz": ((4,), (4,)), "xz": ((3,), (1,)), "zx": ((1,), (1,))}[order]
    return [pltpu.VMEM(shape + one, BF16) for shape in (*first, *second, (3,), (2, 2, 4))] + [
        pltpu.SemaphoreType.DMA((2, 12))
    ]


def sum_chunk(net, order, source, scratch):
    got1, work1, got2, work2, got3, full, sems = scratch
    x, z, other_x = net.x, net.z, net.other_x
    own, rows, plane = full.at[0, x, z], full.at[0, x], full.at[0, :, z]

    def to_z(src, dst, slot):
        return [
            net.copy(src(place), dst(j), sems, slot + j, peer)
            for j, (place, peer) in enumerate(zip(net.z_places, net.z_peers))
        ]

    def one(src, dst, slot, peer):
        return [net.copy(src, dst, sems, slot, peer)]

    last = work1 if order == "xz" else work2
    if order != "xyz":
        over_y = one(full.at[0], full.at[1], 9, net.y_peer)
    if order == "zx":
        spread = to_z(lambda place: source.at[:, place], lambda j: got1.at[j], 2)
        cross = one(work1.at[other_x], got2.at[0], 0, net.x_peer)
        back = one(own, own, 8, net.x_peer)
        gather = to_z(lambda place: plane, lambda j: plane, 5)
    else:
        spread = to_z(lambda place: last.at[place], lambda j: got3.at[j], 2)
        gather = to_z(lambda place: own, lambda j: own, 5)
        if order == "yxz":
            first = one(source.at[1], got1, 0, net.y_peer)
            second = one(work1.at[other_x], got2, 1, net.x_peer)
        elif order == "xyz":
            first = one(source.at[:, other_x], got1, 0, net.x_peer)
            second = one(work1.at[1], got2, 1, net.y_peer)
            over_y = one(rows, full.at[1, x], 8, net.y_peer)
            over_x = one(full.at[:, x], full.at[:, x], 9, net.x_peer)
        else:
            first = one(source.at[other_x], got1, 0, net.x_peer)
        if order != "xyz":
            over_x = one(rows, rows, 8, net.x_peer)

    def begin(copies):
        return lambda: net.start(copies)

    def after(copies, work, then):
        def stage():
            arrive(copies)
            if work is not None:
                target, value = work
                target[...] = value()
            if then is not None:
                net.start(then)

        return stage

    if order == "zx":
        mine = (work1, lambda: added(source[:, z], got1[0], got1[1], got1[2]))
        total = (own, lambda: added(work1[x], got2[0]))
        return [
            begin(spread), after(spread, mine, cross), after(cross, total, back), after(back, None, gather),
            after(gather, None, over_y), after(over_y, None, None),
        ]
    total = (own, lambda: added(last[z], got3[0], got3[1], got3[2]))
    if order == "yxz":
        head = [begin(first), after(first, (work1, lambda: added(source[0], got1[...])), second)]
        head.append(after(second, (work2, lambda: added(work1[x], got2[...])), spread))
    elif order == "xyz":
        head = [begin(first), after(first, (work1, lambda: added(source[:, x], got1[...])), second)]
        head.append(after(second, (work2, lambda: added(work1[0], got2[...])), spread))
    else:
        head = [begin(first), after(first, (work1, lambda: added(source[x], got1[...])), spread)]
    one_way, other_way = (over_y, over_x) if order == "xyz" else (over_x, over_y)
    return head + [
        after(spread, total, gather), after(gather, None, one_way), after(one_way, None, other_way),
        after(other_way, None, None),
    ]


def sum_both(net, parts, both, got, total, core_sems, scratches):
    exchange = [net.copy(both.at[net.other_core], got, core_sems, 0, net.core_peer)]
    chunks, start = [], 0
    for (order, size), scratch in zip(parts, scratches):
        chunks.append(sum_chunk(net, order, total.at[:, :, :, :, pl.ds(start, size)], scratch))
        start += size

    def combine():
        arrive(exchange)
        for place, at in ((0, net.half), (1, net.other_half)):
            total[place] = added(both[net.core, at], got[at])
        for chunk in chunks:
            chunk[0]()

    def together(k):
        def stage():
            for chunk in chunks:
                if k < len(chunk):
                    chunk[k]()

        return stage

    longest = max(len(chunk) for chunk in chunks)
    return [lambda: net.start(exchange), combine] + [together(k) for k in range(1, longest)]


def both_scratch(parts):
    size = sum(part[1] for part in parts)
    return [
        pltpu.VMEM((2,) + SUM_ROWS + (size,), BF16),
        pltpu.VMEM((2,) + SUM_ROWS + (size,), BF16),
        pltpu.SemaphoreType.DMA((2, 1)),
    ] + [shape for part in parts for shape in sum_scratch(*part)]


def split_columns(size):
    count = (size // 2 + LANES - 1) // LANES * LANES
    return (("yxz", count), ("xyz", size - count))


def quarters(ref, *arrays):
    start = 0
    for array in arrays:
        size = array.shape[1] // 4
        for q in range(4):
            ref[q % 2, q // 2, :, start : start + size] = array[:, q * size : (q + 1) * size].astype(BF16)
        start += size


def gelu_parts(hidden):
    cdf = 0.5 + 0.5 * lax.erf(hidden * math.sqrt(0.5))
    density = jnp.exp(-0.5 * hidden * hidden) * (1.0 / math.sqrt(2.0 * math.pi))
    return hidden * cdf, cdf + hidden * density


def feed_core(rows, grads, up_ref, down_ref, act_ref, grad_ref, hidden_step):
    for start in range(0, up_ref.shape[1], hidden_step):
        cols = pl.ds(start, hidden_step)
        hidden = dot_nn(rows, up_ref[:, cols])
        grad_act = dot_nt(grads, down_ref[cols, :])
        activated, slope = gelu_parts(hidden)
        act_ref[:, cols] = activated.astype(BF16)
        grad_ref[:, cols] = (grad_act * slope).astype(BF16)


def shard_index(unit, far):
    return lax.rem(lax.axis_index("mp") + (unit if far else 0), 2 * unit)


def columns_of(ref, size, shard):
    return ref.at[:, pl.ds(pl.multiple_of(shard * size, size), size)]


def rows_at(ref, size, shard):
    return ref.at[pl.ds(pl.multiple_of(shard * size, size), size)]


def load(step, sems, pairs):
    copies = [pltpu.make_async_copy(src, dst, sems.at[j]) for j, (src, dst) in enumerate(pairs)]

    @pl.when(step == 0)
    def _():
        for copy in copies:
            copy.start()
        for copy in copies:
            copy.wait()


def head_weights(unit, triples, right, outputs, output_left, triple_ref, output_ref):
    width = triples[0].shape[0]
    head_width = outputs[0].shape[0]
    size = 3 * head_width
    pairs = []
    for j in range(2):
        shard = shard_index(unit, j == 1)
        cols, rows = pl.ds(j * size, size), pl.ds(j * head_width, head_width)
        pairs += [
            (triples[j], triple_ref.at[pl.ds(0, width), cols]),
            (columns_of(right, size, shard), triple_ref.at[pl.ds(width, LANES), cols]),
            (outputs[j], output_ref.at[rows, pl.ds(0, width)]),
            (rows_at(output_left, head_width, shard), output_ref.at[rows, pl.ds(width, LANES)]),
        ]
    return pairs


def chip_neighbours(unit):
    dp = lax.axis_index("dp")
    mp = lax.axis_index("mp")
    lead = lax.rem(dp, 2)
    return lead, (dp, lax.rem(mp + unit, 2 * unit)), (dp + 1 - 2 * lead, mp)


def leads():
    dp = lax.axis_index("dp")
    return lax.rem(dp, 2), lax.rem(dp // 2, 2)


def group_neighbours():
    dp, mp = lax.axis_index("dp"), lax.axis_index("mp")
    first, second = leads()
    return (dp + 1 - 2 * first, mp), (dp + 2 - 4 * second, mp)


def courier(unit, pairs, chunks, sems):
    first, second = leads()
    mine = first + 2 * second
    y_peer = chip_neighbours(unit)[1]
    x_peer, z_peer = group_neighbours()
    over_y, once, twice = [], [], []
    for k in range(chunks):
        over_y.append([])
        once.append([])
        twice.append([])
        for j, (own, far) in enumerate(pairs):
            count = own.shape[0] // 4 // chunks

            def copy(kind, src, dst, quarter, start, size, peer, k=k, j=j, count=count):
                span = pl.ds(pl.multiple_of((quarter * chunks + k) * count + start, size), size)
                return pltpu.make_async_remote_copy(
                    src_ref=src.at[span], dst_ref=dst.at[span], send_sem=sems.at[0, kind, k, j],
                    recv_sem=sems.at[1, kind, k, j], device_id=peer, device_id_type=MESH,
                )

            by_x, by_z = mine + 1 - 2 * first, mine + 2 - 4 * second
            over_y[-1].append(copy(0, own, far, mine, 0, count, y_peer))
            once[-1] += [copy(1, far, far, mine, 0, count, x_peer), copy(2, far, far, mine, 0, count, z_peer)]
            twice[-1] += [
                copy(3, far, far, by_x, 0, count // 2, z_peer),
                copy(4, far, far, by_z, count // 2, count // 2, x_peer),
            ]
    return over_y, once, twice


def meet(peers):
    barrier = pltpu.get_barrier_semaphore()
    for peer in peers:
        pl.semaphore_signal(barrier, inc=1, device_id=peer, device_id_type=MESH)
    pl.semaphore_wait(barrier, len(peers))


def place_in_unit(unit):
    mp = lax.axis_index("mp")
    return lax.rem(mp, unit), mp - lax.rem(mp, unit)


def unit_peers(unit):
    place, base = place_in_unit(unit)
    return [(lax.axis_index("dp"), base + lax.rem(place + unit - s, unit)) for s in range(1, unit)]


def halo_copies(unit, x_ref, halo_ref, y_sems, unit_sems):
    own_rows = x_ref.shape[0]
    chunk = math.gcd(own_rows, 128)
    dp = lax.axis_index("dp")
    found = []
    for k in range(SHORT // chunk):
        row = unit * own_rows - SHORT + k * chunk
        holder, start = row // own_rows, row % own_rows
        target = halo_ref.at[pl.ds(k * chunk, chunk)]
        over_y = pltpu.make_async_remote_copy(
            src_ref=x_ref.at[pl.ds(start, chunk)], dst_ref=target, send_sem=y_sems.at[0, k], recv_sem=y_sems.at[1, k],
            device_id=(dp, unit + holder), device_id_type=MESH,
        )
        spread = [
            pltpu.make_async_remote_copy(
                src_ref=target, dst_ref=target, send_sem=unit_sems.at[0, k, s - 1], recv_sem=unit_sems.at[1, k, s - 1],
                device_id=(dp, unit + (holder + s) % unit), device_id_type=MESH,
            )
            for s in range(1, unit)
        ]
        found.append((holder, over_y, spread))
    return found


def feed_first_kernel(
    unit, tile, x_ref, dy_ref, gain1_ref, shift1_ref, gain2_ref, shift2_ref, up_own_ref, up_left_ref, up_right_ref,
    down_own_ref, down_left_ref, output_right_ref, down_right_ref, x_all_ref, dy_all_ref, triple_ref, output_ref, normed1_ref,
    normed_ref, dy_full_ref, low_ref, grad_lows_ref, out_ref, grad_ref, low_act_ref, grad_low_ref, sums_ref,
    triple_far_ref, output_far_ref, halo_ref, up_half_ref, down_half_ref, act_ref, gh_ref, up_ref, down_ref, acc_ref,
    xs_ref, x_got_ref, dy_got_ref, courier_sems, unit_sems, halo_y_sems, halo_unit_sems, local_sems, load_sems,
):
    step = pl.program_id(0)
    width, hidden = up_own_ref.shape
    weights = (
        (up_own_ref, up_ref.at[pl.ds(0, width)]),
        (columns_of(up_right_ref, hidden, shard_index(unit, False)), up_ref.at[pl.ds(width, LANES)]),
        (down_own_ref, down_ref.at[:, pl.ds(0, width)]),
        (rows_at(down_left_ref, hidden, shard_index(unit, False)), down_ref.at[:, pl.ds(width, LANES)]),
    )
    own_rows = x_all_ref.shape[0]
    per_device = own_rows // tile
    steps = unit * per_device
    chunks = courier_sems.shape[2]
    place, base = place_in_unit(unit)
    half = base // unit
    peers = unit_peers(unit)
    over_y, once, twice = courier(
        unit, ((triple_ref, triple_far_ref), (output_ref, output_far_ref)), chunks, courier_sems
    )
    halo = halo_copies(unit, x_all_ref, halo_ref, halo_y_sems, halo_unit_sems)
    rows_out = [
        pltpu.make_async_remote_copy(
            src_ref=src, dst_ref=dst.at[j], send_sem=unit_sems.at[0, which, j], recv_sem=unit_sems.at[1, which, j],
            device_id=peer, device_id_type=MESH,
        )
        for j, peer in enumerate(peers)
        for which, (src, dst) in enumerate(((x_all_ref, x_got_ref), (dy_all_ref, dy_got_ref)))
    ]
    kept_halves = [
        pltpu.make_async_copy(
            src.at[
                pl.ds(pl.multiple_of(lead * dst.shape[0], dst.shape[0]), dst.shape[0]), pl.ds(0, dst.shape[1])
            ],
            dst,
            local_sems.at[j],
        )
        for j, (lead, src, dst) in enumerate(zip(leads(), (up_ref, down_ref), (up_half_ref, down_half_ref)))
    ]

    @pl.when(step == 0)
    def _():
        meet([chip_neighbours(unit)[1], *group_neighbours(), *peers])
        for copy in rows_out:
            copy.start()
        for copies in over_y:
            for copy in copies:
                copy.start()

    for holder, copy, _ in halo:
        pl.when((step == 0) & (half == 0) & (place == holder))(copy.start)
    load(step, load_sems, weights)

    @pl.when(step == 0)
    def _():
        for copy in kept_halves:
            copy.start()
        xs_ref[...] = x_ref[...]
        dy_full_ref[...] = dy_ref[...]

    @pl.when((step > 0) & (step < per_device))
    def _():
        xs_ref[...] = x_ref[...]
        dy_full_ref[...] = dy_ref[...]

    for slot in range(unit - 1):

        @pl.when(step == per_device * (slot + 1))
        def _():
            for which in range(2):
                rows_out[2 * slot + which].wait_recv()

        @pl.when((step >= per_device * (slot + 1)) & (step < per_device * (slot + 2)))
        def _():
            span = pl.ds(pl.multiple_of((step - per_device * (slot + 1)) * tile, tile), tile)
            xs_ref[...] = x_got_ref[slot, span]
            dy_full_ref[...] = dy_got_ref[slot, span]

    for k in range(chunks):

        @pl.when(step == min(k + 2, steps - 1))
        def _():
            for copy in over_y[k]:
                copy.wait_recv()
            for copy in once[k]:
                copy.start()

    for k in range(chunks):

        @pl.when(step == min(k + 4, steps - 1))
        def _():
            for copy in once[k]:
                copy.wait_recv()
            for copy in twice[k]:
                copy.start()

    x = xs_ref[...].astype(F32)
    center = x - jnp.mean(x, axis=-1, keepdims=True)
    spread = jnp.mean(center * center, axis=-1, keepdims=True)
    scaled = center * lax.rsqrt(spread + EPS)
    normed1_ref[...] = (scaled * gain1_ref[...] + shift1_ref[...]).astype(BF16)
    normed = (scaled * gain2_ref[...] + shift2_ref[...]).astype(BF16)
    normed_ref[...] = normed
    dy = dy_full_ref[...]
    low = dot_nn(normed, up_left_ref[...]).astype(BF16)
    low_ref[...] = low
    rights = jnp.concatenate([output_right_ref[...], down_right_ref[...]], axis=0)
    grad_lows = dot_nt(dy, rights).astype(BF16)
    grad_lows_ref[...] = grad_lows
    grad_low = grad_lows[:, LANES:]
    feed_core(
        jnp.concatenate([normed, low], axis=1), jnp.concatenate([dy, grad_low], axis=1), up_ref, down_ref, act_ref,
        gh_ref, 512,
    )
    act = act_ref[...]
    gh = gh_ref[...]
    forward = dot_nn(act, down_ref[...])
    backward = dot_nt(gh, up_ref[...])
    out_ref[...], low_act_ref[...] = forward[:, :width], forward[:, width:]
    grad_ref[...], grad_low_ref[...] = backward[:, :width], backward[:, width:]

    @pl.when(step == 0)
    def _():
        acc_ref[...] = jnp.zeros_like(acc_ref)

    acc_ref[:, :hidden] += dot_tn(low, gh)
    acc_ref[:, hidden:] += dot_tn(grad_low, act)

    @pl.when((step == 0) & (half == 0))
    def _():
        fills = [
            pltpu.make_async_copy(xs_ref, halo_ref.at[pl.ds(k * tile, tile)], local_sems.at[2 + k])
            for k in range(SHORT // tile)
        ]
        for copy in fills:
            copy.start()
        for copy in fills:
            copy.wait()

    @pl.when(step == steps - 1)
    def _():
        sums_ref[...] = acc_ref[...].astype(BF16)
        for holder, copy, spread_copies in halo:

            @pl.when((half == 1) & (place == holder))
            def _():
                copy.wait_recv()
                for other in spread_copies:
                    other.start()

        for holder, copy, spread_copies in halo:
            pl.when((half == 0) & (place == holder))(copy.wait_send)

            @pl.when((half == 1) & (place == holder))
            def _():
                for other in spread_copies:
                    other.wait_send()

            for s in range(1, unit):
                pl.when((half == 1) & (place == (holder + s) % unit))(spread_copies[s - 1].wait_recv)
        for copy in rows_out:
            copy.wait_send()
        for k in range(chunks):
            for copy in over_y[k] + once[k]:
                copy.wait_send()
            for copy in twice[k]:
                copy.wait()
        for copy in kept_halves:
            copy.wait()


def feed_first(unit, x, dy, norms, up, up_left, up_right, down, down_left, output_right, down_right, triple, output,
               tile):
    own_rows, width = x.shape
    rows = own_rows * unit
    hidden = up.shape[1]
    steps, per_device = rows // tile, own_rows // tile
    chunks = math.gcd(2, output.shape[0] // 128)
    halo_chunks = SHORT // math.gcd(own_rows, 128)
    anywhere = pl.BlockSpec(memory_space=pl.ANY)
    here = pl.BlockSpec((tile, width), lambda i: (jnp.minimum(i, per_device - 1), 0))

    def turned(size):
        def index(i):
            return (lax.rem(i + place_in_unit(unit)[0] * per_device, steps), 0)

        return pl.BlockSpec((tile, size), index)

    return pl.pallas_call(
        functools.partial(feed_first_kernel, unit, tile),
        grid=(steps,),
        in_specs=[here, here]
        + [whole((1, width))] * 4
        + [
            anywhere,
            whole(up_left.shape),
            anywhere,
            anywhere,
            anywhere,
            whole(output_right.shape),
            whole(down_right.shape),
        ]
        + [anywhere] * 4,
        out_specs=[
            turned(width),
            turned(width),
            turned(width),
            turned(LANES),
            turned(2 * LANES),
            turned(width),
            turned(width),
            turned(LANES),
            turned(LANES),
            held((LANES, 2 * hidden)),
        ]
        + [anywhere] * 5,
        scratch_shapes=[
            pltpu.VMEM((tile, hidden), BF16),
            pltpu.VMEM((tile, hidden), BF16),
            pltpu.VMEM((width + LANES, hidden), BF16),
            pltpu.VMEM((hidden, width + LANES), BF16),
            pltpu.VMEM((LANES, 2 * hidden), F32),
            pltpu.VMEM((tile, width), BF16),
            pltpu.VMEM((unit - 1, own_rows, width), BF16),
            pltpu.VMEM((unit - 1, own_rows, width), BF16),
            pltpu.SemaphoreType.DMA((2, 5, chunks, 2)),
            pltpu.SemaphoreType.DMA((2, 2, unit - 1)),
            pltpu.SemaphoreType.DMA((2, halo_chunks)),
            pltpu.SemaphoreType.DMA((2, halo_chunks, unit - 1)),
            pltpu.SemaphoreType.DMA((2 + SHORT // tile,)),
            pltpu.SemaphoreType.DMA((4,)),
        ],
        out_shape=[
            shaped((rows, width), BF16),
            shaped((rows, width), BF16),
            shaped((rows, width), BF16),
            shaped((rows, LANES), BF16),
            shaped((rows, 2 * LANES), BF16),
            shaped((rows, width), F32),
            shaped((rows, width), F32),
            shaped((rows, LANES), F32),
            shaped((rows, LANES), F32),
            shaped((LANES, 2 * hidden), BF16),
            shaped(triple.shape, BF16),
            shaped(output.shape, BF16),
            shaped((SHORT, width), BF16),
            shaped((up.shape[0] // 2, up.shape[1]), BF16),
            shaped((down.shape[0] // 2, down.shape[1]), BF16),
        ],
        compiler_params=pltpu.CompilerParams(
            dimension_semantics=("arbitrary",), vmem_limit_bytes=VMEM_LIMIT, collective_id=3, has_side_effects=True
        ),
        cost_estimate=BRIEF,
        name="feed_first",
    )(x, dy, *norms, up, up_left, up_right, down, down_left, output_right, down_right, x, dy, triple, output)


def feed_second_kernel(
    unit, tile, normed_ref, low_ref, dy_ref, grad_lows_ref, out_in_ref, grad_in_ref, low_act_in_ref, grad_low_in_ref,
    x_ref, keep_ref, got1_ref, gain1_ref, gain2_ref, output_right_ref, down_right_ref, up0_ref, up1_ref, up_left_ref,
    up_right_ref, down0_ref, down1_ref, down_left_ref, early_ref, heads_ref, left_ref, y_ref, dx_ref, sums_ref, both_ref,
    heads_out_ref, left_out_ref, act_ref, gh_ref, up_ref, down_ref, send_ref, got_ref, early_got_ref, acc_ref, norms_ref,
    output_right_grad_ref, down_right_grad_ref, up_left_grad_ref, sems, early_sems, out_sems, load_sems, *sum_refs,
):
    step = pl.program_id(0)
    own_rows = got_ref.shape[1]
    per_device = own_rows // tile
    send_tiles = (unit - 1) * per_device
    width, hidden = up_ref.shape[0] - LANES, up_ref.shape[1]
    shard = shard_index(unit, True)
    weights = [
        (columns_of(up_right_ref, hidden, shard), up_ref.at[pl.ds(width, LANES)]),
        (rows_at(down_left_ref, hidden, shard), down_ref.at[:, pl.ds(width, LANES)]),
    ]
    for lead, pieces, ref in zip(leads(), ((up0_ref, up1_ref), (down0_ref, down1_ref)), (up_ref, down_ref)):
        for place, piece in zip((lead, 1 - lead), pieces):
            weights.append((piece, rows_at(ref, piece.shape[0], place).at[:, pl.ds(0, piece.shape[1])]))
    peers = unit_peers(unit)
    copies = [
        [
            pltpu.make_async_remote_copy(
                src_ref=send_ref.at[s, pl.ds(t * tile, tile)], dst_ref=got_ref.at[s, pl.ds(t * tile, tile)],
                send_sem=sems.at[0, s, t], recv_sem=sems.at[1, s, t], device_id=peer, device_id_type=MESH,
            )
            for t in range(per_device)
        ]
        for s, peer in enumerate(peers)
    ]

    steps = unit * per_device
    y_peer = chip_neighbours(unit)[1]
    pieces = early_sems.shape[1]
    count = early_ref.shape[0] // pieces
    early_copies = [
        pltpu.make_async_remote_copy(
            src_ref=early_ref.at[pl.ds(j * count, count)], dst_ref=early_got_ref.at[pl.ds(j * count, count)],
            send_sem=early_sems.at[0, j], recv_sem=early_sems.at[1, j], device_id=y_peer, device_id_type=MESH,
        )
        for j in range(pieces)
    ]
    hosted = len(sum_refs) > 0
    if hosted:
        net = Net()
        size = heads_ref.shape[-1] // 2
        split = len(sum_scratch("yxz", size))
        heads_refs = (sum_refs[:split], sum_refs[split : 2 * split])
        left_refs = sum_refs[2 * split :]
        stages = [
            sum_chunk(net, order, heads_ref.at[:, :, :, :, pl.ds(j * size, size)], heads_refs[j])
            for j, order in enumerate(("yxz", "xyz"))
        ]
        stages.append(sum_both(net, (("yxz", left_ref.shape[-1]),), left_ref, *left_refs[:3], (left_refs[3:],)))

    def advance():
        if hosted:
            for at in range(steps):

                @pl.when(step == at)
                def _():
                    for stage in stages:
                        stage[at]()

    @pl.when(step == 0)
    def _():
        meet([*peers, y_peer] + ([net.x_peer, *net.z_peers] if hosted else []))
        for ref in (norms_ref, output_right_grad_ref, down_right_grad_ref, acc_ref, up_left_grad_ref):
            ref[...] = jnp.zeros_like(ref)

    advance()
    for j, copy in enumerate(early_copies):
        pl.when(step == min(j + 1, steps - 1))(copy.start)
    load(step, load_sems, weights)
    normed = normed_ref[...]
    low = low_ref[...]
    dy = dy_ref[...]
    grad_low = grad_lows_ref[:, LANES:]
    feed_core(
        jnp.concatenate([normed, low], axis=1), jnp.concatenate([dy, grad_low], axis=1), up_ref, down_ref, act_ref,
        gh_ref, 512,
    )
    act = act_ref[...]
    gh = gh_ref[...]
    forward = dot_nn(act, down_ref[...])
    backward = dot_nt(gh, up_ref[...])
    grad_low_up = (grad_low_in_ref[...] + backward[:, width:]).astype(BF16)
    out = out_in_ref[...] + forward[:, :width]
    low_act = low_act_in_ref[...] + forward[:, width:]
    second = grad_in_ref[...] + backward[:, :width] + dot_nt(grad_low_up, up_left_ref[...])
    acc_ref[:, :hidden] += dot_tn(low, gh)
    acc_ref[:, hidden:] += dot_tn(grad_low, act)
    up_left_grad_ref[...] += dot_tn(grad_low_up, normed)

    @pl.when(step < send_tiles)
    def _():
        slot = step // per_device
        span = pl.ds(pl.multiple_of(lax.rem(step, per_device) * tile, tile), tile)
        send_ref[slot, span, :width] = out.astype(BF16)
        send_ref[slot, span, width : 2 * width] = second.astype(BF16)
        send_ref[slot, span, 2 * width :] = low_act.astype(BF16)

    for s in range(unit - 1):
        for t in range(per_device):
            pl.when(step == s * per_device + t)(copies[s][t].start)
            pl.when(step == send_tiles + t)(copies[s][t].wait_recv)

    @pl.when(step >= send_tiles)
    def _():
        span = pl.ds(pl.multiple_of((step - send_tiles) * tile, tile), tile)
        first = keep_ref[:, :width].astype(F32)
        low_att = keep_ref[:, width:].astype(F32)
        total_out, total_second, total_low = out, second, low_act
        for s in range(unit - 1):
            first = first + got1_ref[s, :, :width].astype(F32)
            low_att = low_att + got1_ref[s, :, width:].astype(F32)
            total_out = total_out + got_ref[s, span, :width].astype(F32)
            total_second = total_second + got_ref[s, span, width : 2 * width].astype(F32)
            total_low = total_low + got_ref[s, span, 2 * width :].astype(F32)
        low_att, total_low = low_att.astype(BF16), total_low.astype(BF16)
        x = x_ref[...].astype(F32)
        y_ref[...] = (
            x + total_out + dot_nn(low_att, output_right_ref[...]) + dot_nn(total_low, down_right_ref[...])
        ).astype(BF16)
        center = x - jnp.mean(x, axis=-1, keepdims=True)
        spread = jnp.mean(center * center, axis=-1, keepdims=True)
        inverse = lax.rsqrt(spread + EPS)
        scaled = center * inverse
        total = first * gain1_ref[...] + total_second * gain2_ref[...]
        mean = jnp.mean(total, axis=-1, keepdims=True)
        inner = jnp.mean(total * scaled, axis=-1, keepdims=True)
        dx_ref[...] = dy.astype(F32) + (total - mean - scaled * inner) * inverse
        norms_ref[0:1, :] += jnp.sum(first * scaled, axis=0, keepdims=True)
        norms_ref[1:2, :] += jnp.sum(first, axis=0, keepdims=True)
        norms_ref[2:3, :] += jnp.sum(total_second * scaled, axis=0, keepdims=True)
        norms_ref[3:4, :] += jnp.sum(total_second, axis=0, keepdims=True)
        output_right_grad_ref[...] += dot_tn(low_att, dy)
        down_right_grad_ref[...] += dot_tn(total_low, dy)

    @pl.when(step == steps - 1)
    def _():
        for copy in early_copies:
            copy.wait()
        sums_ref[...] = (acc_ref[...] + early_got_ref[...].astype(F32)).astype(BF16)
        quarters(both_ref, up_left_grad_ref[...], output_right_grad_ref[...], down_right_grad_ref[...])
        start = 3 * (width // 4)
        count = width // LANES
        for q in range(4):
            rows = [norms_ref[q : q + 1, j * LANES : (j + 1) * LANES] for j in range(count)]
            block = jnp.concatenate([*rows, jnp.zeros((LANES - count, LANES), F32)], axis=0)
            both_ref[q % 2, q // 2, :, start:] = block.astype(BF16)
        for group in copies:
            for copy in group:
                copy.wait_send()
        if hosted:
            for at in range(steps, max(len(stage) for stage in stages)):
                for stage in stages:
                    if at < len(stage):
                        stage[at]()
            outs = []
            for j, refs in enumerate((*heads_refs, left_refs[3:])):
                full = refs[5]
                target = left_out_ref if j == 2 else heads_out_ref.at[:, :, :, :, pl.ds(j * size, size)]
                outs.append(pltpu.make_async_copy(full, target, out_sems.at[j]))
                outs[-1].start()
            for copy in net.started:
                copy.wait_send()
            for copy in outs:
                copy.wait()


def feed_second(unit, normed, low, dy, grad_lows, out, grad, low_act, grad_low, x, keep, got, gains, output_right,
                down_right, ups, up_left, up_right, downs, down_left, early, heads, left, hosted, tile):
    rows, width = normed.shape
    own_rows = rows // unit
    anywhere = pl.BlockSpec(memory_space=pl.ANY)
    extra = []
    if hosted:
        heads = heads.reshape((2,) + SUM_ROWS + heads.shape[-1:])
        left = left.reshape((2, 2) + SUM_ROWS + left.shape[-1:])
        extra = sum_scratch("yxz", heads.shape[-1] // 2) + sum_scratch("xyz", heads.shape[-1] // 2)
        extra += both_scratch((("yxz", left.shape[-1]),))
    hidden = ups[0].shape[1]
    steps, per_device = rows // tile, own_rows // tile
    send_tiles = steps - per_device
    wide = 2 * width + LANES

    def turned(size):
        def index(i):
            place, slot = place_in_unit(unit)[0], i // per_device + 1
            return (lax.rem(place + unit - slot, unit) * per_device + lax.rem(i, per_device), 0)

        return pl.BlockSpec((tile, size), index)

    def late(size):
        return pl.BlockSpec((tile, size), lambda i: (jnp.maximum(i - send_tiles, 0), 0))

    return pl.pallas_call(
        functools.partial(feed_second_kernel, unit, tile),
        grid=(steps,),
        in_specs=[
            turned(width),
            turned(LANES),
            turned(width),
            turned(2 * LANES),
            turned(width),
            turned(width),
            turned(LANES),
            turned(LANES),
            late(width),
            late(width + LANES),
            pl.BlockSpec((unit - 1, tile, width + LANES), lambda i: (0, jnp.maximum(i - send_tiles, 0), 0)),
            whole((1, width)),
            whole((1, width)),
            whole(output_right.shape),
            whole(down_right.shape),
            anywhere,
            anywhere,
            whole(up_left.shape),
            anywhere,
            anywhere,
            anywhere,
            anywhere,
            whole(early.shape),
            whole(heads.shape),
            whole(left.shape),
        ],
        out_specs=[
            late(width),
            late(width),
            held((LANES, 2 * hidden)),
            held((2, 2, LANES, 3 * (width // 4) + LANES)),
            anywhere,
            anywhere,
        ],
        scratch_shapes=[
            pltpu.VMEM((tile, hidden), BF16),
            pltpu.VMEM((tile, hidden), BF16),
            pltpu.VMEM((width + LANES, hidden), BF16),
            pltpu.VMEM((hidden, width + LANES), BF16),
            pltpu.VMEM((unit - 1, own_rows, wide), BF16),
            pltpu.VMEM((unit - 1, own_rows, wide), BF16),
            pltpu.VMEM((LANES, 2 * hidden), BF16),
            pltpu.VMEM((LANES, 2 * hidden), F32),
            pltpu.VMEM((8, width), F32),
            pltpu.VMEM((LANES, width), F32),
            pltpu.VMEM((LANES, width), F32),
            pltpu.VMEM((LANES, width), F32),
            pltpu.SemaphoreType.DMA((2, unit - 1, per_device)),
            pltpu.SemaphoreType.DMA((2, 4)),
            pltpu.SemaphoreType.DMA((3,)),
            pltpu.SemaphoreType.DMA((6,)),
        ]
        + extra,
        out_shape=[
            shaped((own_rows, width), BF16),
            shaped((own_rows, width), F32),
            shaped((LANES, 2 * hidden), BF16),
            shaped((2, 2, LANES, 3 * (width // 4) + LANES), BF16),
            shaped(heads.shape, BF16),
            shaped(left.shape[1:] if hosted else left.shape, BF16),
        ],
        compiler_params=pltpu.CompilerParams(
            dimension_semantics=("arbitrary",), vmem_limit_bytes=VMEM_LIMIT, collective_id=4, has_side_effects=True
        ),
        cost_estimate=BRIEF,
        name="feed_second",
    )(normed, low, dy, grad_lows, out, grad, low_act, grad_low, x, keep, got, *gains, output_right, down_right, *ups,
      up_left, up_right, *downs, down_left, early, heads, left)


def project_kernel(
    unit, main_tiles, halo_ref, normed_ref, dy_ref, grad_lows_ref, late_ref, cos0_ref, cos1_ref, minus0_ref, minus1_ref, plus0_ref,
    plus1_ref, gain_ref, shift_ref, triple0_ref, triple1_ref, left_ref, right_ref, output0_ref, output1_ref,
    output_left_ref, low_ref, q_ref, k_ref, v_ref, g_ref, triple_ref, output_ref, load_sems,
):
    step = pl.program_id(0)
    load(
        step, load_sems,
        head_weights(
            unit, (triple0_ref, triple1_ref), right_ref, (output0_ref, output1_ref), output_left_ref, triple_ref,
            output_ref,
        ),
    )

    later = late_ref[0, 0:1, :] > 0.0
    tables = tuple(
        jnp.where(later, two[...], one[...])
        for one, two in ((cos0_ref, cos1_ref), (minus0_ref, minus1_ref), (plus0_ref, plus1_ref))
    )
    head_width = output0_ref.shape[0]
    first = low_lanes()

    def rows(normed, full):
        low = dot_nn(normed, left_ref[...]).astype(BF16)
        if full:
            low_ref[...] = low
        mixed = dot_nn(jnp.concatenate([normed, low], axis=1), triple_ref[...])
        if full:
            grads = jnp.concatenate([dy_ref[...], grad_lows_ref[:, :LANES]], axis=1)
            g_ref[...] = dot_nt(grads, output_ref[...]).astype(BF16)
        for pair in range(2 * head_width // LANES):
            one, two, three = (
                mixed[:, (3 * pair + part) * LANES : (3 * pair + part + 1) * LANES] for part in range(3)
            )
            cols = pl.ds(pair * LANES, LANES)
            key = pltpu.roll(jnp.where(first, three, one), HEAD_DIM, 1)
            k_ref[:, cols] = rotate(key, *tables).astype(BF16)
            v_ref[:, cols] = jnp.where(first, two, three).astype(BF16)
            if full:
                query = rotate(jnp.where(first, one, two), *tables).astype(BF16)
                q_ref[:, cols] = query * HEAD_DIM**-0.5

    @pl.when(step < main_tiles)
    def _():
        rows(normed_ref[...], True)

    @pl.when(step >= main_tiles)
    def _():
        rows(normalize(halo_ref[...].astype(F32), gain_ref[...], shift_ref[...]).astype(BF16), False)


def project(unit, conts, x_halo, normed, dy, grad_lows, gain, shift, triples, left, right, outputs, output_left, tables,
            tile):
    rows, width = dy.shape
    head_width = outputs[0].shape[0]
    anywhere = pl.BlockSpec(memory_space=pl.ANY)
    per_block = SHORT // tile
    main_tiles, halo_tiles = rows // tile, SHORT // tile
    late = jnp.concatenate([jnp.repeat(conts, per_block), jnp.zeros((halo_tiles,), jnp.int32)])
    late = jnp.broadcast_to(late.astype(F32)[:, None, None], (main_tiles + halo_tiles, 8, LANES))

    halo = pl.BlockSpec((tile, width), lambda i: (jnp.maximum(i - main_tiles, 0), 0))

    def table(which):
        return pl.BlockSpec((tile, LANES), lambda i: (which * per_block + lax.rem(i, per_block), 0))

    def main(size):
        return pl.BlockSpec((tile, size), lambda i: (jnp.minimum(i, main_tiles - 1), 0))

    def all_rows(size):
        return pl.BlockSpec((tile, size), lambda i: (jnp.where(i < main_tiles, i + halo_tiles, i - main_tiles), 0))

    return pl.pallas_call(
        functools.partial(project_kernel, unit, main_tiles),
        grid=(main_tiles + halo_tiles,),
        in_specs=[
            halo,
            main(width),
            main(width),
            main(2 * LANES),
            pl.BlockSpec((1, 8, LANES), lambda i: (i, 0, 0)),
            table(0),
            table(1),
            table(0),
            table(1),
            table(0),
            table(1),
            whole(gain.shape),
            whole(shift.shape),
            anywhere,
            anywhere,
            whole(left.shape),
            anywhere,
            anywhere,
            anywhere,
            anywhere,
        ],
        out_specs=[
            main(LANES),
            main(2 * head_width),
            all_rows(2 * head_width),
            all_rows(2 * head_width),
            main(2 * head_width),
        ],
        scratch_shapes=[
            pltpu.VMEM((width + LANES, 6 * head_width), BF16),
            pltpu.VMEM((2 * head_width, width + LANES), BF16),
            pltpu.SemaphoreType.DMA((8,)),
        ],
        out_shape=[
            shaped((rows, LANES), BF16),
            shaped((rows, 2 * head_width), BF16),
            shaped((SHORT + rows, 2 * head_width), BF16),
            shaped((SHORT + rows, 2 * head_width), BF16),
            shaped((rows, 2 * head_width), BF16),
        ],
        compiler_params=params(),
        cost_estimate=BRIEF,
        name="project",
    )(x_halo, normed, dy, grad_lows, late, *[table for table in tables for _ in range(2)], gain, shift, *triples, left, right,
      *outputs, output_left)


def attend_rows(with_prev, pairs, count, allowed, q_ref, k_ref, v_ref, g_ref, kp_ref, vp_ref, tables, att_ref, gq_ref,
                dk_ref, dv_ref, dkp_ref, dvp_ref):
    first = low_lanes()
    zero = jnp.zeros((), BF16)

    def stack(pair):
        return jnp.concatenate([jnp.where(first, pair, zero), jnp.where(first, zero, pair)], axis=0)

    def unstack(both):
        return jnp.where(first, both[:count], both[count:])

    def joined(fold, values):
        return functools.reduce(fold, values)

    pieces = []
    for lanes in pairs:
        for start in range(0, SHORT, count):
            span = pl.ds(start, count)
            parts = []
            if with_prev:
                parts.append((kp_ref[:, lanes], vp_ref[:, lanes], dkp_ref, dvp_ref, pl.ds(0, SHORT)))
            if start:
                before = pl.ds(0, start)
                parts.append((k_ref[before, lanes], v_ref[before, lanes], dk_ref, dv_ref, before))
            parts.append((k_ref[span, lanes], v_ref[span, lanes], dk_ref, dv_ref, span))
            pieces.append((lanes, span, stack(q_ref[span, lanes]), stack(g_ref[span, lanes]), parts))

    scores, grads, weights, lows, inners, slopes = [], [], [], [], [], []
    for _, _, queries, _, parts in pieces:
        found = [dot_nt(queries, part[0]) for part in parts]
        scores.append(found[:-1] + [jnp.where(allowed, found[-1], -1e30)])
    for _, _, _, grad, parts in pieces:
        grads.append([dot_nt(grad, part[1]) for part in parts])
    for found in scores:
        peak = joined(jnp.maximum, [jnp.max(score, axis=1, keepdims=True) for score in found])
        exps = [jnp.exp(score - peak) for score in found]
        scale = 1.0 / joined(jnp.add, [jnp.sum(exp, axis=1, keepdims=True) for exp in exps])
        weights.append([exp * scale for exp in exps])
        lows.append([weight.astype(BF16) for weight in weights[-1]])
    for (lanes, span, _, grad, parts), low in zip(pieces, lows):
        attended = joined(jnp.add, [dot_nn(weight, part[1]) for weight, part in zip(low, parts)])
        att_ref[span, lanes] = unstack(attended).astype(BF16)
        inners.append(jnp.sum(attended * grad.astype(F32), axis=1, keepdims=True))
    for weight, grad, inner in zip(weights, grads, inners):
        slopes.append([(w * (g - inner)).astype(BF16) for w, g in zip(weight, grad)])
    for (lanes, span, queries, grad, parts), low, slope in zip(pieces, lows, slopes):
        grad_query = joined(jnp.add, [dot_nn(ds, part[0]) for ds, part in zip(slope, parts)])
        for ds, weight, (_, _, to_key, to_value, rows) in zip(slope, low, parts):
            to_key[lanes, rows] += dot_tn(queries, ds)
            to_value[lanes, rows] += dot_tn(grad, weight)
        grad_query = unstack(grad_query) * HEAD_DIM**-0.5
        gq_ref[span, lanes] = unrotate(grad_query, *[table[span] for table in tables]).astype(BF16)


def unrotate_tall(ref, lanes, cosine, sine):
    half = ROT // 2
    value = ref[lanes, :]
    halves = []
    for base in (HEAD_DIM, 0):
        one, two = value[base : base + half], value[base + half : base + ROT]
        halves += [one * cosine + two * sine, two * cosine - one * sine, value[base + ROT : base + HEAD_DIM]]
    return jnp.concatenate(halves, axis=0).astype(BF16).T


def attend_kernel(
    blocks, pairs, count, conts_ref, q_ref, k_ref, v_ref, g_ref, kp_ref, vp_ref, cos_ref, minus_ref, plus_ref,
    tall_cos_ref, tall_sin_ref, att_ref, gq_ref, gk_ref, gv_ref, halo_ref, dk_ref, dv_ref,
):
    step = pl.program_id(0)
    block = blocks - 1 - step
    continued = conts_ref[block]
    offset = pl.multiple_of(continued * SHORT, SHORT)
    tables = tuple(ref.at[pl.ds(offset, SHORT)] for ref in (cos_ref, minus_ref, plus_ref))
    now = lax.rem(step, 2)
    own = (dk_ref.at[now], dv_ref.at[now])
    before = (dk_ref.at[1 - now], dv_ref.at[1 - now])

    @pl.when(step == 0)
    def _():
        for ref in own:
            ref[...] = jnp.zeros_like(ref)

    for ref in before:
        ref[...] = jnp.zeros_like(ref)
    row = lax.broadcasted_iota(jnp.int32, (2 * count, count), 0)
    column = lax.broadcasted_iota(jnp.int32, (2 * count, count), 1)
    allowed = column <= jnp.where(row >= count, row - count, row)
    args = (q_ref, k_ref, v_ref, g_ref, kp_ref, vp_ref, tables, att_ref, gq_ref, *own, *before)

    def each(some, work):
        some = math.gcd(some, pairs)

        def body(i, carry):
            work([pl.ds(pl.multiple_of((i * some + j) * LANES, LANES), LANES) for j in range(some)])
            return carry

        lax.fori_loop(0, pairs // some, body, 0)

    pl.when(continued == 0)(lambda: each(2, lambda lanes: attend_rows(False, lanes, count, allowed, *args)))
    pl.when(continued != 0)(lambda: each(2, lambda lanes: attend_rows(True, lanes, count, allowed, *args)))
    turn = tuple(ref.at[:, pl.ds(offset, SHORT)] for ref in (tall_cos_ref, tall_sin_ref))

    def leave(lanes):
        for pair in lanes:
            gk_ref[:, pair] = unrotate_tall(own[0], pair, *[ref[...] for ref in turn])
            gv_ref[:, pair] = own[1][pair, :].astype(BF16).T

    each(1, leave)

    @pl.when(block == 0)
    def _():
        base = tuple(ref.at[:, pl.ds(0, SHORT)] for ref in (tall_cos_ref, tall_sin_ref))

        def leave_halo(lanes):
            for pair in lanes:
                halo_ref[0, :, pair] = unrotate_tall(before[0], pair, *[ref[...] for ref in base])
                halo_ref[1, :, pair] = before[1][pair, :].astype(BF16).T

        each(1, leave_halo)


def attend(conts, q, k, v, g, tables, tall, count):
    rows, head_width = q.shape
    blocks = rows // SHORT
    here = pl.BlockSpec((SHORT, head_width), lambda i, conts: (blocks - 1 - i, 0))
    after = pl.BlockSpec((SHORT, head_width), lambda i, conts: (blocks - i, 0))
    return pl.pallas_call(
        functools.partial(attend_kernel, blocks, head_width // LANES, count),
        grid_spec=pltpu.PrefetchScalarGridSpec(
            num_scalar_prefetch=1,
            grid=(blocks,),
            in_specs=[here, after, after, here, here, here] + [whole(table.shape) for table in (*tables, *tall)],
            out_specs=[here] * 4 + [held((2, SHORT, head_width))],
            scratch_shapes=[pltpu.VMEM((2, head_width, SHORT), F32)] * 2,
        ),
        out_shape=[shaped((rows, head_width), BF16)] * 4 + [shaped((2, SHORT, head_width), BF16)],
        compiler_params=params(),
        cost_estimate=BRIEF,
        name="attend",
    )(conts, q, k, v, g, k, v, *tables, *tall)


def settle_kernel(
    unit, tile, normed_ref, low_ref, grad_lows_ref, out_in_ref, att_ref, gq_ref, gk_ref, gv_ref, halo_ref, triple0_ref,
    triple1_ref, left_ref, output0_ref, output1_ref, right_ref, output_left_ref, out_ref, keep_ref, heads_ref,
    left_sums_ref, got_ref, send_ref, halo_got_ref, key_ref, value_ref, mixed_ref, triple_ref, output_ref, acc_ref,
    out_acc_ref, left_grad_ref, halo_sems, sems, load_sems,
):
    step = pl.program_id(0)
    per_device = got_ref.shape[1] // tile
    steps = unit * per_device
    halo_start = steps - SHORT // tile
    place, base = place_in_unit(unit)
    half = base // unit
    peers = unit_peers(unit)
    y_peer = chip_neighbours(unit)[1]
    halo_copies = []
    for j in range(SHORT // tile):
        part = pl.ds(j * tile, tile)
        halo_copies.append(
            pltpu.make_async_remote_copy(
                src_ref=halo_ref.at[:, part], dst_ref=halo_got_ref.at[:, part], send_sem=halo_sems.at[0, j],
                recv_sem=halo_sems.at[1, j], device_id=y_peer, device_id_type=MESH,
            )
        )
    copies = [
        [
            pltpu.make_async_remote_copy(
                src_ref=send_ref.at[s, pl.ds(t * tile, tile)], dst_ref=got_ref.at[s, pl.ds(t * tile, tile)],
                send_sem=sems.at[0, s, t], recv_sem=sems.at[1, s, t], device_id=peer, device_id_type=MESH,
            )
            for t in range(per_device)
        ]
        for s, peer in enumerate(peers)
    ]
    @pl.when(step == 0)
    def _():
        meet([y_peer, *peers])

        @pl.when(half == 1)
        def _():
            for copy in halo_copies:
                copy.start()

        for ref in (acc_ref, out_acc_ref, left_grad_ref):
            ref[...] = jnp.zeros_like(ref)

    load(
        step, load_sems,
        head_weights(
            unit, (triple0_ref, triple1_ref), right_ref, (output0_ref, output1_ref), output_left_ref, triple_ref,
            output_ref,
        ),
    )

    key_ref[...], value_ref[...] = gk_ref[...], gv_ref[...]
    for j, copy in enumerate(halo_copies):

        @pl.when((half == 0) & (step == halo_start + j))
        def _():
            copy.wait_recv()
            rows = pl.ds(j * tile, tile)
            count = output0_ref.shape[0]
            for ref, which in ((key_ref, 0), (value_ref, 1)):
                for here, there in ((pl.ds(0, count), pl.ds(count, count)), (pl.ds(count, count), pl.ds(0, count))):
                    ref[:, here] = (ref[:, here].astype(F32) + halo_got_ref[which, rows, there].astype(F32)).astype(BF16)

    normed = normed_ref[...]
    low = low_ref[...]
    grad_low_out = grad_lows_ref[:, :LANES]
    head_width = output0_ref.shape[0]
    first = low_lanes()
    for pair in range(2 * head_width // LANES):
        q, k, v = (ref[:, pair * LANES : (pair + 1) * LANES] for ref in (gq_ref, key_ref, value_ref))
        for part, value in enumerate((jnp.where(first, q, k), jnp.where(first, v, q), jnp.where(first, k, v))):
            mixed_ref[:, (3 * pair + part) * LANES : (3 * pair + part + 1) * LANES] = value
    mixed = mixed_ref[...]
    att = att_ref[...]
    width = normed.shape[1]
    backward = dot_nt(mixed, triple_ref[...])
    forward = dot_nn(att, output_ref[...])
    grad_low = backward[:, width:].astype(BF16)
    grad = (backward[:, :width] + dot_nt(grad_low, left_ref[...])).astype(BF16)
    out_ref[...] = out_in_ref[...] + forward[:, :width]
    low_att = forward[:, width:].astype(BF16)

    @pl.when(step // per_device == place)
    def _():
        keep_ref[:, :width] = grad
        keep_ref[:, width:] = low_att

    span = pl.ds(pl.multiple_of(lax.rem(step, per_device) * tile, tile), tile)
    for s in range(unit - 1):
        owner = lax.rem(place + unit - (s + 1), unit)

        @pl.when(step // per_device == owner)
        def _():
            send_ref[s, span, :width] = grad
            send_ref[s, span, width:] = low_att

        for t in range(per_device):
            pl.when(step == owner * per_device + t)(copies[s][t].start)

    acc_ref[...] += dot_tn(low, mixed)
    out_acc_ref[...] += dot_tn(grad_low_out, att)
    left_grad_ref[...] += dot_tn(grad_low, normed)

    @pl.when(step == steps - 1)
    def _():
        size = 3 * head_width
        for j in range(2):
            heads_ref[j, :, :size] = acc_ref[:, j * size : (j + 1) * size].astype(BF16)
            heads_ref[j, :, size:] = out_acc_ref[:, j * head_width : (j + 1) * head_width].astype(BF16)
        quarters(left_sums_ref, left_grad_ref[...])

        @pl.when(half == 1)
        def _():
            for copy in halo_copies:
                copy.wait_send()

        for group in copies:
            for copy in group:
                copy.wait()


def settle(unit, normed, low, grad_lows, out, heads, halo, triples, left, outputs, right, output_left, tile):
    rows, width = normed.shape
    own_rows = rows // unit
    head_width = outputs[0].shape[0]
    steps, per_device = rows // tile, own_rows // tile
    anywhere = pl.BlockSpec(memory_space=pl.ANY)

    def kept(i):
        return (jnp.clip(i - place_in_unit(unit)[0] * per_device, 0, per_device - 1), 0)

    return pl.pallas_call(
        functools.partial(settle_kernel, unit, tile),
        grid=(steps,),
        in_specs=[rows_of(tile, width), rows_of(tile, LANES), rows_of(tile, 2 * LANES), rows_of(tile, width)]
        + [rows_of(tile, 2 * head_width)] * 4
        + [anywhere]
        + [anywhere, anywhere, whole(left.shape), anywhere, anywhere, anywhere, anywhere],
        out_specs=[
            rows_of(tile, width),
            pl.BlockSpec((tile, width + LANES), kept),
            held((2, LANES, 4 * head_width)),
            held((2, 2, LANES, width // 4)),
            anywhere,
        ],
        scratch_shapes=[
            pltpu.VMEM((unit - 1, own_rows, width + LANES), BF16),
            pltpu.VMEM((2, SHORT, 2 * head_width), BF16),
            pltpu.VMEM((tile, 2 * head_width), BF16),
            pltpu.VMEM((tile, 2 * head_width), BF16),
            pltpu.VMEM((tile, 6 * head_width), BF16),
            pltpu.VMEM((width + LANES, 6 * head_width), BF16),
            pltpu.VMEM((2 * head_width, width + LANES), BF16),
            pltpu.VMEM((LANES, 6 * head_width), F32),
            pltpu.VMEM((LANES, 2 * head_width), F32),
            pltpu.VMEM((LANES, width), F32),
            pltpu.SemaphoreType.DMA((2, SHORT // tile)),
            pltpu.SemaphoreType.DMA((2, unit - 1, per_device)),
            pltpu.SemaphoreType.DMA((8,)),
        ],
        out_shape=[
            shaped((rows, width), F32),
            shaped((own_rows, width + LANES), BF16),
            shaped((2, LANES, 4 * head_width), BF16),
            shaped((2, 2, LANES, width // 4), BF16),
            shaped((unit - 1, own_rows, width + LANES), BF16),
        ],
        compiler_params=pltpu.CompilerParams(
            dimension_semantics=("arbitrary",), vmem_limit_bytes=VMEM_LIMIT, collective_id=5, has_side_effects=True
        ),
        cost_estimate=BRIEF,
        name="settle",
    )(normed, low, grad_lows, out, *heads, halo, *triples, left, *outputs, right, output_left)


FEED_ORDERS = ("xz", "zx", "xz", "zx")


def sum_kernel(size, feed_ref, both_ref, heads_ref, left_ref, feed_out_ref, both_out_ref, heads_out_ref, left_out_ref,
               cross_sems, local_sems, *refs):
    net = Net()
    meet([net.x_peer, net.y_peer, net.core_peer, *net.z_peers])
    locals_, crossing = [], []

    def hand_over(slot, full, out, first, second):
        for place, at in ((0, first), (1, second)):
            target = out.at[net.core, at]
            local = pltpu.make_async_copy(full.at[place], target, local_sems.at[slot, place])
            local.start()
            locals_.append(local)
            crossing.append(net.copy(full.at[place], target, cross_sems, 2 * slot + place, net.core_peer))
            net.start(crossing[-1:])

    split = len(sum_scratch("xz", size))
    feed_refs = [refs[j * split : (j + 1) * split] for j in range(len(FEED_ORDERS))]
    both_refs = refs[len(FEED_ORDERS) * split :]
    parts = split_columns(both_ref.shape[-1])
    per_part = (len(both_refs) - 3) // 2
    scratches = (both_refs[3 : 3 + per_part], both_refs[3 + per_part :])
    running = [sum_both(net, parts, both_ref, *both_refs[:3], scratches)]
    running += [
        sum_chunk(net, order, feed_ref.at[:, :, :, pl.ds(j * size, size)], feed_refs[j])
        for j, order in enumerate(FEED_ORDERS)
    ]

    def both_done():
        start = 0
        for j, (_, count) in enumerate(parts):
            columns = both_out_ref.at[:, :, :, :, :, pl.ds(start, count)]
            hand_over(j, scratches[j][5], columns, net.half, net.other_half)
            start += count

    def feed_done(j):
        columns = feed_out_ref.at[:, :, :, :, :, pl.ds(j * size, size)]
        hand_over(4 + j, feed_refs[j][5], columns, net.other_half, net.half)

    for k in range(max(len(stage) for stage in running)):
        for j, stage in enumerate(running):
            if k < len(stage):
                stage[k]()
            if k == len(stage) - 1:
                both_done() if j == 0 else feed_done(j - 1)
        if k == 0:
            hand_over(2, heads_ref, heads_out_ref, net.half, net.other_half)
            hand_over(3, left_ref, left_out_ref, net.half, net.other_half)
    for copy in locals_:
        copy.wait()
    for copy in crossing:
        copy.wait_recv()
    for copy in net.started:
        copy.wait_send()


def sum_all(feed, both, heads, left):
    arrays = (feed.reshape(SUM_ROWS + feed.shape[-1:]), both.reshape((2, 2) + SUM_ROWS + both.shape[-1:]), heads, left)
    size = feed.shape[-1] // len(FEED_ORDERS)
    slots = 4 + len(FEED_ORDERS)
    outs = [shaped((2, 2) + SUM_ROWS + array.shape[-1:], BF16) for array in arrays]
    results = pl.pallas_call(
        functools.partial(sum_kernel, size),
        out_shape=outs,
        in_specs=[pl.BlockSpec(memory_space=pltpu.VMEM)] * 4,
        out_specs=[pl.BlockSpec(memory_space=pl.ANY)] * 4,
        scratch_shapes=[pltpu.SemaphoreType.DMA((2, 2 * slots)), pltpu.SemaphoreType.DMA((slots, 2))]
        + [shape for order in FEED_ORDERS for shape in sum_scratch(order, size)]
        + both_scratch(split_columns(both.shape[-1])),
        compiler_params=pltpu.CompilerParams(
            collective_id=2, has_side_effects=True, vmem_limit_bytes=VMEM_LIMIT
        ),
        cost_estimate=BRIEF,
        name="sum_all",
    )(*arrays)
    return [value.reshape(2, 2, LANES, value.shape[-1]) for value in results]


def unpack_kernel(triple_width, feed_ref, both_ref, heads_ref, left_ref, triple_ref, output_ref, up_ref, down_ref,
                  triple_left_ref, up_left_ref, output_right_ref, down_right_ref, *norm_refs):
    triple_ref[...] = heads_ref[0, 0, :, :triple_width].astype(F32)
    output_ref[...] = heads_ref[0, 0, :, triple_width:].astype(F32).T
    hidden = up_ref.shape[1]
    up_ref[...] = feed_ref[0, 0, :, :hidden].astype(F32)
    down_ref[...] = feed_ref[0, 0, :, hidden:].astype(F32).T
    size = triple_left_ref.shape[0]
    triple_left_ref[...] = left_ref[0, 0].astype(F32).T
    up_left_ref[...] = both_ref[0, 0, :, :size].astype(F32).T
    output_right_ref[...] = both_ref[0, 0, :, size : 2 * size].astype(F32)
    down_right_ref[...] = both_ref[0, 0, :, 2 * size : 3 * size].astype(F32)
    for q, ref in enumerate(norm_refs):

        @pl.when(pl.program_id(0) == q)
        def _():
            ref[...] = both_ref[0, 0, : ref.shape[0], 3 * size :].astype(F32)


def unpack(feed, both, heads, left, triple_width):
    arrays = (feed, both, heads, left)
    hidden, quarter = feed.shape[-1] // 2, left.shape[-1]
    width, head_width = 4 * quarter, heads.shape[-1] - triple_width

    def tall(rows):
        return pl.BlockSpec((rows, LANES), lambda s: (s, 0))

    def wide(cols):
        return pl.BlockSpec((LANES, cols), lambda s: (0, s))

    return pl.pallas_call(
        functools.partial(unpack_kernel, triple_width),
        grid=(4,),
        in_specs=[
            pl.BlockSpec((1, 1) + value.shape[2:], lambda s: (lax.rem(s, 2), s // 2, 0, 0)) for value in arrays
        ],
        out_specs=[
            wide(triple_width), tall(head_width), wide(hidden), tall(hidden), tall(quarter), tall(quarter),
            wide(quarter), wide(quarter), *[held((width // LANES, LANES))] * 4,
        ],
        out_shape=[
            shaped((LANES, 4 * triple_width), F32),
            shaped((4 * head_width, LANES), F32),
            shaped((LANES, 4 * hidden), F32),
            shaped((4 * hidden, LANES), F32),
            shaped((width, LANES), F32),
            shaped((width, LANES), F32),
            shaped((LANES, width), F32),
            shaped((LANES, width), F32),
        ]
        + [shaped((width // LANES, LANES), F32)] * 4,
        compiler_params=params(),
        cost_estimate=BRIEF,
        name="unpack",
    )(*arrays)


def shards(
    ranks,
    groups,
    block_input,
    sequence_lengths,
    first_gain,
    first_shift,
    second_gain,
    second_shift,
    triple_weight,
    triple_left,
    triple_right,
    output_weight,
    output_left,
    output_right,
    expand_weight,
    expand_left,
    expand_right,
    shrink_weight,
    shrink_left,
    shrink_right,
    cotangent,
):
    unit = ranks // 2
    own_rows, width = block_input.shape
    rows = own_rows * unit
    blocks = rows // SHORT
    tile = math.gcd(own_rows, 256)
    triple_width = triple_weight.shape[1]
    head_width = output_weight.shape[0]
    hidden = expand_weight.shape[1]
    mp = lax.axis_index("mp")
    half = mp // unit
    place = lax.rem(mp, unit)
    far = lax.rem(mp + unit, ranks)
    swap = [(m, (m + unit) % ranks) for m in range(ranks)]

    tables = rotary_tables()
    beside = [[(d, d ^ bit) for d in range(groups)] for bit in (1, 2)]
    continues = find_flags(sequence_lengths[0])
    conts = lax.dynamic_slice_in_dim(continues, half * blocks, blocks, 0)
    gain1, shift1 = first_gain[None, :], first_shift[None, :]
    gain2, shift2 = second_gain[None, :], second_shift[None, :]

    (normed1, normed2, dy, low2, grad_lows, out, grad2, low_act, grad_low2, feed_sums, triple_far,
     output_far, x_halo, expand_half, shrink_half) = feed_first(
        unit, block_input, cotangent, (gain1, shift1, gain2, shift2), expand_weight, expand_left, expand_right,
        shrink_weight, shrink_left, output_right, shrink_right, triple_weight, output_weight, tile,
    )
    expand_piece = lax.ppermute(expand_half, "mp", swap)
    shrink_piece = lax.ppermute(shrink_half, "mp", swap)
    low1, q, k, v, g = project(
        unit, conts, x_halo, normed1, dy, grad_lows, gain1, shift1, (triple_weight, triple_far), triple_left,
        triple_right, (output_weight, output_far), output_left, tables, tile,
    )
    att, gq, gk, gv, halo = attend(conts, q, k, v, g, tables, tall_tables(), 256)
    expand_piece, shrink_piece, att = lax.optimization_barrier((expand_piece, shrink_piece, att))
    expand_other = lax.ppermute(expand_piece, "dp", beside[0])
    shrink_other = lax.ppermute(shrink_piece, "dp", beside[1])
    out, keep1, heads, left, got1 = settle(
        unit, normed1, low1, grad_lows, out, (att, gq, gk, gv), halo, (triple_weight, triple_far), triple_left,
        (output_weight, output_far), triple_right, output_left, tile,
    )
    hosted = ranks == 4 and groups == 8
    block_output, input_gradient, feed_sums, both, heads_sum, left_sum = feed_second(
        unit, normed2, low2, dy, grad_lows, out, grad2, low_act, grad_low2, block_input, keep1, got1, (gain1, gain2),
        output_right, shrink_right, (expand_piece, expand_other), expand_left, expand_right,
        (shrink_piece, shrink_other), shrink_left, feed_sums, heads, left, hosted, tile,
    )
    if hosted:
        (triple_right_sum, output_left_sum, expand_right_sum, shrink_left_sum, triple_left_sum, expand_left_sum,
         output_right_sum, shrink_right_sum, *norms) = unpack(
            *sum_all(feed_sums, both, heads_sum, left_sum), triple_width
        )
        norms = [value.reshape(width) for value in norms]
    else:

        def spread(*placed):
            size = placed[0][0].shape[1]
            wide = jnp.zeros((LANES, size * ranks), BF16)
            for value, shard in placed:
                wide = lax.dynamic_update_slice_in_dim(wide, value, shard * size, 1)
            return wide

        def joined(value):
            return value.transpose(2, 1, 0, 3).reshape(LANES, -1)

        def columns(value, start, size):
            return value.reshape(LANES, ranks, -1)[:, :, start : start + size].reshape(LANES, -1).astype(F32)

        heads, feed, left, both = lax.psum(
            (spread((heads[0], mp), (heads[1], far)), spread((feed_sums, far)), left, both), ("dp", "mp")
        )
        triple_right_sum = columns(heads, 0, triple_width)
        output_left_sum = columns(heads, triple_width, head_width).T
        expand_right_sum = columns(feed, 0, hidden)
        shrink_left_sum = columns(feed, hidden, hidden).T
        triple_left_sum = joined(left).astype(F32).T
        quarter = width // 4
        expand_left_sum = joined(both[..., :quarter]).astype(F32).T
        output_right_sum = joined(both[..., quarter : 2 * quarter]).astype(F32)
        shrink_right_sum = joined(both[..., 2 * quarter : 3 * quarter]).astype(F32)
        norms = both[:, :, : width // LANES, 3 * quarter :].transpose(1, 0, 2, 3).reshape(4, width).astype(F32)
    return (
        block_output,
        input_gradient,
        norms[0],
        norms[1],
        norms[2],
        norms[3],
        triple_left_sum,
        triple_right_sum,
        output_left_sum,
        output_right_sum,
        expand_left_sum,
        expand_right_sum,
        shrink_left_sum,
        shrink_right_sum,
    )


def solution(mesh):
    placed = (
        P(("dp", "mp"), None),
        P("dp", None),
        P(),
        P(),
        P(),
        P(),
        P(None, "mp"),
        P(),
        P(),
        P("mp", None),
        P(),
        P(),
        P(None, "mp"),
        P(),
        P(),
        P("mp", None),
        P(),
        P(),
        P(("dp", "mp"), None),
    )
    return jax.shard_map(
        functools.partial(shards, mesh.shape["mp"], mesh.shape["dp"]),
        mesh=mesh,
        in_specs=placed,
        out_specs=(P(("dp", "mp"), None), P(("dp", "mp"), None)) + (P(),) * 12,
        check_vma=False,
    )
```

```python
import functools
import math

import jax
import jax.numpy as jnp
import numpy as np
from jax import lax
from jax.experimental import pallas as pl
from jax.experimental.pallas import tpu as pltpu
from jax.sharding import PartitionSpec as P

HEAD_DIM = 64
ROT = 16
SHORT = 512
TOK_GRP = 3072
SLOTS = 6
EPS = 1e-05
LANES = 128
MESH = pl.DeviceIdType.MESH
BF16 = jnp.bfloat16
F32 = jnp.float32
VMEM_LIMIT = 56 * 1024 * 1024
BRIEF = pl.CostEstimate(flops=1, bytes_accessed=1, transcendentals=0)


def dot_nn(former, latter):
    return lax.dot_general(
        former, latter, (((1,), (0,)), ((), ())), preferred_element_type=F32
    )


def dot_nt(former, latter):
    return lax.dot_general(
        former, latter, (((1,), (1,)), ((), ())), preferred_element_type=F32
    )


def dot_tn(former, latter):
    return lax.dot_general(
        former, latter, (((0,), (0,)), ((), ())), preferred_element_type=F32
    )


def find_flags(group_lengths):
    seq_ends = jnp.cumsum(group_lengths, dtype=jnp.int32)
    starts = seq_ends - group_lengths
    block_starts = jnp.arange(SLOTS, dtype=jnp.int32) * SHORT
    begins = jnp.any(
        (starts[None, :] == block_starts[:, None]) & (group_lengths[None, :] > 0), axis=1
    )
    return jnp.where(begins, 0, 1).astype(jnp.int32)


def rotary_tables():
    half = ROT // 2
    frequency = np.exp(
        np.arange(half, dtype=np.float32) * np.float32(-2.0 * math.log(10000.0) / ROT)
    ).astype(np.float32)
    angles = np.arange(2 * SHORT, dtype=np.float32)[:, None] * frequency[None, :]
    cosine = np.ones((2 * SHORT, LANES), np.float32)
    minus = np.zeros((2 * SHORT, LANES), np.float32)
    plus = np.zeros((2 * SHORT, LANES), np.float32)
    for base in range(0, LANES, HEAD_DIM):
        cosine[:, base : base + half] = np.cos(angles)
        cosine[:, base + half : base + ROT] = np.cos(angles)
        minus[:, base : base + half] = -np.sin(angles)
        plus[:, base + half : base + ROT] = np.sin(angles)
    return jnp.asarray(cosine), jnp.asarray(minus), jnp.asarray(plus)


def tall_tables():
    half = ROT // 2
    frequency = np.exp(
        np.arange(half, dtype=np.float32) * np.float32(-2.0 * math.log(10000.0) / ROT)
    ).astype(np.float32)
    angles = frequency[:, None] * np.arange(2 * SHORT, dtype=np.float32)[None, :]
    return jnp.asarray(np.cos(angles)), jnp.asarray(np.sin(angles))


def low_lanes():
    return lax.broadcasted_iota(jnp.int32, (1, LANES), 1) < HEAD_DIM


def rotate(pair, cosine, minus, plus):
    half = ROT // 2
    return (
        pair * cosine
        + pltpu.roll(pair, LANES - half, 1) * minus
        + pltpu.roll(pair, half, 1) * plus
    )


def unrotate(pair, cosine, minus, plus):
    half = ROT // 2
    return (
        pair * cosine
        - pltpu.roll(pair, LANES - half, 1) * minus
        - pltpu.roll(pair, half, 1) * plus
    )


def normalize(values, gain, shift):
    center = values - jnp.mean(values, axis=-1, keepdims=True)
    spread = jnp.mean(center * center, axis=-1, keepdims=True)
    return center * lax.rsqrt(spread + EPS) * gain + shift


def whole(shape):
    return pl.BlockSpec(
        shape, lambda *idx: (0,) * len(shape), pipeline_mode=pl.Buffered(1)
    )


def held(shape):
    return pl.BlockSpec(shape, lambda *idx: (0,) * len(shape))


def rows_of(tile, width):
    return pl.BlockSpec((tile, width), lambda i, *refs: (i, 0))


def shaped(shape, dtype):
    return jax.ShapeDtypeStruct(shape, dtype)


def params(semantics=1):
    return pltpu.CompilerParams(
        dimension_semantics=("arbitrary",) * semantics, vmem_limit_bytes=VMEM_LIMIT
    )


SUM_ROWS = (2, 4, 16)


class Net:
    def __init__(self):
        dp, mp = lax.axis_index("dp"), lax.axis_index("mp")
        self.half, self.core = mp // 2, lax.rem(mp, 2)
        self.x, self.z = lax.rem(dp, 2), dp // 2
        self.other_half, self.other_core, self.other_x = 1 - self.half, 1 - self.core, 1 - self.x
        self.x_peer = (dp + 1 - 2 * self.x, mp)
        self.y_peer = (dp, mp + 2 - 4 * self.half)
        self.core_peer = (dp, mp + 1 - 2 * self.core)
        self.z_places = [lax.rem(self.z + j, 4) for j in range(1, 4)]
        self.z_peers = [(place * 2 + self.x, mp) for place in self.z_places]
        self.started = []

    def copy(self, src, dst, sems, slot, peer):
        return pltpu.make_async_remote_copy(
            src_ref=src, dst_ref=dst, send_sem=sems.at[0, slot], recv_sem=sems.at[1, slot], device_id=peer,
            device_id_type=MESH,
        )

    def start(self, copies):
        for copy in copies:
            copy.start()
        self.started += copies


def arrive(copies):
    for copy in copies:
        copy.wait_recv()


def added(first, *others):
    total = first.astype(F32)
    for other in others:
        total = total + other.astype(F32)
    return total.astype(BF16)


def sum_scratch(order, size):
    one = (16, size)
    first = {"yxz": ((2, 4), (2, 4)), "xyz": ((2, 4), (2, 4)), "xz": ((4,), (4,)), "zx": ((3, 2), (2,))}[order]
    second = {"yxz": ((4,), (4,)), "xyz": ((4,), (4,)), "xz": ((3,), (1,)), "zx": ((1,), (1,))}[order]
    return [pltpu.VMEM(shape + one, BF16) for shape in (*first, *second, (3,), (2, 2, 4))] + [
        pltpu.SemaphoreType.DMA((2, 12))
    ]


def sum_chunk(net, order, source, scratch):
    got1, work1, got2, work2, got3, full, sems = scratch
    x, z, other_x = net.x, net.z, net.other_x
    own, rows, plane = full.at[0, x, z], full.at[0, x], full.at[0, :, z]

    def to_z(src, dst, slot):
        return [
            net.copy(src(place), dst(j), sems, slot + j, peer)
            for j, (place, peer) in enumerate(zip(net.z_places, net.z_peers))
        ]

    def one(src, dst, slot, peer):
        return [net.copy(src, dst, sems, slot, peer)]

    last = work1 if order == "xz" else work2
    if order != "xyz":
        over_y = one(full.at[0], full.at[1], 9, net.y_peer)
    if order == "zx":
        spread = to_z(lambda place: source.at[:, place], lambda j: got1.at[j], 2)
        cross = one(work1.at[other_x], got2.at[0], 0, net.x_peer)
        back = one(own, own, 8, net.x_peer)
        gather = to_z(lambda place: plane, lambda j: plane, 5)
    else:
        spread = to_z(lambda place: last.at[place], lambda j: got3.at[j], 2)
        gather = to_z(lambda place: own, lambda j: own, 5)
        if order == "yxz":
            first = one(source.at[1], got1, 0, net.y_peer)
            second = one(work1.at[other_x], got2, 1, net.x_peer)
        elif order == "xyz":
            first = one(source.at[:, other_x], got1, 0, net.x_peer)
            second = one(work1.at[1], got2, 1, net.y_peer)
            over_y = one(rows, full.at[1, x], 8, net.y_peer)
            over_x = one(full.at[:, x], full.at[:, x], 9, net.x_peer)
        else:
            first = one(source.at[other_x], got1, 0, net.x_peer)
        if order != "xyz":
            over_x = one(rows, rows, 8, net.x_peer)

    def begin(copies):
        return lambda: net.start(copies)

    def after(copies, work, then):
        def stage():
            arrive(copies)
            if work is not None:
                target, value = work
                target[...] = value()
            if then is not None:
                net.start(then)

        return stage

    if order == "zx":
        mine = (work1, lambda: added(source[:, z], got1[0], got1[1], got1[2]))
        total = (own, lambda: added(work1[x], got2[0]))
        return [
            begin(spread), after(spread, mine, cross), after(cross, total, back), after(back, None, gather),
            after(gather, None, over_y), after(over_y, None, None),
        ]
    total = (own, lambda: added(last[z], got3[0], got3[1], got3[2]))
    if order == "yxz":
        head = [begin(first), after(first, (work1, lambda: added(source[0], got1[...])), second)]
        head.append(after(second, (work2, lambda: added(work1[x], got2[...])), spread))
    elif order == "xyz":
        head = [begin(first), after(first, (work1, lambda: added(source[:, x], got1[...])), second)]
        head.append(after(second, (work2, lambda: added(work1[0], got2[...])), spread))
    else:
        head = [begin(first), after(first, (work1, lambda: added(source[x], got1[...])), spread)]
    one_way, other_way = (over_y, over_x) if order == "xyz" else (over_x, over_y)
    return head + [
        after(spread, total, gather), after(gather, None, one_way), after(one_way, None, other_way),
        after(other_way, None, None),
    ]


def sum_both(net, parts, both, got, total, core_sems, scratches):
    exchange = [net.copy(both.at[net.other_core], got, core_sems, 0, net.core_peer)]
    chunks, start = [], 0
    for (order, size), scratch in zip(parts, scratches):
        chunks.append(sum_chunk(net, order, total.at[:, :, :, :, pl.ds(start, size)], scratch))
        start += size

    def combine():
        arrive(exchange)
        for place, at in ((0, net.half), (1, net.other_half)):
            total[place] = added(both[net.core, at], got[at])
        for chunk in chunks:
            chunk[0]()

    def together(k):
        def stage():
            for chunk in chunks:
                if k < len(chunk):
                    chunk[k]()

        return stage

    longest = max(len(chunk) for chunk in chunks)
    return [lambda: net.start(exchange), combine] + [together(k) for k in range(1, longest)]


def both_scratch(parts):
    size = sum(part[1] for part in parts)
    return [
        pltpu.VMEM((2,) + SUM_ROWS + (size,), BF16),
        pltpu.VMEM((2,) + SUM_ROWS + (size,), BF16),
        pltpu.SemaphoreType.DMA((2, 1)),
    ] + [shape for part in parts for shape in sum_scratch(*part)]


def split_columns(size):
    count = (size // 2 + LANES - 1) // LANES * LANES
    return (("yxz", count), ("xyz", size - count))


def quarters(ref, *arrays):
    start = 0
    for array in arrays:
        size = array.shape[1] // 4
        for q in range(4):
            ref[q % 2, q // 2, :, start : start + size] = array[:, q * size : (q + 1) * size].astype(BF16)
        start += size


def gelu_parts(hidden):
    cdf = 0.5 + 0.5 * lax.erf(hidden * math.sqrt(0.5))
    density = jnp.exp(-0.5 * hidden * hidden) * (1.0 / math.sqrt(2.0 * math.pi))
    return hidden * cdf, cdf + hidden * density


def feed_core(rows, grads, up_ref, down_ref, act_ref, grad_ref, hidden_step):
    for start in range(0, up_ref.shape[1], hidden_step):
        cols = pl.ds(start, hidden_step)
        hidden = dot_nn(rows, up_ref[:, cols])
        grad_act = dot_nt(grads, down_ref[cols, :])
        activated, slope = gelu_parts(hidden)
        act_ref[:, cols] = activated.astype(BF16)
        grad_ref[:, cols] = (grad_act * slope).astype(BF16)


def shard_index(unit, far):
    return lax.rem(lax.axis_index("mp") + (unit if far else 0), 2 * unit)


def columns_of(ref, size, shard):
    return ref.at[:, pl.ds(pl.multiple_of(shard * size, size), size)]


def rows_at(ref, size, shard):
    return ref.at[pl.ds(pl.multiple_of(shard * size, size), size)]


def load(step, sems, pairs, between=None):
    copies = [pltpu.make_async_copy(src, dst, sems.at[j]) for j, (src, dst) in enumerate(pairs)]

    @pl.when(step == 0)
    def _():
        for copy in copies:
            copy.start()
        if between is not None:
            between()
        for copy in copies:
            copy.wait()


def head_weights(unit, triples, right, outputs, output_left, triple_ref, output_ref):
    width = triples[0].shape[0]
    head_width = outputs[0].shape[0]
    size = 3 * head_width
    pairs = []
    for j in range(2):
        shard = shard_index(unit, j == 1)
        cols, rows = pl.ds(j * size, size), pl.ds(j * head_width, head_width)
        pairs += [
            (triples[j], triple_ref.at[pl.ds(0, width), cols]),
            (columns_of(right, size, shard), triple_ref.at[pl.ds(width, LANES), cols]),
            (outputs[j], output_ref.at[rows, pl.ds(0, width)]),
            (rows_at(output_left, head_width, shard), output_ref.at[rows, pl.ds(width, LANES)]),
        ]
    return pairs


def chip_neighbours(unit):
    dp = lax.axis_index("dp")
    mp = lax.axis_index("mp")
    lead = lax.rem(dp, 2)
    return lead, (dp, lax.rem(mp + unit, 2 * unit)), (dp + 1 - 2 * lead, mp)


def leads():
    dp = lax.axis_index("dp")
    return lax.rem(dp, 2), lax.rem(dp // 2, 2)


def group_neighbours():
    dp, mp = lax.axis_index("dp"), lax.axis_index("mp")
    first, second = leads()
    return (dp + 1 - 2 * first, mp), (dp + 2 - 4 * second, mp)


def courier(unit, pairs, chunks, sems):
    first, second = leads()
    mine = first + 2 * second
    y_peer = chip_neighbours(unit)[1]
    x_peer, z_peer = group_neighbours()
    over_y, once, twice = [], [], []
    for k in range(chunks):
        over_y.append([])
        once.append([])
        twice.append([])
        for j, (own, far) in enumerate(pairs):
            count = own.shape[0] // 4 // chunks

            def copy(kind, src, dst, quarter, start, size, peer, k=k, j=j, count=count):
                span = pl.ds(pl.multiple_of((quarter * chunks + k) * count + start, size), size)
                return pltpu.make_async_remote_copy(
                    src_ref=src.at[span], dst_ref=dst.at[span], send_sem=sems.at[0, kind, k, j],
                    recv_sem=sems.at[1, kind, k, j], device_id=peer, device_id_type=MESH,
                )

            by_x, by_z = mine + 1 - 2 * first, mine + 2 - 4 * second
            over_y[-1].append(copy(0, own, far, mine, 0, count, y_peer))
            once[-1] += [copy(1, far, far, mine, 0, count, x_peer), copy(2, far, far, mine, 0, count, z_peer)]
            twice[-1] += [
                copy(3, far, far, by_x, 0, count // 2, z_peer),
                copy(4, far, far, by_z, count // 2, count // 2, x_peer),
            ]
    return over_y, once, twice


def meet(peers):
    barrier = pltpu.get_barrier_semaphore()
    for peer in peers:
        pl.semaphore_signal(barrier, inc=1, device_id=peer, device_id_type=MESH)
    pl.semaphore_wait(barrier, len(peers))


def place_in_unit(unit):
    mp = lax.axis_index("mp")
    return lax.rem(mp, unit), mp - lax.rem(mp, unit)


def unit_peers(unit):
    place, base = place_in_unit(unit)
    return [(lax.axis_index("dp"), base + lax.rem(place + unit - s, unit)) for s in range(1, unit)]


def halo_copies(unit, x_ref, halo_ref, y_sems, unit_sems):
    own_rows = x_ref.shape[0]
    chunk = math.gcd(own_rows, 128)
    dp = lax.axis_index("dp")
    found = []
    for k in range(SHORT // chunk):
        row = unit * own_rows - SHORT + k * chunk
        holder, start = row // own_rows, row % own_rows
        target = halo_ref.at[pl.ds(k * chunk, chunk)]
        over_y = pltpu.make_async_remote_copy(
            src_ref=x_ref.at[pl.ds(start, chunk)], dst_ref=target, send_sem=y_sems.at[0, k], recv_sem=y_sems.at[1, k],
            device_id=(dp, unit + holder), device_id_type=MESH,
        )
        spread = [
            pltpu.make_async_remote_copy(
                src_ref=target, dst_ref=target, send_sem=unit_sems.at[0, k, s - 1], recv_sem=unit_sems.at[1, k, s - 1],
                device_id=(dp, unit + (holder + s) % unit), device_id_type=MESH,
            )
            for s in range(1, unit)
        ]
        found.append((holder, over_y, spread))
    return found


def feed_first_kernel(
    unit, tile, x_ref, dy_ref, gain1_ref, shift1_ref, gain2_ref, shift2_ref, up_own_ref, up_left_ref, up_right_ref,
    down_own_ref, down_left_ref, output_right_ref, down_right_ref, x_all_ref, dy_all_ref, triple_ref, output_ref, normed1_ref,
    normed_ref, dy_full_ref, low_ref, grad_lows_ref, out_ref, grad_ref, low_act_ref, grad_low_ref, sums_ref,
    triple_far_ref, output_far_ref, halo_ref, up_half_ref, down_half_ref, act_ref, gh_ref, up_ref, down_ref, acc_ref,
    xs_ref, x_got_ref, dy_got_ref, courier_sems, unit_sems, halo_y_sems, halo_unit_sems, local_sems, load_sems,
):
    step = pl.program_id(0)
    width, hidden = up_own_ref.shape
    weights = (
        (up_own_ref, up_ref.at[pl.ds(0, width)]),
        (columns_of(up_right_ref, hidden, shard_index(unit, False)), up_ref.at[pl.ds(width, LANES)]),
        (down_own_ref, down_ref.at[:, pl.ds(0, width)]),
        (rows_at(down_left_ref, hidden, shard_index(unit, False)), down_ref.at[:, pl.ds(width, LANES)]),
    )
    own_rows = x_all_ref.shape[0]
    per_device = own_rows // tile
    steps = unit * per_device
    chunks = courier_sems.shape[2]
    place, base = place_in_unit(unit)
    half = base // unit
    peers = unit_peers(unit)
    over_y, once, twice = courier(
        unit, ((triple_ref, triple_far_ref), (output_ref, output_far_ref)), chunks, courier_sems
    )
    halo = halo_copies(unit, x_all_ref, halo_ref, halo_y_sems, halo_unit_sems)
    rows_out = [
        pltpu.make_async_remote_copy(
            src_ref=src, dst_ref=dst.at[j], send_sem=unit_sems.at[0, which, j], recv_sem=unit_sems.at[1, which, j],
            device_id=peer, device_id_type=MESH,
        )
        for j, peer in enumerate(peers)
        for which, (src, dst) in enumerate(((x_all_ref, x_got_ref), (dy_all_ref, dy_got_ref)))
    ]
    kept_halves = [
        pltpu.make_async_copy(
            src.at[
                pl.ds(pl.multiple_of(lead * dst.shape[0], dst.shape[0]), dst.shape[0]), pl.ds(0, dst.shape[1])
            ],
            dst,
            local_sems.at[j],
        )
        for j, (lead, src, dst) in enumerate(zip(leads(), (up_ref, down_ref), (up_half_ref, down_half_ref)))
    ]

    neighbours = [chip_neighbours(unit)[1], *group_neighbours(), *peers]

    def greet():
        meet(neighbours)
        for copy in rows_out:
            copy.start()
        for copies in over_y:
            for copy in copies:
                copy.start()

    load(step, load_sems, weights, greet)
    for holder, copy, _ in halo:
        pl.when((step == 0) & (half == 0) & (place == holder))(copy.start)

    @pl.when(step == 0)
    def _():
        for copy in kept_halves:
            copy.start()
        xs_ref[...] = x_ref[...]
        dy_full_ref[...] = dy_ref[...]

    @pl.when((step > 0) & (step < per_device))
    def _():
        xs_ref[...] = x_ref[...]
        dy_full_ref[...] = dy_ref[...]

    for slot in range(unit - 1):

        @pl.when(step == per_device * (slot + 1))
        def _():
            for which in range(2):
                rows_out[2 * slot + which].wait_recv()

        @pl.when((step >= per_device * (slot + 1)) & (step < per_device * (slot + 2)))
        def _():
            span = pl.ds(pl.multiple_of((step - per_device * (slot + 1)) * tile, tile), tile)
            xs_ref[...] = x_got_ref[slot, span]
            dy_full_ref[...] = dy_got_ref[slot, span]

    for k in range(chunks):

        @pl.when(step == min(k + 2, steps - 1))
        def _():
            for copy in over_y[k]:
                copy.wait_recv()
            for copy in once[k]:
                copy.start()

    for k in range(chunks):

        @pl.when(step == min(k + 4, steps - 1))
        def _():
            for copy in once[k]:
                copy.wait_recv()
            for copy in twice[k]:
                copy.start()

    for holder, copy, spread_copies in halo:

        @pl.when((step == steps - 1) & (half == 1) & (place == holder))
        def _():
            copy.wait_recv()
            for other in spread_copies:
                other.start()

    x = xs_ref[...].astype(F32)
    center = x - jnp.mean(x, axis=-1, keepdims=True)
    spread = jnp.mean(center * center, axis=-1, keepdims=True)
    scaled = center * lax.rsqrt(spread + EPS)
    normed1_ref[...] = (scaled * gain1_ref[...] + shift1_ref[...]).astype(BF16)
    normed = (scaled * gain2_ref[...] + shift2_ref[...]).astype(BF16)
    normed_ref[...] = normed
    dy = dy_full_ref[...]
    low = dot_nn(normed, up_left_ref[...]).astype(BF16)
    low_ref[...] = low
    rights = jnp.concatenate([output_right_ref[...], down_right_ref[...]], axis=0)
    grad_lows = dot_nt(dy, rights).astype(BF16)
    grad_lows_ref[...] = grad_lows
    grad_low = grad_lows[:, LANES:]
    feed_core(
        jnp.concatenate([normed, low], axis=1), jnp.concatenate([dy, grad_low], axis=1), up_ref, down_ref, act_ref,
        gh_ref, 512,
    )
    act = act_ref[...]
    gh = gh_ref[...]
    forward = dot_nn(act, down_ref[...])
    backward = dot_nt(gh, up_ref[...])
    out_ref[...], low_act_ref[...] = forward[:, :width], forward[:, width:]
    grad_ref[...], grad_low_ref[...] = backward[:, :width], backward[:, width:]

    @pl.when(step == 0)
    def _():
        acc_ref[...] = jnp.zeros_like(acc_ref)

    acc_ref[:, :hidden] += dot_tn(low, gh)
    acc_ref[:, hidden:] += dot_tn(grad_low, act)

    @pl.when((step == 0) & (half == 0))
    def _():
        fills = [
            pltpu.make_async_copy(xs_ref, halo_ref.at[pl.ds(k * tile, tile)], local_sems.at[2 + k])
            for k in range(SHORT // tile)
        ]
        for copy in fills:
            copy.start()
        for copy in fills:
            copy.wait()

    @pl.when(step == steps - 1)
    def _():
        sums_ref[...] = acc_ref[...].astype(BF16)
        for holder, copy, spread_copies in halo:
            pl.when((half == 0) & (place == holder))(copy.wait_send)

            @pl.when((half == 1) & (place == holder))
            def _():
                for other in spread_copies:
                    other.wait_send()

            for s in range(1, unit):
                pl.when((half == 1) & (place == (holder + s) % unit))(spread_copies[s - 1].wait_recv)
        for copy in rows_out:
            copy.wait_send()
        for k in range(chunks):
            for copy in over_y[k] + once[k]:
                copy.wait_send()
            for copy in twice[k]:
                copy.wait()
        for copy in kept_halves:
            copy.wait()


def feed_first(unit, x, dy, norms, up, up_left, up_right, down, down_left, output_right, down_right, triple, output,
               tile):
    own_rows, width = x.shape
    rows = own_rows * unit
    hidden = up.shape[1]
    steps, per_device = rows // tile, own_rows // tile
    chunks = math.gcd(2, output.shape[0] // 128)
    halo_chunks = SHORT // math.gcd(own_rows, 128)
    anywhere = pl.BlockSpec(memory_space=pl.ANY)
    here = pl.BlockSpec((tile, width), lambda i: (jnp.minimum(i, per_device - 1), 0))

    def turned(size):
        def index(i):
            return (lax.rem(i + place_in_unit(unit)[0] * per_device, steps), 0)

        return pl.BlockSpec((tile, size), index)

    return pl.pallas_call(
        functools.partial(feed_first_kernel, unit, tile),
        grid=(steps,),
        in_specs=[here, here]
        + [whole((1, width))] * 4
        + [
            anywhere,
            whole(up_left.shape),
            anywhere,
            anywhere,
            anywhere,
            whole(output_right.shape),
            whole(down_right.shape),
        ]
        + [anywhere] * 4,
        out_specs=[
            turned(width),
            turned(width),
            turned(width),
            turned(LANES),
            turned(2 * LANES),
            turned(width),
            turned(width),
            turned(LANES),
            turned(LANES),
            held((LANES, 2 * hidden)),
        ]
        + [anywhere] * 5,
        scratch_shapes=[
            pltpu.VMEM((tile, hidden), BF16),
            pltpu.VMEM((tile, hidden), BF16),
            pltpu.VMEM((width + LANES, hidden), BF16),
            pltpu.VMEM((hidden, width + LANES), BF16),
            pltpu.VMEM((LANES, 2 * hidden), F32),
            pltpu.VMEM((tile, width), BF16),
            pltpu.VMEM((unit - 1, own_rows, width), BF16),
            pltpu.VMEM((unit - 1, own_rows, width), BF16),
            pltpu.SemaphoreType.DMA((2, 5, chunks, 2)),
            pltpu.SemaphoreType.DMA((2, 2, unit - 1)),
            pltpu.SemaphoreType.DMA((2, halo_chunks)),
            pltpu.SemaphoreType.DMA((2, halo_chunks, unit - 1)),
            pltpu.SemaphoreType.DMA((2 + SHORT // tile,)),
            pltpu.SemaphoreType.DMA((4,)),
        ],
        out_shape=[
            shaped((rows, width), BF16),
            shaped((rows, width), BF16),
            shaped((rows, width), BF16),
            shaped((rows, LANES), BF16),
            shaped((rows, 2 * LANES), BF16),
            shaped((rows, width), F32),
            shaped((rows, width), F32),
            shaped((rows, LANES), F32),
            shaped((rows, LANES), F32),
            shaped((LANES, 2 * hidden), BF16),
            shaped(triple.shape, BF16),
            shaped(output.shape, BF16),
            shaped((SHORT, width), BF16),
            shaped((up.shape[0] // 2, up.shape[1]), BF16),
            shaped((down.shape[0] // 2, down.shape[1]), BF16),
        ],
        compiler_params=pltpu.CompilerParams(
            dimension_semantics=("arbitrary",), vmem_limit_bytes=VMEM_LIMIT, collective_id=3, has_side_effects=True
        ),
        cost_estimate=BRIEF,
        name="feed_first",
    )(x, dy, *norms, up, up_left, up_right, down, down_left, output_right, down_right, x, dy, triple, output)


def feed_second_kernel(
    unit, tile, normed_ref, low_ref, dy_ref, grad_lows_ref, out_in_ref, grad_in_ref, low_act_in_ref, grad_low_in_ref,
    x_ref, keep_ref, got1_ref, gain1_ref, gain2_ref, output_right_ref, down_right_ref, up0_ref, up1_ref, up_left_ref,
    up_right_ref, down0_ref, down1_ref, down_left_ref, early_ref, heads_ref, left_ref, y_ref, dx_ref, sums_ref, both_ref,
    heads_out_ref, left_out_ref, act_ref, gh_ref, up_ref, down_ref, send_ref, got_ref, early_got_ref, acc_ref, norms_ref,
    output_right_grad_ref, down_right_grad_ref, up_left_grad_ref, sems, early_sems, out_sems, load_sems, *sum_refs,
):
    step = pl.program_id(0)
    own_rows = got_ref.shape[1]
    per_device = own_rows // tile
    send_tiles = (unit - 1) * per_device
    width, hidden = up_ref.shape[0] - LANES, up_ref.shape[1]
    shard = shard_index(unit, True)
    weights = [
        (columns_of(up_right_ref, hidden, shard), up_ref.at[pl.ds(width, LANES)]),
        (rows_at(down_left_ref, hidden, shard), down_ref.at[:, pl.ds(width, LANES)]),
    ]
    for lead, pieces, ref in zip(leads(), ((up0_ref, up1_ref), (down0_ref, down1_ref)), (up_ref, down_ref)):
        for place, piece in zip((lead, 1 - lead), pieces):
            weights.append((piece, rows_at(ref, piece.shape[0], place).at[:, pl.ds(0, piece.shape[1])]))
    peers = unit_peers(unit)
    copies = [
        [
            pltpu.make_async_remote_copy(
                src_ref=send_ref.at[s, pl.ds(t * tile, tile)], dst_ref=got_ref.at[s, pl.ds(t * tile, tile)],
                send_sem=sems.at[0, s, t], recv_sem=sems.at[1, s, t], device_id=peer, device_id_type=MESH,
            )
            for t in range(per_device)
        ]
        for s, peer in enumerate(peers)
    ]

    steps = unit * per_device
    y_peer = chip_neighbours(unit)[1]
    pieces = early_sems.shape[1]
    count = early_ref.shape[0] // pieces
    early_copies = [
        pltpu.make_async_remote_copy(
            src_ref=early_ref.at[pl.ds(j * count, count)], dst_ref=early_got_ref.at[pl.ds(j * count, count)],
            send_sem=early_sems.at[0, j], recv_sem=early_sems.at[1, j], device_id=y_peer, device_id_type=MESH,
        )
        for j in range(pieces)
    ]
    hosted = len(sum_refs) > 0
    if hosted:
        net = Net()
        size = heads_ref.shape[-1] // 2
        split = len(sum_scratch("yxz", size))
        heads_refs = (sum_refs[:split], sum_refs[split : 2 * split])
        left_refs = sum_refs[2 * split :]
        stages = [
            sum_chunk(net, order, heads_ref.at[:, :, :, :, pl.ds(j * size, size)], heads_refs[j])
            for j, order in enumerate(("yxz", "xyz"))
        ]
        stages.append(sum_both(net, (("yxz", left_ref.shape[-1]),), left_ref, *left_refs[:3], (left_refs[3:],)))

    def advance():
        if hosted:
            for at in range(steps):

                @pl.when(step == at)
                def _():
                    for stage in stages:
                        stage[at]()

    neighbours = [*peers, y_peer] + ([net.x_peer, *net.z_peers] if hosted else [])

    def greet():
        meet(neighbours)
        for ref in (norms_ref, output_right_grad_ref, down_right_grad_ref, acc_ref, up_left_grad_ref):
            ref[...] = jnp.zeros_like(ref)

    load(step, load_sems, weights, greet)
    advance()
    for j, copy in enumerate(early_copies):
        pl.when(step == min(j + 1, steps - 1))(copy.start)
    normed = normed_ref[...]
    low = low_ref[...]
    dy = dy_ref[...]
    grad_low = grad_lows_ref[:, LANES:]
    feed_core(
        jnp.concatenate([normed, low], axis=1), jnp.concatenate([dy, grad_low], axis=1), up_ref, down_ref, act_ref,
        gh_ref, 512,
    )
    act = act_ref[...]
    gh = gh_ref[...]
    forward = dot_nn(act, down_ref[...])
    backward = dot_nt(gh, up_ref[...])
    grad_low_up = (grad_low_in_ref[...] + backward[:, width:]).astype(BF16)
    out = out_in_ref[...] + forward[:, :width]
    low_act = low_act_in_ref[...] + forward[:, width:]
    second = grad_in_ref[...] + backward[:, :width] + dot_nt(grad_low_up, up_left_ref[...])
    acc_ref[:, :hidden] += dot_tn(low, gh)
    acc_ref[:, hidden:] += dot_tn(grad_low, act)
    up_left_grad_ref[...] += dot_tn(grad_low_up, normed)

    @pl.when(step < send_tiles)
    def _():
        slot = step // per_device
        span = pl.ds(pl.multiple_of(lax.rem(step, per_device) * tile, tile), tile)
        send_ref[slot, span, :width] = out.astype(BF16)
        send_ref[slot, span, width : 2 * width] = second.astype(BF16)
        send_ref[slot, span, 2 * width :] = low_act.astype(BF16)

    for s in range(unit - 1):
        for t in range(per_device):
            pl.when(step == s * per_device + t)(copies[s][t].start)
            pl.when(step == send_tiles + t)(copies[s][t].wait_recv)

    @pl.when(step >= send_tiles)
    def _():
        span = pl.ds(pl.multiple_of((step - send_tiles) * tile, tile), tile)
        first = keep_ref[:, :width].astype(F32)
        low_att = keep_ref[:, width:].astype(F32)
        total_out, total_second, total_low = out, second, low_act
        for s in range(unit - 1):
            first = first + got1_ref[s, :, :width].astype(F32)
            low_att = low_att + got1_ref[s, :, width:].astype(F32)
            total_out = total_out + got_ref[s, span, :width].astype(F32)
            total_second = total_second + got_ref[s, span, width : 2 * width].astype(F32)
            total_low = total_low + got_ref[s, span, 2 * width :].astype(F32)
        low_att, total_low = low_att.astype(BF16), total_low.astype(BF16)
        x = x_ref[...].astype(F32)
        y_ref[...] = (
            x + total_out + dot_nn(low_att, output_right_ref[...]) + dot_nn(total_low, down_right_ref[...])
        ).astype(BF16)
        center = x - jnp.mean(x, axis=-1, keepdims=True)
        spread = jnp.mean(center * center, axis=-1, keepdims=True)
        inverse = lax.rsqrt(spread + EPS)
        scaled = center * inverse
        total = first * gain1_ref[...] + total_second * gain2_ref[...]
        mean = jnp.mean(total, axis=-1, keepdims=True)
        inner = jnp.mean(total * scaled, axis=-1, keepdims=True)
        dx_ref[...] = dy.astype(F32) + (total - mean - scaled * inner) * inverse
        norms_ref[0:1, :] += jnp.sum(first * scaled, axis=0, keepdims=True)
        norms_ref[1:2, :] += jnp.sum(first, axis=0, keepdims=True)
        norms_ref[2:3, :] += jnp.sum(total_second * scaled, axis=0, keepdims=True)
        norms_ref[3:4, :] += jnp.sum(total_second, axis=0, keepdims=True)
        output_right_grad_ref[...] += dot_tn(low_att, dy)
        down_right_grad_ref[...] += dot_tn(total_low, dy)

    @pl.when(step == steps - 1)
    def _():
        for copy in early_copies:
            copy.wait()
        sums_ref[...] = (acc_ref[...] + early_got_ref[...].astype(F32)).astype(BF16)
        quarters(both_ref, up_left_grad_ref[...], output_right_grad_ref[...], down_right_grad_ref[...])
        start = 3 * (width // 4)
        count = width // LANES
        for q in range(4):
            rows = [norms_ref[q : q + 1, j * LANES : (j + 1) * LANES] for j in range(count)]
            block = jnp.concatenate([*rows, jnp.zeros((LANES - count, LANES), F32)], axis=0)
            both_ref[q % 2, q // 2, :, start:] = block.astype(BF16)
        for group in copies:
            for copy in group:
                copy.wait_send()
        if hosted:
            for at in range(steps, max(len(stage) for stage in stages)):
                for stage in stages:
                    if at < len(stage):
                        stage[at]()
            outs = []
            for j, refs in enumerate((*heads_refs, left_refs[3:])):
                full = refs[5]
                target = left_out_ref if j == 2 else heads_out_ref.at[:, :, :, :, pl.ds(j * size, size)]
                outs.append(pltpu.make_async_copy(full, target, out_sems.at[j]))
                outs[-1].start()
            for copy in net.started:
                copy.wait_send()
            for copy in outs:
                copy.wait()


def feed_second(unit, normed, low, dy, grad_lows, out, grad, low_act, grad_low, x, keep, got, gains, output_right,
                down_right, ups, up_left, up_right, downs, down_left, early, heads, left, hosted, tile):
    rows, width = normed.shape
    own_rows = rows // unit
    anywhere = pl.BlockSpec(memory_space=pl.ANY)
    extra = []
    if hosted:
        heads = heads.reshape((2,) + SUM_ROWS + heads.shape[-1:])
        left = left.reshape((2, 2) + SUM_ROWS + left.shape[-1:])
        extra = sum_scratch("yxz", heads.shape[-1] // 2) + sum_scratch("xyz", heads.shape[-1] // 2)
        extra += both_scratch((("yxz", left.shape[-1]),))
    hidden = ups[0].shape[1]
    steps, per_device = rows // tile, own_rows // tile
    send_tiles = steps - per_device
    wide = 2 * width + LANES

    def turned(size):
        def index(i):
            place, slot = place_in_unit(unit)[0], i // per_device + 1
            return (lax.rem(place + unit - slot, unit) * per_device + lax.rem(i, per_device), 0)

        return pl.BlockSpec((tile, size), index)

    def late(size):
        return pl.BlockSpec((tile, size), lambda i: (jnp.maximum(i - send_tiles, 0), 0))

    return pl.pallas_call(
        functools.partial(feed_second_kernel, unit, tile),
        grid=(steps,),
        in_specs=[
            turned(width),
            turned(LANES),
            turned(width),
            turned(2 * LANES),
            turned(width),
            turned(width),
            turned(LANES),
            turned(LANES),
            late(width),
            late(width + LANES),
            pl.BlockSpec((unit - 1, tile, width + LANES), lambda i: (0, jnp.maximum(i - send_tiles, 0), 0)),
            whole((1, width)),
            whole((1, width)),
            whole(output_right.shape),
            whole(down_right.shape),
            anywhere,
            anywhere,
            whole(up_left.shape),
            anywhere,
            anywhere,
            anywhere,
            anywhere,
            whole(early.shape),
            whole(heads.shape),
            whole(left.shape),
        ],
        out_specs=[
            late(width),
            late(width),
            held((LANES, 2 * hidden)),
            held((2, 2, LANES, 3 * (width // 4) + LANES)),
            anywhere,
            anywhere,
        ],
        scratch_shapes=[
            pltpu.VMEM((tile, hidden), BF16),
            pltpu.VMEM((tile, hidden), BF16),
            pltpu.VMEM((width + LANES, hidden), BF16),
            pltpu.VMEM((hidden, width + LANES), BF16),
            pltpu.VMEM((unit - 1, own_rows, wide), BF16),
            pltpu.VMEM((unit - 1, own_rows, wide), BF16),
            pltpu.VMEM((LANES, 2 * hidden), BF16),
            pltpu.VMEM((LANES, 2 * hidden), F32),
            pltpu.VMEM((8, width), F32),
            pltpu.VMEM((LANES, width), F32),
            pltpu.VMEM((LANES, width), F32),
            pltpu.VMEM((LANES, width), F32),
            pltpu.SemaphoreType.DMA((2, unit - 1, per_device)),
            pltpu.SemaphoreType.DMA((2, 4)),
            pltpu.SemaphoreType.DMA((3,)),
            pltpu.SemaphoreType.DMA((6,)),
        ]
        + extra,
        out_shape=[
            shaped((own_rows, width), BF16),
            shaped((own_rows, width), F32),
            shaped((LANES, 2 * hidden), BF16),
            shaped((2, 2, LANES, 3 * (width // 4) + LANES), BF16),
            shaped(heads.shape, BF16),
            shaped(left.shape[1:] if hosted else left.shape, BF16),
        ],
        compiler_params=pltpu.CompilerParams(
            dimension_semantics=("arbitrary",), vmem_limit_bytes=VMEM_LIMIT, collective_id=4, has_side_effects=True
        ),
        cost_estimate=BRIEF,
        name="feed_second",
    )(normed, low, dy, grad_lows, out, grad, low_act, grad_low, x, keep, got, *gains, output_right, down_right, *ups,
      up_left, up_right, *downs, down_left, early, heads, left)


def project_kernel(
    unit, main_tiles, halo_ref, normed_ref, dy_ref, grad_lows_ref, late_ref, cos0_ref, cos1_ref, minus0_ref, minus1_ref, plus0_ref,
    plus1_ref, gain_ref, shift_ref, triple0_ref, triple1_ref, left_ref, right_ref, output0_ref, output1_ref,
    output_left_ref, low_ref, q_ref, k_ref, v_ref, g_ref, triple_ref, output_ref, load_sems,
):
    step = pl.program_id(0)
    load(
        step, load_sems,
        head_weights(
            unit, (triple0_ref, triple1_ref), right_ref, (output0_ref, output1_ref), output_left_ref, triple_ref,
            output_ref,
        ),
    )

    later = late_ref[0, 0:1, :] > 0.0
    tables = tuple(
        jnp.where(later, two[...], one[...])
        for one, two in ((cos0_ref, cos1_ref), (minus0_ref, minus1_ref), (plus0_ref, plus1_ref))
    )
    head_width = output0_ref.shape[0]
    first = low_lanes()

    def rows(normed, full):
        low = dot_nn(normed, left_ref[...]).astype(BF16)
        if full:
            low_ref[...] = low
        mixed = dot_nn(jnp.concatenate([normed, low], axis=1), triple_ref[...])
        if full:
            grads = jnp.concatenate([dy_ref[...], grad_lows_ref[:, :LANES]], axis=1)
            g_ref[...] = dot_nt(grads, output_ref[...]).astype(BF16)
        for pair in range(2 * head_width // LANES):
            one, two, three = (
                mixed[:, (3 * pair + part) * LANES : (3 * pair + part + 1) * LANES] for part in range(3)
            )
            cols = pl.ds(pair * LANES, LANES)
            key = pltpu.roll(jnp.where(first, three, one), HEAD_DIM, 1)
            k_ref[:, cols] = rotate(key, *tables).astype(BF16)
            v_ref[:, cols] = jnp.where(first, two, three).astype(BF16)
            if full:
                query = rotate(jnp.where(first, one, two), *tables).astype(BF16)
                q_ref[:, cols] = query * HEAD_DIM**-0.5

    @pl.when(step < main_tiles)
    def _():
        rows(normed_ref[...], True)

    @pl.when(step >= main_tiles)
    def _():
        rows(normalize(halo_ref[...].astype(F32), gain_ref[...], shift_ref[...]).astype(BF16), False)


def project(unit, conts, x_halo, normed, dy, grad_lows, gain, shift, triples, left, right, outputs, output_left, tables,
            tile):
    rows, width = dy.shape
    head_width = outputs[0].shape[0]
    anywhere = pl.BlockSpec(memory_space=pl.ANY)
    per_block = SHORT // tile
    main_tiles, halo_tiles = rows // tile, SHORT // tile
    late = jnp.concatenate([jnp.repeat(conts, per_block), jnp.zeros((halo_tiles,), jnp.int32)])
    late = jnp.broadcast_to(late.astype(F32)[:, None, None], (main_tiles + halo_tiles, 8, LANES))

    halo = pl.BlockSpec((tile, width), lambda i: (jnp.maximum(i - main_tiles, 0), 0))

    def table(which):
        return pl.BlockSpec((tile, LANES), lambda i: (which * per_block + lax.rem(i, per_block), 0))

    def main(size):
        return pl.BlockSpec((tile, size), lambda i: (jnp.minimum(i, main_tiles - 1), 0))

    def all_rows(size):
        return pl.BlockSpec((tile, size), lambda i: (jnp.where(i < main_tiles, i + halo_tiles, i - main_tiles), 0))

    return pl.pallas_call(
        functools.partial(project_kernel, unit, main_tiles),
        grid=(main_tiles + halo_tiles,),
        in_specs=[
            halo,
            main(width),
            main(width),
            main(2 * LANES),
            pl.BlockSpec((1, 8, LANES), lambda i: (i, 0, 0)),
            table(0),
            table(1),
            table(0),
            table(1),
            table(0),
            table(1),
            whole(gain.shape),
            whole(shift.shape),
            anywhere,
            anywhere,
            whole(left.shape),
            anywhere,
            anywhere,
            anywhere,
            anywhere,
        ],
        out_specs=[
            main(LANES),
            main(2 * head_width),
            all_rows(2 * head_width),
            all_rows(2 * head_width),
            main(2 * head_width),
        ],
        scratch_shapes=[
            pltpu.VMEM((width + LANES, 6 * head_width), BF16),
            pltpu.VMEM((2 * head_width, width + LANES), BF16),
            pltpu.SemaphoreType.DMA((8,)),
        ],
        out_shape=[
            shaped((rows, LANES), BF16),
            shaped((rows, 2 * head_width), BF16),
            shaped((SHORT + rows, 2 * head_width), BF16),
            shaped((SHORT + rows, 2 * head_width), BF16),
            shaped((rows, 2 * head_width), BF16),
        ],
        compiler_params=params(),
        cost_estimate=BRIEF,
        name="project",
    )(x_halo, normed, dy, grad_lows, late, *[table for table in tables for _ in range(2)], gain, shift, *triples, left, right,
      *outputs, output_left)


def attend_rows(with_prev, pairs, count, allowed, q_ref, k_ref, v_ref, g_ref, kp_ref, vp_ref, tables, att_ref, gq_ref,
                dk_ref, dv_ref, dkp_ref, dvp_ref):
    first = low_lanes()
    zero = jnp.zeros((), BF16)

    def stack(pair):
        return jnp.concatenate([jnp.where(first, pair, zero), jnp.where(first, zero, pair)], axis=0)

    def unstack(both):
        return jnp.where(first, both[:count], both[count:])

    def joined(fold, values):
        return functools.reduce(fold, values)

    pieces = []
    for lanes in pairs:
        for start in range(0, SHORT, count):
            span = pl.ds(start, count)
            parts = []
            if with_prev:
                parts.append((kp_ref[:, lanes], vp_ref[:, lanes], dkp_ref, dvp_ref, pl.ds(0, SHORT)))
            if start:
                before = pl.ds(0, start)
                parts.append((k_ref[before, lanes], v_ref[before, lanes], dk_ref, dv_ref, before))
            parts.append((k_ref[span, lanes], v_ref[span, lanes], dk_ref, dv_ref, span))
            pieces.append((lanes, span, stack(q_ref[span, lanes]), stack(g_ref[span, lanes]), parts))

    scores, grads, weights, lows, inners, slopes = [], [], [], [], [], []
    for _, _, queries, _, parts in pieces:
        found = [dot_nt(queries, part[0]) for part in parts]
        scores.append(found[:-1] + [jnp.where(allowed, found[-1], -1e30)])
    for _, _, _, grad, parts in pieces:
        grads.append([dot_nt(grad, part[1]) for part in parts])
    for found in scores:
        peak = joined(jnp.maximum, [jnp.max(score, axis=1, keepdims=True) for score in found])
        exps = [jnp.exp(score - peak) for score in found]
        scale = 1.0 / joined(jnp.add, [jnp.sum(exp, axis=1, keepdims=True) for exp in exps])
        weights.append([exp * scale for exp in exps])
        lows.append([weight.astype(BF16) for weight in weights[-1]])
    for (lanes, span, _, grad, parts), low in zip(pieces, lows):
        attended = joined(jnp.add, [dot_nn(weight, part[1]) for weight, part in zip(low, parts)])
        att_ref[span, lanes] = unstack(attended).astype(BF16)
        inners.append(jnp.sum(attended * grad.astype(F32), axis=1, keepdims=True))
    for weight, grad, inner in zip(weights, grads, inners):
        slopes.append([(w * (g - inner)).astype(BF16) for w, g in zip(weight, grad)])
    for (lanes, span, queries, grad, parts), low, slope in zip(pieces, lows, slopes):
        grad_query = joined(jnp.add, [dot_nn(ds, part[0]) for ds, part in zip(slope, parts)])
        for ds, weight, (_, _, to_key, to_value, rows) in zip(slope, low, parts):
            to_key[lanes, rows] += dot_tn(queries, ds)
            to_value[lanes, rows] += dot_tn(grad, weight)
        grad_query = unstack(grad_query) * HEAD_DIM**-0.5
        gq_ref[span, lanes] = unrotate(grad_query, *[table[span] for table in tables]).astype(BF16)


def unrotate_tall(ref, lanes, cosine, sine):
    half = ROT // 2
    value = ref[lanes, :]
    halves = []
    for base in (HEAD_DIM, 0):
        one, two = value[base : base + half], value[base + half : base + ROT]
        halves += [one * cosine + two * sine, two * cosine - one * sine, value[base + ROT : base + HEAD_DIM]]
    return jnp.concatenate(halves, axis=0).astype(BF16).T


def attend_kernel(
    blocks, pairs, count, conts_ref, q_ref, k_ref, v_ref, g_ref, kp_ref, vp_ref, cos_ref, minus_ref, plus_ref,
    tall_cos_ref, tall_sin_ref, att_ref, gq_ref, gk_ref, gv_ref, halo_ref, dk_ref, dv_ref,
):
    step = pl.program_id(0)
    block = blocks - 1 - step
    continued = conts_ref[block]
    offset = pl.multiple_of(continued * SHORT, SHORT)
    tables = tuple(ref.at[pl.ds(offset, SHORT)] for ref in (cos_ref, minus_ref, plus_ref))
    now = lax.rem(step, 2)
    own = (dk_ref.at[now], dv_ref.at[now])
    before = (dk_ref.at[1 - now], dv_ref.at[1 - now])

    @pl.when(step == 0)
    def _():
        for ref in own:
            ref[...] = jnp.zeros_like(ref)

    for ref in before:
        ref[...] = jnp.zeros_like(ref)
    row = lax.broadcasted_iota(jnp.int32, (2 * count, count), 0)
    column = lax.broadcasted_iota(jnp.int32, (2 * count, count), 1)
    allowed = column <= jnp.where(row >= count, row - count, row)
    args = (q_ref, k_ref, v_ref, g_ref, kp_ref, vp_ref, tables, att_ref, gq_ref, *own, *before)

    def each(some, work):
        some = math.gcd(some, pairs)

        def body(i, carry):
            work([pl.ds(pl.multiple_of((i * some + j) * LANES, LANES), LANES) for j in range(some)])
            return carry

        lax.fori_loop(0, pairs // some, body, 0)

    pl.when(continued == 0)(lambda: each(2, lambda lanes: attend_rows(False, lanes, count, allowed, *args)))
    pl.when(continued != 0)(lambda: each(2, lambda lanes: attend_rows(True, lanes, count, allowed, *args)))
    turn = tuple(ref.at[:, pl.ds(offset, SHORT)] for ref in (tall_cos_ref, tall_sin_ref))

    def leave(lanes):
        for pair in lanes:
            gk_ref[:, pair] = unrotate_tall(own[0], pair, *[ref[...] for ref in turn])
            gv_ref[:, pair] = own[1][pair, :].astype(BF16).T

    each(1, leave)

    @pl.when(block == 0)
    def _():
        base = tuple(ref.at[:, pl.ds(0, SHORT)] for ref in (tall_cos_ref, tall_sin_ref))

        def leave_halo(lanes):
            for pair in lanes:
                halo_ref[0, :, pair] = unrotate_tall(before[0], pair, *[ref[...] for ref in base])
                halo_ref[1, :, pair] = before[1][pair, :].astype(BF16).T

        each(1, leave_halo)


def attend(conts, q, k, v, g, tables, tall, count):
    rows, head_width = q.shape
    blocks = rows // SHORT
    here = pl.BlockSpec((SHORT, head_width), lambda i, conts: (blocks - 1 - i, 0))
    after = pl.BlockSpec((SHORT, head_width), lambda i, conts: (blocks - i, 0))
    return pl.pallas_call(
        functools.partial(attend_kernel, blocks, head_width // LANES, count),
        grid_spec=pltpu.PrefetchScalarGridSpec(
            num_scalar_prefetch=1,
            grid=(blocks,),
            in_specs=[here, after, after, here, here, here] + [whole(table.shape) for table in (*tables, *tall)],
            out_specs=[here] * 4 + [held((2, SHORT, head_width))],
            scratch_shapes=[pltpu.VMEM((2, head_width, SHORT), F32)] * 2,
        ),
        out_shape=[shaped((rows, head_width), BF16)] * 4 + [shaped((2, SHORT, head_width), BF16)],
        compiler_params=params(),
        cost_estimate=BRIEF,
        name="attend",
    )(conts, q, k, v, g, k, v, *tables, *tall)


def settle_kernel(
    unit, tile, normed_ref, low_ref, grad_lows_ref, out_in_ref, att_ref, gq_ref, gk_ref, gv_ref, halo_ref, triple0_ref,
    triple1_ref, left_ref, output0_ref, output1_ref, right_ref, output_left_ref, out_ref, keep_ref, heads_ref,
    left_sums_ref, got_ref, send_ref, halo_got_ref, key_ref, value_ref, mixed_ref, triple_ref, output_ref, acc_ref,
    out_acc_ref, left_grad_ref, halo_sems, sems, load_sems,
):
    step = pl.program_id(0)
    per_device = got_ref.shape[1] // tile
    steps = unit * per_device
    halo_start = steps - SHORT // tile
    place, base = place_in_unit(unit)
    half = base // unit
    peers = unit_peers(unit)
    y_peer = chip_neighbours(unit)[1]
    halo_copies = []
    for j in range(SHORT // tile):
        part = pl.ds(j * tile, tile)
        halo_copies.append(
            pltpu.make_async_remote_copy(
                src_ref=halo_ref.at[:, part], dst_ref=halo_got_ref.at[:, part], send_sem=halo_sems.at[0, j],
                recv_sem=halo_sems.at[1, j], device_id=y_peer, device_id_type=MESH,
            )
        )
    copies = [
        [
            pltpu.make_async_remote_copy(
                src_ref=send_ref.at[s, pl.ds(t * tile, tile)], dst_ref=got_ref.at[s, pl.ds(t * tile, tile)],
                send_sem=sems.at[0, s, t], recv_sem=sems.at[1, s, t], device_id=peer, device_id_type=MESH,
            )
            for t in range(per_device)
        ]
        for s, peer in enumerate(peers)
    ]
    neighbours = [y_peer, *peers]

    def greet():
        meet(neighbours)

        @pl.when(half == 1)
        def _():
            for copy in halo_copies:
                copy.start()

        for ref in (acc_ref, out_acc_ref, left_grad_ref):
            ref[...] = jnp.zeros_like(ref)

    load(
        step, load_sems,
        head_weights(
            unit, (triple0_ref, triple1_ref), right_ref, (output0_ref, output1_ref), output_left_ref, triple_ref,
            output_ref,
        ),
        greet,
    )

    key_ref[...], value_ref[...] = gk_ref[...], gv_ref[...]
    for j, copy in enumerate(halo_copies):

        @pl.when((half == 0) & (step == halo_start + j))
        def _():
            copy.wait_recv()
            rows = pl.ds(j * tile, tile)
            count = output0_ref.shape[0]
            for ref, which in ((key_ref, 0), (value_ref, 1)):
                for here, there in ((pl.ds(0, count), pl.ds(count, count)), (pl.ds(count, count), pl.ds(0, count))):
                    ref[:, here] = (ref[:, here].astype(F32) + halo_got_ref[which, rows, there].astype(F32)).astype(BF16)

    normed = normed_ref[...]
    low = low_ref[...]
    grad_low_out = grad_lows_ref[:, :LANES]
    head_width = output0_ref.shape[0]
    first = low_lanes()
    for pair in range(2 * head_width // LANES):
        q, k, v = (ref[:, pair * LANES : (pair + 1) * LANES] for ref in (gq_ref, key_ref, value_ref))
        for part, value in enumerate((jnp.where(first, q, k), jnp.where(first, v, q), jnp.where(first, k, v))):
            mixed_ref[:, (3 * pair + part) * LANES : (3 * pair + part + 1) * LANES] = value
    mixed = mixed_ref[...]
    att = att_ref[...]
    width = normed.shape[1]
    backward = dot_nt(mixed, triple_ref[...])
    forward = dot_nn(att, output_ref[...])
    grad_low = backward[:, width:].astype(BF16)
    grad = (backward[:, :width] + dot_nt(grad_low, left_ref[...])).astype(BF16)
    out_ref[...] = out_in_ref[...] + forward[:, :width]
    low_att = forward[:, width:].astype(BF16)

    @pl.when(step // per_device == place)
    def _():
        keep_ref[:, :width] = grad
        keep_ref[:, width:] = low_att

    span = pl.ds(pl.multiple_of(lax.rem(step, per_device) * tile, tile), tile)
    for s in range(unit - 1):
        owner = lax.rem(place + unit - (s + 1), unit)

        @pl.when(step // per_device == owner)
        def _():
            send_ref[s, span, :width] = grad
            send_ref[s, span, width:] = low_att

        for t in range(per_device):
            pl.when(step == owner * per_device + t)(copies[s][t].start)

    acc_ref[...] += dot_tn(low, mixed)
    out_acc_ref[...] += dot_tn(grad_low_out, att)
    left_grad_ref[...] += dot_tn(grad_low, normed)

    @pl.when(step == steps - 1)
    def _():
        size = 3 * head_width
        for j in range(2):
            heads_ref[j, :, :size] = acc_ref[:, j * size : (j + 1) * size].astype(BF16)
            heads_ref[j, :, size:] = out_acc_ref[:, j * head_width : (j + 1) * head_width].astype(BF16)
        quarters(left_sums_ref, left_grad_ref[...])

        @pl.when(half == 1)
        def _():
            for copy in halo_copies:
                copy.wait_send()

        for group in copies:
            for copy in group:
                copy.wait()


def settle(unit, normed, low, grad_lows, out, heads, halo, triples, left, outputs, right, output_left, tile):
    rows, width = normed.shape
    own_rows = rows // unit
    head_width = outputs[0].shape[0]
    steps, per_device = rows // tile, own_rows // tile
    anywhere = pl.BlockSpec(memory_space=pl.ANY)

    def kept(i):
        return (jnp.clip(i - place_in_unit(unit)[0] * per_device, 0, per_device - 1), 0)

    return pl.pallas_call(
        functools.partial(settle_kernel, unit, tile),
        grid=(steps,),
        in_specs=[rows_of(tile, width), rows_of(tile, LANES), rows_of(tile, 2 * LANES), rows_of(tile, width)]
        + [rows_of(tile, 2 * head_width)] * 4
        + [anywhere]
        + [anywhere, anywhere, whole(left.shape), anywhere, anywhere, anywhere, anywhere],
        out_specs=[
            rows_of(tile, width),
            pl.BlockSpec((tile, width + LANES), kept),
            held((2, LANES, 4 * head_width)),
            held((2, 2, LANES, width // 4)),
            anywhere,
        ],
        scratch_shapes=[
            pltpu.VMEM((unit - 1, own_rows, width + LANES), BF16),
            pltpu.VMEM((2, SHORT, 2 * head_width), BF16),
            pltpu.VMEM((tile, 2 * head_width), BF16),
            pltpu.VMEM((tile, 2 * head_width), BF16),
            pltpu.VMEM((tile, 6 * head_width), BF16),
            pltpu.VMEM((width + LANES, 6 * head_width), BF16),
            pltpu.VMEM((2 * head_width, width + LANES), BF16),
            pltpu.VMEM((LANES, 6 * head_width), F32),
            pltpu.VMEM((LANES, 2 * head_width), F32),
            pltpu.VMEM((LANES, width), F32),
            pltpu.SemaphoreType.DMA((2, SHORT // tile)),
            pltpu.SemaphoreType.DMA((2, unit - 1, per_device)),
            pltpu.SemaphoreType.DMA((8,)),
        ],
        out_shape=[
            shaped((rows, width), F32),
            shaped((own_rows, width + LANES), BF16),
            shaped((2, LANES, 4 * head_width), BF16),
            shaped((2, 2, LANES, width // 4), BF16),
            shaped((unit - 1, own_rows, width + LANES), BF16),
        ],
        compiler_params=pltpu.CompilerParams(
            dimension_semantics=("arbitrary",), vmem_limit_bytes=VMEM_LIMIT, collective_id=5, has_side_effects=True
        ),
        cost_estimate=BRIEF,
        name="settle",
    )(normed, low, grad_lows, out, *heads, halo, *triples, left, *outputs, right, output_left)


FEED_ORDERS = ("xz", "zx", "xz", "zx")


def sum_kernel(size, feed_ref, both_ref, heads_ref, left_ref, feed_out_ref, both_out_ref, heads_out_ref, left_out_ref,
               cross_sems, local_sems, *refs):
    net = Net()
    meet([net.x_peer, net.y_peer, net.core_peer, *net.z_peers])
    locals_, crossing = [], []

    def hand_over(slot, full, out, first, second):
        for place, at in ((0, first), (1, second)):
            target = out.at[net.core, at]
            local = pltpu.make_async_copy(full.at[place], target, local_sems.at[slot, place])
            local.start()
            locals_.append(local)
            crossing.append(net.copy(full.at[place], target, cross_sems, 2 * slot + place, net.core_peer))
            net.start(crossing[-1:])

    split = len(sum_scratch("xz", size))
    feed_refs = [refs[j * split : (j + 1) * split] for j in range(len(FEED_ORDERS))]
    both_refs = refs[len(FEED_ORDERS) * split :]
    parts = split_columns(both_ref.shape[-1])
    per_part = (len(both_refs) - 3) // 2
    scratches = (both_refs[3 : 3 + per_part], both_refs[3 + per_part :])
    running = [sum_both(net, parts, both_ref, *both_refs[:3], scratches)]
    running += [
        sum_chunk(net, order, feed_ref.at[:, :, :, pl.ds(j * size, size)], feed_refs[j])
        for j, order in enumerate(FEED_ORDERS)
    ]

    def both_done():
        start = 0
        for j, (_, count) in enumerate(parts):
            columns = both_out_ref.at[:, :, :, :, :, pl.ds(start, count)]
            hand_over(j, scratches[j][5], columns, net.half, net.other_half)
            start += count

    def feed_done(j):
        columns = feed_out_ref.at[:, :, :, :, :, pl.ds(j * size, size)]
        hand_over(4 + j, feed_refs[j][5], columns, net.other_half, net.half)

    for k in range(max(len(stage) for stage in running)):
        for j, stage in enumerate(running):
            if k < len(stage):
                stage[k]()
            if k == len(stage) - 1:
                both_done() if j == 0 else feed_done(j - 1)
        if k == 0:
            hand_over(2, heads_ref, heads_out_ref, net.half, net.other_half)
            hand_over(3, left_ref, left_out_ref, net.half, net.other_half)
    for copy in locals_:
        copy.wait()
    for copy in crossing:
        copy.wait_recv()
    for copy in net.started:
        copy.wait_send()


def sum_all(feed, both, heads, left):
    arrays = (feed.reshape(SUM_ROWS + feed.shape[-1:]), both.reshape((2, 2) + SUM_ROWS + both.shape[-1:]), heads, left)
    size = feed.shape[-1] // len(FEED_ORDERS)
    slots = 4 + len(FEED_ORDERS)
    outs = [shaped((2, 2) + SUM_ROWS + array.shape[-1:], BF16) for array in arrays]
    results = pl.pallas_call(
        functools.partial(sum_kernel, size),
        out_shape=outs,
        in_specs=[pl.BlockSpec(memory_space=pltpu.VMEM)] * 4,
        out_specs=[pl.BlockSpec(memory_space=pl.ANY)] * 4,
        scratch_shapes=[pltpu.SemaphoreType.DMA((2, 2 * slots)), pltpu.SemaphoreType.DMA((slots, 2))]
        + [shape for order in FEED_ORDERS for shape in sum_scratch(order, size)]
        + both_scratch(split_columns(both.shape[-1])),
        compiler_params=pltpu.CompilerParams(
            collective_id=2, has_side_effects=True, vmem_limit_bytes=VMEM_LIMIT
        ),
        cost_estimate=BRIEF,
        name="sum_all",
    )(*arrays)
    return [value.reshape(2, 2, LANES, value.shape[-1]) for value in results]


def unpack_kernel(triple_width, feed_ref, both_ref, heads_ref, left_ref, triple_ref, output_ref, up_ref, down_ref,
                  triple_left_ref, up_left_ref, output_right_ref, down_right_ref, *norm_refs):
    triple_ref[...] = heads_ref[0, 0, :, :triple_width].astype(F32)
    output_ref[...] = heads_ref[0, 0, :, triple_width:].T.astype(F32)
    hidden = up_ref.shape[1]
    up_ref[...] = feed_ref[0, 0, :, :hidden].astype(F32)
    down_ref[...] = feed_ref[0, 0, :, hidden:].T.astype(F32)
    size = triple_left_ref.shape[0]
    triple_left_ref[...] = left_ref[0, 0].T.astype(F32)
    up_left_ref[...] = both_ref[0, 0, :, :size].T.astype(F32)
    output_right_ref[...] = both_ref[0, 0, :, size : 2 * size].astype(F32)
    down_right_ref[...] = both_ref[0, 0, :, 2 * size : 3 * size].astype(F32)
    for q, ref in enumerate(norm_refs):

        @pl.when(pl.program_id(0) == q)
        def _():
            ref[...] = both_ref[0, 0, : ref.shape[0], 3 * size :].astype(F32)


def unpack(feed, both, heads, left, triple_width):
    arrays = (feed, both, heads, left)
    hidden, quarter = feed.shape[-1] // 2, left.shape[-1]
    width, head_width = 4 * quarter, heads.shape[-1] - triple_width

    def tall(rows):
        return pl.BlockSpec((rows, LANES), lambda s: (s, 0))

    def wide(cols):
        return pl.BlockSpec((LANES, cols), lambda s: (0, s))

    return pl.pallas_call(
        functools.partial(unpack_kernel, triple_width),
        grid=(4,),
        in_specs=[
            pl.BlockSpec((1, 1) + value.shape[2:], lambda s: (lax.rem(s, 2), s // 2, 0, 0)) for value in arrays
        ],
        out_specs=[
            wide(triple_width), tall(head_width), wide(hidden), tall(hidden), tall(quarter), tall(quarter),
            wide(quarter), wide(quarter), *[held((width // LANES, LANES))] * 4,
        ],
        out_shape=[
            shaped((LANES, 4 * triple_width), F32),
            shaped((4 * head_width, LANES), F32),
            shaped((LANES, 4 * hidden), F32),
            shaped((4 * hidden, LANES), F32),
            shaped((width, LANES), F32),
            shaped((width, LANES), F32),
            shaped((LANES, width), F32),
            shaped((LANES, width), F32),
        ]
        + [shaped((width // LANES, LANES), F32)] * 4,
        compiler_params=params(),
        cost_estimate=BRIEF,
        name="unpack",
    )(*arrays)


def shards(
    ranks,
    groups,
    block_input,
    sequence_lengths,
    first_gain,
    first_shift,
    second_gain,
    second_shift,
    triple_weight,
    triple_left,
    triple_right,
    output_weight,
    output_left,
    output_right,
    expand_weight,
    expand_left,
    expand_right,
    shrink_weight,
    shrink_left,
    shrink_right,
    cotangent,
):
    unit = ranks // 2
    own_rows, width = block_input.shape
    rows = own_rows * unit
    blocks = rows // SHORT
    tile = math.gcd(own_rows, 256)
    triple_width = triple_weight.shape[1]
    head_width = output_weight.shape[0]
    hidden = expand_weight.shape[1]
    mp = lax.axis_index("mp")
    half = mp // unit
    place = lax.rem(mp, unit)
    far = lax.rem(mp + unit, ranks)
    swap = [(m, (m + unit) % ranks) for m in range(ranks)]

    tables = rotary_tables()
    beside = [[(d, d ^ bit) for d in range(groups)] for bit in (1, 2)]
    continues = find_flags(sequence_lengths[0])
    conts = lax.dynamic_slice_in_dim(continues, half * blocks, blocks, 0)
    gain1, shift1 = first_gain[None, :], first_shift[None, :]
    gain2, shift2 = second_gain[None, :], second_shift[None, :]

    (normed1, normed2, dy, low2, grad_lows, out, grad2, low_act, grad_low2, feed_sums, triple_far,
     output_far, x_halo, expand_half, shrink_half) = feed_first(
        unit, block_input, cotangent, (gain1, shift1, gain2, shift2), expand_weight, expand_left, expand_right,
        shrink_weight, shrink_left, output_right, shrink_right, triple_weight, output_weight, tile,
    )
    expand_piece = lax.ppermute(expand_half, "mp", swap)
    shrink_piece = lax.ppermute(shrink_half, "mp", swap)
    low1, q, k, v, g = project(
        unit, conts, x_halo, normed1, dy, grad_lows, gain1, shift1, (triple_weight, triple_far), triple_left,
        triple_right, (output_weight, output_far), output_left, tables, tile,
    )
    att, gq, gk, gv, halo = attend(conts, q, k, v, g, tables, tall_tables(), 256)
    expand_piece, shrink_piece, att = lax.optimization_barrier((expand_piece, shrink_piece, att))
    expand_other = lax.ppermute(expand_piece, "dp", beside[0])
    shrink_other = lax.ppermute(shrink_piece, "dp", beside[1])
    out, keep1, heads, left, got1 = settle(
        unit, normed1, low1, grad_lows, out, (att, gq, gk, gv), halo, (triple_weight, triple_far), triple_left,
        (output_weight, output_far), triple_right, output_left, tile,
    )
    hosted = ranks == 4 and groups == 8
    block_output, input_gradient, feed_sums, both, heads_sum, left_sum = feed_second(
        unit, normed2, low2, dy, grad_lows, out, grad2, low_act, grad_low2, block_input, keep1, got1, (gain1, gain2),
        output_right, shrink_right, (expand_piece, expand_other), expand_left, expand_right,
        (shrink_piece, shrink_other), shrink_left, feed_sums, heads, left, hosted, tile,
    )
    if hosted:
        (triple_right_sum, output_left_sum, expand_right_sum, shrink_left_sum, triple_left_sum, expand_left_sum,
         output_right_sum, shrink_right_sum, *norms) = unpack(
            *sum_all(feed_sums, both, heads_sum, left_sum), triple_width
        )
        norms = [value.reshape(width) for value in norms]
    else:

        def spread(*placed):
            size = placed[0][0].shape[1]
            wide = jnp.zeros((LANES, size * ranks), BF16)
            for value, shard in placed:
                wide = lax.dynamic_update_slice_in_dim(wide, value, shard * size, 1)
            return wide

        def joined(value):
            return value.transpose(2, 1, 0, 3).reshape(LANES, -1)

        def columns(value, start, size):
            return value.reshape(LANES, ranks, -1)[:, :, start : start + size].reshape(LANES, -1).astype(F32)

        heads, feed, left, both = lax.psum(
            (spread((heads[0], mp), (heads[1], far)), spread((feed_sums, far)), left, both), ("dp", "mp")
        )
        triple_right_sum = columns(heads, 0, triple_width)
        output_left_sum = columns(heads, triple_width, head_width).T
        expand_right_sum = columns(feed, 0, hidden)
        shrink_left_sum = columns(feed, hidden, hidden).T
        triple_left_sum = joined(left).astype(F32).T
        quarter = width // 4
        expand_left_sum = joined(both[..., :quarter]).astype(F32).T
        output_right_sum = joined(both[..., quarter : 2 * quarter]).astype(F32)
        shrink_right_sum = joined(both[..., 2 * quarter : 3 * quarter]).astype(F32)
        norms = both[:, :, : width // LANES, 3 * quarter :].transpose(1, 0, 2, 3).reshape(4, width).astype(F32)
    return (
        block_output,
        input_gradient,
        norms[0],
        norms[1],
        norms[2],
        norms[3],
        triple_left_sum,
        triple_right_sum,
        output_left_sum,
        output_right_sum,
        expand_left_sum,
        expand_right_sum,
        shrink_left_sum,
        shrink_right_sum,
    )


def solution(mesh):
    placed = (
        P(("dp", "mp"), None),
        P("dp", None),
        P(),
        P(),
        P(),
        P(),
        P(None, "mp"),
        P(),
        P(),
        P("mp", None),
        P(),
        P(),
        P(None, "mp"),
        P(),
        P(),
        P("mp", None),
        P(),
        P(),
        P(("dp", "mp"), None),
    )
    return jax.shard_map(
        functools.partial(shards, mesh.shape["mp"], mesh.shape["dp"]),
        mesh=mesh,
        in_specs=placed,
        out_specs=(P(("dp", "mp"), None), P(("dp", "mp"), None)) + (P(),) * 12,
        check_vma=False,
    )
```

```python
import functools
import math

import jax
import jax.numpy as jnp
import numpy as np
from jax import lax
from jax.experimental import pallas as pl
from jax.experimental.pallas import tpu as pltpu
from jax.sharding import PartitionSpec as P

HEAD_DIM = 64
ROT = 16
SHORT = 512
TOK_GRP = 3072
SLOTS = 6
EPS = 1e-05
LANES = 128
MESH = pl.DeviceIdType.MESH
BF16 = jnp.bfloat16
F32 = jnp.float32
VMEM_LIMIT = 56 * 1024 * 1024
BRIEF = pl.CostEstimate(flops=1, bytes_accessed=1, transcendentals=0)


def dot_nn(former, latter):
    return lax.dot_general(
        former, latter, (((1,), (0,)), ((), ())), preferred_element_type=F32
    )


def dot_nt(former, latter):
    return lax.dot_general(
        former, latter, (((1,), (1,)), ((), ())), preferred_element_type=F32
    )


def dot_tn(former, latter):
    return lax.dot_general(
        former, latter, (((0,), (0,)), ((), ())), preferred_element_type=F32
    )


def find_flags(group_lengths):
    seq_ends = jnp.cumsum(group_lengths, dtype=jnp.int32)
    starts = seq_ends - group_lengths
    block_starts = jnp.arange(SLOTS, dtype=jnp.int32) * SHORT
    begins = jnp.any(
        (starts[None, :] == block_starts[:, None]) & (group_lengths[None, :] > 0), axis=1
    )
    return jnp.where(begins, 0, 1).astype(jnp.int32)


def rotary_tables():
    half = ROT // 2
    frequency = np.exp(
        np.arange(half, dtype=np.float32) * np.float32(-2.0 * math.log(10000.0) / ROT)
    ).astype(np.float32)
    angles = np.arange(2 * SHORT, dtype=np.float32)[:, None] * frequency[None, :]
    cosine = np.ones((2 * SHORT, LANES), np.float32)
    minus = np.zeros((2 * SHORT, LANES), np.float32)
    plus = np.zeros((2 * SHORT, LANES), np.float32)
    for base in range(0, LANES, HEAD_DIM):
        cosine[:, base : base + half] = np.cos(angles)
        cosine[:, base + half : base + ROT] = np.cos(angles)
        minus[:, base : base + half] = -np.sin(angles)
        plus[:, base + half : base + ROT] = np.sin(angles)
    return jnp.asarray(cosine), jnp.asarray(minus), jnp.asarray(plus)


def tall_tables():
    half = ROT // 2
    frequency = np.exp(
        np.arange(half, dtype=np.float32) * np.float32(-2.0 * math.log(10000.0) / ROT)
    ).astype(np.float32)
    angles = frequency[:, None] * np.arange(2 * SHORT, dtype=np.float32)[None, :]
    return jnp.asarray(np.cos(angles)), jnp.asarray(np.sin(angles))


def low_lanes():
    return lax.broadcasted_iota(jnp.int32, (1, LANES), 1) < HEAD_DIM


def rotate(pair, cosine, minus, plus):
    half = ROT // 2
    return (
        pair * cosine
        + pltpu.roll(pair, LANES - half, 1) * minus
        + pltpu.roll(pair, half, 1) * plus
    )


def unrotate(pair, cosine, minus, plus):
    half = ROT // 2
    return (
        pair * cosine
        - pltpu.roll(pair, LANES - half, 1) * minus
        - pltpu.roll(pair, half, 1) * plus
    )


def normalize(values, gain, shift):
    center = values - jnp.mean(values, axis=-1, keepdims=True)
    spread = jnp.mean(center * center, axis=-1, keepdims=True)
    return center * lax.rsqrt(spread + EPS) * gain + shift


def whole(shape):
    return pl.BlockSpec(
        shape, lambda *idx: (0,) * len(shape), pipeline_mode=pl.Buffered(1)
    )


def held(shape):
    return pl.BlockSpec(shape, lambda *idx: (0,) * len(shape))


def rows_of(tile, width):
    return pl.BlockSpec((tile, width), lambda i, *refs: (i, 0))


def shaped(shape, dtype):
    return jax.ShapeDtypeStruct(shape, dtype)


def params(semantics=1):
    return pltpu.CompilerParams(
        dimension_semantics=("arbitrary",) * semantics, vmem_limit_bytes=VMEM_LIMIT
    )


SUM_ROWS = (2, 4, 16)


class Net:
    def __init__(self):
        dp, mp = lax.axis_index("dp"), lax.axis_index("mp")
        self.half, self.core = mp // 2, lax.rem(mp, 2)
        self.x, self.z = lax.rem(dp, 2), dp // 2
        self.other_half, self.other_core, self.other_x = 1 - self.half, 1 - self.core, 1 - self.x
        self.x_peer = (dp + 1 - 2 * self.x, mp)
        self.y_peer = (dp, mp + 2 - 4 * self.half)
        self.core_peer = (dp, mp + 1 - 2 * self.core)
        self.z_places = [lax.rem(self.z + j, 4) for j in range(1, 4)]
        self.z_peers = [(place * 2 + self.x, mp) for place in self.z_places]
        self.started = []

    def copy(self, src, dst, sems, slot, peer):
        return pltpu.make_async_remote_copy(
            src_ref=src, dst_ref=dst, send_sem=sems.at[0, slot], recv_sem=sems.at[1, slot], device_id=peer,
            device_id_type=MESH,
        )

    def start(self, copies):
        for copy in copies:
            copy.start()
        self.started += copies


def arrive(copies):
    for copy in copies:
        copy.wait_recv()


def added(first, *others):
    total = first.astype(F32)
    for other in others:
        total = total + other.astype(F32)
    return total.astype(BF16)


def sum_scratch(order, size):
    one = (16, size)
    first = {"yxz": ((2, 4), (2, 4)), "xyz": ((2, 4), (2, 4)), "xz": ((4,), (4,)), "zx": ((3, 2), (2,))}[order]
    second = {"yxz": ((4,), (4,)), "xyz": ((4,), (4,)), "xz": ((3,), (1,)), "zx": ((1,), (1,))}[order]
    return [pltpu.VMEM(shape + one, BF16) for shape in (*first, *second, (3,), (2, 2, 4))] + [
        pltpu.SemaphoreType.DMA((2, 12))
    ]


def sum_chunk(net, order, source, scratch):
    got1, work1, got2, work2, got3, full, sems = scratch
    x, z, other_x = net.x, net.z, net.other_x
    own, rows, plane = full.at[0, x, z], full.at[0, x], full.at[0, :, z]

    def to_z(src, dst, slot):
        return [
            net.copy(src(place), dst(j), sems, slot + j, peer)
            for j, (place, peer) in enumerate(zip(net.z_places, net.z_peers))
        ]

    def one(src, dst, slot, peer):
        return [net.copy(src, dst, sems, slot, peer)]

    last = work1 if order == "xz" else work2
    if order != "xyz":
        over_y = one(full.at[0], full.at[1], 9, net.y_peer)
    if order == "zx":
        spread = to_z(lambda place: source.at[:, place], lambda j: got1.at[j], 2)
        cross = one(work1.at[other_x], got2.at[0], 0, net.x_peer)
        back = one(own, own, 8, net.x_peer)
        gather = to_z(lambda place: plane, lambda j: plane, 5)
    else:
        spread = to_z(lambda place: last.at[place], lambda j: got3.at[j], 2)
        gather = to_z(lambda place: own, lambda j: own, 5)
        if order == "yxz":
            first = one(source.at[1], got1, 0, net.y_peer)
            second = one(work1.at[other_x], got2, 1, net.x_peer)
        elif order == "xyz":
            first = one(source.at[:, other_x], got1, 0, net.x_peer)
            second = one(work1.at[1], got2, 1, net.y_peer)
            over_y = one(rows, full.at[1, x], 8, net.y_peer)
            over_x = one(full.at[:, x], full.at[:, x], 9, net.x_peer)
        else:
            first = one(source.at[other_x], got1, 0, net.x_peer)
        if order != "xyz":
            over_x = one(rows, rows, 8, net.x_peer)

    def begin(copies):
        return lambda: net.start(copies)

    def after(copies, work, then):
        def stage():
            arrive(copies)
            if work is not None:
                target, value = work
                target[...] = value()
            if then is not None:
                net.start(then)

        return stage

    if order == "zx":
        mine = (work1, lambda: added(source[:, z], got1[0], got1[1], got1[2]))
        total = (own, lambda: added(work1[x], got2[0]))
        return [
            begin(spread), after(spread, mine, cross), after(cross, total, back), after(back, None, gather),
            after(gather, None, over_y), after(over_y, None, None),
        ]
    total = (own, lambda: added(last[z], got3[0], got3[1], got3[2]))
    if order == "yxz":
        head = [begin(first), after(first, (work1, lambda: added(source[0], got1[...])), second)]
        head.append(after(second, (work2, lambda: added(work1[x], got2[...])), spread))
    elif order == "xyz":
        head = [begin(first), after(first, (work1, lambda: added(source[:, x], got1[...])), second)]
        head.append(after(second, (work2, lambda: added(work1[0], got2[...])), spread))
    else:
        head = [begin(first), after(first, (work1, lambda: added(source[x], got1[...])), spread)]
    one_way, other_way = (over_y, over_x) if order == "xyz" else (over_x, over_y)
    return head + [
        after(spread, total, gather), after(gather, None, one_way), after(one_way, None, other_way),
        after(other_way, None, None),
    ]


def sum_both(net, parts, both, got, total, core_sems, scratches):
    exchange = [net.copy(both.at[net.other_core], got, core_sems, 0, net.core_peer)]
    chunks, start = [], 0
    for (order, size), scratch in zip(parts, scratches):
        chunks.append(sum_chunk(net, order, total.at[:, :, :, :, pl.ds(start, size)], scratch))
        start += size

    def combine():
        arrive(exchange)
        for place, at in ((0, net.half), (1, net.other_half)):
            total[place] = added(both[net.core, at], got[at])
        for chunk in chunks:
            chunk[0]()

    def together(k):
        def stage():
            for chunk in chunks:
                if k < len(chunk):
                    chunk[k]()

        return stage

    longest = max(len(chunk) for chunk in chunks)
    return [lambda: net.start(exchange), combine] + [together(k) for k in range(1, longest)]


def both_scratch(parts):
    size = sum(part[1] for part in parts)
    return [
        pltpu.VMEM((2,) + SUM_ROWS + (size,), BF16),
        pltpu.VMEM((2,) + SUM_ROWS + (size,), BF16),
        pltpu.SemaphoreType.DMA((2, 1)),
    ] + [shape for part in parts for shape in sum_scratch(*part)]


def split_columns(size):
    count = (size // 2 + LANES - 1) // LANES * LANES
    return (("yxz", count), ("xyz", size - count))


def quarters(ref, *arrays):
    start = 0
    for array in arrays:
        size = array.shape[1] // 4
        for q in range(4):
            ref[q % 2, q // 2, :, start : start + size] = array[:, q * size : (q + 1) * size].astype(BF16)
        start += size


def gelu_parts(hidden):
    cdf = 0.5 + 0.5 * lax.erf(hidden * math.sqrt(0.5))
    density = jnp.exp(-0.5 * hidden * hidden) * (1.0 / math.sqrt(2.0 * math.pi))
    return hidden * cdf, cdf + hidden * density


def feed_core(rows, grads, up_ref, down_ref, act_ref, grad_ref, hidden_step):
    for start in range(0, up_ref.shape[1], hidden_step):
        cols = pl.ds(start, hidden_step)
        hidden = dot_nn(rows, up_ref[:, cols])
        grad_act = dot_nt(grads, down_ref[cols, :])
        activated, slope = gelu_parts(hidden)
        act_ref[:, cols] = activated.astype(BF16)
        grad_ref[:, cols] = (grad_act * slope).astype(BF16)


def shard_index(unit, far):
    return lax.rem(lax.axis_index("mp") + (unit if far else 0), 2 * unit)


def columns_of(ref, size, shard):
    return ref.at[:, pl.ds(pl.multiple_of(shard * size, size), size)]


def rows_at(ref, size, shard):
    return ref.at[pl.ds(pl.multiple_of(shard * size, size), size)]


def load(step, sems, pairs, between=None):
    copies = [pltpu.make_async_copy(src, dst, sems.at[j]) for j, (src, dst) in enumerate(pairs)]

    @pl.when(step == 0)
    def _():
        for copy in copies:
            copy.start()
        if between is not None:
            between()
        for copy in copies:
            copy.wait()


def head_weights(unit, triples, right, outputs, output_left, triple_ref, output_ref):
    width = triples[0].shape[0]
    head_width = outputs[0].shape[0]
    size = 3 * head_width
    pairs = []
    for j in range(2):
        shard = shard_index(unit, j == 1)
        cols, rows = pl.ds(j * size, size), pl.ds(j * head_width, head_width)
        pairs += [
            (triples[j], triple_ref.at[pl.ds(0, width), cols]),
            (columns_of(right, size, shard), triple_ref.at[pl.ds(width, LANES), cols]),
            (outputs[j], output_ref.at[rows, pl.ds(0, width)]),
            (rows_at(output_left, head_width, shard), output_ref.at[rows, pl.ds(width, LANES)]),
        ]
    return pairs


def chip_neighbours(unit):
    dp = lax.axis_index("dp")
    mp = lax.axis_index("mp")
    lead = lax.rem(dp, 2)
    return lead, (dp, lax.rem(mp + unit, 2 * unit)), (dp + 1 - 2 * lead, mp)


def leads():
    dp = lax.axis_index("dp")
    return lax.rem(dp, 2), lax.rem(dp // 2, 2)


def group_neighbours():
    dp, mp = lax.axis_index("dp"), lax.axis_index("mp")
    first, second = leads()
    return (dp + 1 - 2 * first, mp), (dp + 2 - 4 * second, mp)


def courier(unit, pairs, chunks, sems):
    first, second = leads()
    mine = first + 2 * second
    y_peer = chip_neighbours(unit)[1]
    x_peer, z_peer = group_neighbours()
    over_y, once, twice = [], [], []
    for k in range(chunks):
        over_y.append([])
        once.append([])
        twice.append([])
        for j, (own, far) in enumerate(pairs):
            count = own.shape[0] // 4 // chunks

            def copy(kind, src, dst, quarter, start, size, peer, k=k, j=j, count=count):
                span = pl.ds(pl.multiple_of((quarter * chunks + k) * count + start, size), size)
                return pltpu.make_async_remote_copy(
                    src_ref=src.at[span], dst_ref=dst.at[span], send_sem=sems.at[0, kind, k, j],
                    recv_sem=sems.at[1, kind, k, j], device_id=peer, device_id_type=MESH,
                )

            by_x, by_z = mine + 1 - 2 * first, mine + 2 - 4 * second
            over_y[-1].append(copy(0, own, far, mine, 0, count, y_peer))
            once[-1] += [copy(1, far, far, mine, 0, count, x_peer), copy(2, far, far, mine, 0, count, z_peer)]
            twice[-1] += [
                copy(3, far, far, by_x, 0, count // 2, z_peer),
                copy(4, far, far, by_z, count // 2, count // 2, x_peer),
            ]
    return over_y, once, twice


def meet(peers):
    barrier = pltpu.get_barrier_semaphore()
    for peer in peers:
        pl.semaphore_signal(barrier, inc=1, device_id=peer, device_id_type=MESH)
    pl.semaphore_wait(barrier, len(peers))


def place_in_unit(unit):
    mp = lax.axis_index("mp")
    return lax.rem(mp, unit), mp - lax.rem(mp, unit)


def unit_peers(unit):
    place, base = place_in_unit(unit)
    return [(lax.axis_index("dp"), base + lax.rem(place + unit - s, unit)) for s in range(1, unit)]


def halo_copies(unit, x_ref, halo_ref, y_sems, unit_sems):
    own_rows = x_ref.shape[0]
    chunk = math.gcd(own_rows, 128)
    dp = lax.axis_index("dp")
    found = []
    for k in range(SHORT // chunk):
        row = unit * own_rows - SHORT + k * chunk
        holder, start = row // own_rows, row % own_rows
        target = halo_ref.at[pl.ds(k * chunk, chunk)]
        over_y = pltpu.make_async_remote_copy(
            src_ref=x_ref.at[pl.ds(start, chunk)], dst_ref=target, send_sem=y_sems.at[0, k], recv_sem=y_sems.at[1, k],
            device_id=(dp, unit + holder), device_id_type=MESH,
        )
        spread = [
            pltpu.make_async_remote_copy(
                src_ref=target, dst_ref=target, send_sem=unit_sems.at[0, k, s - 1], recv_sem=unit_sems.at[1, k, s - 1],
                device_id=(dp, unit + (holder + s) % unit), device_id_type=MESH,
            )
            for s in range(1, unit)
        ]
        found.append((holder, over_y, spread))
    return found


def feed_first_kernel(
    unit, tile, x_ref, dy_ref, gain1_ref, shift1_ref, gain2_ref, shift2_ref, up_own_ref, up_left_ref, up_right_ref,
    down_own_ref, down_left_ref, output_right_ref, down_right_ref, x_all_ref, dy_all_ref, triple_ref, output_ref, normed1_ref,
    normed_ref, dy_full_ref, low_ref, grad_lows_ref, out_ref, grad_ref, low_act_ref, grad_low_ref, sums_ref,
    triple_far_ref, output_far_ref, halo_ref, up_half_ref, down_half_ref, act_ref, gh_ref, up_ref, down_ref, acc_ref,
    xs_ref, x_got_ref, dy_got_ref, courier_sems, unit_sems, halo_y_sems, halo_unit_sems, local_sems, load_sems,
):
    step = pl.program_id(0)
    width, hidden = up_own_ref.shape
    weights = (
        (up_own_ref, up_ref.at[pl.ds(0, width)]),
        (columns_of(up_right_ref, hidden, shard_index(unit, False)), up_ref.at[pl.ds(width, LANES)]),
        (down_own_ref, down_ref.at[:, pl.ds(0, width)]),
        (rows_at(down_left_ref, hidden, shard_index(unit, False)), down_ref.at[:, pl.ds(width, LANES)]),
    )
    own_rows = x_all_ref.shape[0]
    per_device = own_rows // tile
    steps = unit * per_device
    chunks = courier_sems.shape[2]
    place, base = place_in_unit(unit)
    half = base // unit
    peers = unit_peers(unit)
    over_y, once, twice = courier(
        unit, ((triple_ref, triple_far_ref), (output_ref, output_far_ref)), chunks, courier_sems
    )
    halo = halo_copies(unit, x_all_ref, halo_ref, halo_y_sems, halo_unit_sems)
    rows_out = [
        pltpu.make_async_remote_copy(
            src_ref=src, dst_ref=dst.at[j], send_sem=unit_sems.at[0, which, j], recv_sem=unit_sems.at[1, which, j],
            device_id=peer, device_id_type=MESH,
        )
        for j, peer in enumerate(peers)
        for which, (src, dst) in enumerate(((x_all_ref, x_got_ref), (dy_all_ref, dy_got_ref)))
    ]
    kept_halves = [
        pltpu.make_async_copy(
            src.at[
                pl.ds(pl.multiple_of(lead * dst.shape[0], dst.shape[0]), dst.shape[0]), pl.ds(0, dst.shape[1])
            ],
            dst,
            local_sems.at[j],
        )
        for j, (lead, src, dst) in enumerate(zip(leads(), (up_ref, down_ref), (up_half_ref, down_half_ref)))
    ]

    neighbours = [chip_neighbours(unit)[1], *group_neighbours(), *peers]

    def greet():
        meet(neighbours)
        for copy in rows_out:
            copy.start()
        for copies in over_y:
            for copy in copies:
                copy.start()

    load(step, load_sems, weights, greet)
    for holder, copy, _ in halo:
        pl.when((step == 0) & (half == 0) & (place == holder))(copy.start)

    @pl.when(step == 0)
    def _():
        for copy in kept_halves:
            copy.start()
        xs_ref[...] = x_ref[...]
        dy_full_ref[...] = dy_ref[...]

    @pl.when((step > 0) & (step < per_device))
    def _():
        xs_ref[...] = x_ref[...]
        dy_full_ref[...] = dy_ref[...]

    for slot in range(unit - 1):

        @pl.when(step == per_device * (slot + 1))
        def _():
            for which in range(2):
                rows_out[2 * slot + which].wait_recv()

        @pl.when((step >= per_device * (slot + 1)) & (step < per_device * (slot + 2)))
        def _():
            span = pl.ds(pl.multiple_of((step - per_device * (slot + 1)) * tile, tile), tile)
            xs_ref[...] = x_got_ref[slot, span]
            dy_full_ref[...] = dy_got_ref[slot, span]

    for k in range(chunks):

        @pl.when(step == min(k + 2, steps - 1))
        def _():
            for copy in over_y[k]:
                copy.wait_recv()
            for copy in once[k]:
                copy.start()

    for k in range(chunks):

        @pl.when(step == min(k + 4, steps - 1))
        def _():
            for copy in once[k]:
                copy.wait_recv()
            for copy in twice[k]:
                copy.start()

    for holder, copy, spread_copies in halo:

        @pl.when((step == steps - 1) & (half == 1) & (place == holder))
        def _():
            copy.wait_recv()
            for other in spread_copies:
                other.start()

    x = xs_ref[...].astype(F32)
    center = x - jnp.mean(x, axis=-1, keepdims=True)
    spread = jnp.mean(center * center, axis=-1, keepdims=True)
    scaled = center * lax.rsqrt(spread + EPS)
    normed1_ref[...] = (scaled * gain1_ref[...] + shift1_ref[...]).astype(BF16)
    normed = (scaled * gain2_ref[...] + shift2_ref[...]).astype(BF16)
    normed_ref[...] = normed
    dy = dy_full_ref[...]
    low = dot_nn(normed, up_left_ref[...]).astype(BF16)
    low_ref[...] = low
    rights = jnp.concatenate([output_right_ref[...], down_right_ref[...]], axis=0)
    grad_lows = dot_nt(dy, rights).astype(BF16)
    grad_lows_ref[...] = grad_lows
    grad_low = grad_lows[:, LANES:]
    feed_core(
        jnp.concatenate([normed, low], axis=1), jnp.concatenate([dy, grad_low], axis=1), up_ref, down_ref, act_ref,
        gh_ref, 512,
    )
    act = act_ref[...]
    gh = gh_ref[...]
    forward = dot_nn(act, down_ref[...])
    backward = dot_nt(gh, up_ref[...])
    out_ref[...], low_act_ref[...] = forward[:, :width], forward[:, width:]
    grad_ref[...], grad_low_ref[...] = backward[:, :width], backward[:, width:]

    @pl.when(step == 0)
    def _():
        acc_ref[...] = jnp.zeros_like(acc_ref)

    acc_ref[:, :hidden] += dot_tn(low, gh)
    acc_ref[:, hidden:] += dot_tn(grad_low, act)

    @pl.when((step == 0) & (half == 0))
    def _():
        fills = [
            pltpu.make_async_copy(xs_ref, halo_ref.at[pl.ds(k * tile, tile)], local_sems.at[2 + k])
            for k in range(SHORT // tile)
        ]
        for copy in fills:
            copy.start()
        for copy in fills:
            copy.wait()

    @pl.when(step == steps - 1)
    def _():
        sums_ref[...] = acc_ref[...].astype(BF16)
        for holder, copy, spread_copies in halo:
            pl.when((half == 0) & (place == holder))(copy.wait_send)

            @pl.when((half == 1) & (place == holder))
            def _():
                for other in spread_copies:
                    other.wait_send()

            for s in range(1, unit):
                pl.when((half == 1) & (place == (holder + s) % unit))(spread_copies[s - 1].wait_recv)
        for copy in rows_out:
            copy.wait_send()
        for k in range(chunks):
            for copy in over_y[k] + once[k]:
                copy.wait_send()
            for copy in twice[k]:
                copy.wait()
        for copy in kept_halves:
            copy.wait()


def feed_first(unit, x, dy, norms, up, up_left, up_right, down, down_left, output_right, down_right, triple, output,
               tile):
    own_rows, width = x.shape
    rows = own_rows * unit
    hidden = up.shape[1]
    steps, per_device = rows // tile, own_rows // tile
    chunks = math.gcd(2, output.shape[0] // 128)
    halo_chunks = SHORT // math.gcd(own_rows, 128)
    anywhere = pl.BlockSpec(memory_space=pl.ANY)
    here = pl.BlockSpec((tile, width), lambda i: (jnp.minimum(i, per_device - 1), 0))

    def turned(size):
        def index(i):
            return (lax.rem(i + place_in_unit(unit)[0] * per_device, steps), 0)

        return pl.BlockSpec((tile, size), index)

    return pl.pallas_call(
        functools.partial(feed_first_kernel, unit, tile),
        grid=(steps,),
        in_specs=[here, here]
        + [whole((1, width))] * 4
        + [
            anywhere,
            whole(up_left.shape),
            anywhere,
            anywhere,
            anywhere,
            whole(output_right.shape),
            whole(down_right.shape),
        ]
        + [anywhere] * 4,
        out_specs=[
            turned(width),
            turned(width),
            turned(width),
            turned(LANES),
            turned(2 * LANES),
            turned(width),
            turned(width),
            turned(LANES),
            turned(LANES),
            held((LANES, 2 * hidden)),
        ]
        + [anywhere] * 5,
        scratch_shapes=[
            pltpu.VMEM((tile, hidden), BF16),
            pltpu.VMEM((tile, hidden), BF16),
            pltpu.VMEM((width + LANES, hidden), BF16),
            pltpu.VMEM((hidden, width + LANES), BF16),
            pltpu.VMEM((LANES, 2 * hidden), F32),
            pltpu.VMEM((tile, width), BF16),
            pltpu.VMEM((unit - 1, own_rows, width), BF16),
            pltpu.VMEM((unit - 1, own_rows, width), BF16),
            pltpu.SemaphoreType.DMA((2, 5, chunks, 2)),
            pltpu.SemaphoreType.DMA((2, 2, unit - 1)),
            pltpu.SemaphoreType.DMA((2, halo_chunks)),
            pltpu.SemaphoreType.DMA((2, halo_chunks, unit - 1)),
            pltpu.SemaphoreType.DMA((2 + SHORT // tile,)),
            pltpu.SemaphoreType.DMA((4,)),
        ],
        out_shape=[
            shaped((rows, width), BF16),
            shaped((rows, width), BF16),
            shaped((rows, width), BF16),
            shaped((rows, LANES), BF16),
            shaped((rows, 2 * LANES), BF16),
            shaped((rows, width), F32),
            shaped((rows, width), F32),
            shaped((rows, LANES), F32),
            shaped((rows, LANES), F32),
            shaped((LANES, 2 * hidden), BF16),
            shaped(triple.shape, BF16),
            shaped(output.shape, BF16),
            shaped((SHORT, width), BF16),
            shaped((up.shape[0] // 2, up.shape[1]), BF16),
            shaped((down.shape[0] // 2, down.shape[1]), BF16),
        ],
        compiler_params=pltpu.CompilerParams(
            dimension_semantics=("arbitrary",), vmem_limit_bytes=VMEM_LIMIT, collective_id=3, has_side_effects=True
        ),
        cost_estimate=BRIEF,
        name="feed_first",
    )(x, dy, *norms, up, up_left, up_right, down, down_left, output_right, down_right, x, dy, triple, output)


def feed_second_kernel(
    unit, tile, normed_ref, low_ref, dy_ref, grad_lows_ref, out_in_ref, grad_in_ref, low_act_in_ref, grad_low_in_ref,
    x_ref, keep_ref, got1_ref, gain1_ref, gain2_ref, output_right_ref, down_right_ref, up0_ref, up1_ref, up_left_ref,
    up_right_ref, down0_ref, down1_ref, down_left_ref, early_ref, heads_ref, left_ref, y_ref, dx_ref, sums_ref, both_ref,
    heads_out_ref, left_out_ref, act_ref, gh_ref, up_ref, down_ref, send_ref, got_ref, early_got_ref, acc_ref, norms_ref,
    output_right_grad_ref, down_right_grad_ref, up_left_grad_ref, sems, early_sems, out_sems, load_sems, *sum_refs,
):
    step = pl.program_id(0)
    own_rows = got_ref.shape[1]
    per_device = own_rows // tile
    send_tiles = (unit - 1) * per_device
    width, hidden = up_ref.shape[0] - LANES, up_ref.shape[1]
    shard = shard_index(unit, True)
    weights = [
        (columns_of(up_right_ref, hidden, shard), up_ref.at[pl.ds(width, LANES)]),
        (rows_at(down_left_ref, hidden, shard), down_ref.at[:, pl.ds(width, LANES)]),
    ]
    for lead, pieces, ref in zip(leads(), ((up0_ref, up1_ref), (down0_ref, down1_ref)), (up_ref, down_ref)):
        for place, piece in zip((lead, 1 - lead), pieces):
            weights.append((piece, rows_at(ref, piece.shape[0], place).at[:, pl.ds(0, piece.shape[1])]))
    peers = unit_peers(unit)
    copies = [
        [
            pltpu.make_async_remote_copy(
                src_ref=send_ref.at[s, pl.ds(t * tile, tile)], dst_ref=got_ref.at[s, pl.ds(t * tile, tile)],
                send_sem=sems.at[0, s, t], recv_sem=sems.at[1, s, t], device_id=peer, device_id_type=MESH,
            )
            for t in range(per_device)
        ]
        for s, peer in enumerate(peers)
    ]

    steps = unit * per_device
    y_peer = chip_neighbours(unit)[1]
    pieces = early_sems.shape[1]
    count = early_ref.shape[0] // pieces
    early_copies = [
        pltpu.make_async_remote_copy(
            src_ref=early_ref.at[pl.ds(j * count, count)], dst_ref=early_got_ref.at[pl.ds(j * count, count)],
            send_sem=early_sems.at[0, j], recv_sem=early_sems.at[1, j], device_id=y_peer, device_id_type=MESH,
        )
        for j in range(pieces)
    ]
    hosted = len(sum_refs) > 0
    if hosted:
        net = Net()
        size = heads_ref.shape[-1] // 2
        split = len(sum_scratch("yxz", size))
        heads_refs = (sum_refs[:split], sum_refs[split : 2 * split])
        left_refs = sum_refs[2 * split :]
        stages = [
            sum_chunk(net, order, heads_ref.at[:, :, :, :, pl.ds(j * size, size)], heads_refs[j])
            for j, order in enumerate(("yxz", "xyz"))
        ]
        stages.append(sum_both(net, (("yxz", left_ref.shape[-1]),), left_ref, *left_refs[:3], (left_refs[3:],)))

    def advance():
        if hosted:
            for at in range(steps):

                @pl.when(step == at)
                def _():
                    for stage in stages:
                        stage[at]()

    neighbours = [*peers, y_peer] + ([net.x_peer, *net.z_peers] if hosted else [])

    def greet():
        meet(neighbours)
        for ref in (norms_ref, output_right_grad_ref, down_right_grad_ref, acc_ref, up_left_grad_ref):
            ref[...] = jnp.zeros_like(ref)

    load(step, load_sems, weights, greet)
    advance()
    for j, copy in enumerate(early_copies):
        pl.when(step == min(j + 1, steps - 1))(copy.start)
    normed = normed_ref[...]
    low = low_ref[...]
    dy = dy_ref[...]
    grad_low = grad_lows_ref[:, LANES:]
    feed_core(
        jnp.concatenate([normed, low], axis=1), jnp.concatenate([dy, grad_low], axis=1), up_ref, down_ref, act_ref,
        gh_ref, 512,
    )
    act = act_ref[...]
    gh = gh_ref[...]
    forward = dot_nn(act, down_ref[...])
    backward = dot_nt(gh, up_ref[...])
    grad_low_up = (grad_low_in_ref[...] + backward[:, width:]).astype(BF16)
    out = out_in_ref[...] + forward[:, :width]
    low_act = low_act_in_ref[...] + forward[:, width:]
    second = grad_in_ref[...] + backward[:, :width] + dot_nt(grad_low_up, up_left_ref[...])
    acc_ref[:, :hidden] += dot_tn(low, gh)
    acc_ref[:, hidden:] += dot_tn(grad_low, act)
    up_left_grad_ref[...] += dot_tn(grad_low_up, normed)

    @pl.when(step < send_tiles)
    def _():
        slot = step // per_device
        span = pl.ds(pl.multiple_of(lax.rem(step, per_device) * tile, tile), tile)
        send_ref[slot, span, :width] = out.astype(BF16)
        send_ref[slot, span, width : 2 * width] = second.astype(BF16)
        send_ref[slot, span, 2 * width :] = low_act.astype(BF16)

    for s in range(unit - 1):
        for t in range(per_device):
            pl.when(step == s * per_device + t)(copies[s][t].start)
            pl.when(step == send_tiles + t)(copies[s][t].wait_recv)

    @pl.when(step >= send_tiles)
    def _():
        span = pl.ds(pl.multiple_of((step - send_tiles) * tile, tile), tile)
        first = keep_ref[:, :width].astype(F32)
        low_att = keep_ref[:, width:].astype(F32)
        total_out, total_second, total_low = out, second, low_act
        for s in range(unit - 1):
            first = first + got1_ref[s, :, :width].astype(F32)
            low_att = low_att + got1_ref[s, :, width:].astype(F32)
            total_out = total_out + got_ref[s, span, :width].astype(F32)
            total_second = total_second + got_ref[s, span, width : 2 * width].astype(F32)
            total_low = total_low + got_ref[s, span, 2 * width :].astype(F32)
        low_att, total_low = low_att.astype(BF16), total_low.astype(BF16)
        x = x_ref[...].astype(F32)
        y_ref[...] = (
            x + total_out + dot_nn(low_att, output_right_ref[...]) + dot_nn(total_low, down_right_ref[...])
        ).astype(BF16)
        center = x - jnp.mean(x, axis=-1, keepdims=True)
        spread = jnp.mean(center * center, axis=-1, keepdims=True)
        inverse = lax.rsqrt(spread + EPS)
        scaled = center * inverse
        total = first * gain1_ref[...] + total_second * gain2_ref[...]
        mean = jnp.mean(total, axis=-1, keepdims=True)
        inner = jnp.mean(total * scaled, axis=-1, keepdims=True)
        dx_ref[...] = dy.astype(F32) + (total - mean - scaled * inner) * inverse
        norms_ref[0:1, :] += jnp.sum(first * scaled, axis=0, keepdims=True)
        norms_ref[1:2, :] += jnp.sum(first, axis=0, keepdims=True)
        norms_ref[2:3, :] += jnp.sum(total_second * scaled, axis=0, keepdims=True)
        norms_ref[3:4, :] += jnp.sum(total_second, axis=0, keepdims=True)
        output_right_grad_ref[...] += dot_tn(low_att, dy)
        down_right_grad_ref[...] += dot_tn(total_low, dy)

    @pl.when(step == steps - 1)
    def _():
        for copy in early_copies:
            copy.wait()
        sums_ref[...] = (acc_ref[...] + early_got_ref[...].astype(F32)).astype(BF16)
        quarters(both_ref, up_left_grad_ref[...], output_right_grad_ref[...], down_right_grad_ref[...])
        start = 3 * (width // 4)
        count = width // LANES
        for q in range(4):
            rows = [norms_ref[q : q + 1, j * LANES : (j + 1) * LANES] for j in range(count)]
            block = jnp.concatenate([*rows, jnp.zeros((LANES - count, LANES), F32)], axis=0)
            both_ref[q % 2, q // 2, :, start:] = block.astype(BF16)
        for group in copies:
            for copy in group:
                copy.wait_send()
        if hosted:
            for at in range(steps, max(len(stage) for stage in stages)):
                for stage in stages:
                    if at < len(stage):
                        stage[at]()
            outs = []
            for j, refs in enumerate((*heads_refs, left_refs[3:])):
                full = refs[5]
                target = left_out_ref if j == 2 else heads_out_ref.at[:, :, :, :, pl.ds(j * size, size)]
                outs.append(pltpu.make_async_copy(full, target, out_sems.at[j]))
                outs[-1].start()
            for copy in net.started:
                copy.wait_send()
            for copy in outs:
                copy.wait()


def feed_second(unit, normed, low, dy, grad_lows, out, grad, low_act, grad_low, x, keep, got, gains, output_right,
                down_right, ups, up_left, up_right, downs, down_left, early, heads, left, hosted, tile):
    rows, width = normed.shape
    own_rows = rows // unit
    anywhere = pl.BlockSpec(memory_space=pl.ANY)
    extra = []
    if hosted:
        heads = heads.reshape((2,) + SUM_ROWS + heads.shape[-1:])
        left = left.reshape((2, 2) + SUM_ROWS + left.shape[-1:])
        extra = sum_scratch("yxz", heads.shape[-1] // 2) + sum_scratch("xyz", heads.shape[-1] // 2)
        extra += both_scratch((("yxz", left.shape[-1]),))
    hidden = ups[0].shape[1]
    steps, per_device = rows // tile, own_rows // tile
    send_tiles = steps - per_device
    wide = 2 * width + LANES

    def turned(size):
        def index(i):
            place, slot = place_in_unit(unit)[0], i // per_device + 1
            return (lax.rem(place + unit - slot, unit) * per_device + lax.rem(i, per_device), 0)

        return pl.BlockSpec((tile, size), index)

    def late(size):
        return pl.BlockSpec((tile, size), lambda i: (jnp.maximum(i - send_tiles, 0), 0))

    return pl.pallas_call(
        functools.partial(feed_second_kernel, unit, tile),
        grid=(steps,),
        in_specs=[
            turned(width),
            turned(LANES),
            turned(width),
            turned(2 * LANES),
            turned(width),
            turned(width),
            turned(LANES),
            turned(LANES),
            late(width),
            late(width + LANES),
            pl.BlockSpec((unit - 1, tile, width + LANES), lambda i: (0, jnp.maximum(i - send_tiles, 0), 0)),
            whole((1, width)),
            whole((1, width)),
            whole(output_right.shape),
            whole(down_right.shape),
            anywhere,
            anywhere,
            whole(up_left.shape),
            anywhere,
            anywhere,
            anywhere,
            anywhere,
            whole(early.shape),
            whole(heads.shape),
            whole(left.shape),
        ],
        out_specs=[
            late(width),
            late(width),
            held((LANES, 2 * hidden)),
            held((2, 2, LANES, 3 * (width // 4) + LANES)),
            anywhere,
            anywhere,
        ],
        scratch_shapes=[
            pltpu.VMEM((tile, hidden), BF16),
            pltpu.VMEM((tile, hidden), BF16),
            pltpu.VMEM((width + LANES, hidden), BF16),
            pltpu.VMEM((hidden, width + LANES), BF16),
            pltpu.VMEM((unit - 1, own_rows, wide), BF16),
            pltpu.VMEM((unit - 1, own_rows, wide), BF16),
            pltpu.VMEM((LANES, 2 * hidden), BF16),
            pltpu.VMEM((LANES, 2 * hidden), F32),
            pltpu.VMEM((8, width), F32),
            pltpu.VMEM((LANES, width), F32),
            pltpu.VMEM((LANES, width), F32),
            pltpu.VMEM((LANES, width), F32),
            pltpu.SemaphoreType.DMA((2, unit - 1, per_device)),
            pltpu.SemaphoreType.DMA((2, 4)),
            pltpu.SemaphoreType.DMA((3,)),
            pltpu.SemaphoreType.DMA((6,)),
        ]
        + extra,
        out_shape=[
            shaped((own_rows, width), BF16),
            shaped((own_rows, width), F32),
            shaped((LANES, 2 * hidden), BF16),
            shaped((2, 2, LANES, 3 * (width // 4) + LANES), BF16),
            shaped(heads.shape, BF16),
            shaped(left.shape[1:] if hosted else left.shape, BF16),
        ],
        compiler_params=pltpu.CompilerParams(
            dimension_semantics=("arbitrary",), vmem_limit_bytes=VMEM_LIMIT, collective_id=4, has_side_effects=True
        ),
        cost_estimate=BRIEF,
        name="feed_second",
    )(normed, low, dy, grad_lows, out, grad, low_act, grad_low, x, keep, got, *gains, output_right, down_right, *ups,
      up_left, up_right, *downs, down_left, early, heads, left)


def project_kernel(
    unit, main_tiles, halo_ref, normed_ref, dy_ref, grad_lows_ref, late_ref, cos0_ref, cos1_ref, minus0_ref, minus1_ref, plus0_ref,
    plus1_ref, gain_ref, shift_ref, triple0_ref, triple1_ref, left_ref, right_ref, output0_ref, output1_ref,
    output_left_ref, low_ref, q_ref, k_ref, v_ref, g_ref, triple_ref, output_ref, load_sems,
):
    step = pl.program_id(0)
    load(
        step, load_sems,
        head_weights(
            unit, (triple0_ref, triple1_ref), right_ref, (output0_ref, output1_ref), output_left_ref, triple_ref,
            output_ref,
        ),
    )

    later = late_ref[0, 0:1, :] > 0.0
    tables = tuple(
        jnp.where(later, two[...], one[...])
        for one, two in ((cos0_ref, cos1_ref), (minus0_ref, minus1_ref), (plus0_ref, plus1_ref))
    )
    head_width = output0_ref.shape[0]
    first = low_lanes()

    def rows(normed, full):
        low = dot_nn(normed, left_ref[...]).astype(BF16)
        if full:
            low_ref[...] = low
        mixed = dot_nn(jnp.concatenate([normed, low], axis=1), triple_ref[...])
        if full:
            grads = jnp.concatenate([dy_ref[...], grad_lows_ref[:, :LANES]], axis=1)
            g_ref[...] = dot_nt(grads, output_ref[...]).astype(BF16)
        for pair in range(2 * head_width // LANES):
            one, two, three = (
                mixed[:, (3 * pair + part) * LANES : (3 * pair + part + 1) * LANES] for part in range(3)
            )
            cols = pl.ds(pair * LANES, LANES)
            key = pltpu.roll(jnp.where(first, three, one), HEAD_DIM, 1)
            k_ref[:, cols] = rotate(key, *tables).astype(BF16)
            v_ref[:, cols] = jnp.where(first, two, three).astype(BF16)
            if full:
                query = rotate(jnp.where(first, one, two), *tables).astype(BF16)
                q_ref[:, cols] = query * HEAD_DIM**-0.5

    @pl.when(step < main_tiles)
    def _():
        rows(normed_ref[...], True)

    @pl.when(step >= main_tiles)
    def _():
        rows(normalize(halo_ref[...].astype(F32), gain_ref[...], shift_ref[...]).astype(BF16), False)


def project(unit, conts, x_halo, normed, dy, grad_lows, gain, shift, triples, left, right, outputs, output_left, tables,
            tile):
    rows, width = dy.shape
    head_width = outputs[0].shape[0]
    anywhere = pl.BlockSpec(memory_space=pl.ANY)
    per_block = SHORT // tile
    main_tiles, halo_tiles = rows // tile, SHORT // tile
    late = jnp.concatenate([jnp.repeat(conts, per_block), jnp.zeros((halo_tiles,), jnp.int32)])
    late = jnp.broadcast_to(late.astype(F32)[:, None, None], (main_tiles + halo_tiles, 8, LANES))

    halo = pl.BlockSpec((tile, width), lambda i: (jnp.maximum(i - main_tiles, 0), 0))

    def table(which):
        return pl.BlockSpec((tile, LANES), lambda i: (which * per_block + lax.rem(i, per_block), 0))

    def main(size):
        return pl.BlockSpec((tile, size), lambda i: (jnp.minimum(i, main_tiles - 1), 0))

    def all_rows(size):
        return pl.BlockSpec((tile, size), lambda i: (jnp.where(i < main_tiles, i + halo_tiles, i - main_tiles), 0))

    return pl.pallas_call(
        functools.partial(project_kernel, unit, main_tiles),
        grid=(main_tiles + halo_tiles,),
        in_specs=[
            halo,
            main(width),
            main(width),
            main(2 * LANES),
            pl.BlockSpec((1, 8, LANES), lambda i: (i, 0, 0)),
            table(0),
            table(1),
            table(0),
            table(1),
            table(0),
            table(1),
            whole(gain.shape),
            whole(shift.shape),
            anywhere,
            anywhere,
            whole(left.shape),
            anywhere,
            anywhere,
            anywhere,
            anywhere,
        ],
        out_specs=[
            main(LANES),
            main(2 * head_width),
            all_rows(2 * head_width),
            all_rows(2 * head_width),
            main(2 * head_width),
        ],
        scratch_shapes=[
            pltpu.VMEM((width + LANES, 6 * head_width), BF16),
            pltpu.VMEM((2 * head_width, width + LANES), BF16),
            pltpu.SemaphoreType.DMA((8,)),
        ],
        out_shape=[
            shaped((rows, LANES), BF16),
            shaped((rows, 2 * head_width), BF16),
            shaped((SHORT + rows, 2 * head_width), BF16),
            shaped((SHORT + rows, 2 * head_width), BF16),
            shaped((rows, 2 * head_width), BF16),
        ],
        compiler_params=params(),
        cost_estimate=BRIEF,
        name="project",
    )(x_halo, normed, dy, grad_lows, late, *[table for table in tables for _ in range(2)], gain, shift, *triples, left, right,
      *outputs, output_left)


def attend_rows(with_prev, pairs, count, allowed, q_ref, k_ref, v_ref, g_ref, kp_ref, vp_ref, tables, att_ref, gq_ref,
                dk_ref, dv_ref, dkp_ref, dvp_ref):
    first = low_lanes()
    zero = jnp.zeros((), BF16)

    def stack(pair):
        return jnp.concatenate([jnp.where(first, pair, zero), jnp.where(first, zero, pair)], axis=0)

    def unstack(both):
        return jnp.where(first, both[:count], both[count:])

    def joined(fold, values):
        return functools.reduce(fold, values)

    pieces = []
    for lanes in pairs:
        for start in range(0, SHORT, count):
            span = pl.ds(start, count)
            parts = []
            if with_prev:
                parts.append((kp_ref[:, lanes], vp_ref[:, lanes], dkp_ref, dvp_ref, pl.ds(0, SHORT)))
            if start:
                before = pl.ds(0, start)
                parts.append((k_ref[before, lanes], v_ref[before, lanes], dk_ref, dv_ref, before))
            parts.append((k_ref[span, lanes], v_ref[span, lanes], dk_ref, dv_ref, span))
            pieces.append((lanes, span, stack(q_ref[span, lanes]), stack(g_ref[span, lanes]), parts))

    scores, grads, weights, lows, inners, slopes = [], [], [], [], [], []
    for _, _, queries, _, parts in pieces:
        found = [dot_nt(queries, part[0]) for part in parts]
        scores.append(found[:-1] + [jnp.where(allowed, found[-1], -1e30)])
    for _, _, _, grad, parts in pieces:
        grads.append([dot_nt(grad, part[1]) for part in parts])
    for found in scores:
        peak = joined(jnp.maximum, [jnp.max(score, axis=1, keepdims=True) for score in found])
        exps = [jnp.exp(score - peak) for score in found]
        scale = 1.0 / joined(jnp.add, [jnp.sum(exp, axis=1, keepdims=True) for exp in exps])
        weights.append([exp * scale for exp in exps])
        lows.append([weight.astype(BF16) for weight in weights[-1]])
    for (lanes, span, _, grad, parts), low in zip(pieces, lows):
        attended = joined(jnp.add, [dot_nn(weight, part[1]) for weight, part in zip(low, parts)])
        att_ref[span, lanes] = unstack(attended).astype(BF16)
        inners.append(jnp.sum(attended * grad.astype(F32), axis=1, keepdims=True))
    for weight, grad, inner in zip(weights, grads, inners):
        slopes.append([(w * (g - inner)).astype(BF16) for w, g in zip(weight, grad)])
    for (lanes, span, queries, grad, parts), low, slope in zip(pieces, lows, slopes):
        grad_query = joined(jnp.add, [dot_nn(ds, part[0]) for ds, part in zip(slope, parts)])
        for ds, weight, (_, _, to_key, to_value, rows) in zip(slope, low, parts):
            to_key[lanes, rows] += dot_tn(queries, ds)
            to_value[lanes, rows] += dot_tn(grad, weight)
        grad_query = unstack(grad_query) * HEAD_DIM**-0.5
        gq_ref[span, lanes] = unrotate(grad_query, *[table[span] for table in tables]).astype(BF16)


def unrotate_tall(ref, lanes, cosine, sine):
    half = ROT // 2
    value = ref[lanes, :]
    halves = []
    for base in (HEAD_DIM, 0):
        one, two = value[base : base + half], value[base + half : base + ROT]
        halves += [one * cosine + two * sine, two * cosine - one * sine, value[base + ROT : base + HEAD_DIM]]
    return jnp.concatenate(halves, axis=0).astype(BF16).T


def attend_kernel(
    blocks, pairs, count, conts_ref, q_ref, k_ref, v_ref, g_ref, kp_ref, vp_ref, cos_ref, minus_ref, plus_ref,
    tall_cos_ref, tall_sin_ref, att_ref, gq_ref, gk_ref, gv_ref, halo_ref, dk_ref, dv_ref,
):
    step = pl.program_id(0)
    block = blocks - 1 - step
    continued = conts_ref[block]
    offset = pl.multiple_of(continued * SHORT, SHORT)
    tables = tuple(ref.at[pl.ds(offset, SHORT)] for ref in (cos_ref, minus_ref, plus_ref))
    now = lax.rem(step, 2)
    own = (dk_ref.at[now], dv_ref.at[now])
    before = (dk_ref.at[1 - now], dv_ref.at[1 - now])

    @pl.when(step == 0)
    def _():
        for ref in own:
            ref[...] = jnp.zeros_like(ref)

    for ref in before:
        ref[...] = jnp.zeros_like(ref)
    row = lax.broadcasted_iota(jnp.int32, (2 * count, count), 0)
    column = lax.broadcasted_iota(jnp.int32, (2 * count, count), 1)
    allowed = column <= jnp.where(row >= count, row - count, row)
    args = (q_ref, k_ref, v_ref, g_ref, kp_ref, vp_ref, tables, att_ref, gq_ref, *own, *before)

    def each(some, work):
        some = math.gcd(some, pairs)

        def body(i, carry):
            work([pl.ds(pl.multiple_of((i * some + j) * LANES, LANES), LANES) for j in range(some)])
            return carry

        lax.fori_loop(0, pairs // some, body, 0)

    pl.when(continued == 0)(lambda: each(2, lambda lanes: attend_rows(False, lanes, count, allowed, *args)))
    pl.when(continued != 0)(lambda: each(2, lambda lanes: attend_rows(True, lanes, count, allowed, *args)))
    turn = tuple(ref.at[:, pl.ds(offset, SHORT)] for ref in (tall_cos_ref, tall_sin_ref))

    def leave(lanes):
        for pair in lanes:
            gk_ref[:, pair] = unrotate_tall(own[0], pair, *[ref[...] for ref in turn])
            gv_ref[:, pair] = own[1][pair, :].astype(BF16).T

    each(1, leave)

    @pl.when(block == 0)
    def _():
        base = tuple(ref.at[:, pl.ds(0, SHORT)] for ref in (tall_cos_ref, tall_sin_ref))

        def leave_halo(lanes):
            for pair in lanes:
                halo_ref[0, :, pair] = unrotate_tall(before[0], pair, *[ref[...] for ref in base])
                halo_ref[1, :, pair] = before[1][pair, :].astype(BF16).T

        each(1, leave_halo)


def attend(conts, q, k, v, g, tables, tall, count):
    rows, head_width = q.shape
    blocks = rows // SHORT
    here = pl.BlockSpec((SHORT, head_width), lambda i, conts: (blocks - 1 - i, 0))
    after = pl.BlockSpec((SHORT, head_width), lambda i, conts: (blocks - i, 0))
    return pl.pallas_call(
        functools.partial(attend_kernel, blocks, head_width // LANES, count),
        grid_spec=pltpu.PrefetchScalarGridSpec(
            num_scalar_prefetch=1,
            grid=(blocks,),
            in_specs=[here, after, after, here, here, here] + [whole(table.shape) for table in (*tables, *tall)],
            out_specs=[here] * 4 + [held((2, SHORT, head_width))],
            scratch_shapes=[pltpu.VMEM((2, head_width, SHORT), F32)] * 2,
        ),
        out_shape=[shaped((rows, head_width), BF16)] * 4 + [shaped((2, SHORT, head_width), BF16)],
        compiler_params=params(),
        cost_estimate=BRIEF,
        name="attend",
    )(conts, q, k, v, g, k, v, *tables, *tall)


def settle_kernel(
    unit, tile, normed_ref, low_ref, grad_lows_ref, out_in_ref, att_ref, gq_ref, gk_ref, gv_ref, halo_ref, triple0_ref,
    triple1_ref, left_ref, output0_ref, output1_ref, right_ref, output_left_ref, out_ref, keep_ref, heads_ref,
    left_sums_ref, got_ref, send_ref, halo_got_ref, key_ref, value_ref, mixed_ref, triple_ref, output_ref, acc_ref,
    out_acc_ref, left_grad_ref, halo_sems, sems, load_sems,
):
    step = pl.program_id(0)
    per_device = got_ref.shape[1] // tile
    steps = unit * per_device
    halo_start = steps - SHORT // tile
    place, base = place_in_unit(unit)
    half = base // unit
    peers = unit_peers(unit)
    y_peer = chip_neighbours(unit)[1]
    halo_copies = []
    for j in range(SHORT // tile):
        part = pl.ds(j * tile, tile)
        halo_copies.append(
            pltpu.make_async_remote_copy(
                src_ref=halo_ref.at[:, part], dst_ref=halo_got_ref.at[:, part], send_sem=halo_sems.at[0, j],
                recv_sem=halo_sems.at[1, j], device_id=y_peer, device_id_type=MESH,
            )
        )
    copies = [
        [
            pltpu.make_async_remote_copy(
                src_ref=send_ref.at[s, pl.ds(t * tile, tile)], dst_ref=got_ref.at[s, pl.ds(t * tile, tile)],
                send_sem=sems.at[0, s, t], recv_sem=sems.at[1, s, t], device_id=peer, device_id_type=MESH,
            )
            for t in range(per_device)
        ]
        for s, peer in enumerate(peers)
    ]
    neighbours = [y_peer, *peers]

    def greet():
        meet(neighbours)

        @pl.when(half == 1)
        def _():
            for copy in halo_copies:
                copy.start()

        for ref in (acc_ref, out_acc_ref, left_grad_ref):
            ref[...] = jnp.zeros_like(ref)

    load(
        step, load_sems,
        head_weights(
            unit, (triple0_ref, triple1_ref), right_ref, (output0_ref, output1_ref), output_left_ref, triple_ref,
            output_ref,
        ),
        greet,
    )

    key_ref[...], value_ref[...] = gk_ref[...], gv_ref[...]
    for j, copy in enumerate(halo_copies):

        @pl.when((half == 0) & (step == halo_start + j))
        def _():
            copy.wait_recv()
            rows = pl.ds(j * tile, tile)
            count = output0_ref.shape[0]
            for ref, which in ((key_ref, 0), (value_ref, 1)):
                for here, there in ((pl.ds(0, count), pl.ds(count, count)), (pl.ds(count, count), pl.ds(0, count))):
                    ref[:, here] = (ref[:, here].astype(F32) + halo_got_ref[which, rows, there].astype(F32)).astype(BF16)

    normed = normed_ref[...]
    low = low_ref[...]
    grad_low_out = grad_lows_ref[:, :LANES]
    head_width = output0_ref.shape[0]
    first = low_lanes()
    for pair in range(2 * head_width // LANES):
        q, k, v = (ref[:, pair * LANES : (pair + 1) * LANES] for ref in (gq_ref, key_ref, value_ref))
        for part, value in enumerate((jnp.where(first, q, k), jnp.where(first, v, q), jnp.where(first, k, v))):
            mixed_ref[:, (3 * pair + part) * LANES : (3 * pair + part + 1) * LANES] = value
    mixed = mixed_ref[...]
    att = att_ref[...]
    width = normed.shape[1]
    backward = dot_nt(mixed, triple_ref[...])
    forward = dot_nn(att, output_ref[...])
    grad_low = backward[:, width:].astype(BF16)
    grad = (backward[:, :width] + dot_nt(grad_low, left_ref[...])).astype(BF16)
    out_ref[...] = out_in_ref[...] + forward[:, :width]
    low_att = forward[:, width:].astype(BF16)

    @pl.when(step // per_device == place)
    def _():
        keep_ref[:, :width] = grad
        keep_ref[:, width:] = low_att

    span = pl.ds(pl.multiple_of(lax.rem(step, per_device) * tile, tile), tile)
    for s in range(unit - 1):
        owner = lax.rem(place + unit - (s + 1), unit)

        @pl.when(step // per_device == owner)
        def _():
            send_ref[s, span, :width] = grad
            send_ref[s, span, width:] = low_att

        for t in range(per_device):
            pl.when(step == owner * per_device + t)(copies[s][t].start)

    acc_ref[...] += dot_tn(low, mixed)
    out_acc_ref[...] += dot_tn(grad_low_out, att)
    left_grad_ref[...] += dot_tn(grad_low, normed)

    @pl.when(step == steps - 1)
    def _():
        size = 3 * head_width
        for j in range(2):
            heads_ref[j, :, :size] = acc_ref[:, j * size : (j + 1) * size].astype(BF16)
            heads_ref[j, :, size:] = out_acc_ref[:, j * head_width : (j + 1) * head_width].astype(BF16)
        quarters(left_sums_ref, left_grad_ref[...])

        @pl.when(half == 1)
        def _():
            for copy in halo_copies:
                copy.wait_send()

        for group in copies:
            for copy in group:
                copy.wait()


def settle(unit, normed, low, grad_lows, out, heads, halo, triples, left, outputs, right, output_left, tile):
    rows, width = normed.shape
    own_rows = rows // unit
    head_width = outputs[0].shape[0]
    steps, per_device = rows // tile, own_rows // tile
    anywhere = pl.BlockSpec(memory_space=pl.ANY)

    def kept(i):
        return (jnp.clip(i - place_in_unit(unit)[0] * per_device, 0, per_device - 1), 0)

    return pl.pallas_call(
        functools.partial(settle_kernel, unit, tile),
        grid=(steps,),
        in_specs=[rows_of(tile, width), rows_of(tile, LANES), rows_of(tile, 2 * LANES), rows_of(tile, width)]
        + [rows_of(tile, 2 * head_width)] * 4
        + [anywhere]
        + [anywhere, anywhere, whole(left.shape), anywhere, anywhere, anywhere, anywhere],
        out_specs=[
            rows_of(tile, width),
            pl.BlockSpec((tile, width + LANES), kept),
            held((2, LANES, 4 * head_width)),
            held((2, 2, LANES, width // 4)),
            anywhere,
        ],
        scratch_shapes=[
            pltpu.VMEM((unit - 1, own_rows, width + LANES), BF16),
            pltpu.VMEM((2, SHORT, 2 * head_width), BF16),
            pltpu.VMEM((tile, 2 * head_width), BF16),
            pltpu.VMEM((tile, 2 * head_width), BF16),
            pltpu.VMEM((tile, 6 * head_width), BF16),
            pltpu.VMEM((width + LANES, 6 * head_width), BF16),
            pltpu.VMEM((2 * head_width, width + LANES), BF16),
            pltpu.VMEM((LANES, 6 * head_width), F32),
            pltpu.VMEM((LANES, 2 * head_width), F32),
            pltpu.VMEM((LANES, width), F32),
            pltpu.SemaphoreType.DMA((2, SHORT // tile)),
            pltpu.SemaphoreType.DMA((2, unit - 1, per_device)),
            pltpu.SemaphoreType.DMA((8,)),
        ],
        out_shape=[
            shaped((rows, width), F32),
            shaped((own_rows, width + LANES), BF16),
            shaped((2, LANES, 4 * head_width), BF16),
            shaped((2, 2, LANES, width // 4), BF16),
            shaped((unit - 1, own_rows, width + LANES), BF16),
        ],
        compiler_params=pltpu.CompilerParams(
            dimension_semantics=("arbitrary",), vmem_limit_bytes=VMEM_LIMIT, collective_id=5, has_side_effects=True
        ),
        cost_estimate=BRIEF,
        name="settle",
    )(normed, low, grad_lows, out, *heads, halo, *triples, left, *outputs, right, output_left)


FEED_ORDERS = ("xz", "zx", "xz", "zx")


def sum_kernel(size, feed_ref, both_ref, heads_ref, left_ref, feed_out_ref, both_out_ref, heads_out_ref, left_out_ref,
               cross_sems, local_sems, *refs):
    net = Net()
    meet([net.x_peer, net.y_peer, net.core_peer, *net.z_peers])
    locals_, crossing = [], []

    def hand_over(slot, full, out, first, second):
        for place, at in ((0, first), (1, second)):
            target = out.at[net.core, at]
            local = pltpu.make_async_copy(full.at[place], target, local_sems.at[slot, place])
            local.start()
            locals_.append(local)
            crossing.append(net.copy(full.at[place], target, cross_sems, 2 * slot + place, net.core_peer))
            net.start(crossing[-1:])

    split = len(sum_scratch("xz", size))
    feed_refs = [refs[j * split : (j + 1) * split] for j in range(len(FEED_ORDERS))]
    both_refs = refs[len(FEED_ORDERS) * split :]
    parts = split_columns(both_ref.shape[-1])
    per_part = (len(both_refs) - 3) // 2
    scratches = (both_refs[3 : 3 + per_part], both_refs[3 + per_part :])
    running = [sum_both(net, parts, both_ref, *both_refs[:3], scratches)]
    running += [
        sum_chunk(net, order, feed_ref.at[:, :, :, pl.ds(j * size, size)], feed_refs[j])
        for j, order in enumerate(FEED_ORDERS)
    ]

    def both_done():
        start = 0
        for j, (_, count) in enumerate(parts):
            columns = both_out_ref.at[:, :, :, :, :, pl.ds(start, count)]
            hand_over(j, scratches[j][5], columns, net.half, net.other_half)
            start += count

    def feed_done(j):
        columns = feed_out_ref.at[:, :, :, :, :, pl.ds(j * size, size)]
        hand_over(4 + j, feed_refs[j][5], columns, net.other_half, net.half)

    for k in range(max(len(stage) for stage in running)):
        for j, stage in enumerate(running):
            if k < len(stage):
                stage[k]()
            if k == len(stage) - 1:
                both_done() if j == 0 else feed_done(j - 1)
        if k == 0:
            hand_over(2, heads_ref, heads_out_ref, net.half, net.other_half)
            hand_over(3, left_ref, left_out_ref, net.half, net.other_half)
    for copy in locals_:
        copy.wait()
    for copy in crossing:
        copy.wait_recv()
    for copy in net.started:
        copy.wait_send()


def sum_all(feed, both, heads, left):
    arrays = (feed.reshape(SUM_ROWS + feed.shape[-1:]), both.reshape((2, 2) + SUM_ROWS + both.shape[-1:]), heads, left)
    size = feed.shape[-1] // len(FEED_ORDERS)
    slots = 4 + len(FEED_ORDERS)
    outs = [shaped((2, 2) + SUM_ROWS + array.shape[-1:], BF16) for array in arrays]
    results = pl.pallas_call(
        functools.partial(sum_kernel, size),
        out_shape=outs,
        in_specs=[pl.BlockSpec(memory_space=pltpu.VMEM)] * 4,
        out_specs=[pl.BlockSpec(memory_space=pl.ANY)] * 4,
        scratch_shapes=[pltpu.SemaphoreType.DMA((2, 2 * slots)), pltpu.SemaphoreType.DMA((slots, 2))]
        + [shape for order in FEED_ORDERS for shape in sum_scratch(order, size)]
        + both_scratch(split_columns(both.shape[-1])),
        compiler_params=pltpu.CompilerParams(
            collective_id=2, has_side_effects=True, vmem_limit_bytes=VMEM_LIMIT
        ),
        cost_estimate=BRIEF,
        name="sum_all",
    )(*arrays)
    return [value.reshape(2, 2, LANES, value.shape[-1]) for value in results]


def unpack_kernel(triple_width, feed_ref, both_ref, heads_ref, left_ref, triple_ref, output_ref, up_ref, down_ref,
                  triple_left_ref, up_left_ref, output_right_ref, down_right_ref, *norm_refs):
    part = pl.program_id(1)

    def columns(ref, start, size):
        return ref[0, 0, :, pl.ds(pl.multiple_of(start + part * size, LANES), size)]

    triple_ref[...] = columns(heads_ref, 0, triple_ref.shape[1]).astype(F32)
    output_ref[...] = columns(heads_ref, triple_width, output_ref.shape[0]).T.astype(F32)
    hidden = up_ref.shape[1]
    up_ref[...] = columns(feed_ref, 0, hidden).astype(F32)
    down_ref[...] = columns(feed_ref, 2 * hidden, hidden).T.astype(F32)
    size = triple_left_ref.shape[0]
    triple_left_ref[...] = columns(left_ref, 0, size).T.astype(F32)
    up_left_ref[...] = columns(both_ref, 0, size).T.astype(F32)
    output_right_ref[...] = columns(both_ref, 2 * size, size).astype(F32)
    down_right_ref[...] = columns(both_ref, 4 * size, size).astype(F32)
    for q, ref in enumerate(norm_refs):

        @pl.when((pl.program_id(0) == q) & (part == 0))
        def _():
            ref[...] = both_ref[0, 0, : ref.shape[0], 6 * size :].astype(F32)


def unpack(feed, both, heads, left, triple_width):
    arrays = (feed, both, heads, left)
    hidden, quarter = feed.shape[-1] // 2, left.shape[-1]
    width, head_width = 4 * quarter, heads.shape[-1] - triple_width

    def tall(rows):
        return pl.BlockSpec((rows // 2, LANES), lambda s, part: (2 * s + part, 0))

    def wide(cols):
        return pl.BlockSpec((LANES, cols // 2), lambda s, part: (0, 2 * s + part))

    return pl.pallas_call(
        functools.partial(unpack_kernel, triple_width),
        grid=(4, 2),
        in_specs=[
            pl.BlockSpec((1, 1) + value.shape[2:], lambda s, part: (lax.rem(s, 2), s // 2, 0, 0)) for value in arrays
        ],
        out_specs=[
            wide(triple_width), tall(head_width), wide(hidden), tall(hidden), tall(quarter), tall(quarter),
            wide(quarter), wide(quarter), *[held((width // LANES, LANES))] * 4,
        ],
        out_shape=[
            shaped((LANES, 4 * triple_width), F32),
            shaped((4 * head_width, LANES), F32),
            shaped((LANES, 4 * hidden), F32),
            shaped((4 * hidden, LANES), F32),
            shaped((width, LANES), F32),
            shaped((width, LANES), F32),
            shaped((LANES, width), F32),
            shaped((LANES, width), F32),
        ]
        + [shaped((width // LANES, LANES), F32)] * 4,
        compiler_params=params(2),
        cost_estimate=BRIEF,
        name="unpack",
    )(*arrays)


def shards(
    ranks,
    groups,
    block_input,
    sequence_lengths,
    first_gain,
    first_shift,
    second_gain,
    second_shift,
    triple_weight,
    triple_left,
    triple_right,
    output_weight,
    output_left,
    output_right,
    expand_weight,
    expand_left,
    expand_right,
    shrink_weight,
    shrink_left,
    shrink_right,
    cotangent,
):
    unit = ranks // 2
    own_rows, width = block_input.shape
    rows = own_rows * unit
    blocks = rows // SHORT
    tile = math.gcd(own_rows, 256)
    triple_width = triple_weight.shape[1]
    head_width = output_weight.shape[0]
    hidden = expand_weight.shape[1]
    mp = lax.axis_index("mp")
    half = mp // unit
    place = lax.rem(mp, unit)
    far = lax.rem(mp + unit, ranks)
    swap = [(m, (m + unit) % ranks) for m in range(ranks)]

    tables = rotary_tables()
    beside = [[(d, d ^ bit) for d in range(groups)] for bit in (1, 2)]
    continues = find_flags(sequence_lengths[0])
    conts = lax.dynamic_slice_in_dim(continues, half * blocks, blocks, 0)
    gain1, shift1 = first_gain[None, :], first_shift[None, :]
    gain2, shift2 = second_gain[None, :], second_shift[None, :]

    (normed1, normed2, dy, low2, grad_lows, out, grad2, low_act, grad_low2, feed_sums, triple_far,
     output_far, x_halo, expand_half, shrink_half) = feed_first(
        unit, block_input, cotangent, (gain1, shift1, gain2, shift2), expand_weight, expand_left, expand_right,
        shrink_weight, shrink_left, output_right, shrink_right, triple_weight, output_weight, tile,
    )
    expand_piece = lax.ppermute(expand_half, "mp", swap)
    shrink_piece = lax.ppermute(shrink_half, "mp", swap)
    low1, q, k, v, g = project(
        unit, conts, x_halo, normed1, dy, grad_lows, gain1, shift1, (triple_weight, triple_far), triple_left,
        triple_right, (output_weight, output_far), output_left, tables, tile,
    )
    att, gq, gk, gv, halo = attend(conts, q, k, v, g, tables, tall_tables(), 256)
    expand_piece, shrink_piece, att = lax.optimization_barrier((expand_piece, shrink_piece, att))
    expand_other = lax.ppermute(expand_piece, "dp", beside[0])
    shrink_other = lax.ppermute(shrink_piece, "dp", beside[1])
    out, keep1, heads, left, got1 = settle(
        unit, normed1, low1, grad_lows, out, (att, gq, gk, gv), halo, (triple_weight, triple_far), triple_left,
        (output_weight, output_far), triple_right, output_left, tile,
    )
    hosted = ranks == 4 and groups == 8
    block_output, input_gradient, feed_sums, both, heads_sum, left_sum = feed_second(
        unit, normed2, low2, dy, grad_lows, out, grad2, low_act, grad_low2, block_input, keep1, got1, (gain1, gain2),
        output_right, shrink_right, (expand_piece, expand_other), expand_left, expand_right,
        (shrink_piece, shrink_other), shrink_left, feed_sums, heads, left, hosted, tile,
    )
    if hosted:
        (triple_right_sum, output_left_sum, expand_right_sum, shrink_left_sum, triple_left_sum, expand_left_sum,
         output_right_sum, shrink_right_sum, *norms) = unpack(
            *sum_all(feed_sums, both, heads_sum, left_sum), triple_width
        )
        norms = [value.reshape(width) for value in norms]
    else:

        def spread(*placed):
            size = placed[0][0].shape[1]
            wide = jnp.zeros((LANES, size * ranks), BF16)
            for value, shard in placed:
                wide = lax.dynamic_update_slice_in_dim(wide, value, shard * size, 1)
            return wide

        def joined(value):
            return value.transpose(2, 1, 0, 3).reshape(LANES, -1)

        def columns(value, start, size):
            return value.reshape(LANES, ranks, -1)[:, :, start : start + size].reshape(LANES, -1).astype(F32)

        heads, feed, left, both = lax.psum(
            (spread((heads[0], mp), (heads[1], far)), spread((feed_sums, far)), left, both), ("dp", "mp")
        )
        triple_right_sum = columns(heads, 0, triple_width)
        output_left_sum = columns(heads, triple_width, head_width).T
        expand_right_sum = columns(feed, 0, hidden)
        shrink_left_sum = columns(feed, hidden, hidden).T
        triple_left_sum = joined(left).astype(F32).T
        quarter = width // 4
        expand_left_sum = joined(both[..., :quarter]).astype(F32).T
        output_right_sum = joined(both[..., quarter : 2 * quarter]).astype(F32)
        shrink_right_sum = joined(both[..., 2 * quarter : 3 * quarter]).astype(F32)
        norms = both[:, :, : width // LANES, 3 * quarter :].transpose(1, 0, 2, 3).reshape(4, width).astype(F32)
    return (
        block_output,
        input_gradient,
        norms[0],
        norms[1],
        norms[2],
        norms[3],
        triple_left_sum,
        triple_right_sum,
        output_left_sum,
        output_right_sum,
        expand_left_sum,
        expand_right_sum,
        shrink_left_sum,
        shrink_right_sum,
    )


def solution(mesh):
    placed = (
        P(("dp", "mp"), None),
        P("dp", None),
        P(),
        P(),
        P(),
        P(),
        P(None, "mp"),
        P(),
        P(),
        P("mp", None),
        P(),
        P(),
        P(None, "mp"),
        P(),
        P(),
        P("mp", None),
        P(),
        P(),
        P(("dp", "mp"), None),
    )
    return jax.shard_map(
        functools.partial(shards, mesh.shape["mp"], mesh.shape["dp"]),
        mesh=mesh,
        in_specs=placed,
        out_specs=(P(("dp", "mp"), None), P(("dp", "mp"), None)) + (P(),) * 12,
        check_vma=False,
    )
```
